32 devices in a mesh: sweep: 4 (over x, core), cross: 8 (over z, y).
Axes of the slice: x: 2, y: 2, z: 4, core: 2. Of those that a mesh axis runs over, the one named last changes fastest.
Arguments:
- right_sides: bfloat16 [16, 64, 32, 135], P('sweep', 'cross'), may hold values from -0.099609375 to 0.099609375
- initial: bfloat16 [16, 64, 32, 135], P('sweep', 'cross'), may hold values from -0.099609375 to 0.099609375
- inverse_blocks: bfloat16 [16, 64, 135, 135], P('sweep', 'cross'), may hold values from -0.5 to 0.5
- couplings: bfloat16 [16, 64, 6, 45, 135], P('sweep', 'cross'), may hold values from -0.875 to 0.875
- neighbours: int32 [64, 4], P('cross'), may hold values from 0 to 63, as said below
Outputs:
- result: bfloat16 [16, 64, 32, 135], P('sweep', 'cross')
The draws below stay inside these ranges and needn't reach their ends.
Inputs may be any that keep to these rules, and one draw needn't show every extreme that they name: `neighbours`: columns are numbered device by device along cross, 8 to a device. For a column with local index l on cross device k: face b- names column l of device k - 1 and face b+ column l of device k + 1 (cyclically); face c- names a column of device k - 1 or k, face c+ one of device k or k + 1.
All inputs are finite; a program needn't handle non-finite values.
Results may differ from the reference program's by a relative error of at most 0.029.
Values may be sent and summed in bfloat16 or wider, within the bound.
No kernel may reach another device: no remote copies, remote signals or barrier semaphores. Data moves between devices by JAX's collectives and lax.ppermute only.
A program may use at most 64 MiB of HBM per device.

```python
import jax
import jax.numpy as jnp
from jax import lax

NU = 135
NT = 45
R = 32
CC = 8
NPLANES = 16
NCOL = 64


def draw_neighbours(key, part):
    column = jnp.arange(NCOL, dtype=jnp.int32)
    device = column // CC
    key_one, key_two, key_three, key_four = jax.random.split(key, 4)
    face_zero = (column - CC) % NCOL
    face_one = (column + CC) % NCOL
    pick_two = jax.random.randint(key_one, (NCOL,), 0, CC, dtype=jnp.int32)
    step_two = jax.random.randint(key_two, (NCOL,), 0, 2, dtype=jnp.int32)
    pick_three = jax.random.randint(key_three, (NCOL,), 0, CC, dtype=jnp.int32)
    step_three = jax.random.randint(key_four, (NCOL,), 0, 2, dtype=jnp.int32)
    face_two = ((device - step_two) * CC + pick_two) % NCOL
    face_three = ((device + step_three) * CC + pick_three) % NCOL
    return jnp.stack([face_zero, face_one, face_two, face_three], axis=1).astype(jnp.int32)


def levels(stream_key, extent, cuts, smallest, largest):
    factor_of, own = 1.0, jax.random.fold_in(stream_key, 6)
    for dim, blocks in cuts:
        heights = jnp.exp(jax.random.uniform(jax.random.fold_in(own, dim), (blocks,), jnp.float32, smallest / len(cuts), largest / len(cuts)))
        factor_of = factor_of * jnp.repeat(heights, extent[dim] // blocks).reshape([-1 if axis == dim else 1 for axis in range(len(extent))])
    return factor_of


def bell_draw(stream_key, extent, spread, bound, cuts=(), held_as=jnp.bfloat16):
    entries = spread * jax.random.normal(stream_key, extent, jnp.float32)
    if cuts:
        entries = entries * levels(stream_key, extent, cuts, -0.22, 0.18)
    return jnp.clip(entries, -bound, bound).astype(held_as)


def setup_inputs(seed: int = 0) -> dict:
    key_list = jax.random.split(jax.random.key(seed), 6)
    right_sides = jnp.clip(jax.random.uniform(key_list[0], (NPLANES, NCOL, R, NU), jnp.float32, -0.099609375, 0.099609375) * levels(key_list[0], (NPLANES, NCOL, R, NU), ((0, 4), (1, 8)), -0.4, 0.0), -0.099609375, 0.099609375).astype(jnp.bfloat16)
    initial = jnp.clip(jax.random.uniform(key_list[1], (NPLANES, NCOL, R, NU), jnp.float32, -0.099609375, 0.099609375) * levels(key_list[1], (NPLANES, NCOL, R, NU), ((0, 4), (1, 8)), -0.4, 0.0), -0.099609375, 0.099609375).astype(jnp.bfloat16)
    inverse_blocks = bell_draw(key_list[2], (NPLANES, NCOL, NU, NU), (NU * 10 // 9) ** -0.5, 0.5, ((0, 4), (1, 8)))
    couplings = bell_draw(key_list[3], (NPLANES, NCOL, 6, NT, NU), (NT + 5) ** -0.5, 0.875, ((0, 4), (1, 8)))
    neighbours = draw_neighbours(jax.random.fold_in(key_list[5], 71), 0)
    return {"right_sides": right_sides, "initial": initial, "inverse_blocks": inverse_blocks, "couplings": couplings, "neighbours": neighbours}


CROSS_FACES = ((1, 2), (1, 0), (2, 2), (2, 0))


def face_trace(field, axis_place, which):
    lead = field.shape[:-1]
    cube = field.reshape(lead + (5, 3, 3, 3))
    picked = lax.index_in_dim(cube, which, cube.ndim - 3 + axis_place, keepdims=False)
    return picked.reshape(lead + (45,))


def apply_face(coupling, traces):
    return jnp.einsum('cti,crt->cri', coupling.astype(jnp.float32), traces.astype(jnp.float32))


def plane_cross(old_plane, coupling, neighbours):
    total = jnp.zeros(old_plane.shape, jnp.float32)
    for face, (axis_place, which) in enumerate(CROSS_FACES):
        beside = old_plane[neighbours[:, face]]
        total = total + apply_face(coupling[:, 2 + face], face_trace(beside, axis_place, which))
    return total


def solve_plane(inverse, total):
    residue = total.astype(jnp.bfloat16)
    solved = jnp.einsum('cij,crj->cri', inverse.astype(jnp.float32), residue.astype(jnp.float32))
    return solved.astype(jnp.bfloat16)


def reference(right_sides, initial, inverse_blocks, couplings, neighbours):
    zero_plane = jnp.zeros_like(initial[0])
    upper_source = jnp.concatenate([initial[1:], zero_plane[None]], 0)

    def forward(previous, inputs):
        rhs_plane, inverse, coupling, old_plane, upper_plane = inputs
        total = rhs_plane.astype(jnp.float32) - plane_cross(old_plane, coupling, neighbours)
        total = total - apply_face(coupling[:, 1], face_trace(upper_plane, 0, 0))
        total = total - apply_face(coupling[:, 0], face_trace(previous, 0, 2))
        solved = solve_plane(inverse, total)
        return solved, solved

    _unused, middle = lax.scan(forward, zero_plane, (right_sides, inverse_blocks, couplings, initial, upper_source))
    lower_source = jnp.concatenate([zero_plane[None], middle[:-1]], 0)

    def backward(following, inputs):
        rhs_plane, inverse, coupling, mid_plane, lower_plane = inputs
        total = rhs_plane.astype(jnp.float32) - plane_cross(mid_plane, coupling, neighbours)
        total = total - apply_face(coupling[:, 0], face_trace(lower_plane, 0, 2))
        total = total - apply_face(coupling[:, 1], face_trace(following, 0, 0))
        solved = solve_plane(inverse, total)
        return solved, solved

    _unused, result = lax.scan(backward, zero_plane, (right_sides, inverse_blocks, couplings, middle, lower_source), reverse=True)
    return result
```

```python
import functools

import jax
import jax.numpy as jnp
import numpy as np
from jax import lax
from jax.experimental import pallas as pl
from jax.experimental.pallas import tpu as pltpu
from jax.sharding import PartitionSpec as P

BF = jnp.bfloat16
F32 = jnp.float32
NT = 45
FACE = 48
SLOT = 64
ROWS = 3 * FACE
SHARED = 80
MIB = 1 << 20


def natural(v, a, b, c):
    return v * 27 + a * 9 + b * 3 + c


def inner(v, a, b, c):
    return a * FACE + v * 9 + b * 3 + c


NODES = [(v, a, b, c) for v in range(5) for a in range(3) for b in range(3) for c in range(3)]


def face_nodes(place, which):
    return [n for n in NODES if n[1 + place] == which]


def union_nodes(which):
    return [n for n in NODES if n[2] == which or n[3] == which]


def table(height, width, rows, column_of, value=1.0):
    out = np.zeros((height, width), np.float32)
    for row, node in rows:
        out[row, column_of(*node)] = value
    return out


def block(nodes, start=0):
    return [(start + i, n) for i, n in enumerate(nodes)]


def send_table(width, column_of):
    rows = block(union_nodes(2)) + block(union_nodes(0), SHARED)
    return table(2 * SHARED, width, rows, column_of)


def own_table(width, column_of):
    rows = block(face_nodes(2, 2)) + block(face_nodes(2, 0), FACE)
    return table(2 * FACE, width, rows, column_of)


def receive_table(which):
    place = {n: i for i, n in enumerate(union_nodes(which))}
    rows = block(face_nodes(1, which)) + block(face_nodes(2, which), FACE)
    return table(2 * FACE, SHARED, rows, lambda *n: place[n])


def mm(a, b):
    return lax.dot_general(a, b, (((1,), (0,)), ((), ())), preferred_element_type=F32)


def mt(a, b):
    return lax.dot_general(a, b, (((1,), (1,)), ((), ())), preferred_element_type=F32)


def split_lanes(value, width):
    lanes = value.shape[1]
    value = value.astype(F32)
    owner = lax.broadcasted_iota(jnp.int32, value.shape, 1) // width
    pad = jnp.zeros((SLOT - FACE, lanes), BF)
    parts = []
    for c in range(lanes // width):
        parts += [jnp.where(owner == c, value, 0.0).astype(BF), pad]
    return jnp.concatenate(parts, 0)


def own_lanes(values, width):
    owner = lax.broadcasted_iota(jnp.int32, values[0].shape, 1) // width
    out = values[0]
    for c in range(1, len(values)):
        out = jnp.where(owner == c, values[c], out)
    return out


def one_hot(source, start, height):
    row = lax.broadcasted_iota(jnp.int32, (height, source.shape[1]), 0) + start
    return jnp.where(row == source, 1.0, 0.0).astype(BF)


def chain_step(matrix, trace, rhs):
    half = trace.shape[1] // 2
    return jnp.concatenate(
        [mm(matrix[h], split_lanes(trace[:, h * half : (h + 1) * half], rhs)) for h in range(2)], 1
    )


def first_kernel(initial, send, first_face, up, down, above):
    planes, columns, rhs, width = initial.shape
    for p in range(planes):
        x = initial[p].reshape(columns * rhs, width)
        out = mt(send[...], x).astype(BF)
        up[p] = out[:SHARED]
        down[p] = out[SHARED:]
        if p == 0:
            above[...] = mt(first_face[...], x).astype(BF)


def weight_kernel(
    inverse, couplings, right, initial, source, perm, own_sel, first_face,
    known0, known1, known2, lower0, lower1, lower2, upper0, upper1, upper2, base0, base1, base2,
    own, cum_f, cum_b, faces, prev, backs,
):
    known, lower, upper = (known0, known1, known2), (lower0, lower1, lower2), (upper0, upper1, upper2)
    base = (base0, base1, base2)
    p = pl.program_id(0)
    planes, columns, rhs, width = initial.shape
    half = columns // 2

    @pl.when(p == 0)
    def _():
        faces[...] = jnp.zeros(faces.shape, BF)

    pairs_lower, pairs_upper, bases = [], [], []
    rights = [right[0, h * half : (h + 1) * half].reshape(half * rhs, width) for h in range(2)]
    lane = lax.broadcasted_iota(jnp.int32, (ROWS, 2 * SLOT), 1)
    before = None
    for c in range(columns):
        solve = mm(perm[...], inverse[0, c]).astype(BF)
        for f in range(4):
            faces[c, f * FACE : f * FACE + NT] = couplings[0, c, 2 + f]
        faces[c, 4 * FACE : 4 * FACE + NT] = couplings[0, c, 1]
        faces[c, 256 : 256 + NT] = couplings[0, c, 0]
        faces[c, 256 + SLOT : 256 + SLOT + NT] = couplings[0, c, 1]
        all_known = mt(solve, faces[c, :256]).astype(BF)
        for a in range(3):
            known[a][0, c] = all_known[a * FACE : (a + 1) * FACE]
        both = mt(solve, faces[c, 256:])
        if c % 2 == 0:
            before = both
        else:
            pairs_lower.append(jnp.where(lane < SLOT, before, pltpu.roll(both, SLOT, 1)).astype(BF))
            pairs_upper.append(jnp.where(lane < SLOT, pltpu.roll(before, SLOT, 1), both).astype(BF))
        bases.append(mt(solve, rights[c // half]))
    for h in range(2):
        down = jnp.concatenate(pairs_lower[2 * h : 2 * h + 2], 1)
        up = jnp.concatenate(pairs_upper[2 * h : 2 * h + 2], 1)
        backs[p, h] = up[:FACE]
        here = -own_lanes(bases[h * half : (h + 1) * half], rhs)
        for a in range(3):
            lower[a][0, h] = down[a * FACE : (a + 1) * FACE]
            upper[a][0, h] = up[a * FACE : (a + 1) * FACE]
            base[a][0, :, h * half * rhs : (h + 1) * half * rhs] = here[a * FACE : (a + 1) * FACE]
        step = down[2 * FACE :]

        @pl.when(p == 0)
        def _():
            prev[h] = step.astype(F32)

        @pl.when(p > 0)
        def _():
            prev[h] = mm(step, split_lanes(prev[h], SLOT))

        cum_f[0, h] = prev[h].astype(BF)

    x = initial[p].reshape(columns * rhs, width)
    mine = mt(own_sel[...], x).astype(BF)
    size = columns * rhs
    own[0, :FACE] = mm(mine[:FACE], one_hot(source[0:1], size, size)).astype(BF)
    own[0, FACE : 2 * FACE] = mm(mine[FACE:], one_hot(source[1:2], 0, size)).astype(BF)
    beyond = initial[jnp.minimum(p + 1, planes - 1)].reshape(columns * rhs, width)
    own[0, 2 * FACE :] = mt(first_face[...], beyond).astype(BF)

    @pl.when(p == planes - 1)
    def _():
        for h in range(2):
            total = backs[planes - 1, h].astype(F32)
            cum_b[planes - 1, h] = total.astype(BF)
            for q in range(planes - 2, -1, -1):
                total = mm(backs[q, h], split_lanes(total, SLOT))
                cum_b[q, h] = total.astype(BF)


def gathered(received_up, received_down, own, p, up_sel, down_sel, low_pick, high_pick):
    low = mm(up_sel, received_up[p]).astype(BF)
    high = mm(down_sel, received_down[p]).astype(BF)
    c_low = mm(low[FACE:], low_pick).astype(BF) + own[p, :FACE]
    c_high = mm(high[FACE:], high_pick).astype(BF) + own[p, FACE : 2 * FACE]
    return [low[:FACE], high[:FACE], c_low, c_high]


def known_part(known_c, operand, columns, rhs):
    half = columns // 2
    out = []
    for h in range(2):
        side = operand[:, h * half * rhs : (h + 1) * half * rhs]
        out.append(own_lanes([mm(known_c(h * half + c), side) for c in range(half)], rhs))
    return jnp.concatenate(out, 1)


def forward_chain_kernel(
    up, down, above, own, source, up_sel, down_sel, known, lower, base, operand, part, traces, last, *, rhs
):
    planes = up.shape[0]
    columns = known.shape[1]
    size = columns * rhs
    low_pick = one_hot(source[0:1], 0, size)
    high_pick = one_hot(source[1:2], size, size)
    starts = []
    for p in range(planes):
        parts = gathered(up, down, own, p, up_sel[...], down_sel[...], low_pick, high_pick)
        parts.append(own[p, 2 * FACE :] if p + 1 < planes else above[...])
        parts.append(jnp.zeros((256 - 5 * FACE, size), BF))
        whole = jnp.concatenate(parts, 0)
        operand[p] = whole
        starts.append(base[p] + known_part(lambda c: known[p, c], whole, columns, rhs))
    for p in range(planes):
        part[p] = starts[p]
    trace = starts[0]
    traces[0] = trace
    for p in range(1, planes):
        trace = starts[p] + chain_step(lower[p], trace, rhs)
        traces[p] = trace
    last[...] = trace.astype(BF)


def backward_chain_kernel(
    up, down, own, source, up_sel, down_sel, known, upper, base, operand, part, traces, last, *, rhs
):
    planes = up.shape[0]
    columns = known.shape[1]
    size = columns * rhs
    low_pick = one_hot(source[0:1], 0, size)
    high_pick = one_hot(source[1:2], size, size)
    starts = []
    for p in range(planes):
        parts = gathered(up, down, own, p, up_sel[...], down_sel[...], low_pick, high_pick)
        parts.append(jnp.zeros((256 - 4 * FACE, size), BF))
        whole = jnp.concatenate(parts, 0)
        operand[p] = whole
        starts.append(base[p] + known_part(lambda c: known[p, c], whole, columns, rhs))
    for p in range(planes):
        part[p] = starts[p]
    trace = starts[planes - 1]
    traces[planes - 1] = trace
    for p in range(planes - 2, -1, -1):
        trace = starts[p] + chain_step(upper[p], trace, rhs)
        traces[p] = trace
    last[...] = trace.astype(BF)


def base_kernel(known_one, known_two, operand, base_one, base_two, one, two, *, rhs):
    planes, columns = known_one.shape[:2]
    for p in range(planes):
        for known, base, out in ((known_one, base_one, one), (known_two, base_two, two)):
            out[p] = base[p] + known_part(lambda c: known[p, c], operand[p], columns, rhs)


def incoming(one, two, three, first, second, rhs):
    trace = two[...].astype(F32) + chain_step(second, three[...].astype(F32), rhs)
    return one[...].astype(F32) + chain_step(first, trace, rhs)


def forward_finish_kernel(
    one, two, three, first, second, cum, traces, part0, part1, part2, lower0, lower1, lower2, send, middle, change, up, down, *, rhs
):
    planes = traces.shape[0]
    entry = incoming(one, two, three, first, second, rhs)
    trace = entry
    for p in range(planes):
        matrix = [jnp.concatenate([x[p, h] for x in (lower0, lower1, lower2)], 0) for h in range(2)]
        delta = chain_step(matrix, trace, rhs)
        whole = jnp.concatenate([x[p] for x in (part0, part1, part2)], 0) + delta
        change[p] = delta
        whole = whole.astype(BF)
        middle[p] = whole
        out = mm(send[...], whole).astype(BF)
        up[p] = out[:SHARED]
        down[p] = out[SHARED:]
        if p + 1 < planes:
            trace = traces[p] + chain_step(cum[p], entry, rhs)


def middle_kernel(middle, change, base0, base1, base2, source, own_sel, own, out0, out1, out2):
    planes = middle.shape[0]
    size = middle.shape[2]
    low_pick = one_hot(source[0:1], size, size)
    high_pick = one_hot(source[1:2], 0, size)
    for p in range(planes):
        mine = mm(own_sel[...], middle[p]).astype(BF)
        own[p, :FACE] = mm(mine[:FACE], low_pick).astype(BF)
        own[p, FACE:] = mm(mine[FACE:], high_pick).astype(BF)
        for a, (base, out) in enumerate(((base0, out0), (base1, out1), (base2, out2))):
            out[p] = base[p] + change[p, a * FACE : (a + 1) * FACE]


def backward_finish_kernel(
    one, two, three, first, second, cum, traces, part0, part1, part2, upper0, upper1, upper2, back, result, *, rhs
):
    planes = traces.shape[0]
    entry = incoming(one, two, three, first, second, rhs)
    size = entry.shape[1]
    row = lax.broadcasted_iota(jnp.int32, (size, size), 0)
    column = lax.broadcasted_iota(jnp.int32, (size, size), 1)
    unit = jnp.where(row == column, 1.0, 0.0).astype(BF)
    columns, _, width = result.shape[1:]
    for p in range(planes - 1, -1, -1):
        trace = entry if p + 1 == planes else traces[p + 1] + chain_step(cum[p + 1], entry, rhs)
        matrix = [jnp.concatenate([x[p, h] for x in (upper0, upper1, upper2)], 0) for h in range(2)]
        whole = jnp.concatenate([x[p] for x in (part0, part1, part2)], 0) + chain_step(matrix, trace, rhs)
        turned = mm(back[...], whole.astype(BF)).astype(BF)
        result[p] = mt(unit, turned).astype(BF).reshape(columns, rhs, width)


def cost(flops, nbytes):
    return pl.CostEstimate(flops=int(flops), bytes_accessed=int(nbytes), transcendentals=0)


def call(kernel, outs, operands, name, flops=2e8):
    shapes = [jax.ShapeDtypeStruct(s, d) for s, d in outs]
    nbytes = sum(x.size * x.dtype.itemsize for x in list(operands) + shapes)
    return pl.pallas_call(
        kernel,
        out_shape=shapes,
        in_specs=[pl.BlockSpec(memory_space=pltpu.VMEM)] * len(operands),
        out_specs=[pl.BlockSpec(memory_space=pltpu.VMEM)] * len(shapes),
        compiler_params=pltpu.CompilerParams(vmem_limit_bytes=24 * MIB),
        cost_estimate=cost(flops, nbytes),
        name=name,
    )(*operands)


def weights(inverse, couplings, right, initial, source, perm, own_sel, first_face):
    planes, columns, rhs, width = initial.shape
    size = columns * rhs
    whole = lambda x: pl.BlockSpec(x.shape, lambda p, n=x.ndim: (0,) * n)
    lead = lambda s: pl.BlockSpec((1,) + s[1:], lambda p, n=len(s): (p,) + (0,) * (n - 1))
    known = (planes, columns, FACE, 256)
    pack = (planes, 2, FACE, 256)
    base = (planes, FACE, size)
    own = (planes, ROWS, size)
    outs = [(known, BF)] * 3 + [(pack, BF)] * 6 + [(base, F32)] * 3 + [(own, BF), (pack, BF), (pack, BF)]
    outs = [jax.ShapeDtypeStruct(s, d) for s, d in outs]
    return pl.pallas_call(
        weight_kernel,
        grid=(planes,),
        out_shape=outs,
        in_specs=[lead(x.shape) for x in (inverse, couplings, right)]
        + [whole(x) for x in (initial, source, perm, own_sel, first_face)],
        out_specs=[lead(x.shape) for x in outs[:-1]] + [whole(outs[-1])],
        scratch_shapes=[
            pltpu.VMEM((columns, 256 + 2 * SLOT, width), BF),
            pltpu.VMEM((2, FACE, 256), F32),
            pltpu.VMEM((planes, 2, FACE, 256), BF),
        ],
        compiler_params=pltpu.CompilerParams(
            vmem_limit_bytes=24 * MIB, dimension_semantics=("arbitrary",)
        ),
        cost_estimate=cost(6e9, 12e6),
        name="weights",
    )(inverse, couplings, right, initial, source, perm, own_sel, first_face)


def ring(x, axis, by):
    n = lax.axis_size(axis)
    return lax.ppermute(x, axis, [(i, (i + by) % n) for i in range(n)])


def shift(x, axis, by):
    n = lax.axis_size(axis)
    return lax.ppermute(x, axis, [(i, i + by) for i in range(n) if 0 <= i + by < n])


def local(right_sides, initial, inverse_blocks, couplings, neighbours):
    planes, columns, rhs, width = initial.shape
    size = columns * rhs
    const = lambda x: jnp.asarray(x, BF)
    send_nat = const(send_table(width, natural))
    send_in = const(send_table(ROWS, inner))
    own_nat = const(own_table(width, natural))
    own_in = const(own_table(ROWS, inner))
    first_face = const(table(FACE, width, block(face_nodes(0, 0)), natural))
    perm = const(table(ROWS, width, [(inner(*n), n) for n in NODES], natural, -1.0))
    back = const(table(width, ROWS, [(natural(*n), n) for n in NODES], inner))
    up_sel = const(receive_table(2))
    down_sel = const(receive_table(0))

    place = lax.axis_index("cross")
    total = columns * lax.axis_size("cross")
    low = (neighbours[:, 2] - (place - 1) * columns) % total
    high = (neighbours[:, 3] - place * columns) % total
    lane = jnp.arange(size, dtype=jnp.int32)
    which = jnp.stack([low, high])
    source = jnp.repeat(which, rhs, axis=1) * rhs + lane[None] % rhs

    share = (planes, SHARED, size)
    up, down, above = call(
        first_kernel,
        [(share, BF), (share, BF), ((FACE, size), BF)],
        (initial, send_nat, first_face),
        "initial_traces",
    )
    up, down, above, initial = lax.optimization_barrier((up, down, above, initial))
    from_low = ring(up, "cross", 1)
    from_high = ring(down, "cross", -1)
    from_above = shift(above, "sweep", -1)
    *parts, own, cum_f, cum_b = weights(
        inverse_blocks, couplings, right_sides, initial, source, perm, own_nat, first_face
    )
    known, lower, upper, base = parts[:3], parts[3:6], parts[6:9], parts[9:]
    pass_f, pass_b = cum_f[planes - 1], cum_b[0]
    first_f, second_f = shift(pass_f, "sweep", 1), shift(pass_f, "sweep", 2)
    first_b, second_b = shift(pass_b, "sweep", -1), shift(pass_b, "sweep", -2)

    trace = (planes, FACE, size)
    deep = (planes, ROWS, size)
    chain_outs = [((planes, 256, size), BF), (trace, F32), (trace, F32), ((FACE, size), BF)]
    operand, part2, traces, last = call(
        functools.partial(forward_chain_kernel, rhs=rhs),
        chain_outs,
        (from_low, from_high, from_above, own, source, up_sel, down_sel, known[2], lower[2], base[2]),
        "forward_chain",
    )
    one, two, three = (shift(last, "sweep", by) for by in (1, 2, 3))
    part0, part1 = call(
        functools.partial(base_kernel, rhs=rhs),
        [(trace, F32)] * 2,
        (known[0], known[1], operand, base[0], base[1]),
        "forward_base",
        2e9,
    )
    middle, change, up, down = call(
        functools.partial(forward_finish_kernel, rhs=rhs),
        [(deep, BF), (deep, F32), (share, BF), (share, BF)],
        (one, two, three, first_f, second_f, cum_f, traces, part0, part1, part2, *lower, send_in),
        "forward_finish",
    )
    from_low = ring(up, "cross", 1)
    from_high = ring(down, "cross", -1)
    own, *base = call(
        middle_kernel,
        [((planes, 2 * FACE, size), BF)] + [(trace, F32)] * 3,
        (middle, change, *base, source, own_in),
        "middle",
        2e9,
    )
    operand, part0, traces, last = call(
        functools.partial(backward_chain_kernel, rhs=rhs),
        chain_outs,
        (from_low, from_high, own, source, up_sel, down_sel, known[0], upper[0], base[0]),
        "backward_chain",
    )
    one, two, three = (shift(last, "sweep", -by) for by in (1, 2, 3))
    part1, part2 = call(
        functools.partial(base_kernel, rhs=rhs),
        [(trace, F32)] * 2,
        (known[1], known[2], operand, base[1], base[2]),
        "backward_base",
        2e9,
    )
    (result,) = call(
        functools.partial(backward_finish_kernel, rhs=rhs),
        [(right_sides.shape, BF)],
        (one, two, three, first_b, second_b, cum_b, traces, part0, part1, part2, *upper, back),
        "backward_finish",
    )
    return result


def solution(mesh):
    return jax.shard_map(
        local,
        mesh=mesh,
        in_specs=(
            P("sweep", "cross", None, None),
            P("sweep", "cross", None, None),
            P("sweep", "cross", None, None),
            P("sweep", "cross", None, None, None),
            P("cross", None),
        ),
        out_specs=P("sweep", "cross", None, None),
        check_vma=False,
    )
```

```python
import functools

import jax
import jax.numpy as jnp
import numpy as np
from jax import lax
from jax.experimental import pallas as pl
from jax.experimental.pallas import tpu as pltpu
from jax.sharding import PartitionSpec as P

BF = jnp.bfloat16
F32 = jnp.float32
NT = 45
FACE = 48
SLOT = 64
ROWS = 3 * FACE
SHARED = 80
MIB = 1 << 20


def natural(v, a, b, c):
    return v * 27 + a * 9 + b * 3 + c


def inner(v, a, b, c):
    return a * FACE + v * 9 + b * 3 + c


NODES = [(v, a, b, c) for v in range(5) for a in range(3) for b in range(3) for c in range(3)]


def face_nodes(place, which):
    return [n for n in NODES if n[1 + place] == which]


def union_rows(which):
    others = [b for b in range(3) if b != which]
    spots = [(which, c) for c in range(3)] + [(b, which) for b in others]
    return [
        (v * 16 + a * 5 + j, (v, a, b, c)) for v in range(5) for a in range(3) for j, (b, c) in enumerate(spots)
    ]


def table(height, width, rows, column_of, value=1.0):
    out = np.zeros((height, width), np.float32)
    for row, node in rows:
        out[row, column_of(*node)] = value
    return out


def block(nodes, start=0):
    return [(start + i, n) for i, n in enumerate(nodes)]


def send_table(width, column_of):
    rows = union_rows(2) + [(SHARED + i, n) for i, n in union_rows(0)]
    return table(2 * SHARED, width, rows, column_of)


def own_table(width, column_of):
    rows = block(face_nodes(2, 2)) + block(face_nodes(2, 0), FACE)
    return table(2 * FACE, width, rows, column_of)


def receive_table(which):
    place = {n: i for i, n in union_rows(which)}
    rows = block(face_nodes(1, which)) + block(face_nodes(2, which), FACE)
    return table(2 * FACE, SHARED, rows, lambda *n: place[n])


def mm(a, b):
    return lax.dot_general(a, b, (((1,), (0,)), ((), ())), preferred_element_type=F32)


def mt(a, b):
    return lax.dot_general(a, b, (((1,), (1,)), ((), ())), preferred_element_type=F32)


def split_lanes(value, width):
    lanes = value.shape[1]
    value = value.astype(F32)
    owner = lax.broadcasted_iota(jnp.int32, value.shape, 1) // width
    pad = jnp.zeros((SLOT - FACE, lanes), BF)
    parts = []
    for c in range(lanes // width):
        parts += [jnp.where(owner == c, value, 0.0).astype(BF), pad]
    return jnp.concatenate(parts, 0)


def own_lanes(values, width):
    owner = lax.broadcasted_iota(jnp.int32, values[0].shape, 1) // width
    out = values[0]
    for c in range(1, len(values)):
        out = jnp.where(owner == c, values[c], out)
    return out


def one_hot(source, start, height):
    row = lax.broadcasted_iota(jnp.int32, (height, source.shape[1]), 0) + start
    return jnp.where(row == source, 1.0, 0.0).astype(BF)


def chain_step(matrix, trace, rhs):
    half = trace.shape[1] // 2
    return jnp.concatenate(
        [mm(matrix[h], split_lanes(trace[:, h * half : (h + 1) * half], rhs)) for h in range(2)], 1
    )


def shared_target(row, which):
    v, k = row // 16, row % 16
    a = k // 5
    j = k % 5
    b = jnp.where(j < 3, which, j - 3 if which == 2 else j - 2)
    c = jnp.where(j < 3, j, which)
    return jnp.where(k < 15, v * 27 + a * 9 + b * 3 + c, -1)


def picks(target, width):
    lane = lax.broadcasted_iota(jnp.int32, (target.shape[0], width), 1)
    return jnp.where(lane == target, 1.0, 0.0).astype(BF)


def rows_of(height):
    return lax.broadcasted_iota(jnp.int32, (height, 1), 0)


def first_target(row):
    return jnp.where(row < NT, row // 9 * 27 + row % 9, -1)


def c_target(row, which):
    return jnp.where(row < NT, row * 3 + which, -1)


def sources(neighbours, columns, rhs):
    place = lax.axis_index("cross")
    total = columns * lax.axis_size("cross")
    lane = lax.broadcasted_iota(jnp.int32, (1, columns * rhs), 1)
    out = []
    for face, first in ((2, place - 1), (3, place)):
        which = jnp.zeros_like(lane)
        for c in range(columns):
            at = lax.rem(neighbours[face, c] - first * columns + 2 * total, total)
            which = jnp.where(lane // rhs == c, at, which)
        out.append(which * rhs + lane % rhs)
    return out


def first_kernel(initial, up, down, above):
    planes, columns, rhs, width = initial.shape
    shared = rows_of(SHARED)
    tables = [picks(shared_target(shared, which), width) for which in (2, 0)]
    for p in range(planes):
        x = initial[p].reshape(columns * rhs, width)
        up[p] = mt(tables[0], x).astype(BF)
        down[p] = mt(tables[1], x).astype(BF)
        if p == 0:
            above[...] = mt(picks(first_target(rows_of(FACE)), width), x).astype(BF)


def turned(rows):
    pad = jnp.zeros((FACE - NT,) + rows.shape[1:], rows.dtype)
    return jnp.swapaxes(jnp.concatenate([rows, pad], 0), 0, 1)


def weight_kernel(
    inverse, couplings, right, initial, neighbours,
    known0, known1, known2, lower0, lower1, lower2, upper0, upper1, upper2, base0, base1, base2,
    fore0, fore1, fore2, own, cum_f, cum_b, passes, solves, faces, prev, backs, tables,
):
    known, lower, upper = (known0, known1, known2), (lower0, lower1, lower2), (upper0, upper1, upper2)
    base, fore = (base0, base1, base2), (fore0, fore1, fore2)
    p = pl.program_id(0)
    planes, columns, rhs, width = initial.shape
    size = columns * rhs
    half = columns // 2

    @pl.when(p == 0)
    def _():
        faces[...] = jnp.zeros(faces.shape, BF)
        tables[:FACE] = picks(c_target(rows_of(FACE), 2), width)
        tables[FACE : 2 * FACE] = picks(c_target(rows_of(FACE), 0), width)
        tables[2 * FACE :] = picks(first_target(rows_of(FACE)), width)

    for a in range(3):
        rows = [inverse[0, v * 27 + a * 9 : v * 27 + a * 9 + 9] for v in range(5)]
        solves[:, a * FACE : (a + 1) * FACE] = -turned(jnp.concatenate(rows, 0))
    for f in range(4):
        faces[:, f * FACE : (f + 1) * FACE] = turned(couplings[0, 2 + f])
    faces[:, 4 * FACE : 4 * FACE + rhs] = right[0]
    faces[:, 256 : 256 + FACE] = turned(couplings[0, 0])
    faces[:, 256 + SLOT : 256 + SLOT + FACE] = turned(couplings[0, 1])

    pairs_lower, pairs_upper, bases = [], [], []
    lane = lax.broadcasted_iota(jnp.int32, (ROWS, 2 * SLOT), 1)
    before = None
    for c in range(columns):
        solve = solves[c]
        all_known = mt(solve, faces[c, :256])
        side = all_known[:, 128:]
        move = (c % half * rhs - (4 * FACE - 128)) % 128
        bases.append(pltpu.roll(side, move, 1) if move else side)
        all_known = all_known.astype(BF)
        for a in range(3):
            known[a][0, c] = all_known[a * FACE : (a + 1) * FACE]
        both = mt(solve, faces[c, 256:])
        if c % 2 == 0:
            before = both
        else:
            pairs_lower.append(jnp.where(lane < SLOT, before, pltpu.roll(both, SLOT, 1)).astype(BF))
            pairs_upper.append(jnp.where(lane < SLOT, pltpu.roll(before, SLOT, 1), both).astype(BF))
    x = initial[p].reshape(size, width)
    beyond = initial[jnp.minimum(p + 1, planes - 1)].reshape(size, width)
    after = jnp.where(p + 1 < planes, mt(tables[2 * FACE :], beyond), 0.0)
    for h in range(2):
        lanes = slice(h * half * rhs, (h + 1) * half * rhs)
        down = jnp.concatenate(pairs_lower[2 * h : 2 * h + 2], 1)
        up = jnp.concatenate(pairs_upper[2 * h : 2 * h + 2], 1)
        backs[p, h] = up[:FACE]
        here = -own_lanes(bases[h * half : (h + 1) * half], rhs)
        there = here + mm(up, split_lanes(after[:, lanes], rhs))
        for a in range(3):
            rows = slice(a * FACE, (a + 1) * FACE)
            lower[a][0, h] = down[rows]
            upper[a][0, h] = up[rows]
            base[a][0, :, lanes] = here[rows]
            fore[a][0, :, lanes] = there[rows]
        step = down[2 * FACE :]

        @pl.when(p == 0)
        def _():
            prev[h] = step.astype(F32)

        @pl.when(p > 0)
        def _():
            prev[h] = mm(step, split_lanes(prev[h], SLOT))

        cum_f[0, h] = prev[h].astype(BF)

    mine = mt(tables[: 2 * FACE], x).astype(BF)
    source = sources(neighbours, columns, rhs)
    own[0, :FACE] = mm(mine[:FACE], one_hot(source[0], size, size)).astype(BF)
    own[0, FACE:] = mm(mine[FACE:], one_hot(source[1], 0, size)).astype(BF)

    @pl.when(p == planes - 1)
    def _():
        for h in range(2):
            passes[0, h] = prev[h].astype(BF)
            total = backs[planes - 1, h].astype(F32)
            cum_b[planes - 1, h] = total.astype(BF)
            for q in range(planes - 2, -1, -1):
                total = mm(backs[q, h], split_lanes(total, SLOT))
                cum_b[q, h] = total.astype(BF)
            passes[1, h] = total.astype(BF)


def gathered(received_up, received_down, own, p, up_sel, down_sel, low_pick, high_pick):
    low = mm(up_sel, received_up[p]).astype(BF)
    high = mm(down_sel, received_down[p]).astype(BF)
    c_low = mm(low[FACE:], low_pick).astype(BF) + own[p, :FACE]
    c_high = mm(high[FACE:], high_pick).astype(BF) + own[p, FACE : 2 * FACE]
    return [low[:FACE], high[:FACE], c_low, c_high]


def known_part(known_c, operand, columns, rhs):
    half = columns // 2
    out = []
    for h in range(2):
        side = operand[:, h * half * rhs : (h + 1) * half * rhs]
        out.append(own_lanes([mm(known_c(h * half + c), side) for c in range(half)], rhs))
    return jnp.concatenate(out, 1)


def chain_kernel(known, base, matrix, received, own, neighbours, outs, order, rhs, extra=None):
    up, down, up_sel, down_sel = received
    operand, part, traces, last = outs
    planes, columns = known.shape[:2]
    size = columns * rhs
    source = sources(neighbours, columns, rhs)
    low_pick = one_hot(source[0], 0, size)
    high_pick = one_hot(source[1], size, size)
    starts = {}
    for p in order:
        parts = gathered(up, down, own, p, up_sel[...], down_sel[...], low_pick, high_pick)
        parts.append(jnp.zeros((256 - 4 * FACE, size), BF))
        whole = jnp.concatenate(parts, 0)
        operand[p] = whole
        starts[p] = base[p] + known_part(lambda c: known[p, c], whole, columns, rhs)
        if extra is not None and p == planes - 1:
            starts[p] = starts[p] + chain_step(extra[0][p], extra[1][...], rhs)
        part[p] = starts[p]
    trace = None
    for p in order:
        trace = starts[p] if trace is None else starts[p] + chain_step(matrix[p], trace, rhs)
        traces[p] = trace
    for i in range(last.shape[0]):
        last[i] = trace.astype(BF)


def forward_chain_kernel(
    up, down, above, own, neighbours, up_sel, down_sel, known, lower, upper, base, *outs, rhs
):
    order = range(up.shape[0])
    received = (up, down, up_sel, down_sel)
    chain_kernel(known, base, lower, received, own, neighbours, outs, order, rhs, (upper, above))


def backward_chain_kernel(up, down, own, neighbours, up_sel, down_sel, known, upper, base, *outs, rhs):
    order = range(up.shape[0] - 1, -1, -1)
    chain_kernel(known, base, upper, (up, down, up_sel, down_sel), own, neighbours, outs, order, rhs)


def base_kernel(known_one, known_two, operand, base_one, base_two, *rest, rhs):
    planes, columns = known_one.shape[:2]
    extra, (one, two) = rest[:-2], rest[-2:]
    for p in range(planes):
        for i, (known, base, out) in enumerate(((known_one, base_one, one), (known_two, base_two, two))):
            value = base[p] + known_part(lambda c: known[p, c], operand[p], columns, rhs)
            if extra and p == planes - 1:
                value = value + chain_step(extra[1 + i][p], extra[0][...], rhs)
            out[p] = value


def incoming(last, passes, way, rhs):
    here = lax.axis_index("sweep")
    n = last.shape[0]
    trace = None
    for i in range(n - 1) if way == 0 else range(n - 1, 0, -1):
        value = last[i].astype(F32)
        if trace is None:
            trace = jnp.zeros_like(value)
        else:
            value = value + chain_step(passes[i, way], trace, rhs)
        trace = jnp.where(i < here if way == 0 else i > here, value, trace)
    return trace


def forward_finish_kernel(
    last, passes, cum, traces, part0, part1, part2, lower0, lower1, lower2, send, middle, change, up, down, *, rhs
):
    planes = traces.shape[0]
    entry = incoming(last, passes, 0, rhs)
    trace = entry
    for p in range(planes):
        matrix = [jnp.concatenate([x[p, h] for x in (lower0, lower1, lower2)], 0) for h in range(2)]
        delta = chain_step(matrix, trace, rhs)
        whole = jnp.concatenate([x[p] for x in (part0, part1, part2)], 0) + delta
        change[p] = delta
        whole = whole.astype(BF)
        middle[p] = whole
        out = mm(send[...], whole).astype(BF)
        up[p] = out[:SHARED]
        down[p] = out[SHARED:]
        if p + 1 < planes:
            trace = traces[p] + chain_step(cum[p], entry, rhs)


def middle_kernel(middle, change, base0, base1, base2, neighbours, own_sel, own, out0, out1, out2):
    planes, _, size = middle.shape
    columns = neighbours.shape[1]
    source = sources(neighbours, columns, size // columns)
    low_pick = one_hot(source[0], size, size)
    high_pick = one_hot(source[1], 0, size)
    for p in range(planes):
        mine = mm(own_sel[...], middle[p]).astype(BF)
        own[p, :FACE] = mm(mine[:FACE], low_pick).astype(BF)
        own[p, FACE:] = mm(mine[FACE:], high_pick).astype(BF)
        for a, (base, out) in enumerate(((base0, out0), (base1, out1), (base2, out2))):
            out[p] = base[p] + change[p, a * FACE : (a + 1) * FACE]


def backward_finish_kernel(
    last, passes, cum, traces, part0, part1, part2, upper0, upper1, upper2, back, result, *, rhs
):
    planes = traces.shape[0]
    entry = incoming(last, passes, 1, rhs)
    size = entry.shape[1]
    row = lax.broadcasted_iota(jnp.int32, (size, size), 0)
    column = lax.broadcasted_iota(jnp.int32, (size, size), 1)
    unit = jnp.where(row == column, 1.0, 0.0).astype(BF)
    columns, _, width = result.shape[1:]
    for p in range(planes - 1, -1, -1):
        trace = entry if p + 1 == planes else traces[p + 1] + chain_step(cum[p + 1], entry, rhs)
        matrix = [jnp.concatenate([x[p, h] for x in (upper0, upper1, upper2)], 0) for h in range(2)]
        whole = jnp.concatenate([x[p] for x in (part0, part1, part2)], 0) + chain_step(matrix, trace, rhs)
        turned = mm(back[...], whole.astype(BF)).astype(BF)
        result[p] = mt(unit, turned).astype(BF).reshape(columns, rhs, width)


def cost(flops, nbytes):
    return pl.CostEstimate(flops=int(flops), bytes_accessed=int(nbytes), transcendentals=0)


def call(kernel, outs, operands, name, flops=2e8):
    shapes = [jax.ShapeDtypeStruct(s, d) for s, d in outs]
    nbytes = sum(x.size * x.dtype.itemsize for x in list(operands) + shapes)
    return pl.pallas_call(
        kernel,
        out_shape=shapes,
        in_specs=[
            pl.BlockSpec(memory_space=pltpu.SMEM if x.dtype == jnp.int32 else pltpu.VMEM) for x in operands
        ],
        out_specs=[pl.BlockSpec(memory_space=pltpu.VMEM)] * len(shapes),
        compiler_params=pltpu.CompilerParams(vmem_limit_bytes=24 * MIB),
        cost_estimate=cost(flops, nbytes),
        name=name,
    )(*operands)


def weights(inverse, couplings, right, initial, neighbours):
    planes, columns, rhs, width = initial.shape
    size = columns * rhs
    whole = lambda x: pl.BlockSpec(x.shape, lambda p, n=x.ndim: (0,) * n)
    lead = lambda s: pl.BlockSpec((1,) + s[1:], lambda p, n=len(s): (p,) + (0,) * (n - 1))
    known = (planes, columns, FACE, 256)
    pack = (planes, 2, FACE, 256)
    base = (planes, FACE, size)
    own = (planes, 2 * FACE, size)
    outs = [(known, BF)] * 3 + [(pack, BF)] * 6 + [(base, F32)] * 6
    outs += [(own, BF), (pack, BF), (pack, BF), ((2,) + pack[1:], BF)]
    outs = [jax.ShapeDtypeStruct(s, d) for s, d in outs]
    return pl.pallas_call(
        weight_kernel,
        grid=(planes,),
        out_shape=outs,
        in_specs=[lead(x.shape) for x in (inverse, couplings, right)]
        + [whole(initial), pl.BlockSpec(memory_space=pltpu.SMEM)],
        out_specs=[lead(x.shape) for x in outs[:-2]] + [whole(x) for x in outs[-2:]],
        scratch_shapes=[
            pltpu.VMEM((columns, ROWS, width), BF),
            pltpu.VMEM((columns, 256 + 2 * SLOT, width), BF),
            pltpu.VMEM((2, FACE, 256), F32),
            pltpu.VMEM((planes, 2, FACE, 256), BF),
            pltpu.VMEM((3 * FACE, width), BF),
        ],
        compiler_params=pltpu.CompilerParams(
            vmem_limit_bytes=24 * MIB, dimension_semantics=("arbitrary",)
        ),
        cost_estimate=cost(1e10, 12e6),
        name="weights",
    )(inverse, couplings, right, initial, neighbours)


def ring(x, axis, by):
    n = lax.axis_size(axis)
    return lax.ppermute(x, axis, [(i, (i + by) % n) for i in range(n)])


def shift(x, axis, by):
    n = lax.axis_size(axis)
    return lax.ppermute(x, axis, [(i, i + by) for i in range(n) if 0 <= i + by < n])


def local(right_sides, initial, inverse_blocks, couplings, neighbours):
    planes, columns, rhs, width = initial.shape
    size = columns * rhs
    const = lambda x: jnp.asarray(x, BF)
    send_in = const(send_table(ROWS, inner))
    own_in = const(own_table(ROWS, inner))
    back = const(table(width, ROWS, [(natural(*n), n) for n in NODES], inner))
    up_sel = const(receive_table(2))
    down_sel = const(receive_table(0))
    beside = neighbours.T

    share = (planes, SHARED, size)
    up, down, above = call(
        first_kernel, [(share, BF), (share, BF), ((FACE, size), BF)], (initial,), "initial_traces"
    )
    up, down, above, initial = lax.optimization_barrier((up, down, above, initial))
    from_low = ring(up, "cross", 1)
    from_high = ring(down, "cross", -1)
    from_above = shift(above, "sweep", -1)
    *parts, own, cum_f, cum_b, passes = weights(
        inverse_blocks.transpose(0, 2, 1, 3), couplings.transpose(0, 2, 3, 1, 4), right_sides, initial, beside
    )
    known, lower, upper, base, fore = (parts[i : i + 3] for i in range(0, 15, 3))
    from_low, from_high, from_above, passes = lax.optimization_barrier((from_low, from_high, from_above, passes))
    passes = lax.all_gather(passes, "sweep")

    sections = lax.axis_size("sweep")
    trace = (planes, FACE, size)
    deep = (planes, ROWS, size)
    chain_outs = [((planes, 256, size), BF), (trace, F32), (trace, F32), ((sections, FACE, size), BF)]
    operand, part2, traces, last = call(
        functools.partial(forward_chain_kernel, rhs=rhs),
        chain_outs,
        (from_low, from_high, from_above, own, beside, up_sel, down_sel, known[2], lower[2], upper[2], fore[2]),
        "forward_chain",
    )
    last = lax.all_to_all(last, "sweep", 0, 0)
    part0, part1 = call(
        functools.partial(base_kernel, rhs=rhs),
        [(trace, F32)] * 2,
        (known[0], known[1], operand, fore[0], fore[1], from_above, upper[0], upper[1]),
        "forward_base",
        2e9,
    )
    middle, change, up, down = call(
        functools.partial(forward_finish_kernel, rhs=rhs),
        [(deep, BF), (deep, F32), (share, BF), (share, BF)],
        (last, passes, cum_f, traces, part0, part1, part2, *lower, send_in),
        "forward_finish",
    )
    from_low = ring(up, "cross", 1)
    from_high = ring(down, "cross", -1)
    own, *base = call(
        middle_kernel,
        [((planes, 2 * FACE, size), BF)] + [(trace, F32)] * 3,
        (middle, change, *base, beside, own_in),
        "middle",
        2e9,
    )
    operand, part0, traces, last = call(
        functools.partial(backward_chain_kernel, rhs=rhs),
        chain_outs,
        (from_low, from_high, own, beside, up_sel, down_sel, known[0], upper[0], base[0]),
        "backward_chain",
    )
    last = lax.all_to_all(last, "sweep", 0, 0)
    part1, part2 = call(
        functools.partial(base_kernel, rhs=rhs),
        [(trace, F32)] * 2,
        (known[1], known[2], operand, base[1], base[2]),
        "backward_base",
        2e9,
    )
    (result,) = call(
        functools.partial(backward_finish_kernel, rhs=rhs),
        [(right_sides.shape, BF)],
        (last, passes, cum_b, traces, part0, part1, part2, *upper, back),
        "backward_finish",
    )
    return result


def solution(mesh):
    return jax.shard_map(
        local,
        mesh=mesh,
        in_specs=(
            P("sweep", "cross", None, None),
            P("sweep", "cross", None, None),
            P("sweep", "cross", None, None),
            P("sweep", "cross", None, None, None),
            P("cross", None),
        ),
        out_specs=P("sweep", "cross", None, None),
        check_vma=False,
    )
```

```python
import functools

import jax
import jax.numpy as jnp
import numpy as np
from jax import lax
from jax.experimental import pallas as pl
from jax.experimental.pallas import tpu as pltpu
from jax.sharding import PartitionSpec as P

BF = jnp.bfloat16
F32 = jnp.float32
NT = 45
FACE = 48
SLOT = 64
ROWS = 3 * FACE
SHARED = 80
MIB = 1 << 20


def natural(v, a, b, c):
    return v * 27 + a * 9 + b * 3 + c


def inner(v, a, b, c):
    return a * FACE + v * 9 + b * 3 + c


NODES = [(v, a, b, c) for v in range(5) for a in range(3) for b in range(3) for c in range(3)]


def face_nodes(place, which):
    return [n for n in NODES if n[1 + place] == which]


def union_rows(which):
    others = [b for b in range(3) if b != which]
    spots = [(which, c) for c in range(3)] + [(b, which) for b in others]
    return [
        (v * 16 + a * 5 + j, (v, a, b, c)) for v in range(5) for a in range(3) for j, (b, c) in enumerate(spots)
    ]


def table(height, width, rows, column_of, value=1.0):
    out = np.zeros((height, width), np.float32)
    for row, node in rows:
        out[row, column_of(*node)] = value
    return out


def block(nodes, start=0):
    return [(start + i, n) for i, n in enumerate(nodes)]


def send_table(width, column_of):
    rows = union_rows(2) + [(SHARED + i, n) for i, n in union_rows(0)]
    return table(2 * SHARED, width, rows, column_of)


def own_table(width, column_of):
    rows = block(face_nodes(2, 2)) + block(face_nodes(2, 0), FACE)
    return table(2 * FACE, width, rows, column_of)


def receive_table(which):
    place = {n: i for i, n in union_rows(which)}
    rows = block(face_nodes(1, which)) + block(face_nodes(2, which), FACE)
    return table(2 * FACE, SHARED, rows, lambda *n: place[n])


def mm(a, b):
    return lax.dot_general(a, b, (((1,), (0,)), ((), ())), preferred_element_type=F32)


def mt(a, b):
    return lax.dot_general(a, b, (((1,), (1,)), ((), ())), preferred_element_type=F32)


def split_lanes(value, width):
    lanes = value.shape[1]
    value = value.astype(F32)
    owner = lax.broadcasted_iota(jnp.int32, value.shape, 1) // width
    pad = jnp.zeros((SLOT - FACE, lanes), BF)
    parts = []
    for c in range(lanes // width):
        parts += [jnp.where(owner == c, value, 0.0).astype(BF), pad]
    return jnp.concatenate(parts, 0)


def own_lanes(values, width):
    owner = lax.broadcasted_iota(jnp.int32, values[0].shape, 1) // width
    out = values[0]
    for c in range(1, len(values)):
        out = jnp.where(owner == c, values[c], out)
    return out


def one_hot(source, start, height):
    row = lax.broadcasted_iota(jnp.int32, (height, source.shape[1]), 0) + start
    return jnp.where(row == source, 1.0, 0.0).astype(BF)


def chain_step(matrix, trace, rhs, rows=slice(None)):
    half = trace.shape[1] // 2
    return jnp.concatenate(
        [mm(matrix[h, rows], split_lanes(trace[:, h * half : (h + 1) * half], rhs)) for h in range(2)], 1
    )


def shared_target(row, which):
    v, k = row // 16, row % 16
    a = k // 5
    j = k % 5
    b = jnp.where(j < 3, which, j - 3 if which == 2 else j - 2)
    c = jnp.where(j < 3, j, which)
    return jnp.where(k < 15, v * 27 + a * 9 + b * 3 + c, -1)


def picks(target, width):
    lane = lax.broadcasted_iota(jnp.int32, (target.shape[0], width), 1)
    return jnp.where(lane == target, 1.0, 0.0).astype(BF)


def rows_of(height):
    return lax.broadcasted_iota(jnp.int32, (height, 1), 0)


def first_target(row):
    return jnp.where(row < NT, row // 9 * 27 + row % 9, -1)


def c_target(row, which):
    return jnp.where(row < NT, row * 3 + which, -1)


def sources(neighbours, columns, rhs):
    place = lax.axis_index("cross")
    total = columns * lax.axis_size("cross")
    lane = lax.broadcasted_iota(jnp.int32, (1, columns * rhs), 1)
    out = []
    for face, first in ((2, place - 1), (3, place)):
        which = jnp.zeros_like(lane)
        for c in range(columns):
            at = lax.rem(neighbours[face, c] - first * columns + 2 * total, total)
            which = jnp.where(lane // rhs == c, at, which)
        out.append(which * rhs + lane % rhs)
    return out


def first_kernel(initial, up, down, above):
    planes, columns, rhs, width = initial.shape
    shared = rows_of(SHARED)
    tables = [picks(shared_target(shared, which), width) for which in (2, 0)]
    for p in range(planes):
        x = initial[p].reshape(columns * rhs, width)
        up[p] = mt(tables[0], x).astype(BF)
        down[p] = mt(tables[1], x).astype(BF)
        if p == 0:
            above[...] = mt(picks(first_target(rows_of(FACE)), width), x).astype(BF)


def turned(rows):
    pad = jnp.zeros((FACE - NT,) + rows.shape[1:], rows.dtype)
    return jnp.swapaxes(jnp.concatenate([rows, pad], 0), 0, 1)


def weight_kernel(
    inverse, couplings, right, initial, neighbours,
    known, lower, upper, base, fore, own,
    inverse_in, couplings_in, right_in, initial_in, solves, faces, prev, tables, done,
):
    planes, columns, rhs, width = initial.shape
    size = columns * rhs
    half = columns // 2

    def arrivals(p):
        pairs = ((inverse, inverse_in), (couplings, couplings_in), (right, right_in))
        return [pltpu.make_async_copy(x.at[p], y.at[p], done.at[i, p]) for i, (x, y) in enumerate(pairs)]

    start = pltpu.make_async_copy(initial, initial_in, done.at[3, 0])
    for p in range(planes):
        for copy in arrivals(p):
            copy.start()
    start.start()
    faces[...] = jnp.zeros(faces.shape, BF)
    tables[:FACE] = picks(c_target(rows_of(FACE), 2), width)
    tables[FACE : 2 * FACE] = picks(c_target(rows_of(FACE), 0), width)
    tables[2 * FACE :] = picks(first_target(rows_of(FACE)), width)
    source = sources(neighbours, columns, rhs)
    lane = lax.broadcasted_iota(jnp.int32, (ROWS, 2 * SLOT), 1)
    start.wait()

    @pl.loop(0, planes)
    def _(p):
        x = initial_in[p].reshape(size, width)
        beyond = initial_in[jnp.minimum(p + 1, planes - 1)].reshape(size, width)
        after = jnp.where(p + 1 < planes, mt(tables[2 * FACE :], beyond), 0.0)
        mine = mt(tables[: 2 * FACE], x).astype(BF)
        own[p, :FACE] = mm(mine[:FACE], one_hot(source[0], size, size)).astype(BF)
        own[p, FACE:] = mm(mine[FACE:], one_hot(source[1], 0, size)).astype(BF)
        for copy in arrivals(p):
            copy.wait()
        for a in range(3):
            rows = [inverse_in[p, v * 27 + a * 9 : v * 27 + a * 9 + 9] for v in range(5)]
            solves[:, a * FACE : (a + 1) * FACE] = -turned(jnp.concatenate(rows, 0))
        for f in range(4):
            faces[:, f * FACE : (f + 1) * FACE] = turned(couplings_in[p, 2 + f])
        faces[:, 4 * FACE : 4 * FACE + rhs] = right_in[p]
        faces[:, 256 : 256 + FACE] = turned(couplings_in[p, 0])
        faces[:, 256 + SLOT : 256 + SLOT + FACE] = turned(couplings_in[p, 1])

        bases = []
        before = None
        for c in range(columns):
            solve = solves[c]
            all_known = mt(solve, faces[c, :256])
            side = all_known[:, 128:]
            move = (c % half * rhs - (4 * FACE - 128)) % 128
            bases.append(pltpu.roll(side, move, 1) if move else side)
            known[p, c] = all_known.astype(BF)
            both = mt(solve, faces[c, 256:])
            if c % 2 == 0:
                before = both
            else:
                h, at = c // half, c % half // 2 * 2 * SLOT
                lanes = slice(at, at + 2 * SLOT)
                lower[p, h, :ROWS, lanes] = jnp.where(lane < SLOT, before, pltpu.roll(both, SLOT, 1)).astype(BF)
                upper[p, h, :ROWS, lanes] = jnp.where(lane < SLOT, pltpu.roll(before, SLOT, 1), both).astype(BF)
        for h in range(2):
            lanes = slice(h * half * rhs, (h + 1) * half * rhs)
            here = -own_lanes(bases[h * half : (h + 1) * half], rhs)
            base[p, :, lanes] = here
            fore[p, :, lanes] = here + mm(upper[p, h, :ROWS], split_lanes(after[:, lanes], rhs))
            step = lower[p, h, 2 * FACE : ROWS]

            @pl.when(p == 0)
            def _():
                prev[h] = step.astype(F32)

            @pl.when(p > 0)
            def _():
                prev[h] = mm(step, split_lanes(prev[h], SLOT))

            lower[p, h, ROWS:] = prev[h].astype(BF)

    for h in range(2):
        total = upper[planes - 1, h, :FACE].astype(F32)
        upper[planes - 1, h, ROWS:] = total.astype(BF)
        for q in range(planes - 2, -1, -1):
            total = mm(upper[q, h, :FACE], split_lanes(total, SLOT))
            upper[q, h, ROWS:] = total.astype(BF)


def gathered(received_up, received_down, own, p, up_sel, down_sel, low_pick, high_pick):
    low = mm(up_sel, received_up[p]).astype(BF)
    high = mm(down_sel, received_down[p]).astype(BF)
    c_low = mm(low[FACE:], low_pick).astype(BF) + own[p, :FACE]
    c_high = mm(high[FACE:], high_pick).astype(BF) + own[p, FACE : 2 * FACE]
    return [low[:FACE], high[:FACE], c_low, c_high]


def known_part(known_c, operand, columns, rhs):
    half = columns // 2
    out = []
    for h in range(2):
        side = operand[:, h * half * rhs : (h + 1) * half * rhs]
        out.append(own_lanes([mm(known_c(h * half + c), side) for c in range(half)], rhs))
    return jnp.concatenate(out, 1)


FIRST = slice(0, FACE)
LAST = slice(2 * FACE, ROWS)
FULL = slice(0, ROWS)
PRODUCT = slice(ROWS, ROWS + FACE)


def chain_kernel(known, base, matrix, received, own, neighbours, outs, order, rows, rhs, extra=None):
    up, down, up_sel, down_sel = received
    state, message = outs
    planes, columns = known.shape[:2]
    size = columns * rhs
    source = sources(neighbours, columns, rhs)
    low_pick = one_hot(source[0], 0, size)
    high_pick = one_hot(source[1], size, size)
    trace = None
    for p in order:
        parts = gathered(up, down, own, p, up_sel[...], down_sel[...], low_pick, high_pick)
        parts.append(jnp.zeros((256 - 4 * FACE, size), BF))
        whole = jnp.concatenate(parts, 0)
        start = base[p] + known_part(lambda c: known[p, c], whole, columns, rhs)
        if extra is not None and p == planes - 1:
            start = start + chain_step(extra[0].at[p], extra[1][...], rhs, FULL)
        state[p, FULL] = start
        start = start[rows]
        trace = start if trace is None else start + chain_step(matrix.at[p], trace, rhs, rows)
        state[p, PRODUCT] = trace
    for i in range(message.shape[0]):
        message[i, FIRST] = trace.astype(BF)
        for h in range(2):
            message[i, (1 + h) * FACE : (2 + h) * FACE] = matrix[order[-1], h, PRODUCT]


def forward_chain_kernel(
    up, down, above, own, neighbours, up_sel, down_sel, known, lower, upper, base, *outs, rhs
):
    order = range(up.shape[0])
    received = (up, down, up_sel, down_sel)
    chain_kernel(known, base, lower, received, own, neighbours, outs, order, LAST, rhs, (upper, above))


def backward_chain_kernel(up, down, own, neighbours, up_sel, down_sel, known, upper, base, *outs, rhs):
    order = range(up.shape[0] - 1, -1, -1)
    chain_kernel(
        known, base, upper, (up, down, up_sel, down_sel), own, neighbours, outs, order, FIRST, rhs
    )


def incoming(message, forward, rhs):
    here = lax.axis_index("sweep")
    n = message.shape[0]
    trace = None
    for i in range(n - 1) if forward else range(n - 1, 0, -1):
        value = message[i, FIRST].astype(F32)
        if trace is None:
            trace = jnp.zeros_like(value)
        else:
            product = [message[i, (1 + h) * FACE : (2 + h) * FACE] for h in range(2)]
            half = value.shape[1] // 2
            halves = [trace[:, h * half : (h + 1) * half] for h in range(2)]
            value = value + jnp.concatenate([mm(m, split_lanes(t, rhs)) for m, t in zip(product, halves)], 1)
        trace = jnp.where(i < here if forward else i > here, value, trace)
    return trace


def copied(source, target, sem):
    copies = [pltpu.make_async_copy(x, y, sem.at[i]) for i, (x, y) in enumerate(zip(source, target))]
    for copy in copies:
        copy.start()
    return copies


def forward_finish_kernel(
    message, state_there, lower_there, send, middle, change, up, down, state, lower, sem, *, rhs
):
    planes = state.shape[0]
    copies = copied((state_there, lower_there), (state, lower), sem)
    entry = incoming(message, True, rhs)
    for copy in copies:
        copy.wait()
    trace = entry
    for p in range(planes):
        delta = chain_step(lower.at[p], trace, rhs, FULL)
        change[p] = delta
        whole = (state[p, FULL] + delta).astype(BF)
        middle[p] = whole
        out = mm(send[...], whole).astype(BF)
        up[p] = out[:SHARED]
        down[p] = out[SHARED:]
        if p + 1 < planes:
            trace = state[p, PRODUCT] + chain_step(lower.at[p], entry, rhs, PRODUCT)


def middle_kernel(middle, change, base, neighbours, own_sel, own, out):
    planes, _, size = middle.shape
    columns = neighbours.shape[1]
    source = sources(neighbours, columns, size // columns)
    low_pick = one_hot(source[0], size, size)
    high_pick = one_hot(source[1], 0, size)
    for p in range(planes):
        mine = mm(own_sel[...], middle[p]).astype(BF)
        own[p, :FACE] = mm(mine[:FACE], low_pick).astype(BF)
        own[p, FACE:] = mm(mine[FACE:], high_pick).astype(BF)
        out[p] = base[p] + change[p]


def backward_finish_kernel(message, state_there, upper_there, back, result, state, upper, sem, *, rhs):
    planes = state.shape[0]
    copies = copied((state_there, upper_there), (state, upper), sem)
    entry = incoming(message, False, rhs)
    size = entry.shape[1]
    row = lax.broadcasted_iota(jnp.int32, (size, size), 0)
    column = lax.broadcasted_iota(jnp.int32, (size, size), 1)
    unit = jnp.where(row == column, 1.0, 0.0).astype(BF)
    columns, _, width = result.shape[1:]
    for copy in copies:
        copy.wait()
    trace = entry
    for p in range(planes - 1, -1, -1):
        whole = state[p, FULL] + chain_step(upper.at[p], trace, rhs, FULL)
        flat = mm(back[...], whole.astype(BF)).astype(BF)
        result[p] = mt(unit, flat).astype(BF).reshape(columns, rhs, width)
        if p:
            trace = state[p, PRODUCT] + chain_step(upper.at[p], entry, rhs, PRODUCT)


def call(kernel, outs, operands, name, flops=2e8, far=(), scratch=()):
    shapes = [jax.ShapeDtypeStruct(s, d) for s, d in outs]
    nbytes = sum(x.size * x.dtype.itemsize for x in list(operands) + shapes)
    spaces = [pltpu.SMEM if x.dtype == jnp.int32 else pltpu.VMEM for x in operands]
    spaces = [pltpu.HBM if i in far else space for i, space in enumerate(spaces)]
    scratch = list(scratch)
    if far and not scratch:
        scratch = [pltpu.VMEM(operands[i].shape, operands[i].dtype) for i in far]
        scratch.append(pltpu.SemaphoreType.DMA((len(far),)))
    return pl.pallas_call(
        kernel,
        out_shape=shapes,
        in_specs=[pl.BlockSpec(memory_space=space) for space in spaces],
        out_specs=[pl.BlockSpec(memory_space=pltpu.VMEM)] * len(shapes),
        scratch_shapes=scratch,
        compiler_params=pltpu.CompilerParams(vmem_limit_bytes=24 * MIB),
        cost_estimate=pl.CostEstimate(flops=int(flops), bytes_accessed=int(nbytes), transcendentals=0),
        name=name,
    )(*operands)


def weights(inverse, couplings, right, initial, neighbours):
    planes, columns, rhs, width = initial.shape
    size = columns * rhs
    pack = (planes, 2, ROWS + FACE, 256)
    field = (planes, ROWS, size)
    outs = [((planes, columns, ROWS, 256), BF), (pack, BF), (pack, BF), (field, F32), (field, F32)]
    outs.append(((planes, 2 * FACE, size), BF))
    operands = (inverse, couplings, right, initial, neighbours)
    scratch = [pltpu.VMEM(x.shape, x.dtype) for x in operands[:4]] + [
        pltpu.VMEM((columns, ROWS, width), BF),
        pltpu.VMEM((columns, 256 + 2 * SLOT, width), BF),
        pltpu.VMEM((2, FACE, 256), F32),
        pltpu.VMEM((3 * FACE, width), BF),
        pltpu.SemaphoreType.DMA((4, planes)),
    ]
    return call(weight_kernel, outs, operands, "weights", 1e10, (0, 1, 2, 3), scratch)


def ring(x, axis, by):
    n = lax.axis_size(axis)
    return lax.ppermute(x, axis, [(i, (i + by) % n) for i in range(n)])


def shift(x, axis, by):
    n = lax.axis_size(axis)
    return lax.ppermute(x, axis, [(i, i + by) for i in range(n) if 0 <= i + by < n])


def local(right_sides, initial, inverse_blocks, couplings, neighbours):
    planes, columns, rhs, width = initial.shape
    size = columns * rhs
    const = lambda x: jnp.asarray(x, BF)
    send_in = const(send_table(ROWS, inner))
    own_in = const(own_table(ROWS, inner))
    back = const(table(width, ROWS, [(natural(*n), n) for n in NODES], inner))
    up_sel = const(receive_table(2))
    down_sel = const(receive_table(0))
    beside = neighbours.T

    share = (planes, SHARED, size)
    up, down, above = call(
        first_kernel, [(share, BF), (share, BF), ((FACE, size), BF)], (initial,), "initial_traces"
    )
    up, down, above, initial = lax.optimization_barrier((up, down, above, initial))
    from_low = ring(up, "cross", 1)
    from_high = ring(down, "cross", -1)
    from_above = shift(above, "sweep", -1)
    known, lower, upper, base, fore, own = weights(
        inverse_blocks.transpose(0, 2, 1, 3), couplings.transpose(0, 2, 3, 1, 4), right_sides, initial, beside
    )

    field = (planes, ROWS, size)
    chain_outs = [((planes, ROWS + FACE, size), F32), ((lax.axis_size("sweep"), 3 * FACE, size), BF)]
    state, message = call(
        functools.partial(forward_chain_kernel, rhs=rhs),
        chain_outs,
        (from_low, from_high, from_above, own, beside, up_sel, down_sel, known, lower, upper, fore),
        "forward_chain",
    )
    message = lax.all_to_all(message, "sweep", 0, 0)
    middle, change, up, down = call(
        functools.partial(forward_finish_kernel, rhs=rhs),
        [(field, BF), (field, F32), (share, BF), (share, BF)],
        (message, state, lower, send_in),
        "forward_finish",
        far=(1, 2),
    )
    from_low = ring(up, "cross", 1)
    from_high = ring(down, "cross", -1)
    own, base = call(
        middle_kernel,
        [((planes, 2 * FACE, size), BF), (field, F32)],
        (middle, change, base, beside, own_in),
        "middle",
        2e9,
    )
    state, message = call(
        functools.partial(backward_chain_kernel, rhs=rhs),
        chain_outs,
        (from_low, from_high, own, beside, up_sel, down_sel, known, upper, base),
        "backward_chain",
    )
    message = lax.all_to_all(message, "sweep", 0, 0)
    (result,) = call(
        functools.partial(backward_finish_kernel, rhs=rhs),
        [(right_sides.shape, BF)],
        (message, state, upper, back),
        "backward_finish",
        far=(1, 2),
    )
    return result


def solution(mesh):
    return jax.shard_map(
        local,
        mesh=mesh,
        in_specs=(
            P("sweep", "cross", None, None),
            P("sweep", "cross", None, None),
            P("sweep", "cross", None, None),
            P("sweep", "cross", None, None, None),
            P("cross", None),
        ),
        out_specs=P("sweep", "cross", None, None),
        check_vma=False,
    )
```

```python
import functools

import jax
import jax.numpy as jnp
import numpy as np
from jax import lax
from jax.experimental import pallas as pl
from jax.experimental.pallas import tpu as pltpu
from jax.sharding import PartitionSpec as P

BF = jnp.bfloat16
F32 = jnp.float32
NT = 45
FACE = 48
SLOT = 64
ROWS = 3 * FACE
SHARED = 80
MIB = 1 << 20


def natural(v, a, b, c):
    return v * 27 + a * 9 + b * 3 + c


def inner(v, a, b, c):
    return a * FACE + v * 9 + b * 3 + c


NODES = [(v, a, b, c) for v in range(5) for a in range(3) for b in range(3) for c in range(3)]


def face_nodes(place, which):
    return [n for n in NODES if n[1 + place] == which]


def union_rows(which):
    others = [b for b in range(3) if b != which]
    spots = [(which, c) for c in range(3)] + [(b, which) for b in others]
    return [
        (v * 16 + a * 5 + j, (v, a, b, c)) for v in range(5) for a in range(3) for j, (b, c) in enumerate(spots)
    ]


def table(height, width, rows, column_of, value=1.0):
    out = np.zeros((height, width), np.float32)
    for row, node in rows:
        out[row, column_of(*node)] = value
    return out


def block(nodes, start=0):
    return [(start + i, n) for i, n in enumerate(nodes)]


def send_table(width, column_of):
    rows = union_rows(2) + [(SHARED + i, n) for i, n in union_rows(0)]
    return table(2 * SHARED, width, rows, column_of)


def own_table(width, column_of):
    rows = block(face_nodes(2, 2)) + block(face_nodes(2, 0), FACE)
    return table(2 * FACE, width, rows, column_of)


def receive_table(which):
    place = {n: i for i, n in union_rows(which)}
    rows = block(face_nodes(1, which)) + block(face_nodes(2, which), FACE)
    return table(2 * FACE, SHARED, rows, lambda *n: place[n])


def mm(a, b):
    return lax.dot_general(a, b, (((1,), (0,)), ((), ())), preferred_element_type=F32)


def mt(a, b):
    return lax.dot_general(a, b, (((1,), (1,)), ((), ())), preferred_element_type=F32)


def split_lanes(value, width):
    lanes = value.shape[1]
    value = value.astype(F32)
    owner = lax.broadcasted_iota(jnp.int32, value.shape, 1) // width
    pad = jnp.zeros((SLOT - FACE, lanes), BF)
    parts = []
    for c in range(lanes // width):
        parts += [jnp.where(owner == c, value, 0.0).astype(BF), pad]
    return jnp.concatenate(parts, 0)


def own_lanes(values, width):
    owner = lax.broadcasted_iota(jnp.int32, values[0].shape, 1) // width
    out = values[0]
    for c in range(1, len(values)):
        out = jnp.where(owner == c, values[c], out)
    return out


def one_hot(source, start, height):
    row = lax.broadcasted_iota(jnp.int32, (height, source.shape[1]), 0) + start
    return jnp.where(row == source, 1.0, 0.0).astype(BF)


def chain_step(matrix, trace, rhs, rows=slice(None)):
    half = trace.shape[1] // 2
    return jnp.concatenate(
        [mm(matrix[h, rows], split_lanes(trace[:, h * half : (h + 1) * half], rhs)) for h in range(2)], 1
    )


def shared_target(row, which):
    v, k = row // 16, row % 16
    a = k // 5
    j = k % 5
    b = jnp.where(j < 3, which, j - 3 if which == 2 else j - 2)
    c = jnp.where(j < 3, j, which)
    return jnp.where(k < 15, v * 27 + a * 9 + b * 3 + c, -1)


def picks(target, width):
    lane = lax.broadcasted_iota(jnp.int32, (target.shape[0], width), 1)
    return jnp.where(lane == target, 1.0, 0.0).astype(BF)


def rows_of(height):
    return lax.broadcasted_iota(jnp.int32, (height, 1), 0)


def first_target(row):
    return jnp.where(row < NT, row // 9 * 27 + row % 9, -1)


def c_target(row, which):
    return jnp.where(row < NT, row * 3 + which, -1)


def sources(neighbours, columns, rhs):
    place = lax.axis_index("cross")
    total = columns * lax.axis_size("cross")
    lane = lax.broadcasted_iota(jnp.int32, (1, columns * rhs), 1)
    out = []
    for face, first in ((2, place - 1), (3, place)):
        which = jnp.zeros_like(lane)
        for c in range(columns):
            at = lax.rem(neighbours[face, c] - first * columns + 2 * total, total)
            which = jnp.where(lane // rhs == c, at, which)
        out.append(which * rhs + lane % rhs)
    return out


def first_kernel(initial, up, down, above):
    planes, columns, rhs, width = initial.shape
    shared = rows_of(SHARED)
    tables = [picks(shared_target(shared, which), width) for which in (2, 0)]
    for p in range(planes):
        x = initial[p].reshape(columns * rhs, width)
        up[p] = mt(tables[0], x).astype(BF)
        down[p] = mt(tables[1], x).astype(BF)
        if p == 0:
            above[...] = mt(picks(first_target(rows_of(FACE)), width), x).astype(BF)


def turned(rows):
    pad = jnp.zeros((FACE - NT,) + rows.shape[1:], rows.dtype)
    return jnp.swapaxes(jnp.concatenate([rows, pad], 0), 0, 1)


def weight_kernel(
    inverse, couplings, right, initial, neighbours,
    known, lower, upper, base, fore, own,
    inverse_in, couplings_in, right_in, initial_in, solves, faces, prev, tables, done,
):
    planes, columns, rhs, width = initial.shape
    size = columns * rhs
    half = columns // 2

    def arrivals(p):
        pairs = ((inverse, inverse_in), (couplings, couplings_in), (right, right_in))
        return [pltpu.make_async_copy(x.at[p], y.at[p], done.at[i, p]) for i, (x, y) in enumerate(pairs)]

    start = pltpu.make_async_copy(initial, initial_in, done.at[3, 0])
    for p in range(planes):
        for copy in arrivals(p):
            copy.start()
    start.start()
    faces[...] = jnp.zeros(faces.shape, BF)
    tables[:FACE] = picks(c_target(rows_of(FACE), 2), width)
    tables[FACE : 2 * FACE] = picks(c_target(rows_of(FACE), 0), width)
    tables[2 * FACE :] = picks(first_target(rows_of(FACE)), width)
    source = sources(neighbours, columns, rhs)
    lane = lax.broadcasted_iota(jnp.int32, (ROWS, 2 * SLOT), 1)
    start.wait()

    @pl.loop(0, planes)
    def _(p):
        x = initial_in[p].reshape(size, width)
        beyond = initial_in[jnp.minimum(p + 1, planes - 1)].reshape(size, width)
        after = jnp.where(p + 1 < planes, mt(tables[2 * FACE :], beyond), 0.0)
        mine = mt(tables[: 2 * FACE], x).astype(BF)
        own[p, :FACE] = mm(mine[:FACE], one_hot(source[0], size, size)).astype(BF)
        own[p, FACE:] = mm(mine[FACE:], one_hot(source[1], 0, size)).astype(BF)
        for copy in arrivals(p):
            copy.wait()
        for a in range(3):
            rows = [inverse_in[p, v * 27 + a * 9 : v * 27 + a * 9 + 9] for v in range(5)]
            solves[:, a * FACE : (a + 1) * FACE] = -turned(jnp.concatenate(rows, 0))
        for f in range(4):
            faces[:, f * FACE : (f + 1) * FACE] = turned(couplings_in[p, 2 + f])
        faces[:, 4 * FACE : 4 * FACE + rhs] = right_in[p]
        faces[:, 256 : 256 + FACE] = turned(couplings_in[p, 0])
        faces[:, 256 + SLOT : 256 + SLOT + FACE] = turned(couplings_in[p, 1])

        bases = []
        before = None
        for c in range(columns):
            solve = solves[c]
            all_known = mt(solve, faces[c, :256])
            side = all_known[:, 128:]
            move = (c % half * rhs - (4 * FACE - 128)) % 128
            bases.append(pltpu.roll(side, move, 1) if move else side)
            known[p, c] = all_known.astype(BF)
            both = mt(solve, faces[c, 256:])
            if c % 2 == 0:
                before = both
            else:
                h, at = c // half, c % half // 2 * 2 * SLOT
                lanes = slice(at, at + 2 * SLOT)
                lower[p, h, :ROWS, lanes] = jnp.where(lane < SLOT, before, pltpu.roll(both, SLOT, 1)).astype(BF)
                upper[p, h, :ROWS, lanes] = jnp.where(lane < SLOT, pltpu.roll(before, SLOT, 1), both).astype(BF)
        for h in range(2):
            lanes = slice(h * half * rhs, (h + 1) * half * rhs)
            here = -own_lanes(bases[h * half : (h + 1) * half], rhs)
            base[p, :, lanes] = here
            fore[p, :, lanes] = here + mm(upper[p, h, :ROWS], split_lanes(after[:, lanes], rhs))
            step = lower[p, h, 2 * FACE : ROWS]

            @pl.when(p == 0)
            def _():
                prev[h] = step.astype(F32)

            @pl.when(p > 0)
            def _():
                prev[h] = mm(step, split_lanes(prev[h], SLOT))

            lower[p, h, ROWS:] = prev[h].astype(BF)

    for h in range(2):
        total = upper[planes - 1, h, :FACE].astype(F32)
        upper[planes - 1, h, ROWS:] = total.astype(BF)
        for q in range(planes - 2, -1, -1):
            total = mm(upper[q, h, :FACE], split_lanes(total, SLOT))
            upper[q, h, ROWS:] = total.astype(BF)


def gathered(received_up, received_down, own, p, up_sel, down_sel, low_pick, high_pick):
    low = mm(up_sel, received_up[p]).astype(BF)
    high = mm(down_sel, received_down[p]).astype(BF)
    c_low = mm(low[FACE:], low_pick).astype(BF) + own[p, :FACE]
    c_high = mm(high[FACE:], high_pick).astype(BF) + own[p, FACE : 2 * FACE]
    return [low[:FACE], high[:FACE], c_low, c_high]


def known_part(known_c, operand, columns, rhs):
    half = columns // 2
    out = []
    for h in range(2):
        side = operand[:, h * half * rhs : (h + 1) * half * rhs]
        out.append(own_lanes([mm(known_c(h * half + c), side) for c in range(half)], rhs))
    return jnp.concatenate(out, 1)


FIRST = slice(0, FACE)
LAST = slice(2 * FACE, ROWS)
FULL = slice(0, ROWS)
PRODUCT = slice(ROWS, ROWS + FACE)


def chain_kernel(known, base, matrix, received, own, neighbours, outs, order, rows, rhs, extra=None):
    up, down, up_sel, down_sel = received
    state, message = outs
    planes, columns = known.shape[:2]
    size = columns * rhs
    source = sources(neighbours, columns, rhs)
    low_pick = one_hot(source[0], 0, size)
    high_pick = one_hot(source[1], size, size)
    trace = None
    for p in order:
        parts = gathered(up, down, own, p, up_sel[...], down_sel[...], low_pick, high_pick)
        parts.append(jnp.zeros((256 - 4 * FACE, size), BF))
        whole = jnp.concatenate(parts, 0)
        start = base[p] + known_part(lambda c: known[p, c], whole, columns, rhs)
        if extra is not None and p == planes - 1:
            start = start + chain_step(extra[0].at[p], extra[1][...], rhs, FULL)
        state[p, FULL] = start
        start = start[rows]
        trace = start if trace is None else start + chain_step(matrix.at[p], trace, rhs, rows)
        state[p, PRODUCT] = trace
    for i in range(message.shape[0]):
        message[i] = trace.astype(BF)


def forward_chain_kernel(
    up, down, above, own, neighbours, up_sel, down_sel, known, lower, upper, base, *outs, rhs
):
    order = range(up.shape[0])
    received = (up, down, up_sel, down_sel)
    chain_kernel(known, base, lower, received, own, neighbours, outs, order, LAST, rhs, (upper, above))


def backward_chain_kernel(up, down, own, neighbours, up_sel, down_sel, known, upper, base, *outs, rhs):
    order = range(up.shape[0] - 1, -1, -1)
    chain_kernel(
        known, base, upper, (up, down, up_sel, down_sel), own, neighbours, outs, order, FIRST, rhs
    )


def incoming(message, near, next_near, forward, rhs):
    here = lax.axis_index("sweep")
    n = message.shape[0]
    trace = None
    for i in range(n - 1) if forward else range(n - 1, 0, -1):
        value = message[i].astype(F32)
        if trace is None:
            trace = jnp.zeros_like(value)
        else:
            step = here - 1 if forward else here + 1
            product = [jnp.where(step == i, near[h], next_near[h]) for h in range(2)]
            half = value.shape[1] // 2
            halves = [trace[:, h * half : (h + 1) * half] for h in range(2)]
            value = value + jnp.concatenate([mm(m, split_lanes(t, rhs)) for m, t in zip(product, halves)], 1)
        trace = jnp.where(i < here if forward else i > here, value, trace)
    return trace


def copied(source, target, sem):
    copies = [pltpu.make_async_copy(x, y, sem.at[i]) for i, (x, y) in enumerate(zip(source, target))]
    for copy in copies:
        copy.start()
    return copies


def forward_finish_kernel(
    message, near, next_near, state_there, lower_there, send, middle, change, up, down, state, lower, sem, *, rhs
):
    planes = state.shape[0]
    copies = copied((state_there, lower_there), (state, lower), sem)
    entry = incoming(message, near, next_near, True, rhs)
    for copy in copies:
        copy.wait()
    trace = entry
    for p in range(planes):
        delta = chain_step(lower.at[p], trace, rhs, FULL)
        change[p] = delta
        whole = (state[p, FULL] + delta).astype(BF)
        middle[p] = whole
        out = mm(send[...], whole).astype(BF)
        up[p] = out[:SHARED]
        down[p] = out[SHARED:]
        if p + 1 < planes:
            trace = state[p, PRODUCT] + chain_step(lower.at[p], entry, rhs, PRODUCT)


def middle_kernel(middle, change, base, neighbours, own_sel, own, out):
    planes, _, size = middle.shape
    columns = neighbours.shape[1]
    source = sources(neighbours, columns, size // columns)
    low_pick = one_hot(source[0], size, size)
    high_pick = one_hot(source[1], 0, size)
    for p in range(planes):
        mine = mm(own_sel[...], middle[p]).astype(BF)
        own[p, :FACE] = mm(mine[:FACE], low_pick).astype(BF)
        own[p, FACE:] = mm(mine[FACE:], high_pick).astype(BF)
        out[p] = base[p] + change[p]


def backward_finish_kernel(
    message, near, next_near, state_there, upper_there, back, result, state, upper, sem, *, rhs
):
    planes = state.shape[0]
    copies = copied((state_there, upper_there), (state, upper), sem)
    entry = incoming(message, near, next_near, False, rhs)
    size = entry.shape[1]
    row = lax.broadcasted_iota(jnp.int32, (size, size), 0)
    column = lax.broadcasted_iota(jnp.int32, (size, size), 1)
    unit = jnp.where(row == column, 1.0, 0.0).astype(BF)
    columns, _, width = result.shape[1:]
    for copy in copies:
        copy.wait()
    trace = entry
    for p in range(planes - 1, -1, -1):
        whole = state[p, FULL] + chain_step(upper.at[p], trace, rhs, FULL)
        flat = mm(back[...], whole.astype(BF)).astype(BF)
        result[p] = mt(unit, flat).astype(BF).reshape(columns, rhs, width)
        if p:
            trace = state[p, PRODUCT] + chain_step(upper.at[p], entry, rhs, PRODUCT)


def call(kernel, outs, operands, name, flops=2e8, far=(), scratch=()):
    shapes = [jax.ShapeDtypeStruct(s, d) for s, d in outs]
    nbytes = sum(x.size * x.dtype.itemsize for x in list(operands) + shapes)
    spaces = [pltpu.SMEM if x.dtype == jnp.int32 else pltpu.VMEM for x in operands]
    spaces = [pltpu.HBM if i in far else space for i, space in enumerate(spaces)]
    operands = [
        pltpu.with_memory_space_constraint(x, pltpu.HBM) if i in far else x for i, x in enumerate(operands)
    ]
    scratch = list(scratch)
    if far and not scratch:
        scratch = [pltpu.VMEM(operands[i].shape, operands[i].dtype) for i in far]
        scratch.append(pltpu.SemaphoreType.DMA((len(far),)))
    return pl.pallas_call(
        kernel,
        out_shape=shapes,
        in_specs=[pl.BlockSpec(memory_space=space) for space in spaces],
        out_specs=[pl.BlockSpec(memory_space=pltpu.VMEM)] * len(shapes),
        scratch_shapes=scratch,
        compiler_params=pltpu.CompilerParams(vmem_limit_bytes=24 * MIB),
        cost_estimate=pl.CostEstimate(flops=int(flops), bytes_accessed=int(nbytes), transcendentals=0),
        name=name,
    )(*operands)


def products(x, by):
    n = lax.axis_size("sweep")
    inner = range(1, n - 1)
    return [
        lax.ppermute(x, "sweep", [(i, i + step) for i in inner if 0 <= i + step < n]) for step in (by, 2 * by)
    ]


def weights(inverse, couplings, right, initial, neighbours):
    planes, columns, rhs, width = initial.shape
    size = columns * rhs
    pack = (planes, 2, ROWS + FACE, 256)
    field = (planes, ROWS, size)
    outs = [((planes, columns, ROWS, 256), BF), (pack, BF), (pack, BF), (field, F32), (field, F32)]
    outs.append(((planes, 2 * FACE, size), BF))
    operands = (inverse, couplings, right, initial, neighbours)
    scratch = [pltpu.VMEM(x.shape, x.dtype) for x in operands[:4]] + [
        pltpu.VMEM((columns, ROWS, width), BF),
        pltpu.VMEM((columns, 256 + 2 * SLOT, width), BF),
        pltpu.VMEM((2, FACE, 256), F32),
        pltpu.VMEM((3 * FACE, width), BF),
        pltpu.SemaphoreType.DMA((4, planes)),
    ]
    return call(weight_kernel, outs, operands, "weights", 1e10, (0, 1, 2, 3), scratch)


def ring(x, axis, by):
    n = lax.axis_size(axis)
    return lax.ppermute(x, axis, [(i, (i + by) % n) for i in range(n)])


def shift(x, axis, by):
    n = lax.axis_size(axis)
    return lax.ppermute(x, axis, [(i, i + by) for i in range(n) if 0 <= i + by < n])


def local(right_sides, initial, inverse_blocks, couplings, neighbours):
    planes, columns, rhs, width = initial.shape
    size = columns * rhs
    const = lambda x: jnp.asarray(x, BF)
    send_in = const(send_table(ROWS, inner))
    own_in = const(own_table(ROWS, inner))
    back = const(table(width, ROWS, [(natural(*n), n) for n in NODES], inner))
    up_sel = const(receive_table(2))
    down_sel = const(receive_table(0))
    beside = neighbours.T

    share = (planes, SHARED, size)
    up, down, above = call(
        first_kernel, [(share, BF), (share, BF), ((FACE, size), BF)], (initial,), "initial_traces"
    )
    up, down, above, initial = lax.optimization_barrier((up, down, above, initial))
    from_low = ring(up, "cross", 1)
    from_high = ring(down, "cross", -1)
    from_above = shift(above, "sweep", -1)
    known, lower, upper, base, fore, own = weights(
        inverse_blocks.transpose(0, 2, 1, 3), couplings.transpose(0, 2, 3, 1, 4), right_sides, initial, beside
    )

    pass_f = lower[planes - 1, :, PRODUCT]
    from_low, from_high, from_above, pass_f = lax.optimization_barrier((from_low, from_high, from_above, pass_f))
    passes = products(pass_f, 1)

    field = (planes, ROWS, size)
    chain_outs = [((planes, ROWS + FACE, size), F32), ((lax.axis_size("sweep"), FACE, size), BF)]
    state, message = call(
        functools.partial(forward_chain_kernel, rhs=rhs),
        chain_outs,
        (from_low, from_high, from_above, own, beside, up_sel, down_sel, known, lower, upper, fore),
        "forward_chain",
    )
    message = lax.all_to_all(message, "sweep", 0, 0)
    middle, change, up, down = call(
        functools.partial(forward_finish_kernel, rhs=rhs),
        [(field, BF), (field, F32), (share, BF), (share, BF)],
        (message, *passes, state, lower, send_in),
        "forward_finish",
        far=(3, 4),
    )
    from_low = ring(up, "cross", 1)
    from_high = ring(down, "cross", -1)
    own, base = call(
        middle_kernel,
        [((planes, 2 * FACE, size), BF), (field, F32)],
        (middle, change, base, beside, own_in),
        "middle",
        2e9,
    )
    own, pass_b = lax.optimization_barrier((own, upper[0, :, PRODUCT]))
    passes = products(pass_b, -1)
    from_low, from_high, *passes = lax.optimization_barrier((from_low, from_high, *passes))
    state, message = call(
        functools.partial(backward_chain_kernel, rhs=rhs),
        chain_outs,
        (from_low, from_high, own, beside, up_sel, down_sel, known, upper, base),
        "backward_chain",
    )
    message = lax.all_to_all(message, "sweep", 0, 0)
    (result,) = call(
        functools.partial(backward_finish_kernel, rhs=rhs),
        [(right_sides.shape, BF)],
        (message, *passes, state, upper, back),
        "backward_finish",
        far=(3, 4),
    )
    return result


def solution(mesh):
    return jax.shard_map(
        local,
        mesh=mesh,
        in_specs=(
            P("sweep", "cross", None, None),
            P("sweep", "cross", None, None),
            P("sweep", "cross", None, None),
            P("sweep", "cross", None, None, None),
            P("cross", None),
        ),
        out_specs=P("sweep", "cross", None, None),
        check_vma=False,
    )
```

```python
import functools

import jax
import jax.numpy as jnp
import numpy as np
from jax import lax
from jax.experimental import pallas as pl
from jax.experimental.pallas import tpu as pltpu
from jax.sharding import PartitionSpec as P

BF = jnp.bfloat16
F32 = jnp.float32
NT = 45
FACE = 48
SLOT = 64
ROWS = 3 * FACE
SHARED = 80
MIB = 1 << 20


def natural(v, a, b, c):
    return v * 27 + a * 9 + b * 3 + c


def inner(v, a, b, c):
    return a * FACE + v * 9 + b * 3 + c


NODES = [(v, a, b, c) for v in range(5) for a in range(3) for b in range(3) for c in range(3)]


def face_nodes(place, which):
    return [n for n in NODES if n[1 + place] == which]


def union_rows(which):
    others = [b for b in range(3) if b != which]
    spots = [(which, c) for c in range(3)] + [(b, which) for b in others]
    return [
        (v * 16 + a * 5 + j, (v, a, b, c)) for v in range(5) for a in range(3) for j, (b, c) in enumerate(spots)
    ]


def table(height, width, rows, column_of, value=1.0):
    out = np.zeros((height, width), np.float32)
    for row, node in rows:
        out[row, column_of(*node)] = value
    return out


def block(nodes, start=0):
    return [(start + i, n) for i, n in enumerate(nodes)]


def send_table(width, column_of):
    rows = union_rows(2) + [(SHARED + i, n) for i, n in union_rows(0)]
    return table(2 * SHARED, width, rows, column_of)


def own_table(width, column_of):
    rows = block(face_nodes(2, 2)) + block(face_nodes(2, 0), FACE)
    return table(2 * FACE, width, rows, column_of)


def receive_table(which):
    place = {n: i for i, n in union_rows(which)}
    rows = block(face_nodes(1, which)) + block(face_nodes(2, which), FACE)
    return table(2 * FACE, SHARED, rows, lambda *n: place[n])


def mm(a, b):
    return lax.dot_general(a, b, (((1,), (0,)), ((), ())), preferred_element_type=F32)


def mt(a, b):
    return lax.dot_general(a, b, (((1,), (1,)), ((), ())), preferred_element_type=F32)


def split_lanes(value, width):
    lanes = value.shape[1]
    value = value.astype(F32)
    owner = lax.broadcasted_iota(jnp.int32, value.shape, 1) // width
    pad = jnp.zeros((SLOT - FACE, lanes), BF)
    parts = []
    for c in range(lanes // width):
        parts += [jnp.where(owner == c, value, 0.0).astype(BF), pad]
    return jnp.concatenate(parts, 0)


def own_lanes(values, width):
    owner = lax.broadcasted_iota(jnp.int32, values[0].shape, 1) // width
    out = values[0]
    for c in range(1, len(values)):
        out = jnp.where(owner == c, values[c], out)
    return out


def one_hot(source, start, height):
    row = lax.broadcasted_iota(jnp.int32, (height, source.shape[1]), 0) + start
    return jnp.where(row == source, 1.0, 0.0).astype(BF)


def chain_step(matrix, trace, rhs, rows=slice(None)):
    half = trace.shape[1] // 2
    return jnp.concatenate(
        [mm(matrix[h, rows], split_lanes(trace[:, h * half : (h + 1) * half], rhs)) for h in range(2)], 1
    )


def shared_target(row, which):
    v, k = row // 16, row % 16
    a = k // 5
    j = k % 5
    b = jnp.where(j < 3, which, j - 3 if which == 2 else j - 2)
    c = jnp.where(j < 3, j, which)
    return jnp.where(k < 15, v * 27 + a * 9 + b * 3 + c, -1)


def picks(target, width):
    lane = lax.broadcasted_iota(jnp.int32, (target.shape[0], width), 1)
    return jnp.where(lane == target, 1.0, 0.0).astype(BF)


def rows_of(height):
    return lax.broadcasted_iota(jnp.int32, (height, 1), 0)


def first_target(row):
    return jnp.where(row < NT, row // 9 * 27 + row % 9, -1)


def c_target(row, which):
    return jnp.where(row < NT, row * 3 + which, -1)


def sources(neighbours, columns, rhs):
    place = lax.axis_index("cross")
    total = columns * lax.axis_size("cross")
    lane = lax.broadcasted_iota(jnp.int32, (1, columns * rhs), 1)
    out = []
    for face, first in ((2, place - 1), (3, place)):
        which = jnp.zeros_like(lane)
        for c in range(columns):
            at = lax.rem(neighbours[face, c] - first * columns + 2 * total, total)
            which = jnp.where(lane // rhs == c, at, which)
        out.append(which * rhs + lane % rhs)
    return out


def first_kernel(initial, up, down, above):
    planes, columns, rhs, width = initial.shape
    shared = rows_of(SHARED)
    tables = [picks(shared_target(shared, which), width) for which in (2, 0)]
    for p in range(planes):
        x = initial[p].reshape(columns * rhs, width)
        up[p] = mt(tables[0], x).astype(BF)
        down[p] = mt(tables[1], x).astype(BF)
        if p == 0:
            above[...] = mt(picks(first_target(rows_of(FACE)), width), x).astype(BF)


def turned(rows):
    pad = jnp.zeros((FACE - NT,) + rows.shape[1:], rows.dtype)
    return jnp.swapaxes(jnp.concatenate([rows, pad], 0), 0, 1)


def weight_kernel(
    inverse, couplings, right, initial, neighbours,
    known, lower, upper, base, fore, own,
    inverse_in, couplings_in, right_in, initial_in, solves, faces, prev, tables, done,
):
    planes, columns, rhs, width = initial.shape
    size = columns * rhs
    half = columns // 2

    def arrivals(p):
        pairs = ((inverse, inverse_in), (couplings, couplings_in), (right, right_in))
        return [pltpu.make_async_copy(x.at[p], y.at[p], done.at[i, p]) for i, (x, y) in enumerate(pairs)]

    start = pltpu.make_async_copy(initial, initial_in, done.at[3, 0])
    for p in range(planes):
        for copy in arrivals(p):
            copy.start()
    start.start()
    faces[...] = jnp.zeros(faces.shape, BF)
    tables[:FACE] = picks(c_target(rows_of(FACE), 2), width)
    tables[FACE : 2 * FACE] = picks(c_target(rows_of(FACE), 0), width)
    tables[2 * FACE :] = picks(first_target(rows_of(FACE)), width)
    source = sources(neighbours, columns, rhs)
    lane = lax.broadcasted_iota(jnp.int32, (ROWS, 2 * SLOT), 1)
    start.wait()

    @pl.loop(0, planes)
    def _(p):
        x = initial_in[p].reshape(size, width)
        beyond = initial_in[jnp.minimum(p + 1, planes - 1)].reshape(size, width)
        after = jnp.where(p + 1 < planes, mt(tables[2 * FACE :], beyond), 0.0)
        mine = mt(tables[: 2 * FACE], x).astype(BF)
        own[p, :FACE] = mm(mine[:FACE], one_hot(source[0], size, size)).astype(BF)
        own[p, FACE:] = mm(mine[FACE:], one_hot(source[1], 0, size)).astype(BF)
        for copy in arrivals(p):
            copy.wait()
        for a in range(3):
            rows = [inverse_in[p, v * 27 + a * 9 : v * 27 + a * 9 + 9] for v in range(5)]
            solves[:, a * FACE : (a + 1) * FACE] = -turned(jnp.concatenate(rows, 0))
        for f in range(4):
            faces[:, f * FACE : (f + 1) * FACE] = turned(couplings_in[p, 2 + f])
        faces[:, 4 * FACE : 4 * FACE + rhs] = right_in[p]
        faces[:, 256 : 256 + FACE] = turned(couplings_in[p, 0])
        faces[:, 256 + SLOT : 256 + SLOT + FACE] = turned(couplings_in[p, 1])

        bases = []
        before = None
        for c in range(columns):
            solve = solves[c]
            all_known = mt(solve, faces[c, :256])
            side = all_known[:, 128:]
            move = (c % half * rhs - (4 * FACE - 128)) % 128
            bases.append(pltpu.roll(side, move, 1) if move else side)
            known[p, c] = all_known.astype(BF)
            both = mt(solve, faces[c, 256:])
            if c % 2 == 0:
                before = both
            else:
                h, at = c // half, c % half // 2 * 2 * SLOT
                lanes = slice(at, at + 2 * SLOT)
                lower[p, h, :ROWS, lanes] = jnp.where(lane < SLOT, before, pltpu.roll(both, SLOT, 1)).astype(BF)
                upper[p, h, :ROWS, lanes] = jnp.where(lane < SLOT, pltpu.roll(before, SLOT, 1), both).astype(BF)
        for h in range(2):
            lanes = slice(h * half * rhs, (h + 1) * half * rhs)
            here = -own_lanes(bases[h * half : (h + 1) * half], rhs)
            base[p, :, lanes] = here
            fore[p, :, lanes] = here + mm(upper[p, h, :ROWS], split_lanes(after[:, lanes], rhs))
            step = lower[p, h, 2 * FACE : ROWS]

            @pl.when(p == 0)
            def _():
                prev[h] = step.astype(F32)

            @pl.when(p > 0)
            def _():
                prev[h] = mm(step, split_lanes(prev[h], SLOT))

            lower[p, h, ROWS:] = prev[h].astype(BF)

    for h in range(2):
        total = upper[planes - 1, h, :FACE].astype(F32)
        upper[planes - 1, h, ROWS:] = total.astype(BF)
        for q in range(planes - 2, -1, -1):
            total = mm(upper[q, h, :FACE], split_lanes(total, SLOT))
            upper[q, h, ROWS:] = total.astype(BF)


def gathered(received_up, received_down, own, p, up_sel, down_sel, low_pick, high_pick):
    low = mm(up_sel, received_up[p]).astype(BF)
    high = mm(down_sel, received_down[p]).astype(BF)
    c_low = mm(low[FACE:], low_pick).astype(BF) + own[p, :FACE]
    c_high = mm(high[FACE:], high_pick).astype(BF) + own[p, FACE : 2 * FACE]
    return [low[:FACE], high[:FACE], c_low, c_high]


def known_part(known_c, operand, columns, rhs):
    half = columns // 2
    out = []
    for h in range(2):
        side = operand[:, h * half * rhs : (h + 1) * half * rhs]
        out.append(own_lanes([mm(known_c(h * half + c), side) for c in range(half)], rhs))
    return jnp.concatenate(out, 1)


FIRST = slice(0, FACE)
LAST = slice(2 * FACE, ROWS)
FULL = slice(0, ROWS)
PRODUCT = slice(ROWS, ROWS + FACE)


def chain_kernel(known, base, matrix, received, own, neighbours, outs, order, rows, rhs, extra=None):
    up, down, up_sel, down_sel = received
    operand, start, traces, message = outs
    planes, columns = known.shape[:2]
    size = columns * rhs
    source = sources(neighbours, columns, rhs)
    low_pick = one_hot(source[0], 0, size)
    high_pick = one_hot(source[1], size, size)
    trace = None
    for p in order:
        parts = gathered(up, down, own, p, up_sel[...], down_sel[...], low_pick, high_pick)
        parts.append(jnp.zeros((256 - 4 * FACE, size), BF))
        whole = jnp.concatenate(parts, 0)
        operand[p] = whole
        value = base[p, rows] + known_part(lambda c: known[p, c, rows], whole, columns, rhs)
        if extra is not None and p == planes - 1:
            value = value + chain_step(extra[0].at[p], extra[1][...], rhs, rows)
        start[p] = value
        trace = value if trace is None else value + chain_step(matrix.at[p], trace, rhs, rows)
        traces[p] = trace
    message[FIRST] = trace.astype(BF)
    if message.shape[0] > FACE:
        for h in range(2):
            message[(1 + h) * FACE : (2 + h) * FACE] = matrix[order[-1], h, PRODUCT]


def base_kernel(known, operand, base, *rest, rows, rhs):
    planes, columns = known.shape[:2]
    out = rest[-1]
    for p in range(planes):
        value = base[p, rows] + known_part(lambda c: known[p, c, rows], operand[p], columns, rhs)
        if len(rest) > 1 and p == planes - 1:
            value = value + chain_step(rest[1].at[p], rest[0][...], rhs, rows)
        out[p] = value


def forward_chain_kernel(
    up, down, above, own, neighbours, up_sel, down_sel, known, lower, upper, base, *outs, rhs
):
    order = range(up.shape[0])
    received = (up, down, up_sel, down_sel)
    chain_kernel(known, base, lower, received, own, neighbours, outs, order, LAST, rhs, (upper, above))


def backward_chain_kernel(up, down, own, neighbours, up_sel, down_sel, known, upper, base, *outs, rhs):
    order = range(up.shape[0] - 1, -1, -1)
    chain_kernel(
        known, base, upper, (up, down, up_sel, down_sel), own, neighbours, outs, order, FIRST, rhs
    )


def incoming(one, two, three, near, next_near, rhs):
    def carried(product, trace):
        half = trace.shape[1] // 2
        halves = [trace[:, h * half : (h + 1) * half] for h in range(2)]
        return jnp.concatenate([mm(m, split_lanes(t, rhs)) for m, t in zip(product, halves)], 1)

    trace = two[FIRST].astype(F32) + carried(next_near, three[FIRST])
    return one[FIRST].astype(F32) + carried(near, trace)


def inside(message):
    return [message[(1 + h) * FACE : (2 + h) * FACE] for h in range(2)]


def forward_finish_kernel(
    one, two, three, start, rest, traces, lower, send, middle, change, up, down, *, rhs
):
    planes = start.shape[0]
    entry = incoming(one, two, three, inside(one), inside(two), rhs)
    trace = entry
    for p in range(planes):
        delta = chain_step(lower.at[p], trace, rhs, FULL)
        change[p] = delta
        whole = (jnp.concatenate([rest[p], start[p]], 0) + delta).astype(BF)
        middle[p] = whole
        out = mm(send[...], whole).astype(BF)
        up[p] = out[:SHARED]
        down[p] = out[SHARED:]
        if p + 1 < planes:
            trace = traces[p] + chain_step(lower.at[p], entry, rhs, PRODUCT)


def middle_kernel(middle, change, base, neighbours, own_sel, own, out):
    planes, _, size = middle.shape
    columns = neighbours.shape[1]
    source = sources(neighbours, columns, size // columns)
    low_pick = one_hot(source[0], size, size)
    high_pick = one_hot(source[1], 0, size)
    for p in range(planes):
        mine = mm(own_sel[...], middle[p]).astype(BF)
        own[p, :FACE] = mm(mine[:FACE], low_pick).astype(BF)
        own[p, FACE:] = mm(mine[FACE:], high_pick).astype(BF)
        out[p] = base[p] + change[p]


def backward_finish_kernel(
    one, two, three, near, next_near, start, rest, traces, upper, back, result, *, rhs
):
    planes = start.shape[0]
    entry = incoming(one, two, three, [near[0], near[1]], [next_near[0], next_near[1]], rhs)
    size = entry.shape[1]
    row = lax.broadcasted_iota(jnp.int32, (size, size), 0)
    column = lax.broadcasted_iota(jnp.int32, (size, size), 1)
    unit = jnp.where(row == column, 1.0, 0.0).astype(BF)
    columns, _, width = result.shape[1:]
    trace = entry
    for p in range(planes - 1, -1, -1):
        whole = jnp.concatenate([start[p], rest[p]], 0) + chain_step(upper.at[p], trace, rhs, FULL)
        flat = mm(back[...], whole.astype(BF)).astype(BF)
        result[p] = mt(unit, flat).astype(BF).reshape(columns, rhs, width)
        if p:
            trace = traces[p] + chain_step(upper.at[p], entry, rhs, PRODUCT)


def call(kernel, outs, operands, name, flops=2e8, far=(), scratch=()):
    shapes = [jax.ShapeDtypeStruct(s, d) for s, d in outs]
    nbytes = sum(x.size * x.dtype.itemsize for x in list(operands) + shapes)
    spaces = [pltpu.SMEM if x.dtype == jnp.int32 else pltpu.VMEM for x in operands]
    spaces = [pltpu.HBM if i in far else space for i, space in enumerate(spaces)]
    operands = [
        pltpu.with_memory_space_constraint(x, pltpu.HBM) if i in far else x for i, x in enumerate(operands)
    ]
    scratch = list(scratch)
    if far and not scratch:
        scratch = [pltpu.VMEM(operands[i].shape, operands[i].dtype) for i in far]
        scratch.append(pltpu.SemaphoreType.DMA((len(far),)))
    return pl.pallas_call(
        kernel,
        out_shape=shapes,
        in_specs=[pl.BlockSpec(memory_space=space) for space in spaces],
        out_specs=[pl.BlockSpec(memory_space=pltpu.VMEM)] * len(shapes),
        scratch_shapes=scratch,
        compiler_params=pltpu.CompilerParams(vmem_limit_bytes=24 * MIB),
        cost_estimate=pl.CostEstimate(flops=int(flops), bytes_accessed=int(nbytes), transcendentals=0),
        name=name,
    )(*operands)


def products(x, by):
    n = lax.axis_size("sweep")
    inner = range(1, n - 1)
    return [
        lax.ppermute(x, "sweep", [(i, i + step) for i in inner if 0 <= i + step < n]) for step in (by, 2 * by)
    ]


def weights(inverse, couplings, right, initial, neighbours):
    planes, columns, rhs, width = initial.shape
    size = columns * rhs
    pack = (planes, 2, ROWS + FACE, 256)
    field = (planes, ROWS, size)
    outs = [((planes, columns, ROWS, 256), BF), (pack, BF), (pack, BF), (field, F32), (field, F32)]
    outs.append(((planes, 2 * FACE, size), BF))
    operands = (inverse, couplings, right, initial, neighbours)
    scratch = [pltpu.VMEM(x.shape, x.dtype) for x in operands[:4]] + [
        pltpu.VMEM((columns, ROWS, width), BF),
        pltpu.VMEM((columns, 256 + 2 * SLOT, width), BF),
        pltpu.VMEM((2, FACE, 256), F32),
        pltpu.VMEM((3 * FACE, width), BF),
        pltpu.SemaphoreType.DMA((4, planes)),
    ]
    return call(weight_kernel, outs, operands, "weights", 1e10, (0, 1, 2, 3), scratch)


def ring(x, axis, by):
    n = lax.axis_size(axis)
    return lax.ppermute(x, axis, [(i, (i + by) % n) for i in range(n)])


def shift(x, axis, by):
    n = lax.axis_size(axis)
    return lax.ppermute(x, axis, [(i, i + by) for i in range(n) if 0 <= i + by < n])


def local(right_sides, initial, inverse_blocks, couplings, neighbours):
    planes, columns, rhs, width = initial.shape
    size = columns * rhs
    const = lambda x: jnp.asarray(x, BF)
    send_in = const(send_table(ROWS, inner))
    own_in = const(own_table(ROWS, inner))
    back = const(table(width, ROWS, [(natural(*n), n) for n in NODES], inner))
    up_sel = const(receive_table(2))
    down_sel = const(receive_table(0))
    beside = neighbours.T

    share = (planes, SHARED, size)
    up, down, above = call(
        first_kernel, [(share, BF), (share, BF), ((FACE, size), BF)], (initial,), "initial_traces"
    )
    up, down, above, initial = lax.optimization_barrier((up, down, above, initial))
    from_low = ring(up, "cross", 1)
    from_high = ring(down, "cross", -1)
    from_above = shift(above, "sweep", -1)
    known, lower, upper, base, fore, own = weights(
        inverse_blocks.transpose(0, 2, 1, 3), couplings.transpose(0, 2, 3, 1, 4), right_sides, initial, beside
    )

    field = (planes, ROWS, size)
    trace = (planes, FACE, size)
    most = (planes, 2 * FACE, size)
    chain_outs = [((planes, 256, size), BF), (trace, F32), (trace, F32)]
    operand, start, traces, message = call(
        functools.partial(forward_chain_kernel, rhs=rhs),
        chain_outs + [((3 * FACE, size), BF)],
        (from_low, from_high, from_above, own, beside, up_sel, down_sel, known, lower, upper, fore),
        "forward_chain",
    )
    one, two = (shift(message, "sweep", by) for by in (1, 2))
    three = shift(message[:FACE], "sweep", 3)
    (rest,) = call(
        functools.partial(base_kernel, rows=slice(0, 2 * FACE), rhs=rhs),
        [(most, F32)],
        (known, operand, fore, from_above, upper),
        "forward_base",
    )
    middle, change, up, down = call(
        functools.partial(forward_finish_kernel, rhs=rhs),
        [(field, BF), (field, F32), (share, BF), (share, BF)],
        (one, two, three, start, rest, traces, lower, send_in),
        "forward_finish",
    )
    from_low = ring(up, "cross", 1)
    from_high = ring(down, "cross", -1)
    own, base = call(
        middle_kernel,
        [((planes, 2 * FACE, size), BF), (field, F32)],
        (middle, change, base, beside, own_in),
        "middle",
        2e9,
    )
    own, pass_b = lax.optimization_barrier((own, upper[0, :, PRODUCT]))
    passes = products(pass_b, -1)
    from_low, from_high, *passes = lax.optimization_barrier((from_low, from_high, *passes))
    operand, start, traces, message = call(
        functools.partial(backward_chain_kernel, rhs=rhs),
        chain_outs + [((FACE, size), BF)],
        (from_low, from_high, own, beside, up_sel, down_sel, known, upper, base),
        "backward_chain",
    )
    one, two, three = (shift(message, "sweep", -by) for by in (1, 2, 3))
    (rest,) = call(
        functools.partial(base_kernel, rows=slice(FACE, ROWS), rhs=rhs),
        [(most, F32)],
        (known, operand, base),
        "backward_base",
    )
    (result,) = call(
        functools.partial(backward_finish_kernel, rhs=rhs),
        [(right_sides.shape, BF)],
        (one, two, three, *passes, start, rest, traces, upper, back),
        "backward_finish",
    )
    return result


def solution(mesh):
    return jax.shard_map(
        local,
        mesh=mesh,
        in_specs=(
            P("sweep", "cross", None, None),
            P("sweep", "cross", None, None),
            P("sweep", "cross", None, None),
            P("sweep", "cross", None, None, None),
            P("cross", None),
        ),
        out_specs=P("sweep", "cross", None, None),
        check_vma=False,
    )
```

```python
import functools

import jax
import jax.numpy as jnp
import numpy as np
from jax import lax
from jax.experimental import pallas as pl
from jax.experimental.pallas import tpu as pltpu
from jax.sharding import PartitionSpec as P

BF = jnp.bfloat16
F32 = jnp.float32
NT = 45
FACE = 48
SLOT = 64
ROWS = 3 * FACE
SHARED = 80
MIB = 1 << 20


def natural(v, a, b, c):
    return v * 27 + a * 9 + b * 3 + c


def inner(v, a, b, c):
    return a * FACE + v * 9 + b * 3 + c


NODES = [(v, a, b, c) for v in range(5) for a in range(3) for b in range(3) for c in range(3)]


def face_nodes(place, which):
    return [n for n in NODES if n[1 + place] == which]


def union_rows(which):
    others = [b for b in range(3) if b != which]
    spots = [(which, c) for c in range(3)] + [(b, which) for b in others]
    return [
        (v * 16 + a * 5 + j, (v, a, b, c)) for v in range(5) for a in range(3) for j, (b, c) in enumerate(spots)
    ]


def table(height, width, rows, column_of, value=1.0):
    out = np.zeros((height, width), np.float32)
    for row, node in rows:
        out[row, column_of(*node)] = value
    return out


def block(nodes, start=0):
    return [(start + i, n) for i, n in enumerate(nodes)]


def send_table(width, column_of):
    rows = union_rows(2) + [(SHARED + i, n) for i, n in union_rows(0)]
    return table(2 * SHARED, width, rows, column_of)


def own_table(width, column_of):
    rows = block(face_nodes(2, 2)) + block(face_nodes(2, 0), FACE)
    return table(2 * FACE, width, rows, column_of)


def receive_table(which):
    place = {n: i for i, n in union_rows(which)}
    rows = block(face_nodes(1, which)) + block(face_nodes(2, which), FACE)
    return table(2 * FACE, SHARED, rows, lambda *n: place[n])


def mm(a, b):
    return lax.dot_general(a, b, (((1,), (0,)), ((), ())), preferred_element_type=F32)


def mt(a, b):
    return lax.dot_general(a, b, (((1,), (1,)), ((), ())), preferred_element_type=F32)


def split_lanes(value, width):
    lanes = value.shape[1]
    value = value.astype(F32)
    owner = lax.broadcasted_iota(jnp.int32, value.shape, 1) // width
    pad = jnp.zeros((SLOT - FACE, lanes), BF)
    parts = []
    for c in range(lanes // width):
        parts += [jnp.where(owner == c, value, 0.0).astype(BF), pad]
    return jnp.concatenate(parts, 0)


def own_lanes(values, width):
    owner = lax.broadcasted_iota(jnp.int32, values[0].shape, 1) // width
    out = values[0]
    for c in range(1, len(values)):
        out = jnp.where(owner == c, values[c], out)
    return out


def one_hot(source, start, height):
    row = lax.broadcasted_iota(jnp.int32, (height, source.shape[1]), 0) + start
    return jnp.where(row == source, 1.0, 0.0).astype(BF)


def chain_step(matrix, trace, rhs, rows=slice(None)):
    half = trace.shape[1] // 2
    return jnp.concatenate(
        [mm(matrix[h, rows], split_lanes(trace[:, h * half : (h + 1) * half], rhs)) for h in range(2)], 1
    )


def shared_target(row, which):
    v, k = row // 16, row % 16
    a = k // 5
    j = k % 5
    b = jnp.where(j < 3, which, j - 3 if which == 2 else j - 2)
    c = jnp.where(j < 3, j, which)
    return jnp.where(k < 15, v * 27 + a * 9 + b * 3 + c, -1)


def picks(target, width):
    lane = lax.broadcasted_iota(jnp.int32, (target.shape[0], width), 1)
    return jnp.where(lane == target, 1.0, 0.0).astype(BF)


def rows_of(height):
    return lax.broadcasted_iota(jnp.int32, (height, 1), 0)


def first_target(row):
    return jnp.where(row < NT, row // 9 * 27 + row % 9, -1)


def c_target(row, which):
    return jnp.where(row < NT, row * 3 + which, -1)


def sources(neighbours, columns, rhs):
    place = lax.axis_index("cross")
    total = columns * lax.axis_size("cross")
    lane = lax.broadcasted_iota(jnp.int32, (1, columns * rhs), 1)
    out = []
    for face, first in ((2, place - 1), (3, place)):
        which = jnp.zeros_like(lane)
        for c in range(columns):
            at = lax.rem(neighbours[face, c] - first * columns + 2 * total, total)
            which = jnp.where(lane // rhs == c, at, which)
        out.append(which * rhs + lane % rhs)
    return out


def first_kernel(initial, up, down, above):
    planes, columns, rhs, width = initial.shape
    shared = rows_of(SHARED)
    tables = [picks(shared_target(shared, which), width) for which in (2, 0)]
    for p in range(planes):
        x = initial[p].reshape(columns * rhs, width)
        up[p] = mt(tables[0], x).astype(BF)
        down[p] = mt(tables[1], x).astype(BF)
        if p == 0:
            above[...] = mt(picks(first_target(rows_of(FACE)), width), x).astype(BF)


def turned(rows, raw, put):
    count, columns, width = rows.shape
    raw[0, : count * columns] = rows[:, :, :128].astype(F32).reshape(count * columns, 128)
    raw[1, : count * columns, : width - 128] = rows[:, :, 128:].astype(F32).reshape(count * columns, width - 128)
    for c in range(columns):
        put(c, jnp.concatenate([raw[i, pl.ds(c, FACE, stride=columns), :] for i in range(2)], 1))


def weight_kernel(
    inverse, couplings, right, initial, neighbours,
    known, lower, upper, base, fore, own,
    inverse_in, couplings_in, right_in, initial_in, solves, faces, prev, tables, raw, done,
):
    planes, columns, rhs, width = initial.shape
    size = columns * rhs
    half = columns // 2

    def arrivals(p):
        pairs = ((inverse, inverse_in), (couplings, couplings_in), (right, right_in))
        return [pltpu.make_async_copy(x.at[p], y.at[p], done.at[i, p]) for i, (x, y) in enumerate(pairs)]

    start = pltpu.make_async_copy(initial, initial_in, done.at[3, 0])
    for p in range(planes):
        for copy in arrivals(p):
            copy.start()
    start.start()
    faces[...] = jnp.zeros(faces.shape, BF)
    raw[...] = jnp.zeros(raw.shape, F32)
    tables[:FACE] = picks(c_target(rows_of(FACE), 2), width)
    tables[FACE : 2 * FACE] = picks(c_target(rows_of(FACE), 0), width)
    tables[2 * FACE :] = picks(first_target(rows_of(FACE)), width)
    source = sources(neighbours, columns, rhs)
    lane = lax.broadcasted_iota(jnp.int32, (ROWS, 2 * SLOT), 1)
    start.wait()

    @pl.loop(0, planes)
    def _(p):
        x = initial_in[p].reshape(size, width)
        beyond = initial_in[jnp.minimum(p + 1, planes - 1)].reshape(size, width)
        after = jnp.where(p + 1 < planes, mt(tables[2 * FACE :], beyond), 0.0)
        mine = mt(tables[: 2 * FACE], x).astype(BF)
        own[p, :FACE] = mm(mine[:FACE], one_hot(source[0], size, size)).astype(BF)
        own[p, FACE:] = mm(mine[FACE:], one_hot(source[1], 0, size)).astype(BF)
        for copy in arrivals(p):
            copy.wait()
        for a in range(3):
            rows = [inverse_in[p, v * 27 + a * 9 : v * 27 + a * 9 + 9] for v in range(5)]


            def put(c, value):
                solves[c, a * FACE : (a + 1) * FACE] = (-value).astype(BF)

            turned(jnp.concatenate(rows, 0), raw.at[a], put)
        places = (256, 256 + SLOT, 0, FACE, 2 * FACE, 3 * FACE)
        for f, place in enumerate(places):

            def put(c, value):
                faces[c, place : place + FACE] = value.astype(BF)

            turned(couplings_in[p, f], raw.at[3 + f], put)
        faces[:, 4 * FACE : 4 * FACE + rhs, :width] = right_in[p]

        bases = []
        before = None
        for c in range(columns):
            solve = solves[c]
            all_known = mt(solve, faces[c, :256])
            side = all_known[:, 128:]
            move = (c % half * rhs - (4 * FACE - 128)) % 128
            bases.append(pltpu.roll(side, move, 1) if move else side)
            known[p, c] = all_known.astype(BF)
            both = mt(solve, faces[c, 256:])
            if c % 2 == 0:
                before = both
            else:
                h, at = c // half, c % half // 2 * 2 * SLOT
                lanes = slice(at, at + 2 * SLOT)
                lower[p, h, :ROWS, lanes] = jnp.where(lane < SLOT, before, pltpu.roll(both, SLOT, 1)).astype(BF)
                upper[p, h, :ROWS, lanes] = jnp.where(lane < SLOT, pltpu.roll(before, SLOT, 1), both).astype(BF)
        for h in range(2):
            lanes = slice(h * half * rhs, (h + 1) * half * rhs)
            here = -own_lanes(bases[h * half : (h + 1) * half], rhs)
            base[p, :, lanes] = here
            fore[p, :, lanes] = here + mm(upper[p, h, :ROWS], split_lanes(after[:, lanes], rhs))
            step = lower[p, h, 2 * FACE : ROWS]

            @pl.when(p == 0)
            def _():
                prev[h] = step.astype(F32)

            @pl.when(p > 0)
            def _():
                prev[h] = mm(step, split_lanes(prev[h], SLOT))

            lower[p, h, ROWS:] = prev[h].astype(BF)

    for h in range(2):
        total = upper[planes - 1, h, :FACE].astype(F32)
        upper[planes - 1, h, ROWS:] = total.astype(BF)
        for q in range(planes - 2, -1, -1):
            total = mm(upper[q, h, :FACE], split_lanes(total, SLOT))
            upper[q, h, ROWS:] = total.astype(BF)


def gathered(received_up, received_down, own, p, up_sel, down_sel, low_pick, high_pick):
    low = mm(up_sel, received_up[p]).astype(BF)
    high = mm(down_sel, received_down[p]).astype(BF)
    c_low = mm(low[FACE:], low_pick).astype(BF) + own[p, :FACE]
    c_high = mm(high[FACE:], high_pick).astype(BF) + own[p, FACE : 2 * FACE]
    return [low[:FACE], high[:FACE], c_low, c_high]


def known_part(known_c, operand, columns, rhs):
    half = columns // 2
    out = []
    for h in range(2):
        side = operand[:, h * half * rhs : (h + 1) * half * rhs]
        out.append(own_lanes([mm(known_c(h * half + c), side) for c in range(half)], rhs))
    return jnp.concatenate(out, 1)


FIRST = slice(0, FACE)
LAST = slice(2 * FACE, ROWS)
FULL = slice(0, ROWS)
PRODUCT = slice(ROWS, ROWS + FACE)


def chain_kernel(known, base, matrix, received, own, neighbours, outs, order, rows, rhs, extra=None):
    up, down, up_sel, down_sel = received
    operand, start, traces, message, *wide = outs
    planes, columns = known.shape[:2]
    size = columns * rhs
    source = sources(neighbours, columns, rhs)
    low_pick = one_hot(source[0], 0, size)
    high_pick = one_hot(source[1], size, size)
    trace = None
    for p in order:
        parts = gathered(up, down, own, p, up_sel[...], down_sel[...], low_pick, high_pick)
        parts.append(jnp.zeros((256 - 4 * FACE, size), BF))
        whole = jnp.concatenate(parts, 0)
        operand[p] = whole
        value = base[p, rows] + known_part(lambda c: known[p, c, rows], whole, columns, rhs)
        if extra is not None and p == planes - 1:
            value = value + chain_step(extra[0].at[p], extra[1][...], rhs, rows)
        start[p] = value
        trace = value if trace is None else value + chain_step(matrix.at[p], trace, rhs, rows)
        traces[p] = trace
    message[...] = trace.astype(BF)
    for both in wide:
        both[FIRST] = trace.astype(BF)
        for h in range(2):
            both[(1 + h) * FACE : (2 + h) * FACE] = matrix[order[-1], h, PRODUCT]


def base_kernel(known, operand, base, *rest, rows, rhs):
    planes, columns = known.shape[:2]
    out = rest[-1]
    for p in range(planes):
        value = base[p, rows] + known_part(lambda c: known[p, c, rows], operand[p], columns, rhs)
        if len(rest) > 1 and p == planes - 1:
            value = value + chain_step(rest[1].at[p], rest[0][...], rhs, rows)
        out[p] = value


def forward_chain_kernel(
    up, down, above, own, neighbours, up_sel, down_sel, known, lower, upper, base, *outs, rhs
):
    order = range(up.shape[0])
    received = (up, down, up_sel, down_sel)
    chain_kernel(known, base, lower, received, own, neighbours, outs, order, LAST, rhs, (upper, above))


def backward_chain_kernel(up, down, own, neighbours, up_sel, down_sel, known, upper, base, *outs, rhs):
    order = range(up.shape[0] - 1, -1, -1)
    chain_kernel(
        known, base, upper, (up, down, up_sel, down_sel), own, neighbours, outs, order, FIRST, rhs
    )


def incoming(one, two, three, near, next_near, rhs):
    def carried(product, trace):
        half = trace.shape[1] // 2
        halves = [trace[:, h * half : (h + 1) * half] for h in range(2)]
        return jnp.concatenate([mm(m, split_lanes(t, rhs)) for m, t in zip(product, halves)], 1)

    trace = two[FIRST].astype(F32) + carried(next_near, three[FIRST])
    return one[FIRST].astype(F32) + carried(near, trace)


def inside(message):
    return [message[(1 + h) * FACE : (2 + h) * FACE] for h in range(2)]


def forward_finish_kernel(
    one, two, three, start, rest, traces, lower, send, middle, change, up, down, *, rhs
):
    planes = start.shape[0]
    entry = incoming(one, two, three, inside(one), inside(two), rhs)
    trace = entry
    for p in range(planes):
        delta = chain_step(lower.at[p], trace, rhs, FULL)
        change[p] = delta
        whole = (jnp.concatenate([rest[p], start[p]], 0) + delta).astype(BF)
        middle[p] = whole
        out = mm(send[...], whole).astype(BF)
        up[p] = out[:SHARED]
        down[p] = out[SHARED:]
        if p + 1 < planes:
            trace = traces[p] + chain_step(lower.at[p], entry, rhs, PRODUCT)


def middle_kernel(middle, change, base, neighbours, own_sel, own, out):
    planes, _, size = middle.shape
    columns = neighbours.shape[1]
    source = sources(neighbours, columns, size // columns)
    low_pick = one_hot(source[0], size, size)
    high_pick = one_hot(source[1], 0, size)
    for p in range(planes):
        mine = mm(own_sel[...], middle[p]).astype(BF)
        own[p, :FACE] = mm(mine[:FACE], low_pick).astype(BF)
        own[p, FACE:] = mm(mine[FACE:], high_pick).astype(BF)
        out[p] = base[p] + change[p]


def backward_finish_kernel(
    one, two, three, near, next_near, start, rest, traces, upper, back, result, *, rhs
):
    planes = start.shape[0]
    entry = incoming(one, two, three, [near[0], near[1]], [next_near[0], next_near[1]], rhs)
    size = entry.shape[1]
    row = lax.broadcasted_iota(jnp.int32, (size, size), 0)
    column = lax.broadcasted_iota(jnp.int32, (size, size), 1)
    unit = jnp.where(row == column, 1.0, 0.0).astype(BF)
    columns, _, width = result.shape[1:]
    trace = entry
    for p in range(planes - 1, -1, -1):
        whole = jnp.concatenate([start[p], rest[p]], 0) + chain_step(upper.at[p], trace, rhs, FULL)
        flat = mm(back[...], whole.astype(BF)).astype(BF)
        result[p] = mt(unit, flat).astype(BF).reshape(columns, rhs, width)
        if p:
            trace = traces[p] + chain_step(upper.at[p], entry, rhs, PRODUCT)


def call(kernel, outs, operands, name, flops=2e8, far=(), scratch=()):
    shapes = [jax.ShapeDtypeStruct(s, d) for s, d in outs]
    nbytes = sum(x.size * x.dtype.itemsize for x in list(operands) + shapes)
    spaces = [pltpu.SMEM if x.dtype == jnp.int32 else pltpu.VMEM for x in operands]
    spaces = [pltpu.HBM if i in far else space for i, space in enumerate(spaces)]
    operands = [
        pltpu.with_memory_space_constraint(x, pltpu.HBM) if i in far else x for i, x in enumerate(operands)
    ]
    scratch = list(scratch)
    if far and not scratch:
        scratch = [pltpu.VMEM(operands[i].shape, operands[i].dtype) for i in far]
        scratch.append(pltpu.SemaphoreType.DMA((len(far),)))
    return pl.pallas_call(
        kernel,
        out_shape=shapes,
        in_specs=[pl.BlockSpec(memory_space=space) for space in spaces],
        out_specs=[pl.BlockSpec(memory_space=pltpu.VMEM)] * len(shapes),
        scratch_shapes=scratch,
        compiler_params=pltpu.CompilerParams(vmem_limit_bytes=24 * MIB),
        cost_estimate=pl.CostEstimate(flops=int(flops), bytes_accessed=int(nbytes), transcendentals=0),
        name=name,
    )(*operands)


def products(x, by):
    n = lax.axis_size("sweep")
    inner = range(1, n - 1)
    return [
        lax.ppermute(x, "sweep", [(i, i + step) for i in inner if 0 <= i + step < n]) for step in (by, 2 * by)
    ]


def weights(inverse, couplings, right, initial, neighbours):
    planes, columns, rhs, width = initial.shape
    size = columns * rhs
    pack = (planes, 2, ROWS + FACE, 256)
    field = (planes, ROWS, size)
    outs = [((planes, columns, ROWS, 256), BF), (pack, BF), (pack, BF), (field, F32), (field, F32)]
    outs.append(((planes, 2 * FACE, size), BF))
    operands = (inverse, couplings, right, initial, neighbours)
    scratch = [pltpu.VMEM(x.shape, x.dtype) for x in operands[:4]] + [
        pltpu.VMEM((columns, ROWS, 256), BF),
        pltpu.VMEM((columns, 256 + 2 * SLOT, 256), BF),
        pltpu.VMEM((2, FACE, 256), F32),
        pltpu.VMEM((3 * FACE, width), BF),
        pltpu.VMEM((9, 2, FACE * columns, 128), F32),
        pltpu.SemaphoreType.DMA((4, planes)),
    ]
    return call(weight_kernel, outs, operands, "weights", 1e10, (0, 1, 2, 3), scratch)


def ring(x, axis, by):
    n = lax.axis_size(axis)
    return lax.ppermute(x, axis, [(i, (i + by) % n) for i in range(n)])


def shift(x, axis, by):
    n = lax.axis_size(axis)
    return lax.ppermute(x, axis, [(i, i + by) for i in range(n) if 0 <= i + by < n])


def local(right_sides, initial, inverse_blocks, couplings, neighbours):
    planes, columns, rhs, width = initial.shape
    size = columns * rhs
    const = lambda x: jnp.asarray(x, BF)
    send_in = const(send_table(ROWS, inner))
    own_in = const(own_table(ROWS, inner))
    back = const(table(width, ROWS, [(natural(*n), n) for n in NODES], inner))
    up_sel = const(receive_table(2))
    down_sel = const(receive_table(0))
    beside = neighbours.T

    share = (planes, SHARED, size)
    up, down, above = call(
        first_kernel, [(share, BF), (share, BF), ((FACE, size), BF)], (initial,), "initial_traces"
    )
    up, down, above, initial = lax.optimization_barrier((up, down, above, initial))
    from_low = ring(up, "cross", 1)
    from_high = ring(down, "cross", -1)
    from_above = shift(above, "sweep", -1)
    known, lower, upper, base, fore, own = weights(
        inverse_blocks.transpose(0, 2, 1, 3), couplings.transpose(0, 2, 3, 1, 4), right_sides, initial, beside
    )

    field = (planes, ROWS, size)
    trace = (planes, FACE, size)
    most = (planes, 2 * FACE, size)
    chain_outs = [((planes, 256, size), BF), (trace, F32), (trace, F32)]
    operand, start, traces, message, wide = call(
        functools.partial(forward_chain_kernel, rhs=rhs),
        chain_outs + [((FACE, size), BF), ((3 * FACE, size), BF)],
        (from_low, from_high, from_above, own, beside, up_sel, down_sel, known, lower, upper, fore),
        "forward_chain",
    )
    three = shift(message, "sweep", 3)
    two, one = (shift(wide, "sweep", by) for by in (2, 1))
    (rest,) = call(
        functools.partial(base_kernel, rows=slice(0, 2 * FACE), rhs=rhs),
        [(most, F32)],
        (known, operand, fore, from_above, upper),
        "forward_base",
    )
    middle, change, up, down = call(
        functools.partial(forward_finish_kernel, rhs=rhs),
        [(field, BF), (field, F32), (share, BF), (share, BF)],
        (one, two, three, start, rest, traces, lower, send_in),
        "forward_finish",
    )
    from_low = ring(up, "cross", 1)
    from_high = ring(down, "cross", -1)
    own, base = call(
        middle_kernel,
        [((planes, 2 * FACE, size), BF), (field, F32)],
        (middle, change, base, beside, own_in),
        "middle",
        2e9,
    )
    own, pass_b = lax.optimization_barrier((own, upper[0, :, PRODUCT]))
    passes = products(pass_b, -1)
    operand, start, traces, message = call(
        functools.partial(backward_chain_kernel, rhs=rhs),
        chain_outs + [((FACE, size), BF)],
        (from_low, from_high, own, beside, up_sel, down_sel, known, upper, base),
        "backward_chain",
    )
    three, two, one = (shift(message, "sweep", -by) for by in (3, 2, 1))
    (rest,) = call(
        functools.partial(base_kernel, rows=slice(FACE, ROWS), rhs=rhs),
        [(most, F32)],
        (known, operand, base),
        "backward_base",
    )
    (result,) = call(
        functools.partial(backward_finish_kernel, rhs=rhs),
        [(right_sides.shape, BF)],
        (one, two, three, *passes, start, rest, traces, upper, back),
        "backward_finish",
    )
    return result


def solution(mesh):
    return jax.shard_map(
        local,
        mesh=mesh,
        in_specs=(
            P("sweep", "cross", None, None),
            P("sweep", "cross", None, None),
            P("sweep", "cross", None, None),
            P("sweep", "cross", None, None, None),
            P("cross", None),
        ),
        out_specs=P("sweep", "cross", None, None),
        check_vma=False,
    )
```

```python
import functools

import jax
import jax.numpy as jnp
import numpy as np
from jax import lax
from jax.experimental import pallas as pl
from jax.experimental.pallas import tpu as pltpu
from jax.sharding import PartitionSpec as P

BF = jnp.bfloat16
F32 = jnp.float32
NT = 45
FACE = 48
SLOT = 64
ROWS = 3 * FACE
SHARED = 80
MIB = 1 << 20
FIRST = slice(0, FACE)
LAST = slice(2 * FACE, ROWS)
FULL = slice(0, ROWS)
PRODUCT = slice(ROWS, ROWS + FACE)


def natural(v, a, b, c):
    return v * 27 + a * 9 + b * 3 + c


def inner(v, a, b, c):
    return a * FACE + v * 9 + b * 3 + c


NODES = [(v, a, b, c) for v in range(5) for a in range(3) for b in range(3) for c in range(3)]


def face_nodes(place, which):
    return [n for n in NODES if n[1 + place] == which]


def union_rows(which):
    others = [b for b in range(3) if b != which]
    spots = [(which, c) for c in range(3)] + [(b, which) for b in others]
    return [
        (v * 16 + a * 5 + j, (v, a, b, c)) for v in range(5) for a in range(3) for j, (b, c) in enumerate(spots)
    ]


def table(height, width, rows, column_of, value=1.0):
    out = np.zeros((height, width), np.float32)
    for row, node in rows:
        out[row, column_of(*node)] = value
    return out


def block(nodes, start=0):
    return [(start + i, n) for i, n in enumerate(nodes)]


def send_table(width, column_of):
    rows = union_rows(2) + [(SHARED + i, n) for i, n in union_rows(0)]
    return table(2 * SHARED, width, rows, column_of)


def own_table(width, column_of):
    rows = block(face_nodes(2, 2)) + block(face_nodes(2, 0), FACE)
    return table(2 * FACE, width, rows, column_of)


def receive_table(which):
    place = {n: i for i, n in union_rows(which)}
    rows = block(face_nodes(1, which)) + block(face_nodes(2, which), FACE)
    return table(2 * FACE, SHARED, rows, lambda *n: place[n])


def mm(a, b):
    return lax.dot_general(a, b, (((1,), (0,)), ((), ())), preferred_element_type=F32)


def mt(a, b):
    return lax.dot_general(a, b, (((1,), (1,)), ((), ())), preferred_element_type=F32)


def split_lanes(value, width):
    lanes = value.shape[1]
    value = value.astype(F32)
    owner = lax.broadcasted_iota(jnp.int32, value.shape, 1) // width
    pad = jnp.zeros((SLOT - FACE, lanes), BF)
    parts = []
    for c in range(lanes // width):
        parts += [jnp.where(owner == c, value, 0.0).astype(BF), pad]
    return jnp.concatenate(parts, 0)


def own_lanes(values, width):
    owner = lax.broadcasted_iota(jnp.int32, values[0].shape, 1) // width
    out = values[0]
    for c in range(1, len(values)):
        out = jnp.where(owner == c, values[c], out)
    return out


def one_hot(source, start, height):
    row = lax.broadcasted_iota(jnp.int32, (height, source.shape[1]), 0) + start
    return jnp.where(row == source, 1.0, 0.0).astype(BF)


def chain_step(matrix, trace, rhs, rows=slice(None)):
    half = trace.shape[1] // 2
    return jnp.concatenate(
        [mm(matrix[h, rows], split_lanes(trace[:, h * half : (h + 1) * half], rhs)) for h in range(2)], 1
    )


def shared_target(row, which):
    v, k = row // 16, row % 16
    a = k // 5
    j = k % 5
    b = jnp.where(j < 3, which, j - 3 if which == 2 else j - 2)
    c = jnp.where(j < 3, j, which)
    return jnp.where(k < 15, v * 27 + a * 9 + b * 3 + c, -1)


def picks(target, width):
    lane = lax.broadcasted_iota(jnp.int32, (target.shape[0], width), 1)
    return jnp.where(lane == target, 1.0, 0.0).astype(BF)


def rows_of(height):
    return lax.broadcasted_iota(jnp.int32, (height, 1), 0)


def first_target(row):
    return jnp.where(row < NT, row // 9 * 27 + row % 9, -1)


def c_target(row, which):
    return jnp.where(row < NT, row * 3 + which, -1)


def sources(neighbours, columns, rhs):
    place = lax.axis_index("cross")
    total = columns * lax.axis_size("cross")
    lane = lax.broadcasted_iota(jnp.int32, (1, columns * rhs), 1)
    out = []
    for face, first in ((2, place - 1), (3, place)):
        which = jnp.zeros_like(lane)
        for c in range(columns):
            at = lax.rem(neighbours[face, c] - first * columns + 2 * total, total)
            which = jnp.where(lane // rhs == c, at, which)
        out.append(which * rhs + lane % rhs)
    return out


def first_kernel(initial, up, down, above):
    planes, columns, rhs, width = initial.shape
    shared = rows_of(SHARED)
    tables = [picks(shared_target(shared, which), width) for which in (2, 0)]
    for p in range(planes):
        x = initial[p].reshape(columns * rhs, width)
        up[p] = mt(tables[0], x).astype(BF)
        down[p] = mt(tables[1], x).astype(BF)
        if p == 0:
            above[...] = mt(picks(first_target(rows_of(FACE)), width), x).astype(BF)


def turned(rows, raw, put):
    count, columns, width = rows.shape
    raw[0, : count * columns] = rows[:, :, :128].astype(F32).reshape(count * columns, 128)
    raw[1, : count * columns, : width - 128] = rows[:, :, 128:].astype(F32).reshape(count * columns, width - 128)
    for c in range(columns):
        put(c, jnp.concatenate([raw[i, pl.ds(c, FACE, stride=columns), :] for i in range(2)], 1))


def weight_kernel(
    inverse, couplings, right, initial, neighbours,
    known, lower, upper, base, fore, own, gathers,
    inverse_in, right_in, solves, faces, raw, done,
):
    planes, columns, rhs, width = initial.shape
    size = columns * rhs
    half = columns // 2
    copies = []
    for p in range(planes):
        pairs = ((inverse, inverse_in), (right, right_in))
        copies.append([pltpu.make_async_copy(x.at[p], y.at[p], done.at[i, p]) for i, (x, y) in enumerate(pairs)])
        for copy in copies[p]:
            copy.start()
    faces[...] = jnp.zeros(faces.shape, BF)
    raw[...] = jnp.zeros(raw.shape, F32)
    source = sources(neighbours, columns, rhs)
    for i, start in enumerate((0, size)):
        for j in range(2):
            gathers[i, j] = one_hot(source[j], start, size)
    own_table = [picks(c_target(rows_of(FACE), which), width) for which in (2, 0)]
    first_table = picks(first_target(rows_of(FACE)), width)
    fields = [initial[p].reshape(size, width) for p in range(planes)]
    for j in range(2):
        mine = jnp.concatenate([mt(own_table[j], x).astype(BF) for x in fields], 0)
        mine = mm(mine, gathers[1 - j, j]).astype(BF)
        for p in range(planes):
            own[p, j * FACE : (j + 1) * FACE] = mine[p * FACE : (p + 1) * FACE]
    lane = lax.broadcasted_iota(jnp.int32, (ROWS, 2 * SLOT), 1)

    for p in range(planes):
        slot = p % 2
        for c in range(columns):
            for f, place in enumerate((256, 256 + SLOT, 0, FACE, 2 * FACE, 3 * FACE)):
                faces[slot, c, place : place + NT, :width] = couplings[p, c, f]
        for copy in copies[p]:
            copy.wait()
        faces[slot, :, 4 * FACE : 4 * FACE + rhs, :width] = right_in[p]
        for a in range(3):
            rows = [inverse_in[p, v * 27 + a * 9 : v * 27 + a * 9 + 9] for v in range(5)]

            def put(c, value):
                solves[slot, c, a * FACE : (a + 1) * FACE] = (-value).astype(BF)

            turned(jnp.concatenate(rows, 0), raw.at[slot, a], put)
        bases, lowers, uppers = [], [], []
        before = None
        for c in range(columns):
            solve = solves[slot, c]
            all_known = mt(solve, faces[slot, c, :256])
            side = all_known[:, 128:]
            move = (c % half * rhs - (4 * FACE - 128)) % 128
            bases.append(pltpu.roll(side, move, 1) if move else side)
            known[p, c] = all_known.astype(BF)
            both = mt(solve, faces[slot, c, 256:])
            if c % 2 == 0:
                before = both
            else:
                lowers.append(jnp.where(lane < SLOT, before, pltpu.roll(both, SLOT, 1)).astype(BF))
                uppers.append(jnp.where(lane < SLOT, pltpu.roll(before, SLOT, 1), both).astype(BF))
        for h in range(2):
            lanes = slice(h * half * rhs, (h + 1) * half * rhs)
            lower[p, h, :ROWS] = jnp.concatenate(lowers[2 * h : 2 * h + 2], 1)
            up = jnp.concatenate(uppers[2 * h : 2 * h + 2], 1)
            upper[p, h, :ROWS] = up
            here = -own_lanes(bases[h * half : (h + 1) * half], rhs)
            base[p, :, lanes] = here
            if p + 1 < planes:
                here = here + mm(up, split_lanes(mt(first_table, fields[p + 1])[:, lanes], rhs))
            fore[p, :, lanes] = here

    for h in range(2):
        for matrix, rows, order in ((lower, LAST, range(planes)), (upper, FIRST, range(planes - 1, -1, -1))):
            total = None
            for q in order:
                step = matrix[q, h, rows]
                total = step.astype(F32) if total is None else mm(step, split_lanes(total, SLOT))
                matrix[q, h, PRODUCT] = total.astype(BF)


def gathered(received_up, received_down, own, up_sel, down_sel, gathers):
    planes, _, size = received_up.shape
    low = [mm(up_sel[...], received_up[p]).astype(BF) for p in range(planes)]
    high = [mm(down_sel[...], received_down[p]).astype(BF) for p in range(planes)]
    sides = []
    for j, side in enumerate((low, high)):
        picked = mm(jnp.concatenate([x[FACE:] for x in side], 0), gathers[j, j]).astype(BF)
        sides.append([picked[p * FACE : (p + 1) * FACE] + own[p, j * FACE : (j + 1) * FACE] for p in range(planes)])
    pad = jnp.zeros((256 - 4 * FACE, size), BF)
    return [jnp.concatenate([low[p][:FACE], high[p][:FACE], sides[0][p], sides[1][p], pad], 0) for p in range(planes)]


def known_part(known_c, operand, columns, rhs):
    half = columns // 2
    out = []
    for h in range(2):
        side = operand[:, h * half * rhs : (h + 1) * half * rhs]
        out.append(own_lanes([mm(known_c(h * half + c), side) for c in range(half)], rhs))
    return jnp.concatenate(out, 1)


def chain_kernel(known, base, matrix, received, own, gathers, outs, order, rows, rhs, extra=None):
    up, down, up_sel, down_sel = received
    operand, start, traces, message, *wide = outs
    planes, columns = known.shape[:2]
    wholes = gathered(up, down, own, up_sel, down_sel, gathers)
    trace = None
    for p in order:
        whole = wholes[p]
        operand[p] = whole
        value = base[p, rows] + known_part(lambda c: known[p, c, rows], whole, columns, rhs)
        if extra is not None and p == planes - 1:
            value = value + chain_step(extra[0].at[p], extra[1][...], rhs, rows)
        start[p] = value
        trace = value if trace is None else value + chain_step(matrix.at[p], trace, rhs, rows)
        traces[p] = trace
    message[...] = trace.astype(BF)
    for both in wide:
        both[FIRST] = trace.astype(BF)
        for h in range(2):
            both[(1 + h) * FACE : (2 + h) * FACE] = matrix[order[-1], h, PRODUCT]


def base_kernel(known, operand, base, *rest, rows, rhs):
    planes, columns = known.shape[:2]
    out = rest[-1]
    for p in range(planes):
        value = base[p, rows] + known_part(lambda c: known[p, c, rows], operand[p], columns, rhs)
        if len(rest) > 1 and p == planes - 1:
            value = value + chain_step(rest[1].at[p], rest[0][...], rhs, rows)
        out[p] = value


def forward_chain_kernel(
    up, down, above, own, gathers, up_sel, down_sel, known, lower, upper, base, *outs, rhs
):
    order = range(up.shape[0])
    received = (up, down, up_sel, down_sel)
    chain_kernel(known, base, lower, received, own, gathers, outs, order, LAST, rhs, (upper, above))


def backward_chain_kernel(up, down, own, gathers, up_sel, down_sel, known, upper, base, *outs, rhs):
    order = range(up.shape[0] - 1, -1, -1)
    chain_kernel(
        known, base, upper, (up, down, up_sel, down_sel), own, gathers, outs, order, FIRST, rhs
    )


def incoming(one, two, three, near, next_near, rhs):
    def carried(product, trace):
        half = trace.shape[1] // 2
        halves = [trace[:, h * half : (h + 1) * half] for h in range(2)]
        return jnp.concatenate([mm(m, split_lanes(t, rhs)) for m, t in zip(product, halves)], 1)

    trace = two[FIRST].astype(F32) + carried(next_near, three[FIRST])
    return one[FIRST].astype(F32) + carried(near, trace)


def inside(message):
    return [message[(1 + h) * FACE : (2 + h) * FACE] for h in range(2)]


def forward_finish_kernel(
    one, two, three, start, rest, traces, lower, send, middle, change, up, down, *, rhs
):
    planes = start.shape[0]
    entry = incoming(one, two, three, inside(one), inside(two), rhs)
    trace = entry
    for p in range(planes):
        delta = chain_step(lower.at[p], trace, rhs, FULL)
        change[p] = delta
        whole = (jnp.concatenate([rest[p], start[p]], 0) + delta).astype(BF)
        middle[p] = whole
        out = mm(send[...], whole).astype(BF)
        up[p] = out[:SHARED]
        down[p] = out[SHARED:]
        if p + 1 < planes:
            trace = traces[p] + chain_step(lower.at[p], entry, rhs, PRODUCT)


def middle_kernel(middle, change, base, gathers, own_sel, own, out):
    planes = middle.shape[0]
    mine = [mm(own_sel[...], middle[p]).astype(BF) for p in range(planes)]
    for j in range(2):
        side = jnp.concatenate([x[j * FACE : (j + 1) * FACE] for x in mine], 0)
        side = mm(side, gathers[1 - j, j]).astype(BF)
        for p in range(planes):
            own[p, j * FACE : (j + 1) * FACE] = side[p * FACE : (p + 1) * FACE]
    for p in range(planes):
        out[p] = base[p] + change[p]


def backward_finish_kernel(
    one, two, three, near, next_near, start, rest, traces, upper, back, result, *, rhs
):
    planes = start.shape[0]
    entry = incoming(one, two, three, [near[0], near[1]], [next_near[0], next_near[1]], rhs)
    size = entry.shape[1]
    row = lax.broadcasted_iota(jnp.int32, (size, size), 0)
    column = lax.broadcasted_iota(jnp.int32, (size, size), 1)
    unit = jnp.where(row == column, 1.0, 0.0).astype(BF)
    columns, _, width = result.shape[1:]
    trace = entry
    for p in range(planes - 1, -1, -1):
        whole = jnp.concatenate([start[p], rest[p]], 0) + chain_step(upper.at[p], trace, rhs, FULL)
        flat = mm(back[...], whole.astype(BF)).astype(BF)
        result[p] = mt(unit, flat).astype(BF).reshape(columns, rhs, width)
        if p:
            trace = traces[p] + chain_step(upper.at[p], entry, rhs, PRODUCT)


def call(kernel, outs, operands, name, flops=2e8, far=(), scratch=()):
    shapes = [jax.ShapeDtypeStruct(s, d) for s, d in outs]
    nbytes = sum(x.size * x.dtype.itemsize for x in list(operands) + shapes)
    spaces = [pltpu.SMEM if x.dtype == jnp.int32 else pltpu.VMEM for x in operands]
    spaces = [pltpu.HBM if i in far else space for i, space in enumerate(spaces)]
    operands = [
        pltpu.with_memory_space_constraint(x, pltpu.HBM) if i in far else x for i, x in enumerate(operands)
    ]
    scratch = list(scratch)
    if far and not scratch:
        scratch = [pltpu.VMEM(operands[i].shape, operands[i].dtype) for i in far]
        scratch.append(pltpu.SemaphoreType.DMA((len(far),)))
    return pl.pallas_call(
        kernel,
        out_shape=shapes,
        in_specs=[pl.BlockSpec(memory_space=space) for space in spaces],
        out_specs=[pl.BlockSpec(memory_space=pltpu.VMEM)] * len(shapes),
        scratch_shapes=scratch,
        compiler_params=pltpu.CompilerParams(vmem_limit_bytes=24 * MIB),
        cost_estimate=pl.CostEstimate(flops=int(flops), bytes_accessed=int(nbytes), transcendentals=0),
        name=name,
    )(*operands)


def products(x, by):
    n = lax.axis_size("sweep")
    inner = range(1, n - 1)
    return [
        lax.ppermute(x, "sweep", [(i, i + step) for i in inner if 0 <= i + step < n]) for step in (by, 2 * by)
    ]


def weights(inverse, couplings, right, initial, neighbours):
    planes, columns, rhs, width = initial.shape
    size = columns * rhs
    pack = (planes, 2, ROWS + FACE, 256)
    field = (planes, ROWS, size)
    outs = [((planes, columns, ROWS, 256), BF), (pack, BF), (pack, BF), (field, F32), (field, F32)]
    outs += [((planes, 2 * FACE, size), BF), ((2, 2, size, size), BF)]
    operands = (inverse, couplings, right, initial, neighbours)
    scratch = [
        pltpu.VMEM(inverse.shape, BF),
        pltpu.VMEM(right.shape, BF),
        pltpu.VMEM((2, columns, ROWS, 256), BF),
        pltpu.VMEM((2, columns, 256 + 2 * SLOT, 256), BF),
        pltpu.VMEM((2, 3, 2, FACE * columns, 128), F32),
        pltpu.SemaphoreType.DMA((2, planes)),
    ]
    return call(weight_kernel, outs, operands, "weights", 1e10, (0, 2), scratch)


def ring(x, axis, by):
    n = lax.axis_size(axis)
    return lax.ppermute(x, axis, [(i, (i + by) % n) for i in range(n)])


def shift(x, axis, by):
    n = lax.axis_size(axis)
    return lax.ppermute(x, axis, [(i, i + by) for i in range(n) if 0 <= i + by < n])


def local(right_sides, initial, inverse_blocks, couplings, neighbours):
    planes, columns, rhs, width = initial.shape
    size = columns * rhs
    const = lambda x: jnp.asarray(x, BF)
    send_in = const(send_table(ROWS, inner))
    own_in = const(own_table(ROWS, inner))
    back = const(table(width, ROWS, [(natural(*n), n) for n in NODES], inner))
    up_sel = const(receive_table(2))
    down_sel = const(receive_table(0))
    beside = neighbours.T

    share = (planes, SHARED, size)
    up, down, above = call(
        first_kernel, [(share, BF), (share, BF), ((FACE, size), BF)], (initial,), "initial_traces"
    )
    up, down, above, initial = lax.optimization_barrier((up, down, above, initial))
    from_low = ring(up, "cross", 1)
    from_high = ring(down, "cross", -1)
    from_above = shift(above, "sweep", -1)
    known, lower, upper, base, fore, own, gathers = weights(
        inverse_blocks.transpose(0, 2, 1, 3), couplings, right_sides, initial, beside
    )

    field = (planes, ROWS, size)
    trace = (planes, FACE, size)
    most = (planes, 2 * FACE, size)
    chain_outs = [((planes, 256, size), BF), (trace, F32), (trace, F32)]
    operand, start, traces, message, wide = call(
        functools.partial(forward_chain_kernel, rhs=rhs),
        chain_outs + [((FACE, size), BF), ((3 * FACE, size), BF)],
        (from_low, from_high, from_above, own, gathers, up_sel, down_sel, known, lower, upper, fore),
        "forward_chain",
    )
    three = shift(message, "sweep", 3)
    two, one = (shift(wide, "sweep", by) for by in (2, 1))
    (rest,) = call(
        functools.partial(base_kernel, rows=slice(0, 2 * FACE), rhs=rhs),
        [(most, F32)],
        (known, operand, fore, from_above, upper),
        "forward_base",
    )
    middle, change, up, down = call(
        functools.partial(forward_finish_kernel, rhs=rhs),
        [(field, BF), (field, F32), (share, BF), (share, BF)],
        (one, two, three, start, rest, traces, lower, send_in),
        "forward_finish",
    )
    from_low = ring(up, "cross", 1)
    from_high = ring(down, "cross", -1)
    own, base = call(
        middle_kernel,
        [((planes, 2 * FACE, size), BF), (field, F32)],
        (middle, change, base, gathers, own_in),
        "middle",
        2e9,
    )
    own, pass_b = lax.optimization_barrier((own, upper[0, :, PRODUCT]))
    passes = products(pass_b, -1)
    operand, start, traces, message = call(
        functools.partial(backward_chain_kernel, rhs=rhs),
        chain_outs + [((FACE, size), BF)],
        (from_low, from_high, own, gathers, up_sel, down_sel, known, upper, base),
        "backward_chain",
    )
    three, two, one = (shift(message, "sweep", -by) for by in (3, 2, 1))
    (rest,) = call(
        functools.partial(base_kernel, rows=slice(FACE, ROWS), rhs=rhs),
        [(most, F32)],
        (known, operand, base),
        "backward_base",
    )
    (result,) = call(
        functools.partial(backward_finish_kernel, rhs=rhs),
        [(right_sides.shape, BF)],
        (one, two, three, *passes, start, rest, traces, upper, back),
        "backward_finish",
    )
    return result


def solution(mesh):
    return jax.shard_map(
        local,
        mesh=mesh,
        in_specs=(
            P("sweep", "cross", None, None),
            P("sweep", "cross", None, None),
            P("sweep", "cross", None, None),
            P("sweep", "cross", None, None, None),
            P("cross", None),
        ),
        out_specs=P("sweep", "cross", None, None),
        check_vma=False,
    )
```

```python
import functools

import jax
import jax.numpy as jnp
import numpy as np
from jax import lax
from jax.experimental import pallas as pl
from jax.experimental.pallas import tpu as pltpu
from jax.sharding import PartitionSpec as P

BF = jnp.bfloat16
F32 = jnp.float32
NT = 45
FACE = 48
SLOT = 64
ROWS = 3 * FACE
SHARED = 80
MIB = 1 << 20
FIRST = slice(0, FACE)
LAST = slice(2 * FACE, ROWS)
FULL = slice(0, ROWS)
PRODUCT = slice(ROWS, ROWS + FACE)


def natural(v, a, b, c):
    return v * 27 + a * 9 + b * 3 + c


def inner(v, a, b, c):
    return a * FACE + v * 9 + b * 3 + c


NODES = [(v, a, b, c) for v in range(5) for a in range(3) for b in range(3) for c in range(3)]


def face_nodes(place, which):
    return [n for n in NODES if n[1 + place] == which]


def union_rows(which):
    others = [b for b in range(3) if b != which]
    spots = [(which, c) for c in range(3)] + [(b, which) for b in others]
    return [
        (v * 16 + a * 5 + j, (v, a, b, c)) for v in range(5) for a in range(3) for j, (b, c) in enumerate(spots)
    ]


def table(height, width, rows, column_of, value=1.0):
    out = np.zeros((height, width), np.float32)
    for row, node in rows:
        out[row, column_of(*node)] = value
    return out


def block(nodes, start=0):
    return [(start + i, n) for i, n in enumerate(nodes)]


def send_table(width, column_of):
    rows = union_rows(2) + [(SHARED + i, n) for i, n in union_rows(0)]
    return table(2 * SHARED, width, rows, column_of)


def own_table(width, column_of):
    rows = block(face_nodes(2, 2)) + block(face_nodes(2, 0), FACE)
    return table(2 * FACE, width, rows, column_of)


def receive_table(which):
    place = {n: i for i, n in union_rows(which)}
    rows = block(face_nodes(1, which)) + block(face_nodes(2, which), FACE)
    return table(2 * FACE, SHARED, rows, lambda *n: place[n])


def mm(a, b):
    return lax.dot_general(a, b, (((1,), (0,)), ((), ())), preferred_element_type=F32)


def mt(a, b):
    return lax.dot_general(a, b, (((1,), (1,)), ((), ())), preferred_element_type=F32)


def group(shape, width, at):
    lane = lax.broadcasted_iota(jnp.int32, shape, 1)
    return (lane >= at * width) & (lane < (at + 1) * width)


def split_lanes(value, width):
    lanes = value.shape[1]
    value = value.astype(F32)
    pad = jnp.zeros((SLOT - FACE, lanes), BF)
    parts = []
    for c in range(lanes // width):
        parts += [jnp.where(group(value.shape, width, c), value, 0.0).astype(BF), pad]
    return jnp.concatenate(parts, 0)


def own_lanes(values, width):
    out = values[0]
    for c in range(1, len(values)):
        out = jnp.where(group(out.shape, width, c), values[c], out)
    return out


def one_hot(source, start, height):
    row = lax.broadcasted_iota(jnp.int32, (height, source.shape[1]), 0) + start
    return jnp.where(row == source, 1.0, 0.0).astype(BF)


def chain_step(matrix, trace, rhs, rows=slice(None)):
    half = trace.shape[1] // 2
    return jnp.concatenate(
        [mm(matrix[h, rows], split_lanes(trace[:, h * half : (h + 1) * half], rhs)) for h in range(2)], 1
    )


def shared_target(row, which):
    v, k = row // 16, row % 16
    a = k // 5
    j = k % 5
    b = jnp.where(j < 3, which, j - 3 if which == 2 else j - 2)
    c = jnp.where(j < 3, j, which)
    return jnp.where(k < 15, v * 27 + a * 9 + b * 3 + c, -1)


def picks(target, width):
    lane = lax.broadcasted_iota(jnp.int32, (target.shape[0], width), 1)
    return jnp.where(lane == target, 1.0, 0.0).astype(BF)


def rows_of(height):
    return lax.broadcasted_iota(jnp.int32, (height, 1), 0)


def first_target(row):
    return jnp.where(row < NT, row // 9 * 27 + row % 9, -1)


def c_target(row, which):
    return jnp.where(row < NT, row * 3 + which, -1)


def sources(neighbours, columns, rhs):
    place = lax.axis_index("cross")
    total = columns * lax.axis_size("cross")
    lane = lax.broadcasted_iota(jnp.int32, (1, columns * rhs), 1)
    out = []
    for face, first in ((2, place - 1), (3, place)):
        source = lane
        for c in range(columns):
            at = neighbours[face, c] - first * columns
            at = jnp.where(at < 0, at + total, at)
            at = jnp.where(at >= total, at - total, at)
            source = jnp.where(lane >= c * rhs, lane + (at - c) * rhs, source)
        out.append(source)
    return out


def first_kernel(initial, up, down, above):
    planes, columns, rhs, width = initial.shape
    shared = rows_of(SHARED)
    tables = [picks(shared_target(shared, which), width) for which in (2, 0)]
    for p in range(planes):
        x = initial[p].reshape(columns * rhs, width)
        up[p] = mt(tables[0], x).astype(BF)
        down[p] = mt(tables[1], x).astype(BF)
        if p == 0:
            above[...] = mt(picks(first_target(rows_of(FACE)), width), x).astype(BF)


def turned(rows, raw, put):
    count, columns, width = rows.shape
    raw[0, : count * columns] = rows[:, :, :128].astype(F32).reshape(count * columns, 128)
    raw[1, : count * columns, : width - 128] = rows[:, :, 128:].astype(F32).reshape(count * columns, width - 128)
    for c in range(columns):
        put(c, jnp.concatenate([raw[i, pl.ds(c, FACE, stride=columns), :] for i in range(2)], 1))


def weight_kernel(
    inverse, couplings, right, initial, neighbours,
    known, lower, base, own, gathers,
    inverse_in, couplings_in, right_in, solves, faces, raw, done,
):
    planes, columns, rhs, width = initial.shape
    size = columns * rhs
    half = columns // 2
    copies = []
    for p in range(planes):
        pairs = ((inverse, inverse_in), (couplings, couplings_in), (right, right_in))
        copies.append([pltpu.make_async_copy(x.at[p], y.at[p], done.at[i, p]) for i, (x, y) in enumerate(pairs)])
        for copy in copies[p]:
            copy.start()
    faces[...] = jnp.zeros(faces.shape, BF)
    raw[...] = jnp.zeros(raw.shape, F32)
    source = sources(neighbours, columns, rhs)
    for i, start in enumerate((0, size)):
        for j in range(2):
            gathers[i, j] = one_hot(source[j], start, size)
    own_table = [picks(c_target(rows_of(FACE), which), width) for which in (2, 0)]
    first_table = picks(first_target(rows_of(FACE)), width)
    fields = [initial[p].reshape(size, width) for p in range(planes)]
    for j in range(2):
        mine = jnp.concatenate([mt(own_table[j], x).astype(BF) for x in fields], 0)
        mine = mm(mine, gathers[1 - j, j]).astype(BF)
        for p in range(planes):
            own[p, j * FACE : (j + 1) * FACE] = mine[p * FACE : (p + 1) * FACE]
    for p in range(planes):
        own[p, LAST] = mt(first_table, fields[min(p + 1, planes - 1)]).astype(BF)
    lane = lax.broadcasted_iota(jnp.int32, (ROWS, 2 * SLOT), 1)

    for p in range(planes):
        slot = p % 2
        for copy in copies[p]:
            copy.wait()
        faces[slot, :, 256 + SLOT : 256 + SLOT + rhs, :width] = right_in[p]
        for a in range(3):
            rows = [inverse_in[p, v * 27 + a * 9 : v * 27 + a * 9 + 9] for v in range(5)]

            def put(c, value):
                solves[slot, c, a * FACE : (a + 1) * FACE] = (-value).astype(BF)

            turned(jnp.concatenate(rows, 0), raw.at[slot, a], put)
        for f, place in enumerate((256, 4 * FACE, 0, FACE, 2 * FACE, 3 * FACE)):

            def put(c, value):
                faces[slot, c, place : place + FACE] = value.astype(BF)

            turned(couplings_in[p, f], raw.at[slot, 3 + f], put)
        bases, lowers = [], []
        before = None
        for c in range(columns):
            solve = solves[slot, c]
            known[p, c] = mt(solve, faces[slot, c, :256]).astype(BF)
            both = mt(solve, faces[slot, c, 256:])
            move = (c % half * rhs - SLOT) % 128
            bases.append(pltpu.roll(both, move, 1) if move else both)
            if c % 2 == 0:
                before = both
            else:
                lowers.append(jnp.where(lane < SLOT, before, pltpu.roll(both, SLOT, 1)).astype(BF))
        for h in range(2):
            lanes = slice(h * half * rhs, (h + 1) * half * rhs)
            lower[p, h, :ROWS] = jnp.concatenate(lowers[2 * h : 2 * h + 2], 1)
            base[p, :, lanes] = -own_lanes(bases[h * half : (h + 1) * half], rhs)
    chain_products(lower, LAST, range(planes))


def chain_products(matrix, rows, order):
    for h in range(2):
        total = None
        for q in order:
            step = matrix[q, h, rows]
            total = step.astype(F32) if total is None else mm(step, split_lanes(total, SLOT))
            matrix[q, h, PRODUCT] = total.astype(BF)


def gathered(received_up, received_down, own, up_sel, down_sel, gathers):
    planes = received_up.shape[0]
    low = [mm(up_sel[...], received_up[p]).astype(BF) for p in range(planes)]
    high = [mm(down_sel[...], received_down[p]).astype(BF) for p in range(planes)]
    sides = []
    for j, side in enumerate((low, high)):
        picked = mm(jnp.concatenate([x[FACE:] for x in side], 0), gathers[j, j]).astype(BF)
        sides.append([picked[p * FACE : (p + 1) * FACE] + own[p, j * FACE : (j + 1) * FACE] for p in range(planes)])
    return [[low[p][:FACE], high[p][:FACE], sides[0][p], sides[1][p]] for p in range(planes)]


def known_part(known_c, operand, columns, rhs):
    half = columns // 2
    out = []
    for h in range(2):
        side = operand[:, h * half * rhs : (h + 1) * half * rhs]
        out.append(own_lanes([mm(known_c(h * half + c), side) for c in range(half)], rhs))
    return jnp.concatenate(out, 1)


def chain_kernel(known, base, matrix, received, own, gathers, outs, order, rows, rhs, above=None):
    up, down, up_sel, down_sel = received
    operand, start, traces, message, *wide = outs
    planes, columns = known.shape[:2]
    size = operand.shape[2]
    wholes = gathered(up, down, own, up_sel, down_sel, gathers)
    trace = None
    for p in order:
        if above is None:
            last_face = jnp.zeros((256 - 4 * FACE, size), BF)
        else:
            face = own[p, LAST] if p + 1 < planes else above[...]
            last_face = jnp.concatenate([face, jnp.zeros((256 - 5 * FACE, size), BF)], 0)
        whole = jnp.concatenate(wholes[p] + [last_face], 0)
        operand[p] = whole
        value = base[p, rows] + known_part(lambda c: known[p, c, rows], whole, columns, rhs)
        start[p] = value
        trace = value if trace is None else value + chain_step(matrix.at[p], trace, rhs, rows)
        traces[p] = trace
    message[...] = trace.astype(BF)
    for both in wide:
        both[FIRST] = trace.astype(BF)
        for h in range(2):
            both[(1 + h) * FACE : (2 + h) * FACE] = matrix[order[-1], h, PRODUCT]


def base_kernel(known, operand, base, out, *, rows, rhs):
    planes, columns = known.shape[:2]
    for p in range(planes):
        out[p] = base[p, rows] + known_part(lambda c: known[p, c, rows], operand[p], columns, rhs)


def forward_chain_kernel(up, down, above, own, gathers, up_sel, down_sel, known, lower, base, *outs, rhs):
    order = range(up.shape[0])
    received = (up, down, up_sel, down_sel)
    chain_kernel(known, base, lower, received, own, gathers, outs, order, LAST, rhs, above)


def backward_chain_kernel(up, down, own, gathers, up_sel, down_sel, known, upper, base, *outs, rhs):
    order = range(up.shape[0] - 1, -1, -1)
    received = (up, down, up_sel, down_sel)
    chain_kernel(known, base, upper, received, own, gathers, outs, order, FIRST, rhs)


def incoming(one, two, three, near, next_near, rhs):
    def carried(product, trace):
        half = trace.shape[1] // 2
        halves = [trace[:, h * half : (h + 1) * half] for h in range(2)]
        return jnp.concatenate([mm(m, split_lanes(t, rhs)) for m, t in zip(product, halves)], 1)

    trace = two[FIRST].astype(F32) + carried(next_near, three[FIRST])
    return one[FIRST].astype(F32) + carried(near, trace)


def inside(message):
    return [message[(1 + h) * FACE : (2 + h) * FACE] for h in range(2)]


def forward_finish_kernel(
    one, two, three, start, rest, traces, lower, send, middle, change, up, down, *, rhs
):
    planes = start.shape[0]
    entry = incoming(one, two, three, inside(one), inside(two), rhs)
    trace = entry
    for p in range(planes):
        delta = chain_step(lower.at[p], trace, rhs, FULL)
        change[p] = delta
        whole = (jnp.concatenate([rest[p], start[p]], 0) + delta).astype(BF)
        middle[p] = whole
        out = mm(send[...], whole).astype(BF)
        up[p] = out[:SHARED]
        down[p] = out[SHARED:]
        if p + 1 < planes:
            trace = traces[p] + chain_step(lower.at[p], entry, rhs, PRODUCT)


def middle_kernel(middle, change, base, gathers, own_sel, known, own, out, upper):
    planes = middle.shape[0]
    mine = [mm(own_sel[...], middle[p]).astype(BF) for p in range(planes)]
    for j in range(2):
        side = jnp.concatenate([x[j * FACE : (j + 1) * FACE] for x in mine], 0)
        side = mm(side, gathers[1 - j, j]).astype(BF)
        for p in range(planes):
            own[p, j * FACE : (j + 1) * FACE] = side[p * FACE : (p + 1) * FACE]
    for p in range(planes):
        out[p] = base[p] + change[p]
    columns = known.shape[1]
    lane = lax.broadcasted_iota(jnp.int32, (ROWS, 2 * SLOT), 1)
    for p in range(planes):
        pairs = []
        for c in range(0, columns, 2):
            one, two = (known[p, c + i, :, 128:].astype(F32) for i in range(2))
            pairs.append(jnp.where(lane < SLOT, pltpu.roll(one, SLOT, 1), two).astype(BF))
        for h in range(2):
            upper[p, h, :ROWS] = jnp.concatenate(pairs[2 * h : 2 * h + 2], 1)
    chain_products(upper, FIRST, range(planes - 1, -1, -1))


def backward_finish_kernel(
    one, two, three, near, next_near, start, rest, traces, upper, back, result, results, sem, *, rhs
):
    planes = start.shape[0]
    entry = incoming(one, two, three, [near[0], near[1]], [next_near[0], next_near[1]], rhs)
    size = entry.shape[1]
    row = lax.broadcasted_iota(jnp.int32, (size, size), 0)
    column = lax.broadcasted_iota(jnp.int32, (size, size), 1)
    unit = jnp.where(row == column, 1.0, 0.0).astype(BF)
    columns, _, width = result.shape[1:]
    copies = []
    trace = entry
    for p in range(planes - 1, -1, -1):
        whole = jnp.concatenate([start[p], rest[p]], 0) + chain_step(upper.at[p], trace, rhs, FULL)
        flat = mm(back[...], whole.astype(BF)).astype(BF)
        results[p] = mt(unit, flat).astype(BF).reshape(columns, rhs, width)
        copies.append(pltpu.make_async_copy(results.at[p], result.at[p], sem.at[p]))
        copies[-1].start()
        if p:
            trace = traces[p] + chain_step(upper.at[p], entry, rhs, PRODUCT)
    for copy in copies:
        copy.wait()


def call(kernel, outs, operands, name, flops=2e8, far=(), scratch=(), out_space=pltpu.VMEM):
    shapes = [jax.ShapeDtypeStruct(s, d) for s, d in outs]
    nbytes = sum(x.size * x.dtype.itemsize for x in list(operands) + shapes)
    spaces = [pltpu.SMEM if x.dtype == jnp.int32 else pltpu.VMEM for x in operands]
    spaces = [pltpu.HBM if i in far else space for i, space in enumerate(spaces)]
    operands = [
        pltpu.with_memory_space_constraint(x, pltpu.HBM) if i in far else x for i, x in enumerate(operands)
    ]
    return pl.pallas_call(
        kernel,
        out_shape=shapes,
        in_specs=[pl.BlockSpec(memory_space=space) for space in spaces],
        out_specs=[pl.BlockSpec(memory_space=out_space)] * len(shapes),
        scratch_shapes=list(scratch),
        compiler_params=pltpu.CompilerParams(vmem_limit_bytes=24 * MIB),
        cost_estimate=pl.CostEstimate(flops=int(flops), bytes_accessed=int(nbytes), transcendentals=0),
        name=name,
    )(*operands)


def products(x, by):
    n = lax.axis_size("sweep")
    inner = range(1, n - 1)
    return [
        lax.ppermute(x, "sweep", [(i, i + step) for i in inner if 0 <= i + step < n]) for step in (by, 2 * by)
    ]


def weights(inverse, couplings, right, initial, neighbours):
    planes, columns, rhs, width = initial.shape
    size = columns * rhs
    pack = (planes, 2, ROWS + FACE, 256)
    field = (planes, ROWS, size)
    outs = [((planes, columns, ROWS, 256), BF), (pack, BF), (field, F32), (field, BF), ((2, 2, size, size), BF)]
    operands = (inverse, couplings, right, initial, neighbours)
    scratch = [pltpu.VMEM(x.shape, BF) for x in operands[:3]] + [
        pltpu.VMEM((2, columns, ROWS, 256), BF),
        pltpu.VMEM((2, columns, 256 + 2 * SLOT, 256), BF),
        pltpu.VMEM((2, 9, 2, FACE * columns, 128), F32),
        pltpu.SemaphoreType.DMA((3, planes)),
    ]
    return call(weight_kernel, outs, operands, "weights", 1e10, (0, 1, 2), scratch)


def ring(x, axis, by):
    n = lax.axis_size(axis)
    return lax.ppermute(x, axis, [(i, (i + by) % n) for i in range(n)])


def shift(x, axis, by):
    n = lax.axis_size(axis)
    return lax.ppermute(x, axis, [(i, i + by) for i in range(n) if 0 <= i + by < n])


def local(right_sides, initial, inverse_blocks, couplings, neighbours):
    planes, columns, rhs, width = initial.shape
    size = columns * rhs
    const = lambda x: jnp.asarray(x, BF)
    send_in = const(send_table(ROWS, inner))
    own_in = const(own_table(ROWS, inner))
    back = const(table(width, ROWS, [(natural(*n), n) for n in NODES], inner))
    up_sel = const(receive_table(2))
    down_sel = const(receive_table(0))
    beside = neighbours.T

    share = (planes, SHARED, size)
    up, down, above = call(
        first_kernel, [(share, BF), (share, BF), ((FACE, size), BF)], (initial,), "initial_traces"
    )
    up, down, above, initial = lax.optimization_barrier((up, down, above, initial))
    from_low = ring(up, "cross", 1)
    from_high = ring(down, "cross", -1)
    from_above = shift(above, "sweep", -1)
    known, lower, base, own, gathers = weights(
        inverse_blocks.transpose(0, 2, 1, 3), couplings.transpose(0, 2, 3, 1, 4), right_sides, initial, beside
    )

    field = (planes, ROWS, size)
    trace = (planes, FACE, size)
    most = (planes, 2 * FACE, size)
    chain_outs = [((planes, 256, size), BF), (trace, F32), (trace, F32)]
    operand, start, traces, message, wide = call(
        functools.partial(forward_chain_kernel, rhs=rhs),
        chain_outs + [((FACE, size), BF), ((3 * FACE, size), BF)],
        (from_low, from_high, from_above, own, gathers, up_sel, down_sel, known, lower, base),
        "forward_chain",
    )
    three = shift(message, "sweep", 3)
    two, one = (shift(wide, "sweep", by) for by in (2, 1))
    (rest,) = call(
        functools.partial(base_kernel, rows=slice(0, 2 * FACE), rhs=rhs),
        [(most, F32)],
        (known, operand, base),
        "forward_base",
    )
    middle, change, up, down = call(
        functools.partial(forward_finish_kernel, rhs=rhs),
        [(field, BF), (field, F32), (share, BF), (share, BF)],
        (one, two, three, start, rest, traces, lower, send_in),
        "forward_finish",
    )
    from_low = ring(up, "cross", 1)
    from_high = ring(down, "cross", -1)
    own, base, upper = call(
        middle_kernel,
        [((planes, 2 * FACE, size), BF), (field, F32), (lower.shape, BF)],
        (middle, change, base, gathers, own_in, known),
        "middle",
        2e9,
    )
    own, pass_b = lax.optimization_barrier((own, upper[0, :, PRODUCT]))
    passes = products(pass_b, -1)
    operand, start, traces, message = call(
        functools.partial(backward_chain_kernel, rhs=rhs),
        chain_outs + [((FACE, size), BF)],
        (from_low, from_high, own, gathers, up_sel, down_sel, known, upper, base),
        "backward_chain",
    )
    three, two, one = (shift(message, "sweep", -by) for by in (3, 2, 1))
    (rest,) = call(
        functools.partial(base_kernel, rows=slice(FACE, ROWS), rhs=rhs),
        [(most, F32)],
        (known, operand, base),
        "backward_base",
    )
    (result,) = call(
        functools.partial(backward_finish_kernel, rhs=rhs),
        [(right_sides.shape, BF)],
        (one, two, three, *passes, start, rest, traces, upper, back),
        "backward_finish",
        scratch=[pltpu.VMEM(right_sides.shape, BF), pltpu.SemaphoreType.DMA((planes,))],
        out_space=pltpu.HBM,
    )
    return result


def solution(mesh):
    return jax.shard_map(
        local,
        mesh=mesh,
        in_specs=(
            P("sweep", "cross", None, None),
            P("sweep", "cross", None, None),
            P("sweep", "cross", None, None),
            P("sweep", "cross", None, None, None),
            P("cross", None),
        ),
        out_specs=P("sweep", "cross", None, None),
        check_vma=False,
    )
```

```python
import functools

import jax
import jax.numpy as jnp
import numpy as np
from jax import lax
from jax.experimental import pallas as pl
from jax.experimental.pallas import tpu as pltpu
from jax.sharding import PartitionSpec as P

BF = jnp.bfloat16
F32 = jnp.float32
NT = 45
FACE = 48
SLOT = 64
ROWS = 3 * FACE
SHARED = 80
MIB = 1 << 20
FIRST = slice(0, FACE)
LAST = slice(2 * FACE, ROWS)
FULL = slice(0, ROWS)
PRODUCT = slice(ROWS, ROWS + FACE)


def natural(v, a, b, c):
    return v * 27 + a * 9 + b * 3 + c


def inner(v, a, b, c):
    return a * FACE + v * 9 + b * 3 + c


NODES = [(v, a, b, c) for v in range(5) for a in range(3) for b in range(3) for c in range(3)]


def face_nodes(place, which):
    return [n for n in NODES if n[1 + place] == which]


def union_rows(which):
    others = [b for b in range(3) if b != which]
    spots = [(which, c) for c in range(3)] + [(b, which) for b in others]
    return [
        (v * 16 + a * 5 + j, (v, a, b, c)) for v in range(5) for a in range(3) for j, (b, c) in enumerate(spots)
    ]


def table(height, width, rows, column_of, value=1.0):
    out = np.zeros((height, width), np.float32)
    for row, node in rows:
        out[row, column_of(*node)] = value
    return out


def block(nodes, start=0):
    return [(start + i, n) for i, n in enumerate(nodes)]


def send_table(width, column_of):
    rows = union_rows(2) + [(SHARED + i, n) for i, n in union_rows(0)]
    return table(2 * SHARED, width, rows, column_of)


def own_table(width, column_of):
    rows = block(face_nodes(2, 2)) + block(face_nodes(2, 0), FACE)
    return table(2 * FACE, width, rows, column_of)


def receive_table(which):
    place = {n: i for i, n in union_rows(which)}
    rows = block(face_nodes(1, which)) + block(face_nodes(2, which), FACE)
    return table(2 * FACE, SHARED, rows, lambda *n: place[n])


def mm(a, b):
    return lax.dot_general(a, b, (((1,), (0,)), ((), ())), preferred_element_type=F32)


def mt(a, b):
    return lax.dot_general(a, b, (((1,), (1,)), ((), ())), preferred_element_type=F32)


def group(shape, width, at):
    lane = lax.broadcasted_iota(jnp.int32, shape, 1)
    return (lane >= at * width) & (lane < (at + 1) * width)


def split_lanes(value, width):
    lanes = value.shape[1]
    value = value.astype(F32)
    pad = jnp.zeros((SLOT - FACE, lanes), BF)
    parts = []
    for c in range(lanes // width):
        parts += [jnp.where(group(value.shape, width, c), value, 0.0).astype(BF), pad]
    return jnp.concatenate(parts, 0)


def own_lanes(values, width):
    out = values[0]
    for c in range(1, len(values)):
        out = jnp.where(group(out.shape, width, c), values[c], out)
    return out


def one_hot(source, start, height):
    row = lax.broadcasted_iota(jnp.int32, (height, source.shape[1]), 0) + start
    return jnp.where(row == source, 1.0, 0.0).astype(BF)


def chain_step(matrix, trace, rhs, rows=slice(None)):
    half = trace.shape[1] // 2
    return jnp.concatenate(
        [mm(matrix[h, rows], split_lanes(trace[:, h * half : (h + 1) * half], rhs)) for h in range(2)], 1
    )


def shared_target(row, which):
    v, k = row // 16, row % 16
    a = k // 5
    j = k % 5
    b = jnp.where(j < 3, which, j - 3 if which == 2 else j - 2)
    c = jnp.where(j < 3, j, which)
    return jnp.where(k < 15, v * 27 + a * 9 + b * 3 + c, -1)


def picks(target, width):
    lane = lax.broadcasted_iota(jnp.int32, (target.shape[0], width), 1)
    return jnp.where(lane == target, 1.0, 0.0).astype(BF)


def rows_of(height):
    return lax.broadcasted_iota(jnp.int32, (height, 1), 0)


def first_target(row):
    return jnp.where(row < NT, row // 9 * 27 + row % 9, -1)


def c_target(row, which):
    return jnp.where(row < NT, row * 3 + which, -1)


def sources(neighbours, columns, rhs):
    place = lax.axis_index("cross")
    total = columns * lax.axis_size("cross")
    lane = lax.broadcasted_iota(jnp.int32, (1, columns * rhs), 1)
    out = []
    for face, first in ((2, place - 1), (3, place)):
        source = lane
        for c in range(columns):
            at = neighbours[face, c] - first * columns
            at = jnp.where(at < 0, at + total, at)
            at = jnp.where(at >= total, at - total, at)
            source = jnp.where(lane >= c * rhs, lane + (at - c) * rhs, source)
        out.append(source)
    return out


def first_kernel(initial, up, down, above):
    planes, columns, rhs, width = initial.shape
    shared = rows_of(SHARED)
    tables = [picks(shared_target(shared, which), width) for which in (2, 0)]
    for p in range(planes):
        x = initial[p].reshape(columns * rhs, width)
        up[p] = mt(tables[0], x).astype(BF)
        down[p] = mt(tables[1], x).astype(BF)
        if p == 0:
            above[...] = mt(picks(first_target(rows_of(FACE)), width), x).astype(BF)


def turned(rows, raw, put):
    count, columns, width = rows.shape
    raw[0, : count * columns] = rows[:, :, :128].astype(F32).reshape(count * columns, 128)
    raw[1, : count * columns, : width - 128] = rows[:, :, 128:].astype(F32).reshape(count * columns, width - 128)
    for c in range(columns):
        put(c, jnp.concatenate([raw[i, pl.ds(c, FACE, stride=columns), :] for i in range(2)], 1))


def weight_kernel(
    inverse, couplings, right, initial, neighbours,
    known, lower, base, own, gathers,
    inverse_in, couplings_in, right_in, solves, faces, raw, done,
):
    planes, columns, rhs, width = initial.shape
    size = columns * rhs
    half = columns // 2
    copies = []
    for p in range(planes):
        pairs = ((inverse, inverse_in), (couplings, couplings_in), (right, right_in))
        copies.append([pltpu.make_async_copy(x.at[p], y.at[p], done.at[i, p]) for i, (x, y) in enumerate(pairs)])
        for copy in copies[p]:
            copy.start()
    faces[...] = jnp.zeros(faces.shape, BF)
    raw[...] = jnp.zeros(raw.shape, F32)
    source = sources(neighbours, columns, rhs)
    for i, start in enumerate((0, size)):
        for j in range(2):
            gathers[i, j] = one_hot(source[j], start, size)
    own_table = [picks(c_target(rows_of(FACE), which), width) for which in (2, 0)]
    first_table = picks(first_target(rows_of(FACE)), width)
    fields = [initial[p].reshape(size, width) for p in range(planes)]
    for j in range(2):
        mine = jnp.concatenate([mt(own_table[j], x).astype(BF) for x in fields], 0)
        mine = mm(mine, gathers[1 - j, j]).astype(BF)
        for p in range(planes):
            own[p, j * FACE : (j + 1) * FACE] = mine[p * FACE : (p + 1) * FACE]
    for p in range(planes):
        own[p, LAST] = mt(first_table, fields[min(p + 1, planes - 1)]).astype(BF)
    lane = lax.broadcasted_iota(jnp.int32, (ROWS, 2 * SLOT), 1)

    for p in range(planes):
        slot = p % 2
        for copy in copies[p]:
            copy.wait()
        faces[slot, :, 256 + SLOT : 256 + SLOT + rhs, :width] = right_in[p]
        for a in range(3):
            rows = [inverse_in[p, v * 27 + a * 9 : v * 27 + a * 9 + 9] for v in range(5)]

            def put(c, value):
                solves[slot, c, a * FACE : (a + 1) * FACE] = (-value).astype(BF)

            turned(jnp.concatenate(rows, 0), raw.at[slot, a], put)
        for f, place in enumerate((256, 4 * FACE, 0, FACE, 2 * FACE, 3 * FACE)):

            def put(c, value):
                faces[slot, c, place : place + FACE] = value.astype(BF)

            turned(couplings_in[p, f], raw.at[slot, 3 + f], put)
        bases, lowers = [], []
        before = None
        for c in range(columns):
            solve = solves[slot, c]
            known[p, c] = mt(solve, faces[slot, c, :256]).astype(BF)
            both = mt(solve, faces[slot, c, 256:])
            move = (c % half * rhs - SLOT) % 128
            bases.append(pltpu.roll(both, move, 1) if move else both)
            if c % 2 == 0:
                before = both
            else:
                lowers.append(jnp.where(lane < SLOT, before, pltpu.roll(both, SLOT, 1)).astype(BF))
        for h in range(2):
            lanes = slice(h * half * rhs, (h + 1) * half * rhs)
            lower[p, h, :ROWS] = jnp.concatenate(lowers[2 * h : 2 * h + 2], 1)
            base[p, :, lanes] = -own_lanes(bases[h * half : (h + 1) * half], rhs)
    chain_products(lower, LAST, range(planes))


def chain_products(matrix, rows, order):
    for h in range(2):
        total = None
        for q in order:
            step = matrix[q, h, rows]
            total = step.astype(F32) if total is None else mm(step, split_lanes(total, SLOT))
            matrix[q, h, PRODUCT] = total.astype(BF)


def gathered(received_up, received_down, own, up_sel, down_sel, gathers):
    planes = received_up.shape[0]
    low = [mm(up_sel[...], received_up[p]).astype(BF) for p in range(planes)]
    high = [mm(down_sel[...], received_down[p]).astype(BF) for p in range(planes)]
    sides = []
    for j, side in enumerate((low, high)):
        picked = mm(jnp.concatenate([x[FACE:] for x in side], 0), gathers[j, j]).astype(BF)
        sides.append([picked[p * FACE : (p + 1) * FACE] + own[p, j * FACE : (j + 1) * FACE] for p in range(planes)])
    return [[low[p][:FACE], high[p][:FACE], sides[0][p], sides[1][p]] for p in range(planes)]


def known_part(known_c, operand, columns, rhs):
    half = columns // 2
    out = []
    for h in range(2):
        side = operand[:, h * half * rhs : (h + 1) * half * rhs]
        out.append(own_lanes([mm(known_c(h * half + c), side) for c in range(half)], rhs))
    return jnp.concatenate(out, 1)


def chain_kernel(known, base, matrix, received, own, gathers, outs, order, rows, rhs, above=None):
    up, down, up_sel, down_sel = received
    operand, start, traces, message = outs
    planes, columns = known.shape[:2]
    size = operand.shape[2]
    wholes = gathered(up, down, own, up_sel, down_sel, gathers)
    trace = None
    for p in order:
        if above is None:
            last_face = jnp.zeros((256 - 4 * FACE, size), BF)
        else:
            face = own[p, LAST] if p + 1 < planes else above[...]
            last_face = jnp.concatenate([face, jnp.zeros((256 - 5 * FACE, size), BF)], 0)
        whole = jnp.concatenate(wholes[p] + [last_face], 0)
        operand[p] = whole
        value = base[p, rows] + known_part(lambda c: known[p, c, rows], whole, columns, rhs)
        start[p] = value
        trace = value if trace is None else value + chain_step(matrix.at[p], trace, rhs, rows)
        traces[p] = trace
    message[FIRST] = trace.astype(BF)
    if message.shape[0] > FACE:
        for h in range(2):
            message[(1 + h) * FACE : (2 + h) * FACE] = matrix[order[-1], h, PRODUCT]


def base_kernel(known, operand, base, out, *, rows, rhs):
    planes, columns = known.shape[:2]
    for p in range(planes):
        out[p] = base[p, rows] + known_part(lambda c: known[p, c, rows], operand[p], columns, rhs)


def forward_chain_kernel(up, down, above, own, gathers, up_sel, down_sel, known, lower, base, *outs, rhs):
    order = range(up.shape[0])
    received = (up, down, up_sel, down_sel)
    chain_kernel(known, base, lower, received, own, gathers, outs, order, LAST, rhs, above)


def backward_chain_kernel(up, down, own, gathers, up_sel, down_sel, known, upper, base, *outs, rhs):
    order = range(up.shape[0] - 1, -1, -1)
    received = (up, down, up_sel, down_sel)
    chain_kernel(known, base, upper, received, own, gathers, outs, order, FIRST, rhs)


def incoming(messages, products, forward, rhs):
    here = lax.axis_index("sweep")
    n = messages.shape[0]
    trace = None
    for i in range(n - 1) if forward else range(n - 1, 0, -1):
        value = messages[i, FIRST].astype(F32)
        if trace is None:
            trace = jnp.zeros_like(value)
        else:
            half = value.shape[1] // 2
            halves = [trace[:, h * half : (h + 1) * half] for h in range(2)]
            value = value + jnp.concatenate([mm(m, split_lanes(t, rhs)) for m, t in zip(products(i), halves)], 1)
        trace = jnp.where(i < here if forward else i > here, value, trace)
    return trace


def forward_finish_kernel(
    messages, start, rest, traces, lower, send, middle, change, up, down, *, rhs
):
    planes = start.shape[0]
    inside = lambda i: [messages[i, (1 + h) * FACE : (2 + h) * FACE] for h in range(2)]
    entry = incoming(messages, inside, True, rhs)
    trace = entry
    for p in range(planes):
        delta = chain_step(lower.at[p], trace, rhs, FULL)
        change[p] = delta
        whole = (jnp.concatenate([rest[p], start[p]], 0) + delta).astype(BF)
        middle[p] = whole
        out = mm(send[...], whole).astype(BF)
        up[p] = out[:SHARED]
        down[p] = out[SHARED:]
        if p + 1 < planes:
            trace = traces[p] + chain_step(lower.at[p], entry, rhs, PRODUCT)


def middle_kernel(middle, change, base, gathers, own_sel, known, own, out, upper):
    planes = middle.shape[0]
    mine = [mm(own_sel[...], middle[p]).astype(BF) for p in range(planes)]
    for j in range(2):
        side = jnp.concatenate([x[j * FACE : (j + 1) * FACE] for x in mine], 0)
        side = mm(side, gathers[1 - j, j]).astype(BF)
        for p in range(planes):
            own[p, j * FACE : (j + 1) * FACE] = side[p * FACE : (p + 1) * FACE]
    for p in range(planes):
        out[p] = base[p] + change[p]
    columns = known.shape[1]
    lane = lax.broadcasted_iota(jnp.int32, (ROWS, 2 * SLOT), 1)
    for p in range(planes):
        pairs = []
        for c in range(0, columns, 2):
            one, two = (known[p, c + i, :, 128:].astype(F32) for i in range(2))
            pairs.append(jnp.where(lane < SLOT, pltpu.roll(one, SLOT, 1), two).astype(BF))
        for h in range(2):
            upper[p, h, :ROWS] = jnp.concatenate(pairs[2 * h : 2 * h + 2], 1)
    chain_products(upper, FIRST, range(planes - 1, -1, -1))


def backward_finish_kernel(
    messages, near, next_near, start, rest, traces, upper, back, result, results, sem, *, rhs
):
    planes = start.shape[0]
    here = lax.axis_index("sweep")
    beside = lambda i: [jnp.where(here + 1 == i, near[h], next_near[h]) for h in range(2)]
    entry = incoming(messages, beside, False, rhs)
    size = entry.shape[1]
    row = lax.broadcasted_iota(jnp.int32, (size, size), 0)
    column = lax.broadcasted_iota(jnp.int32, (size, size), 1)
    unit = jnp.where(row == column, 1.0, 0.0).astype(BF)
    columns, _, width = result.shape[1:]
    copies = []
    trace = entry
    for p in range(planes - 1, -1, -1):
        whole = jnp.concatenate([start[p], rest[p]], 0) + chain_step(upper.at[p], trace, rhs, FULL)
        flat = mm(back[...], whole.astype(BF)).astype(BF)
        results[p] = mt(unit, flat).astype(BF).reshape(columns, rhs, width)
        copies.append(pltpu.make_async_copy(results.at[p], result.at[p], sem.at[p]))
        copies[-1].start()
        if p:
            trace = traces[p] + chain_step(upper.at[p], entry, rhs, PRODUCT)
    for copy in copies:
        copy.wait()


def call(kernel, outs, operands, name, flops=2e8, far=(), scratch=(), out_space=pltpu.VMEM):
    shapes = [jax.ShapeDtypeStruct(s, d) for s, d in outs]
    nbytes = sum(x.size * x.dtype.itemsize for x in list(operands) + shapes)
    spaces = [pltpu.SMEM if x.dtype == jnp.int32 else pltpu.VMEM for x in operands]
    spaces = [pltpu.HBM if i in far else space for i, space in enumerate(spaces)]
    operands = [
        pltpu.with_memory_space_constraint(x, pltpu.HBM) if i in far else x for i, x in enumerate(operands)
    ]
    return pl.pallas_call(
        kernel,
        out_shape=shapes,
        in_specs=[pl.BlockSpec(memory_space=space) for space in spaces],
        out_specs=[pl.BlockSpec(memory_space=out_space)] * len(shapes),
        scratch_shapes=list(scratch),
        compiler_params=pltpu.CompilerParams(vmem_limit_bytes=24 * MIB),
        cost_estimate=pl.CostEstimate(flops=int(flops), bytes_accessed=int(nbytes), transcendentals=0),
        name=name,
    )(*operands)


def products(x, by):
    n = lax.axis_size("sweep")
    inner = range(1, n - 1)
    return [
        lax.ppermute(x, "sweep", [(i, i + step) for i in inner if 0 <= i + step < n]) for step in (by, 2 * by)
    ]


def weights(inverse, couplings, right, initial, neighbours):
    planes, columns, rhs, width = initial.shape
    size = columns * rhs
    pack = (planes, 2, ROWS + FACE, 256)
    field = (planes, ROWS, size)
    outs = [((planes, columns, ROWS, 256), BF), (pack, BF), (field, F32), (field, BF), ((2, 2, size, size), BF)]
    operands = (inverse, couplings, right, initial, neighbours)
    scratch = [pltpu.VMEM(x.shape, BF) for x in operands[:3]] + [
        pltpu.VMEM((2, columns, ROWS, 256), BF),
        pltpu.VMEM((2, columns, 256 + 2 * SLOT, 256), BF),
        pltpu.VMEM((2, 9, 2, FACE * columns, 128), F32),
        pltpu.SemaphoreType.DMA((3, planes)),
    ]
    return call(weight_kernel, outs, operands, "weights", 1e10, (0, 1, 2), scratch)


def ring(x, axis, by):
    n = lax.axis_size(axis)
    return lax.ppermute(x, axis, [(i, (i + by) % n) for i in range(n)])


def shift(x, axis, by):
    n = lax.axis_size(axis)
    return lax.ppermute(x, axis, [(i, i + by) for i in range(n) if 0 <= i + by < n])


def local(right_sides, initial, inverse_blocks, couplings, neighbours):
    planes, columns, rhs, width = initial.shape
    size = columns * rhs
    const = lambda x: jnp.asarray(x, BF)
    send_in = const(send_table(ROWS, inner))
    own_in = const(own_table(ROWS, inner))
    back = const(table(width, ROWS, [(natural(*n), n) for n in NODES], inner))
    up_sel = const(receive_table(2))
    down_sel = const(receive_table(0))
    beside = neighbours.T

    share = (planes, SHARED, size)
    up, down, above = call(
        first_kernel, [(share, BF), (share, BF), ((FACE, size), BF)], (initial,), "initial_traces"
    )
    up, down, above, initial = lax.optimization_barrier((up, down, above, initial))
    from_low = ring(up, "cross", 1)
    from_high = ring(down, "cross", -1)
    from_above = shift(above, "sweep", -1)
    known, lower, base, own, gathers = weights(
        inverse_blocks.transpose(0, 2, 1, 3), couplings.transpose(0, 2, 3, 1, 4), right_sides, initial, beside
    )

    field = (planes, ROWS, size)
    trace = (planes, FACE, size)
    most = (planes, 2 * FACE, size)
    chain_outs = [((planes, 256, size), BF), (trace, F32), (trace, F32)]
    operand, start, traces, message = call(
        functools.partial(forward_chain_kernel, rhs=rhs),
        chain_outs + [((3 * FACE, size), BF)],
        (from_low, from_high, from_above, own, gathers, up_sel, down_sel, known, lower, base),
        "forward_chain",
    )
    messages = lax.all_gather(message, "sweep")
    (rest,) = call(
        functools.partial(base_kernel, rows=slice(0, 2 * FACE), rhs=rhs),
        [(most, F32)],
        (known, operand, base),
        "forward_base",
    )
    middle, change, up, down = call(
        functools.partial(forward_finish_kernel, rhs=rhs),
        [(field, BF), (field, F32), (share, BF), (share, BF)],
        (messages, start, rest, traces, lower, send_in),
        "forward_finish",
    )
    from_low = ring(up, "cross", 1)
    from_high = ring(down, "cross", -1)
    own, base, upper = call(
        middle_kernel,
        [((planes, 2 * FACE, size), BF), (field, F32), (lower.shape, BF)],
        (middle, change, base, gathers, own_in, known),
        "middle",
        2e9,
    )
    own, pass_b = lax.optimization_barrier((own, upper[0, :, PRODUCT]))
    passes = products(pass_b, -1)
    operand, start, traces, message = call(
        functools.partial(backward_chain_kernel, rhs=rhs),
        chain_outs + [((FACE, size), BF)],
        (from_low, from_high, own, gathers, up_sel, down_sel, known, upper, base),
        "backward_chain",
    )
    messages = lax.all_gather(message, "sweep")
    (rest,) = call(
        functools.partial(base_kernel, rows=slice(FACE, ROWS), rhs=rhs),
        [(most, F32)],
        (known, operand, base),
        "backward_base",
    )
    (result,) = call(
        functools.partial(backward_finish_kernel, rhs=rhs),
        [(right_sides.shape, BF)],
        (messages, *passes, start, rest, traces, upper, back),
        "backward_finish",
        scratch=[pltpu.VMEM(right_sides.shape, BF), pltpu.SemaphoreType.DMA((planes,))],
        out_space=pltpu.HBM,
    )
    return result


def solution(mesh):
    return jax.shard_map(
        local,
        mesh=mesh,
        in_specs=(
            P("sweep", "cross", None, None),
            P("sweep", "cross", None, None),
            P("sweep", "cross", None, None),
            P("sweep", "cross", None, None, None),
            P("cross", None),
        ),
        out_specs=P("sweep", "cross", None, None),
        check_vma=False,
    )
```

```python
import functools

import jax
import jax.numpy as jnp
import numpy as np
from jax import lax
from jax.experimental import pallas as pl
from jax.experimental.pallas import tpu as pltpu
from jax.sharding import PartitionSpec as P

BF = jnp.bfloat16
F32 = jnp.float32
NT = 45
FACE = 48
SLOT = 64
ROWS = 3 * FACE
SHARED = 80
MIB = 1 << 20
FIRST = slice(0, FACE)
LAST = slice(2 * FACE, ROWS)
FULL = slice(0, ROWS)
PRODUCT = slice(ROWS, ROWS + FACE)


def natural(v, a, b, c):
    return v * 27 + a * 9 + b * 3 + c


def inner(v, a, b, c):
    return a * FACE + v * 9 + b * 3 + c


NODES = [(v, a, b, c) for v in range(5) for a in range(3) for b in range(3) for c in range(3)]


def face_nodes(place, which):
    return [n for n in NODES if n[1 + place] == which]


def union_rows(which):
    others = [b for b in range(3) if b != which]
    spots = [(which, c) for c in range(3)] + [(b, which) for b in others]
    return [
        (v * 16 + a * 5 + j, (v, a, b, c)) for v in range(5) for a in range(3) for j, (b, c) in enumerate(spots)
    ]


def table(height, width, rows, column_of, value=1.0):
    out = np.zeros((height, width), np.float32)
    for row, node in rows:
        out[row, column_of(*node)] = value
    return out


def block(nodes, start=0):
    return [(start + i, n) for i, n in enumerate(nodes)]


def send_table(width, column_of):
    rows = union_rows(2) + [(SHARED + i, n) for i, n in union_rows(0)]
    return table(2 * SHARED, width, rows, column_of)


def own_table(width, column_of):
    rows = block(face_nodes(2, 2)) + block(face_nodes(2, 0), FACE)
    return table(2 * FACE, width, rows, column_of)


def receive_table(which):
    place = {n: i for i, n in union_rows(which)}
    rows = block(face_nodes(1, which)) + block(face_nodes(2, which), FACE)
    return table(2 * FACE, SHARED, rows, lambda *n: place[n])


def mm(a, b):
    return lax.dot_general(a, b, (((1,), (0,)), ((), ())), preferred_element_type=F32)


def mt(a, b):
    return lax.dot_general(a, b, (((1,), (1,)), ((), ())), preferred_element_type=F32)


def group(shape, width, at):
    lane = lax.broadcasted_iota(jnp.int32, shape, 1)
    return (lane >= at * width) & (lane < (at + 1) * width)


def split_lanes(value, width):
    lanes = value.shape[1]
    value = value.astype(F32)
    pad = jnp.zeros((SLOT - FACE, lanes), BF)
    parts = []
    for c in range(lanes // width):
        parts += [jnp.where(group(value.shape, width, c), value, 0.0).astype(BF), pad]
    return jnp.concatenate(parts, 0)


def own_lanes(values, width):
    out = values[0]
    for c in range(1, len(values)):
        out = jnp.where(group(out.shape, width, c), values[c], out)
    return out


def one_hot(source, start, height):
    row = lax.broadcasted_iota(jnp.int32, (height, source.shape[1]), 0) + start
    return jnp.where(row == source, 1.0, 0.0).astype(BF)


def chain_step(matrix, trace, rhs, rows=slice(None)):
    half = trace.shape[1] // 2
    return jnp.concatenate(
        [mm(matrix[h, rows], split_lanes(trace[:, h * half : (h + 1) * half], rhs)) for h in range(2)], 1
    )


def shared_target(row, which):
    v, k = row // 16, row % 16
    a = k // 5
    j = k % 5
    b = jnp.where(j < 3, which, j - 3 if which == 2 else j - 2)
    c = jnp.where(j < 3, j, which)
    return jnp.where(k < 15, v * 27 + a * 9 + b * 3 + c, -1)


def picks(target, width):
    lane = lax.broadcasted_iota(jnp.int32, (target.shape[0], width), 1)
    return jnp.where(lane == target, 1.0, 0.0).astype(BF)


def rows_of(height):
    return lax.broadcasted_iota(jnp.int32, (height, 1), 0)


def first_target(row):
    return jnp.where(row < NT, row // 9 * 27 + row % 9, -1)


def c_target(row, which):
    return jnp.where(row < NT, row * 3 + which, -1)


def sources(neighbours, columns, rhs):
    place = lax.axis_index("cross")
    total = columns * lax.axis_size("cross")
    lane = lax.broadcasted_iota(jnp.int32, (1, columns * rhs), 1)
    out = []
    for face, first in ((2, place - 1), (3, place)):
        source = lane
        for c in range(columns):
            at = neighbours[face, c] - first * columns
            at = jnp.where(at < 0, at + total, at)
            at = jnp.where(at >= total, at - total, at)
            source = jnp.where(lane >= c * rhs, lane + (at - c) * rhs, source)
        out.append(source)
    return out


def first_kernel(initial, up, down, above, initial_in, sem):
    planes, columns, rhs, width = initial.shape
    copies = [pltpu.make_async_copy(initial.at[p], initial_in.at[p], sem.at[p]) for p in range(planes)]
    for copy in copies:
        copy.start()
    shared = rows_of(SHARED)
    tables = [picks(shared_target(shared, which), width) for which in (2, 0)]
    first_table = picks(first_target(rows_of(FACE)), width)
    for p in range(planes):
        copies[p].wait()
        x = initial_in[p].reshape(columns * rhs, width)
        up[p] = mt(tables[0], x).astype(BF)
        down[p] = mt(tables[1], x).astype(BF)
        if p == 0:
            above[...] = mt(first_table, x).astype(BF)


def turned(rows, raw, put):
    count, columns, width = rows.shape
    raw[0, : count * columns] = rows[:, :, :128].astype(F32).reshape(count * columns, 128)
    raw[1, : count * columns, : width - 128] = rows[:, :, 128:].astype(F32).reshape(count * columns, width - 128)
    for c in range(columns):
        put(c, jnp.concatenate([raw[i, pl.ds(c, FACE, stride=columns), :] for i in range(2)], 1))


def weight_kernel(
    inverse, couplings, right, initial_there, neighbours_there,
    known, lower, base, own, gathers,
    inverse_in, couplings_in, right_in, initial, neighbours, solves, faces, raw, done,
):
    planes, columns, rhs, width = initial.shape
    size = columns * rhs
    half = columns // 2
    early = [
        pltpu.make_async_copy(neighbours_there, neighbours, done.at[3, 0]),
        pltpu.make_async_copy(initial_there, initial, done.at[3, 1]),
    ]
    for copy in early:
        copy.start()
    copies = []
    for p in range(planes):
        pairs = ((inverse, inverse_in), (couplings, couplings_in), (right, right_in))
        copies.append([pltpu.make_async_copy(x.at[p], y.at[p], done.at[i, p]) for i, (x, y) in enumerate(pairs)])
        for copy in copies[p]:
            copy.start()
    faces[...] = jnp.zeros(faces.shape, BF)
    raw[...] = jnp.zeros(raw.shape, F32)
    for copy in early:
        copy.wait()
    source = sources(neighbours, columns, rhs)
    for i, start in enumerate((0, size)):
        for j in range(2):
            gathers[i, j] = one_hot(source[j], start, size)
    own_table = [picks(c_target(rows_of(FACE), which), width) for which in (2, 0)]
    first_table = picks(first_target(rows_of(FACE)), width)
    fields = [initial[p].reshape(size, width) for p in range(planes)]
    for j in range(2):
        mine = jnp.concatenate([mt(own_table[j], x).astype(BF) for x in fields], 0)
        mine = mm(mine, gathers[1 - j, j]).astype(BF)
        for p in range(planes):
            own[p, j * FACE : (j + 1) * FACE] = mine[p * FACE : (p + 1) * FACE]
    for p in range(planes):
        own[p, LAST] = mt(first_table, fields[min(p + 1, planes - 1)]).astype(BF)
    lane = lax.broadcasted_iota(jnp.int32, (ROWS, 2 * SLOT), 1)

    for p in range(planes):
        slot = p % 2
        for copy in copies[p]:
            copy.wait()
        faces[slot, :, 256 + SLOT : 256 + SLOT + rhs, :width] = right_in[p]
        for a in range(3):
            rows = [inverse_in[p, v * 27 + a * 9 : v * 27 + a * 9 + 9] for v in range(5)]

            def put(c, value):
                solves[slot, c, a * FACE : (a + 1) * FACE] = (-value).astype(BF)

            turned(jnp.concatenate(rows, 0), raw.at[slot, a], put)
        for f, place in enumerate((256, 4 * FACE, 0, FACE, 2 * FACE, 3 * FACE)):

            def put(c, value):
                faces[slot, c, place : place + FACE] = value.astype(BF)

            turned(couplings_in[p, f], raw.at[slot, 3 + f], put)
        bases, lowers = [], []
        before = None
        for c in range(columns):
            solve = solves[slot, c]
            known[p, c] = mt(solve, faces[slot, c, :256]).astype(BF)
            both = mt(solve, faces[slot, c, 256:])
            move = (c % half * rhs - SLOT) % 128
            bases.append(pltpu.roll(both, move, 1) if move else both)
            if c % 2 == 0:
                before = both
            else:
                lowers.append(jnp.where(lane < SLOT, before, pltpu.roll(both, SLOT, 1)).astype(BF))
        for h in range(2):
            lanes = slice(h * half * rhs, (h + 1) * half * rhs)
            lower[p, h, :ROWS] = jnp.concatenate(lowers[2 * h : 2 * h + 2], 1)
            base[p, :, lanes] = -own_lanes(bases[h * half : (h + 1) * half], rhs)
    chain_products(lower, LAST, range(planes))


def chain_products(matrix, rows, order):
    for h in range(2):
        total = None
        for q in order:
            step = matrix[q, h, rows]
            total = step.astype(F32) if total is None else mm(step, split_lanes(total, SLOT))
            matrix[q, h, PRODUCT] = total.astype(BF)


def gathered(received_up, received_down, own, up_sel, down_sel, gathers):
    planes = received_up.shape[0]
    low = [mm(up_sel[...], received_up[p]).astype(BF) for p in range(planes)]
    high = [mm(down_sel[...], received_down[p]).astype(BF) for p in range(planes)]
    sides = []
    for j, side in enumerate((low, high)):
        picked = mm(jnp.concatenate([x[FACE:] for x in side], 0), gathers[j, j]).astype(BF)
        sides.append([picked[p * FACE : (p + 1) * FACE] + own[p, j * FACE : (j + 1) * FACE] for p in range(planes)])
    return [[low[p][:FACE], high[p][:FACE], sides[0][p], sides[1][p]] for p in range(planes)]


def known_part(known_c, operand, columns, rhs):
    half = columns // 2
    out = []
    for h in range(2):
        side = operand[:, h * half * rhs : (h + 1) * half * rhs]
        out.append(own_lanes([mm(known_c(h * half + c), side) for c in range(half)], rhs))
    return jnp.concatenate(out, 1)


def chain_kernel(known, base, matrix, received, own, gathers, outs, order, rows, rhs, above=None):
    up, down, up_sel, down_sel = received
    part, traces, message = outs
    planes, columns = known.shape[:2]
    size = part.shape[2]
    wholes = gathered(up, down, own, up_sel, down_sel, gathers)
    trace = None
    for p in order:
        if above is None:
            last_face = jnp.zeros((256 - 4 * FACE, size), BF)
        else:
            face = own[p, LAST] if p + 1 < planes else above[...]
            last_face = jnp.concatenate([face, jnp.zeros((256 - 5 * FACE, size), BF)], 0)
        whole = jnp.concatenate(wholes[p] + [last_face], 0)
        value = base[p] + known_part(lambda c: known[p, c], whole, columns, rhs)
        part[p] = value
        value = value[rows]
        trace = value if trace is None else value + chain_step(matrix.at[p], trace, rhs, rows)
        traces[p] = trace
    message[FIRST] = trace.astype(BF)
    if message.shape[0] > FACE:
        for h in range(2):
            message[(1 + h) * FACE : (2 + h) * FACE] = matrix[order[-1], h, PRODUCT]


def forward_chain_kernel(up, down, above, own, gathers, up_sel, down_sel, known, lower, base, *outs, rhs):
    order = range(up.shape[0])
    received = (up, down, up_sel, down_sel)
    chain_kernel(known, base, lower, received, own, gathers, outs, order, LAST, rhs, above)


def backward_chain_kernel(up, down, own, gathers, up_sel, down_sel, known, upper, base, *outs, rhs):
    order = range(up.shape[0] - 1, -1, -1)
    received = (up, down, up_sel, down_sel)
    chain_kernel(known, base, upper, received, own, gathers, outs, order, FIRST, rhs)


def incoming(messages, products, forward, rhs):
    here = lax.axis_index("sweep")
    n = messages.shape[0]
    trace = None
    for i in range(n - 1) if forward else range(n - 1, 0, -1):
        value = messages[i, FIRST].astype(F32)
        if trace is None:
            trace = jnp.zeros_like(value)
        else:
            half = value.shape[1] // 2
            halves = [trace[:, h * half : (h + 1) * half] for h in range(2)]
            value = value + jnp.concatenate([mm(m, split_lanes(t, rhs)) for m, t in zip(products(i), halves)], 1)
        trace = jnp.where(i < here if forward else i > here, value, trace)
    return trace


def forward_finish_kernel(
    messages, part, traces, lower, send, middle, change, up, down, *, rhs
):
    planes = part.shape[0]
    inside = lambda i: [messages[i, (1 + h) * FACE : (2 + h) * FACE] for h in range(2)]
    entry = incoming(messages, inside, True, rhs)
    trace = entry
    for p in range(planes):
        delta = chain_step(lower.at[p], trace, rhs, FULL)
        change[p] = delta
        whole = (part[p] + delta).astype(BF)
        middle[p] = whole
        out = mm(send[...], whole).astype(BF)
        up[p] = out[:SHARED]
        down[p] = out[SHARED:]
        if p + 1 < planes:
            trace = traces[p] + chain_step(lower.at[p], entry, rhs, PRODUCT)


def middle_kernel(middle, change, base, gathers, own_sel, known, own, out, upper):
    planes = middle.shape[0]
    mine = [mm(own_sel[...], middle[p]).astype(BF) for p in range(planes)]
    for j in range(2):
        side = jnp.concatenate([x[j * FACE : (j + 1) * FACE] for x in mine], 0)
        side = mm(side, gathers[1 - j, j]).astype(BF)
        for p in range(planes):
            own[p, j * FACE : (j + 1) * FACE] = side[p * FACE : (p + 1) * FACE]
    for p in range(planes):
        out[p] = base[p] + change[p]
    columns = known.shape[1]
    lane = lax.broadcasted_iota(jnp.int32, (ROWS, 2 * SLOT), 1)
    for p in range(planes):
        pairs = []
        for c in range(0, columns, 2):
            one, two = (known[p, c + i, :, 128:].astype(F32) for i in range(2))
            pairs.append(jnp.where(lane < SLOT, pltpu.roll(one, SLOT, 1), two).astype(BF))
        for h in range(2):
            upper[p, h, :ROWS] = jnp.concatenate(pairs[2 * h : 2 * h + 2], 1)
    chain_products(upper, FIRST, range(planes - 1, -1, -1))


def backward_finish_kernel(
    messages, near, next_near, part, traces, upper, back, result, results, sem, *, rhs
):
    planes = part.shape[0]
    here = lax.axis_index("sweep")
    beside = lambda i: [jnp.where(here + 1 == i, near[h], next_near[h]) for h in range(2)]
    entry = incoming(messages, beside, False, rhs)
    size = entry.shape[1]
    row = lax.broadcasted_iota(jnp.int32, (size, size), 0)
    column = lax.broadcasted_iota(jnp.int32, (size, size), 1)
    unit = jnp.where(row == column, 1.0, 0.0).astype(BF)
    columns, _, width = result.shape[1:]
    copies = []
    trace = entry
    for p in range(planes - 1, -1, -1):
        whole = part[p] + chain_step(upper.at[p], trace, rhs, FULL)
        flat = mm(back[...], whole.astype(BF)).astype(BF)
        results[p] = mt(unit, flat).astype(BF).reshape(columns, rhs, width)
        copies.append(pltpu.make_async_copy(results.at[p], result.at[p], sem.at[p]))
        copies[-1].start()
        if p:
            trace = traces[p] + chain_step(upper.at[p], entry, rhs, PRODUCT)
    for copy in copies:
        copy.wait()


def call(kernel, outs, operands, name, flops=2e8, far=(), scratch=(), out_space=pltpu.VMEM):
    shapes = [jax.ShapeDtypeStruct(s, d) for s, d in outs]
    nbytes = sum(x.size * x.dtype.itemsize for x in list(operands) + shapes)
    spaces = [pltpu.SMEM if x.dtype == jnp.int32 else pltpu.VMEM for x in operands]
    spaces = [pltpu.HBM if i in far else space for i, space in enumerate(spaces)]
    operands = [
        pltpu.with_memory_space_constraint(x, pltpu.HBM) if i in far else x for i, x in enumerate(operands)
    ]
    return pl.pallas_call(
        kernel,
        out_shape=shapes,
        in_specs=[pl.BlockSpec(memory_space=space) for space in spaces],
        out_specs=[pl.BlockSpec(memory_space=out_space)] * len(shapes),
        scratch_shapes=list(scratch),
        compiler_params=pltpu.CompilerParams(vmem_limit_bytes=24 * MIB),
        cost_estimate=pl.CostEstimate(flops=int(flops), bytes_accessed=int(nbytes), transcendentals=0),
        name=name,
    )(*operands)


def products(x, by):
    n = lax.axis_size("sweep")
    inner = range(1, n - 1)
    return [
        lax.ppermute(x, "sweep", [(i, i + step) for i in inner if 0 <= i + step < n]) for step in (by, 2 * by)
    ]


def weights(inverse, couplings, right, initial, neighbours):
    planes, columns, rhs, width = initial.shape
    size = columns * rhs
    pack = (planes, 2, ROWS + FACE, 256)
    field = (planes, ROWS, size)
    outs = [((planes, columns, ROWS, 256), BF), (pack, BF), (field, F32), (field, BF), ((2, 2, size, size), BF)]
    operands = (inverse, couplings, right, initial, neighbours)
    scratch = [pltpu.VMEM(x.shape, BF) for x in operands[:4]] + [
        pltpu.SMEM(neighbours.shape, jnp.int32),
        pltpu.VMEM((2, columns, ROWS, 256), BF),
        pltpu.VMEM((2, columns, 256 + 2 * SLOT, 256), BF),
        pltpu.VMEM((2, 9, 2, FACE * columns, 128), F32),
        pltpu.SemaphoreType.DMA((4, planes)),
    ]
    return call(weight_kernel, outs, operands, "weights", 1e10, (0, 1, 2, 3, 4), scratch)


def ring(x, axis, by):
    n = lax.axis_size(axis)
    return lax.ppermute(x, axis, [(i, (i + by) % n) for i in range(n)])


def shift(x, axis, by):
    n = lax.axis_size(axis)
    return lax.ppermute(x, axis, [(i, i + by) for i in range(n) if 0 <= i + by < n])


def local(right_sides, initial, inverse_blocks, couplings, neighbours):
    planes, columns, rhs, width = initial.shape
    size = columns * rhs
    const = lambda x: jnp.asarray(x, BF)
    send_in = const(send_table(ROWS, inner))
    own_in = const(own_table(ROWS, inner))
    back = const(table(width, ROWS, [(natural(*n), n) for n in NODES], inner))
    up_sel = const(receive_table(2))
    down_sel = const(receive_table(0))
    beside = neighbours.T

    share = (planes, SHARED, size)
    up, down, above = call(
        first_kernel,
        [(share, BF), (share, BF), ((FACE, size), BF)],
        (initial,),
        "initial_traces",
        far=(0,),
        scratch=[pltpu.VMEM(initial.shape, BF), pltpu.SemaphoreType.DMA((planes,))],
    )
    up, down, above, initial = lax.optimization_barrier((up, down, above, initial))
    from_low = ring(up, "cross", 1)
    from_high = ring(down, "cross", -1)
    from_above = shift(above, "sweep", -1)
    known, lower, base, own, gathers = weights(
        inverse_blocks.transpose(0, 2, 1, 3), couplings.transpose(0, 2, 3, 1, 4), right_sides, initial, beside
    )

    field = (planes, ROWS, size)
    trace = (planes, FACE, size)
    chain_outs = [(field, F32), (trace, F32)]
    part, traces, message = call(
        functools.partial(forward_chain_kernel, rhs=rhs),
        chain_outs + [((3 * FACE, size), BF)],
        (from_low, from_high, from_above, own, gathers, up_sel, down_sel, known, lower, base),
        "forward_chain",
    )
    messages = lax.all_gather(message, "sweep")
    middle, change, up, down = call(
        functools.partial(forward_finish_kernel, rhs=rhs),
        [(field, BF), (field, F32), (share, BF), (share, BF)],
        (messages, part, traces, lower, send_in),
        "forward_finish",
    )
    from_low = ring(up, "cross", 1)
    from_high = ring(down, "cross", -1)
    own, base, upper = call(
        middle_kernel,
        [((planes, 2 * FACE, size), BF), (field, F32), (lower.shape, BF)],
        (middle, change, base, gathers, own_in, known),
        "middle",
        2e9,
    )
    own, pass_b = lax.optimization_barrier((own, upper[0, :, PRODUCT]))
    passes = products(pass_b, -1)
    part, traces, message = call(
        functools.partial(backward_chain_kernel, rhs=rhs),
        chain_outs + [((FACE, size), BF)],
        (from_low, from_high, own, gathers, up_sel, down_sel, known, upper, base),
        "backward_chain",
    )
    messages = lax.all_gather(message, "sweep")
    (result,) = call(
        functools.partial(backward_finish_kernel, rhs=rhs),
        [(right_sides.shape, BF)],
        (messages, *passes, part, traces, upper, back),
        "backward_finish",
        scratch=[pltpu.VMEM(right_sides.shape, BF), pltpu.SemaphoreType.DMA((planes,))],
        out_space=pltpu.HBM,
    )
    return result


def solution(mesh):
    return jax.shard_map(
        local,
        mesh=mesh,
        in_specs=(
            P("sweep", "cross", None, None),
            P("sweep", "cross", None, None),
            P("sweep", "cross", None, None),
            P("sweep", "cross", None, None, None),
            P("cross", None),
        ),
        out_specs=P("sweep", "cross", None, None),
        check_vma=False,
    )
```

```python
import functools

import jax
import jax.numpy as jnp
import numpy as np
from jax import lax
from jax.experimental import pallas as pl
from jax.experimental.pallas import tpu as pltpu
from jax.sharding import PartitionSpec as P

BF = jnp.bfloat16
F32 = jnp.float32
NT = 45
FACE = 48
SLOT = 64
ROWS = 3 * FACE
SHARED = 75
MAIN = 64
MIB = 1 << 20
FIRST = slice(0, FACE)
LAST = slice(2 * FACE, ROWS)
FULL = slice(0, ROWS)
PRODUCT = slice(ROWS, ROWS + FACE)


def natural(v, a, b, c):
    return v * 27 + a * 9 + b * 3 + c


def inner(v, a, b, c):
    return a * FACE + v * 9 + b * 3 + c


NODES = [(v, a, b, c) for v in range(5) for a in range(3) for b in range(3) for c in range(3)]


def face_nodes(place, which):
    return [n for n in NODES if n[1 + place] == which]


def table(height, width, rows, column_of):
    out = np.zeros((height, width), np.float32)
    for row, node in rows:
        out[row, column_of(*node)] = 1
    return out


def block(nodes, start=0):
    return [(start + i, n) for i, n in enumerate(nodes)]


def tail_rows(planes):
    return -(-planes * (SHARED - MAIN) // 16) * 16


def union_nodes(which):
    others = [b for b in range(3) if b != which]
    spots = [(which, c) for c in range(3)] + [(b, which) for b in others]
    return [(v, a, b, c) for v in range(5) for a in range(3) for b, c in spots]


def place_of(i, plane):
    return i if i < MAIN else i + plane * (SHARED - MAIN)


def send_table(width, column_of, planes):
    height = MAIN + tail_rows(planes)
    out = []
    for p in range(planes):
        rows = [(place_of(i, p), n) for i, n in enumerate(union_nodes(2))]
        rows += [(height + place_of(i, p), n) for i, n in enumerate(union_nodes(0))]
        out.append(table(2 * height, width, rows, column_of))
    return np.stack(out)


def own_table(width, column_of):
    rows = block(face_nodes(2, 2)) + block(face_nodes(2, 0), FACE)
    return table(2 * FACE, width, rows, column_of)


def receive_table(which, planes):
    rows = block(face_nodes(1, which)) + block(face_nodes(2, which), FACE)
    out = []
    for p in range(planes):
        place = {n: place_of(i, p) for i, n in enumerate(union_nodes(which))}
        out.append(table(2 * FACE, MAIN + tail_rows(planes), rows, lambda *n: place[n]))
    return np.stack(out)


def mm(a, b):
    return lax.dot_general(a, b, (((1,), (0,)), ((), ())), preferred_element_type=F32)


def mt(a, b):
    return lax.dot_general(a, b, (((1,), (1,)), ((), ())), preferred_element_type=F32)


def group(shape, width, at):
    lane = lax.broadcasted_iota(jnp.int32, shape, 1)
    return (lane >= at * width) & (lane < (at + 1) * width)


def split_lanes(value, width):
    lanes = value.shape[1]
    value = value.astype(F32)
    pad = jnp.zeros((SLOT - FACE, lanes), BF)
    parts = []
    for c in range(lanes // width):
        parts += [jnp.where(group(value.shape, width, c), value, 0.0).astype(BF), pad]
    return jnp.concatenate(parts, 0)


def own_lanes(values, width):
    out = values[0]
    for c in range(1, len(values)):
        out = jnp.where(group(out.shape, width, c), values[c], out)
    return out


def one_hot(source, start, height):
    row = lax.broadcasted_iota(jnp.int32, (height, source.shape[1]), 0) + start
    return jnp.where(row == source, 1.0, 0.0).astype(BF)


def chain_step(matrix, trace, rhs, rows=slice(None)):
    half = trace.shape[1] // 2
    return jnp.concatenate(
        [mm(matrix[h, rows], split_lanes(trace[:, h * half : (h + 1) * half], rhs)) for h in range(2)], 1
    )


def shared_target(row, which, plane, planes):
    rest = SHARED - MAIN
    i = jnp.where(row < MAIN, row, row - plane * rest)
    k = i % 15
    a = k // 5
    j = k % 5
    b = jnp.where(j < 3, which, j - 3 if which == 2 else j - 2)
    c = jnp.where(j < 3, j, which)
    inside = (row < MAIN) | ((i >= MAIN) & (i < SHARED))
    return jnp.where(inside, i // 15 * 27 + a * 9 + b * 3 + c, -1)


def picks(target, width):
    lane = lax.broadcasted_iota(jnp.int32, (target.shape[0], width), 1)
    return jnp.where(lane == target, 1.0, 0.0).astype(BF)


def rows_of(height):
    return lax.broadcasted_iota(jnp.int32, (height, 1), 0)


def first_target(row):
    return jnp.where(row < NT, row // 9 * 27 + row % 9, -1)


def c_target(row, which):
    return jnp.where(row < NT, row * 3 + which, -1)


def sources(neighbours, columns, rhs):
    place = lax.axis_index("cross")
    total = columns * lax.axis_size("cross")
    lane = lax.broadcasted_iota(jnp.int32, (1, columns * rhs), 1)
    out = []
    for face, first in ((2, place - 1), (3, place)):
        source = lane
        for c in range(columns):
            at = neighbours[face, c] - first * columns
            at = jnp.where(at < 0, at + total, at)
            at = jnp.where(at >= total, at - total, at)
            source = jnp.where(lane >= c * rhs, lane + (at - c) * rhs, source)
        out.append(source)
    return out


def put_shared(out, ups, downs):
    planes = len(out)
    height = out[0].shape[0] // 2
    for target, start in ((ups, 0), (downs, height)):
        for p in range(planes):
            target[p * MAIN : (p + 1) * MAIN] = out[p][start : start + MAIN].astype(BF)
        tails = [x[start + MAIN : start + height] for x in out]
        target[planes * MAIN :] = sum(tails[1:], tails[0]).astype(BF)


def first_kernel(initial, up, down, above):
    planes, columns, rhs, width = initial.shape
    row = rows_of(MAIN + tail_rows(planes))
    out = []
    for p in range(planes):
        x = initial[p].reshape(columns * rhs, width)
        tables = [picks(shared_target(row, which, p, planes), width) for which in (2, 0)]
        out.append(mt(jnp.concatenate(tables, 0), x))
        if p == 0:
            above[...] = mt(picks(first_target(rows_of(FACE)), width), x).astype(BF)
    put_shared(out, up, down)


def turned(rows, raw, put):
    count, columns, width = rows.shape
    raw[0, : count * columns] = rows[:, :, :128].astype(F32).reshape(count * columns, 128)
    raw[1, : count * columns, : width - 128] = rows[:, :, 128:].astype(F32).reshape(count * columns, width - 128)
    for c in range(columns):
        put(c, jnp.concatenate([raw[i, pl.ds(c, FACE, stride=columns), :] for i in range(2)], 1))


def weight_kernel(
    inverse, couplings, right, initial_there, neighbours_there,
    known, lower, base, own, gathers,
    inverse_in, couplings_in, right_in, initial, neighbours, solves, faces, raw, done,
):
    planes, columns, rhs, width = initial.shape
    size = columns * rhs
    half = columns // 2
    early = [
        pltpu.make_async_copy(neighbours_there, neighbours, done.at[3, 0]),
        pltpu.make_async_copy(initial_there, initial, done.at[3, 1]),
    ]
    for copy in early:
        copy.start()
    copies = []
    for p in range(planes):
        pairs = ((inverse, inverse_in), (couplings, couplings_in), (right, right_in))
        copies.append([pltpu.make_async_copy(x.at[p], y.at[p], done.at[i, p]) for i, (x, y) in enumerate(pairs)])
        for copy in copies[p]:
            copy.start()
    faces[...] = jnp.zeros(faces.shape, BF)
    raw[...] = jnp.zeros(raw.shape, F32)
    for copy in early:
        copy.wait()
    source = sources(neighbours, columns, rhs)
    for i, start in enumerate((0, size)):
        for j in range(2):
            gathers[i, j] = one_hot(source[j], start, size)
    own_table = [picks(c_target(rows_of(FACE), which), width) for which in (2, 0)]
    first_table = picks(first_target(rows_of(FACE)), width)
    fields = [initial[p].reshape(size, width) for p in range(planes)]
    for j in range(2):
        mine = jnp.concatenate([mt(own_table[j], x).astype(BF) for x in fields], 0)
        mine = mm(mine, gathers[1 - j, j]).astype(BF)
        for p in range(planes):
            own[p, j * FACE : (j + 1) * FACE] = mine[p * FACE : (p + 1) * FACE]
    for p in range(planes):
        own[p, LAST] = mt(first_table, fields[min(p + 1, planes - 1)]).astype(BF)
    lane = lax.broadcasted_iota(jnp.int32, (ROWS, 2 * SLOT), 1)

    for p in range(planes):
        slot = p % 2
        for copy in copies[p]:
            copy.wait()
        faces[slot, :, 256 + SLOT : 256 + SLOT + rhs, :width] = right_in[p]
        for a in range(3):
            rows = [inverse_in[p, v * 27 + a * 9 : v * 27 + a * 9 + 9] for v in range(5)]

            def put(c, value):
                solves[slot, c, a * FACE : (a + 1) * FACE] = (-value).astype(BF)

            turned(jnp.concatenate(rows, 0), raw.at[slot, a], put)
        for f, place in enumerate((256, 4 * FACE, 0, FACE, 2 * FACE, 3 * FACE)):

            def put(c, value):
                faces[slot, c, place : place + FACE] = value.astype(BF)

            turned(couplings_in[p, f], raw.at[slot, 3 + f], put)
        bases, lowers = [], []
        before = None
        for c in range(columns):
            solve = solves[slot, c]
            known[p, c] = mt(solve, faces[slot, c, :256]).astype(BF)
            both = mt(solve, faces[slot, c, 256:])
            move = (c % half * rhs - SLOT) % 128
            bases.append(pltpu.roll(both, move, 1) if move else both)
            if c % 2 == 0:
                before = both
            else:
                lowers.append(jnp.where(lane < SLOT, before, pltpu.roll(both, SLOT, 1)).astype(BF))
        for h in range(2):
            lanes = slice(h * half * rhs, (h + 1) * half * rhs)
            lower[p, h, :ROWS] = jnp.concatenate(lowers[2 * h : 2 * h + 2], 1)
            base[p, :, lanes] = -own_lanes(bases[h * half : (h + 1) * half], rhs)
    chain_products(lower, LAST, range(planes))


def chain_products(matrix, rows, order):
    for h in range(2):
        total = None
        for q in order:
            step = matrix[q, h, rows]
            total = step.astype(F32) if total is None else mm(step, split_lanes(total, SLOT))
            matrix[q, h, PRODUCT] = total.astype(BF)


def gathered(received_up, received_down, own, up_sel, down_sel, gathers):
    planes = up_sel.shape[0]

    def faces(received, select):
        tail = received[planes * MAIN :]
        wholes = [jnp.concatenate([received[p * MAIN : (p + 1) * MAIN], tail], 0) for p in range(planes)]
        return [mm(select[p], wholes[p]).astype(BF) for p in range(planes)]

    low, high = faces(received_up, up_sel), faces(received_down, down_sel)
    sides = []
    for j, side in enumerate((low, high)):
        picked = mm(jnp.concatenate([x[FACE:] for x in side], 0), gathers[j, j]).astype(BF)
        sides.append([picked[p * FACE : (p + 1) * FACE] + own[p, j * FACE : (j + 1) * FACE] for p in range(planes)])
    return [jnp.concatenate([low[p][:FACE], high[p][:FACE], sides[0][p], sides[1][p]], 0) for p in range(planes)]


def gather_kernel(up, down, own, gathers, up_sel, down_sel, operand):
    for p, whole in enumerate(gathered(up, down, own, up_sel, down_sel, gathers)):
        operand[p] = whole


def known_part(known_c, operand, columns, rhs):
    half = columns // 2
    out = []
    for h in range(2):
        side = operand[:, h * half * rhs : (h + 1) * half * rhs]
        out.append(own_lanes([mm(known_c(h * half + c), side) for c in range(half)], rhs))
    return jnp.concatenate(out, 1)


def chain_kernel(known, base, matrix, wholes, outs, order, rows, rhs, last_face):
    part, traces, message = outs
    planes, columns = known.shape[:2]
    trace = None
    for p in order:
        whole = jnp.concatenate([wholes[p], last_face(p)], 0)
        value = base[p] + known_part(lambda c: known[p, c], whole, columns, rhs)
        part[p] = value
        value = value[rows]
        trace = value if trace is None else value + chain_step(matrix.at[p], trace, rhs, rows)
        traces[p] = trace
    message[FIRST] = trace.astype(BF)
    if message.shape[0] > FACE:
        for h in range(2):
            message[(1 + h) * FACE : (2 + h) * FACE] = matrix[order[-1], h, PRODUCT]


def forward_chain_kernel(operand, above, own, known, lower, base, *outs, rhs):
    planes, _, size = operand.shape
    pad = jnp.zeros((256 - 5 * FACE, size), BF)
    last_face = lambda p: jnp.concatenate([own[p, LAST] if p + 1 < planes else above[...], pad], 0)
    chain_kernel(known, base, lower, operand, outs, range(planes), LAST, rhs, last_face)


def backward_chain_kernel(up, down, own, gathers, up_sel, down_sel, known, upper, base, *outs, rhs):
    wholes = gathered(up, down, own, up_sel, down_sel, gathers)
    last_face = lambda p: jnp.zeros((256 - 4 * FACE, up.shape[1]), BF)
    chain_kernel(known, base, upper, wholes, outs, range(len(wholes) - 1, -1, -1), FIRST, rhs, last_face)


def incoming(messages, products, forward, rhs):
    here = lax.axis_index("sweep")
    n = messages.shape[0]
    trace = None
    for i in range(n - 1) if forward else range(n - 1, 0, -1):
        value = messages[i, FIRST].astype(F32)
        if trace is None:
            trace = jnp.zeros_like(value)
        else:
            half = value.shape[1] // 2
            halves = [trace[:, h * half : (h + 1) * half] for h in range(2)]
            value = value + jnp.concatenate([mm(m, split_lanes(t, rhs)) for m, t in zip(products(i), halves)], 1)
        trace = jnp.where(i < here if forward else i > here, value, trace)
    return trace


def forward_finish_kernel(
    messages, part, traces, lower, send, middle, change, up, down, *, rhs
):
    planes = part.shape[0]
    inside = lambda i: [messages[i, (1 + h) * FACE : (2 + h) * FACE] for h in range(2)]
    entry = incoming(messages, inside, True, rhs)
    out = []
    trace = entry
    for p in range(planes):
        delta = chain_step(lower.at[p], trace, rhs, FULL)
        change[p] = delta
        whole = (part[p] + delta).astype(BF)
        middle[p] = whole
        out.append(mm(send[p], whole))
        if p + 1 < planes:
            trace = traces[p] + chain_step(lower.at[p], entry, rhs, PRODUCT)
    put_shared(out, up, down)


def middle_kernel(middle, change, base, gathers, own_sel, known, own, out, upper):
    planes = middle.shape[0]
    mine = [mm(own_sel[...], middle[p]).astype(BF) for p in range(planes)]
    for j in range(2):
        side = jnp.concatenate([x[j * FACE : (j + 1) * FACE] for x in mine], 0)
        side = mm(side, gathers[1 - j, j]).astype(BF)
        for p in range(planes):
            own[p, j * FACE : (j + 1) * FACE] = side[p * FACE : (p + 1) * FACE]
    for p in range(planes):
        out[p] = base[p] + change[p]
    columns = known.shape[1]
    lane = lax.broadcasted_iota(jnp.int32, (ROWS, 2 * SLOT), 1)
    for p in range(planes):
        pairs = []
        for c in range(0, columns, 2):
            one, two = (known[p, c + i, :, 128:].astype(F32) for i in range(2))
            pairs.append(jnp.where(lane < SLOT, pltpu.roll(one, SLOT, 1), two).astype(BF))
        for h in range(2):
            upper[p, h, :ROWS] = jnp.concatenate(pairs[2 * h : 2 * h + 2], 1)
    chain_products(upper, FIRST, range(planes - 1, -1, -1))


def backward_finish_kernel(
    messages, near, next_near, part, traces, upper, back, result, results, sem, *, rhs
):
    planes = part.shape[0]
    here = lax.axis_index("sweep")
    beside = lambda i: [jnp.where(here + 1 == i, near[h], next_near[h]) for h in range(2)]
    entry = incoming(messages, beside, False, rhs)
    size = entry.shape[1]
    row = lax.broadcasted_iota(jnp.int32, (size, size), 0)
    column = lax.broadcasted_iota(jnp.int32, (size, size), 1)
    unit = jnp.where(row == column, 1.0, 0.0).astype(BF)
    columns, _, width = result.shape[1:]
    copies = []
    trace = entry
    for p in range(planes - 1, -1, -1):
        whole = part[p] + chain_step(upper.at[p], trace, rhs, FULL)
        flat = mm(back[...], whole.astype(BF)).astype(BF)
        results[p] = mt(unit, flat).astype(BF).reshape(columns, rhs, width)
        copies.append(pltpu.make_async_copy(results.at[p], result.at[p], sem.at[p]))
        copies[-1].start()
        if p:
            trace = traces[p] + chain_step(upper.at[p], entry, rhs, PRODUCT)
    for copy in copies:
        copy.wait()


def call(kernel, outs, operands, name, flops=2e8, far=(), scratch=(), out_space=pltpu.VMEM):
    shapes = [jax.ShapeDtypeStruct(s, d) for s, d in outs]
    nbytes = sum(x.size * x.dtype.itemsize for x in list(operands) + shapes)
    spaces = [pltpu.SMEM if x.dtype == jnp.int32 else pltpu.VMEM for x in operands]
    spaces = [pltpu.HBM if i in far else space for i, space in enumerate(spaces)]
    operands = [
        pltpu.with_memory_space_constraint(x, pltpu.HBM) if i in far else x for i, x in enumerate(operands)
    ]
    return pl.pallas_call(
        kernel,
        out_shape=shapes,
        in_specs=[pl.BlockSpec(memory_space=space) for space in spaces],
        out_specs=[pl.BlockSpec(memory_space=out_space)] * len(shapes),
        scratch_shapes=list(scratch),
        compiler_params=pltpu.CompilerParams(vmem_limit_bytes=24 * MIB),
        cost_estimate=pl.CostEstimate(flops=int(flops), bytes_accessed=int(nbytes), transcendentals=0),
        name=name,
    )(*operands)


def products(x, by):
    n = lax.axis_size("sweep")
    inner = range(1, n - 1)
    return [
        lax.ppermute(x, "sweep", [(i, i + step) for i in inner if 0 <= i + step < n]) for step in (by, 2 * by)
    ]


def weights(inverse, couplings, right, initial, neighbours):
    planes, columns, rhs, width = initial.shape
    size = columns * rhs
    pack = (planes, 2, ROWS + FACE, 256)
    field = (planes, ROWS, size)
    outs = [((planes, columns, ROWS, 256), BF), (pack, BF), (field, F32), (field, BF), ((2, 2, size, size), BF)]
    operands = (inverse, couplings, right, initial, neighbours)
    scratch = [pltpu.VMEM(x.shape, BF) for x in operands[:4]] + [
        pltpu.SMEM(neighbours.shape, jnp.int32),
        pltpu.VMEM((2, columns, ROWS, 256), BF),
        pltpu.VMEM((2, columns, 256 + 2 * SLOT, 256), BF),
        pltpu.VMEM((2, 9, 2, FACE * columns, 128), F32),
        pltpu.SemaphoreType.DMA((4, planes)),
    ]
    return call(weight_kernel, outs, operands, "weights", 1e10, (0, 1, 2, 3, 4), scratch)


def ring(x, axis, by):
    n = lax.axis_size(axis)
    return lax.ppermute(x, axis, [(i, (i + by) % n) for i in range(n)])


def shift(x, axis, by):
    n = lax.axis_size(axis)
    return lax.ppermute(x, axis, [(i, i + by) for i in range(n) if 0 <= i + by < n])


def local(right_sides, initial, inverse_blocks, couplings, neighbours):
    planes, columns, rhs, width = initial.shape
    size = columns * rhs
    const = lambda x: jnp.asarray(x, BF)
    send_in = const(send_table(ROWS, inner, planes))
    own_in = const(own_table(ROWS, inner))
    back = const(table(width, ROWS, [(natural(*n), n) for n in NODES], inner))
    up_sel = const(receive_table(2, planes))
    down_sel = const(receive_table(0, planes))
    beside = neighbours.T

    share = (planes * MAIN + tail_rows(planes), size)
    up, down, above = call(
        first_kernel,
        [(share, BF), (share, BF), ((FACE, size), BF)],
        (initial,),
        "initial_traces",
    )
    up, down, above, initial = lax.optimization_barrier((up, down, above, initial))
    from_low = ring(up, "cross", 1)
    from_high = ring(down, "cross", -1)
    from_above = shift(above, "sweep", -1)
    known, lower, base, own, gathers = weights(
        inverse_blocks.transpose(0, 2, 1, 3), couplings.transpose(0, 2, 3, 1, 4), right_sides, initial, beside
    )

    field = (planes, ROWS, size)
    trace = (planes, FACE, size)
    chain_outs = [(field, F32), (trace, F32)]
    (operand,) = call(
        gather_kernel,
        [((planes, 4 * FACE, size), BF)],
        (from_low, from_high, own, gathers, up_sel, down_sel),
        "forward_gather",
    )
    part, traces, message = call(
        functools.partial(forward_chain_kernel, rhs=rhs),
        chain_outs + [((3 * FACE, size), BF)],
        (operand, from_above, own, known, lower, base),
        "forward_chain",
    )
    messages = lax.all_gather(message, "sweep")
    middle, change, up, down = call(
        functools.partial(forward_finish_kernel, rhs=rhs),
        [(field, BF), (field, F32), (share, BF), (share, BF)],
        (messages, part, traces, lower, send_in),
        "forward_finish",
    )
    from_low = ring(up, "cross", 1)
    from_high = ring(down, "cross", -1)
    own, base, upper = call(
        middle_kernel,
        [((planes, 2 * FACE, size), BF), (field, F32), (lower.shape, BF)],
        (middle, change, base, gathers, own_in, known),
        "middle",
        2e9,
    )
    own, pass_b = lax.optimization_barrier((own, upper[0, :, PRODUCT]))
    passes = products(pass_b, -1)
    part, traces, message = call(
        functools.partial(backward_chain_kernel, rhs=rhs),
        chain_outs + [((FACE, size), BF)],
        (from_low, from_high, own, gathers, up_sel, down_sel, known, upper, base),
        "backward_chain",
    )
    messages = lax.all_gather(message, "sweep")
    (result,) = call(
        functools.partial(backward_finish_kernel, rhs=rhs),
        [(right_sides.shape, BF)],
        (messages, *passes, part, traces, upper, back),
        "backward_finish",
        scratch=[pltpu.VMEM(right_sides.shape, BF), pltpu.SemaphoreType.DMA((planes,))],
        out_space=pltpu.HBM,
    )
    return result


def solution(mesh):
    return jax.shard_map(
        local,
        mesh=mesh,
        in_specs=(
            P("sweep", "cross", None, None),
            P("sweep", "cross", None, None),
            P("sweep", "cross", None, None),
            P("sweep", "cross", None, None, None),
            P("cross", None),
        ),
        out_specs=P("sweep", "cross", None, None),
        check_vma=False,
    )
```

```python
import functools

import jax
import jax.numpy as jnp
import numpy as np
from jax import lax
from jax.experimental import pallas as pl
from jax.experimental.pallas import tpu as pltpu
from jax.sharding import PartitionSpec as P

BF = jnp.bfloat16
F32 = jnp.float32
NT = 45
FACE = 48
SLOT = 64
ROWS = 3 * FACE
SHARED = 75
MAIN = 64
MIB = 1 << 20
FIRST = slice(0, FACE)
LAST = slice(2 * FACE, ROWS)
FULL = slice(0, ROWS)
PRODUCT = slice(ROWS, ROWS + FACE)


def natural(v, a, b, c):
    return v * 27 + a * 9 + b * 3 + c


def inner(v, a, b, c):
    return a * FACE + v * 9 + b * 3 + c


NODES = [(v, a, b, c) for v in range(5) for a in range(3) for b in range(3) for c in range(3)]


def face_nodes(place, which):
    return [n for n in NODES if n[1 + place] == which]


def table(height, width, rows, column_of):
    out = np.zeros((height, width), np.float32)
    for row, node in rows:
        out[row, column_of(*node)] = 1
    return out


def block(nodes, start=0):
    return [(start + i, n) for i, n in enumerate(nodes)]


def tail_rows(planes):
    return -(-planes * (SHARED - MAIN) // 16) * 16


def union_nodes(which):
    others = [b for b in range(3) if b != which]
    spots = [(which, c) for c in range(3)] + [(b, which) for b in others]
    return [(v, a, b, c) for v in range(5) for a in range(3) for b, c in spots]


def place_of(i, plane):
    return i if i < MAIN else i + plane * (SHARED - MAIN)


def send_table(width, column_of, planes):
    height = MAIN + tail_rows(planes)
    out = []
    for p in range(planes):
        rows = [(place_of(i, p), n) for i, n in enumerate(union_nodes(2))]
        rows += [(height + place_of(i, p), n) for i, n in enumerate(union_nodes(0))]
        out.append(table(2 * height, width, rows, column_of))
    return np.stack(out)


def own_table(width, column_of):
    rows = block(face_nodes(2, 2)) + block(face_nodes(2, 0), FACE)
    return table(2 * FACE, width, rows, column_of)


def receive_table(which, planes):
    rows = block(face_nodes(1, which)) + block(face_nodes(2, which), FACE)
    out = []
    for p in range(planes):
        place = {n: place_of(i, p) for i, n in enumerate(union_nodes(which))}
        out.append(table(2 * FACE, MAIN + tail_rows(planes), rows, lambda *n: place[n]))
    return np.stack(out)


def mm(a, b):
    return lax.dot_general(a, b, (((1,), (0,)), ((), ())), preferred_element_type=F32)


def mt(a, b):
    return lax.dot_general(a, b, (((1,), (1,)), ((), ())), preferred_element_type=F32)


def group(shape, width, at):
    lane = lax.broadcasted_iota(jnp.int32, shape, 1)
    return (lane >= at * width) & (lane < (at + 1) * width)


def split_lanes(value, width):
    lanes = value.shape[1]
    value = value.astype(F32)
    pad = jnp.zeros((SLOT - FACE, lanes), BF)
    parts = []
    for c in range(lanes // width):
        parts += [jnp.where(group(value.shape, width, c), value, 0.0).astype(BF), pad]
    return jnp.concatenate(parts, 0)


def own_lanes(values, width):
    out = values[0]
    for c in range(1, len(values)):
        out = jnp.where(group(out.shape, width, c), values[c], out)
    return out


def one_hot(source, start, height):
    row = lax.broadcasted_iota(jnp.int32, (height, source.shape[1]), 0) + start
    return jnp.where(row == source, 1.0, 0.0).astype(BF)


def chain_step(matrix, trace, rhs, rows=slice(None)):
    half = trace.shape[1] // 2
    return jnp.concatenate(
        [mm(matrix[h, rows], split_lanes(trace[:, h * half : (h + 1) * half], rhs)) for h in range(2)], 1
    )


def shared_target(row, which, plane, planes):
    rest = SHARED - MAIN
    i = jnp.where(row < MAIN, row, row - plane * rest)
    k = i % 15
    a = k // 5
    j = k % 5
    b = jnp.where(j < 3, which, j - 3 if which == 2 else j - 2)
    c = jnp.where(j < 3, j, which)
    inside = (row < MAIN) | ((i >= MAIN) & (i < SHARED))
    return jnp.where(inside, i // 15 * 27 + a * 9 + b * 3 + c, -1)


def picks(target, width):
    lane = lax.broadcasted_iota(jnp.int32, (target.shape[0], width), 1)
    return jnp.where(lane == target, 1.0, 0.0).astype(BF)


def rows_of(height):
    return lax.broadcasted_iota(jnp.int32, (height, 1), 0)


def first_target(row):
    return jnp.where(row < NT, row // 9 * 27 + row % 9, -1)


def c_target(row, which):
    return jnp.where(row < NT, row * 3 + which, -1)


def sources(neighbours, columns, rhs):
    place = lax.axis_index("cross")
    total = columns * lax.axis_size("cross")
    lane = lax.broadcasted_iota(jnp.int32, (1, columns * rhs), 1)
    out = []
    for face, first in ((2, place - 1), (3, place)):
        source = lane
        for c in range(columns):
            at = neighbours[face, c] - first * columns
            at = jnp.where(at < 0, at + total, at)
            at = jnp.where(at >= total, at - total, at)
            source = jnp.where(lane >= c * rhs, lane + (at - c) * rhs, source)
        out.append(source)
    return out


def put_shared(out, ups, downs):
    height = out[0].shape[0] // 2
    for pieces, start in ((ups, 0), (downs, height)):
        tails = [x[start + MAIN : start + height] for x in out]
        parts = [x[start : start + MAIN] for x in out] + [sum(tails[1:], tails[0])]
        whole = jnp.concatenate(parts, 0).astype(BF)
        first = 0
        for piece in pieces:
            piece[...] = whole[first : first + piece.shape[0]]
            first += piece.shape[0]


def first_kernel(initial, up, down, above):
    planes, columns, rhs, width = initial.shape
    row = rows_of(MAIN + tail_rows(planes))
    out = []
    for p in range(planes):
        x = initial[p].reshape(columns * rhs, width)
        tables = [picks(shared_target(row, which, p, planes), width) for which in (2, 0)]
        out.append(mt(jnp.concatenate(tables, 0), x))
        if p == 0:
            above[...] = mt(picks(first_target(rows_of(FACE)), width), x).astype(BF)
    put_shared(out, [up], [down])


def turned(rows, raw, put):
    count, columns, width = rows.shape
    raw[0, : count * columns] = rows[:, :, :128].astype(F32).reshape(count * columns, 128)
    raw[1, : count * columns, : width - 128] = rows[:, :, 128:].astype(F32).reshape(count * columns, width - 128)
    for c in range(columns):
        put(c, jnp.concatenate([raw[i, pl.ds(c, FACE, stride=columns), :] for i in range(2)], 1))


def weight_kernel(
    inverse, couplings, right, initial_there, neighbours_there,
    known, lower, base, own, gathers,
    inverse_in, couplings_in, right_in, initial, neighbours, solves, faces, raw, done,
):
    planes, columns, rhs, width = initial.shape
    size = columns * rhs
    half = columns // 2
    early = [
        pltpu.make_async_copy(neighbours_there, neighbours, done.at[3, 0]),
        pltpu.make_async_copy(initial_there, initial, done.at[3, 1]),
    ]
    for copy in early:
        copy.start()
    copies = []
    for p in range(planes):
        pairs = ((inverse, inverse_in), (couplings, couplings_in), (right, right_in))
        copies.append([pltpu.make_async_copy(x.at[p], y.at[p], done.at[i, p]) for i, (x, y) in enumerate(pairs)])
        for copy in copies[p]:
            copy.start()
    faces[...] = jnp.zeros(faces.shape, BF)
    raw[...] = jnp.zeros(raw.shape, F32)
    for copy in early:
        copy.wait()
    source = sources(neighbours, columns, rhs)
    for i, start in enumerate((0, size)):
        for j in range(2):
            gathers[i, j] = one_hot(source[j], start, size)
    own_table = [picks(c_target(rows_of(FACE), which), width) for which in (2, 0)]
    first_table = picks(first_target(rows_of(FACE)), width)
    fields = [initial[p].reshape(size, width) for p in range(planes)]
    for j in range(2):
        mine = jnp.concatenate([mt(own_table[j], x).astype(BF) for x in fields], 0)
        mine = mm(mine, gathers[1 - j, j]).astype(BF)
        for p in range(planes):
            own[p, j * FACE : (j + 1) * FACE] = mine[p * FACE : (p + 1) * FACE]
    for p in range(planes):
        own[p, LAST] = mt(first_table, fields[min(p + 1, planes - 1)]).astype(BF)
    lane = lax.broadcasted_iota(jnp.int32, (ROWS, 2 * SLOT), 1)

    for p in range(planes):
        slot = p % 2
        for copy in copies[p]:
            copy.wait()
        faces[slot, :, 256 + SLOT : 256 + SLOT + rhs, :width] = right_in[p]
        for a in range(3):
            rows = [inverse_in[p, v * 27 + a * 9 : v * 27 + a * 9 + 9] for v in range(5)]

            def put(c, value):
                solves[slot, c, a * FACE : (a + 1) * FACE] = (-value).astype(BF)

            turned(jnp.concatenate(rows, 0), raw.at[slot, a], put)
        for f, place in enumerate((256, 4 * FACE, 0, FACE, 2 * FACE, 3 * FACE)):

            def put(c, value):
                faces[slot, c, place : place + FACE] = value.astype(BF)

            turned(couplings_in[p, f], raw.at[slot, 3 + f], put)
        bases, lowers = [], []
        before = None
        for c in range(columns):
            solve = solves[slot, c]
            known[p, c] = mt(solve, faces[slot, c, :256]).astype(BF)
            both = mt(solve, faces[slot, c, 256:])
            move = (c % half * rhs - SLOT) % 128
            bases.append(pltpu.roll(both, move, 1) if move else both)
            if c % 2 == 0:
                before = both
            else:
                lowers.append(jnp.where(lane < SLOT, before, pltpu.roll(both, SLOT, 1)).astype(BF))
        for h in range(2):
            lanes = slice(h * half * rhs, (h + 1) * half * rhs)
            lower[p, h, :ROWS] = jnp.concatenate(lowers[2 * h : 2 * h + 2], 1)
            base[p, :, lanes] = -own_lanes(bases[h * half : (h + 1) * half], rhs)
    chain_products(lower, LAST, range(planes))


def chain_products(matrix, rows, order):
    for h in range(2):
        total = None
        for q in order:
            step = matrix[q, h, rows]
            total = step.astype(F32) if total is None else mm(step, split_lanes(total, SLOT))
            matrix[q, h, PRODUCT] = total.astype(BF)


def gathered(received_up, received_down, own, up_sel, down_sel, gathers):
    planes = up_sel.shape[0]

    def faces(received, select):
        received = jnp.concatenate([x[...] for x in received], 0)
        tail = received[planes * MAIN :]
        wholes = [jnp.concatenate([received[p * MAIN : (p + 1) * MAIN], tail], 0) for p in range(planes)]
        return [mm(select[p], wholes[p]).astype(BF) for p in range(planes)]

    low, high = faces(received_up, up_sel), faces(received_down, down_sel)
    sides = []
    for j, side in enumerate((low, high)):
        picked = mm(jnp.concatenate([x[FACE:] for x in side], 0), gathers[j, j]).astype(BF)
        sides.append([picked[p * FACE : (p + 1) * FACE] + own[p, j * FACE : (j + 1) * FACE] for p in range(planes)])
    return [jnp.concatenate([low[p][:FACE], high[p][:FACE], sides[0][p], sides[1][p]], 0) for p in range(planes)]


def known_part(known_c, operand, columns, rhs):
    half = columns // 2
    out = []
    for h in range(2):
        side = operand[:, h * half * rhs : (h + 1) * half * rhs]
        out.append(own_lanes([mm(known_c(h * half + c), side) for c in range(half)], rhs))
    return jnp.concatenate(out, 1)


def chain_kernel(known, base, matrix, wholes, outs, order, rows, rhs, last_face):
    part, traces, message = outs
    planes, columns = known.shape[:2]
    trace = None
    for p in order:
        whole = jnp.concatenate([wholes[p], last_face(p)], 0)
        value = base[p] + known_part(lambda c: known[p, c], whole, columns, rhs)
        part[p] = value
        value = value[rows]
        trace = value if trace is None else value + chain_step(matrix.at[p], trace, rhs, rows)
        traces[p] = trace
    message[FIRST] = trace.astype(BF)
    if message.shape[0] > FACE:
        for h in range(2):
            message[(1 + h) * FACE : (2 + h) * FACE] = matrix[order[-1], h, PRODUCT]


def forward_chain_kernel(up, down, above, own, gathers, up_sel, down_sel, known, lower, base, *outs, rhs):
    wholes = gathered([up], [down], own, up_sel, down_sel, gathers)
    planes, size = len(wholes), above.shape[1]
    pad = jnp.zeros((256 - 5 * FACE, size), BF)
    last_face = lambda p: jnp.concatenate([own[p, LAST] if p + 1 < planes else above[...], pad], 0)
    chain_kernel(known, base, lower, wholes, outs, range(planes), LAST, rhs, last_face)


def backward_chain_kernel(
    up, up_rest, down, down_rest, own, gathers, up_sel, down_sel, known, upper, base, *outs, rhs
):
    wholes = gathered([up, up_rest], [down, down_rest], own, up_sel, down_sel, gathers)
    last_face = lambda p: jnp.zeros((256 - 4 * FACE, up.shape[1]), BF)
    chain_kernel(known, base, upper, wholes, outs, range(len(wholes) - 1, -1, -1), FIRST, rhs, last_face)


def incoming(messages, products, forward, rhs):
    here = lax.axis_index("sweep")
    n = messages.shape[0]
    trace = None
    for i in range(n - 1) if forward else range(n - 1, 0, -1):
        value = messages[i, FIRST].astype(F32)
        if trace is None:
            trace = jnp.zeros_like(value)
        else:
            half = value.shape[1] // 2
            halves = [trace[:, h * half : (h + 1) * half] for h in range(2)]
            value = value + jnp.concatenate([mm(m, split_lanes(t, rhs)) for m, t in zip(products(i), halves)], 1)
        trace = jnp.where(i < here if forward else i > here, value, trace)
    return trace


def forward_finish_kernel(
    messages, part, traces, lower, send, middle, change, *pieces, rhs
):
    planes = part.shape[0]
    inside = lambda i: [messages[i, (1 + h) * FACE : (2 + h) * FACE] for h in range(2)]
    entry = incoming(messages, inside, True, rhs)
    out = []
    trace = entry
    for p in range(planes):
        delta = chain_step(lower.at[p], trace, rhs, FULL)
        change[p] = delta
        whole = (part[p] + delta).astype(BF)
        middle[p] = whole
        out.append(mm(send[p], whole))
        if p + 1 < planes:
            trace = traces[p] + chain_step(lower.at[p], entry, rhs, PRODUCT)
    put_shared(out, pieces[:2], pieces[2:])


def middle_kernel(middle, change, base, gathers, own_sel, known, own, out, upper):
    planes = middle.shape[0]
    mine = [mm(own_sel[...], middle[p]).astype(BF) for p in range(planes)]
    for j in range(2):
        side = jnp.concatenate([x[j * FACE : (j + 1) * FACE] for x in mine], 0)
        side = mm(side, gathers[1 - j, j]).astype(BF)
        for p in range(planes):
            own[p, j * FACE : (j + 1) * FACE] = side[p * FACE : (p + 1) * FACE]
    for p in range(planes):
        out[p] = base[p] + change[p]
    columns = known.shape[1]
    lane = lax.broadcasted_iota(jnp.int32, (ROWS, 2 * SLOT), 1)
    for p in range(planes):
        pairs = []
        for c in range(0, columns, 2):
            one, two = (known[p, c + i, :, 128:].astype(F32) for i in range(2))
            pairs.append(jnp.where(lane < SLOT, pltpu.roll(one, SLOT, 1), two).astype(BF))
        for h in range(2):
            upper[p, h, :ROWS] = jnp.concatenate(pairs[2 * h : 2 * h + 2], 1)
    chain_products(upper, FIRST, range(planes - 1, -1, -1))


def backward_finish_kernel(
    messages, near, next_near, part, traces, upper, back, result, results, sem, *, rhs
):
    planes = part.shape[0]
    here = lax.axis_index("sweep")
    beside = lambda i: [jnp.where(here + 1 == i, near[h], next_near[h]) for h in range(2)]
    entry = incoming(messages, beside, False, rhs)
    size = entry.shape[1]
    row = lax.broadcasted_iota(jnp.int32, (size, size), 0)
    column = lax.broadcasted_iota(jnp.int32, (size, size), 1)
    unit = jnp.where(row == column, 1.0, 0.0).astype(BF)
    columns, _, width = result.shape[1:]
    copies = []
    trace = entry
    for p in range(planes - 1, -1, -1):
        whole = part[p] + chain_step(upper.at[p], trace, rhs, FULL)
        flat = mm(back[...], whole.astype(BF)).astype(BF)
        results[p] = mt(unit, flat).astype(BF).reshape(columns, rhs, width)
        copies.append(pltpu.make_async_copy(results.at[p], result.at[p], sem.at[p]))
        copies[-1].start()
        if p:
            trace = traces[p] + chain_step(upper.at[p], entry, rhs, PRODUCT)
    for copy in copies:
        copy.wait()


def call(kernel, outs, operands, name, flops=2e8, far=(), scratch=(), out_space=pltpu.VMEM):
    shapes = [jax.ShapeDtypeStruct(s, d) for s, d in outs]
    nbytes = sum(x.size * x.dtype.itemsize for x in list(operands) + shapes)
    spaces = [pltpu.SMEM if x.dtype == jnp.int32 else pltpu.VMEM for x in operands]
    spaces = [pltpu.HBM if i in far else space for i, space in enumerate(spaces)]
    operands = [
        pltpu.with_memory_space_constraint(x, pltpu.HBM) if i in far else x for i, x in enumerate(operands)
    ]
    return pl.pallas_call(
        kernel,
        out_shape=shapes,
        in_specs=[pl.BlockSpec(memory_space=space) for space in spaces],
        out_specs=[pl.BlockSpec(memory_space=out_space)] * len(shapes),
        scratch_shapes=list(scratch),
        compiler_params=pltpu.CompilerParams(vmem_limit_bytes=24 * MIB),
        cost_estimate=pl.CostEstimate(flops=int(flops), bytes_accessed=int(nbytes), transcendentals=0),
        name=name,
    )(*operands)


def products(x, by):
    n = lax.axis_size("sweep")
    inner = range(1, n - 1)
    return [
        lax.ppermute(x, "sweep", [(i, i + step) for i in inner if 0 <= i + step < n]) for step in (by, 2 * by)
    ]


def weights(inverse, couplings, right, initial, neighbours):
    planes, columns, rhs, width = initial.shape
    size = columns * rhs
    pack = (planes, 2, ROWS + FACE, 256)
    field = (planes, ROWS, size)
    outs = [((planes, columns, ROWS, 256), BF), (pack, BF), (field, F32), (field, BF), ((2, 2, size, size), BF)]
    operands = (inverse, couplings, right, initial, neighbours)
    scratch = [pltpu.VMEM(x.shape, BF) for x in operands[:4]] + [
        pltpu.SMEM(neighbours.shape, jnp.int32),
        pltpu.VMEM((2, columns, ROWS, 256), BF),
        pltpu.VMEM((2, columns, 256 + 2 * SLOT, 256), BF),
        pltpu.VMEM((2, 9, 2, FACE * columns, 128), F32),
        pltpu.SemaphoreType.DMA((4, planes)),
    ]
    return call(weight_kernel, outs, operands, "weights", 1e10, (0, 1, 2, 3, 4), scratch)


def ring(x, axis, by):
    n = lax.axis_size(axis)
    return lax.ppermute(x, axis, [(i, (i + by) % n) for i in range(n)])


def shift(x, axis, by):
    n = lax.axis_size(axis)
    return lax.ppermute(x, axis, [(i, i + by) for i in range(n) if 0 <= i + by < n])


def local(right_sides, initial, inverse_blocks, couplings, neighbours):
    planes, columns, rhs, width = initial.shape
    size = columns * rhs
    const = lambda x: jnp.asarray(x, BF)
    send_in = const(send_table(ROWS, inner, planes))
    own_in = const(own_table(ROWS, inner))
    back = const(table(width, ROWS, [(natural(*n), n) for n in NODES], inner))
    up_sel = const(receive_table(2, planes))
    down_sel = const(receive_table(0, planes))
    beside = neighbours.T

    share = (planes * MAIN + tail_rows(planes), size)
    up, down, above = call(
        first_kernel,
        [(share, BF), (share, BF), ((FACE, size), BF)],
        (initial,),
        "initial_traces",
    )
    up, down, above, initial = lax.optimization_barrier((up, down, above, initial))
    from_low = ring(up, "cross", 1)
    from_high = ring(down, "cross", -1)
    from_above = shift(above, "sweep", -1)
    known, lower, base, own, gathers = weights(
        inverse_blocks.transpose(0, 2, 1, 3), couplings.transpose(0, 2, 3, 1, 4), right_sides, initial, beside
    )

    field = (planes, ROWS, size)
    trace = (planes, FACE, size)
    chain_outs = [(field, F32), (trace, F32)]
    part, traces, message = call(
        functools.partial(forward_chain_kernel, rhs=rhs),
        chain_outs + [((3 * FACE, size), BF)],
        (from_low, from_high, from_above, own, gathers, up_sel, down_sel, known, lower, base),
        "forward_chain",
    )
    messages = lax.all_gather(message, "sweep")
    split = share[0] // 32 * 16
    halves = [((rows, size), BF) for rows in (share[0] - split, split)]
    middle, change, *pieces = call(
        functools.partial(forward_finish_kernel, rhs=rhs),
        [(field, BF), (field, F32)] + halves * 2,
        (messages, part, traces, lower, send_in),
        "forward_finish",
    )
    from_low = [ring(x, "cross", 1) for x in pieces[:2]]
    from_high = [ring(x, "cross", -1) for x in pieces[2:]]
    own, base, upper = call(
        middle_kernel,
        [((planes, 2 * FACE, size), BF), (field, F32), (lower.shape, BF)],
        (middle, change, base, gathers, own_in, known),
        "middle",
        2e9,
    )
    own, pass_b = lax.optimization_barrier((own, upper[0, :, PRODUCT]))
    passes = products(pass_b, -1)
    part, traces, message = call(
        functools.partial(backward_chain_kernel, rhs=rhs),
        chain_outs + [((FACE, size), BF)],
        (*from_low, *from_high, own, gathers, up_sel, down_sel, known, upper, base),
        "backward_chain",
    )
    messages = lax.all_gather(message, "sweep")
    (result,) = call(
        functools.partial(backward_finish_kernel, rhs=rhs),
        [(right_sides.shape, BF)],
        (messages, *passes, part, traces, upper, back),
        "backward_finish",
        scratch=[pltpu.VMEM(right_sides.shape, BF), pltpu.SemaphoreType.DMA((planes,))],
        out_space=pltpu.HBM,
    )
    return result


def solution(mesh):
    return jax.shard_map(
        local,
        mesh=mesh,
        in_specs=(
            P("sweep", "cross", None, None),
            P("sweep", "cross", None, None),
            P("sweep", "cross", None, None),
            P("sweep", "cross", None, None, None),
            P("cross", None),
        ),
        out_specs=P("sweep", "cross", None, None),
        check_vma=False,
    )
```

```python
import functools

import jax
import jax.numpy as jnp
import numpy as np
from jax import lax
from jax.experimental import pallas as pl
from jax.experimental.pallas import tpu as pltpu
from jax.sharding import PartitionSpec as P

BF = jnp.bfloat16
F32 = jnp.float32
NT = 45
FACE = 48
SLOT = 64
ROWS = 3 * FACE
SHARED = 75
MAIN = 64
MIB = 1 << 20
FIRST = slice(0, FACE)
LAST = slice(2 * FACE, ROWS)
FULL = slice(0, ROWS)
PRODUCT = slice(ROWS, ROWS + FACE)


def natural(v, a, b, c):
    return v * 27 + a * 9 + b * 3 + c


def inner(v, a, b, c):
    return a * FACE + v * 9 + b * 3 + c


NODES = [(v, a, b, c) for v in range(5) for a in range(3) for b in range(3) for c in range(3)]


def face_nodes(place, which):
    return [n for n in NODES if n[1 + place] == which]


def table(height, width, rows, column_of):
    out = np.zeros((height, width), np.float32)
    for row, node in rows:
        out[row, column_of(*node)] = 1
    return out


def block(nodes, start=0):
    return [(start + i, n) for i, n in enumerate(nodes)]


def tail_rows(planes):
    return -(-planes * (SHARED - MAIN) // 16) * 16


def union_nodes(which):
    others = [b for b in range(3) if b != which]
    spots = [(which, c) for c in range(3)] + [(b, which) for b in others]
    return [(v, a, b, c) for v in range(5) for a in range(3) for b, c in spots]


def place_of(i, plane):
    return i if i < MAIN else i + plane * (SHARED - MAIN)


def send_table(width, column_of, planes):
    height = MAIN + tail_rows(planes)
    out = []
    for p in range(planes):
        rows = [(place_of(i, p), n) for i, n in enumerate(union_nodes(2))]
        rows += [(height + place_of(i, p), n) for i, n in enumerate(union_nodes(0))]
        out.append(table(2 * height, width, rows, column_of))
    return np.stack(out)


def own_table(width, column_of):
    rows = block(face_nodes(2, 2)) + block(face_nodes(2, 0), FACE)
    return table(2 * FACE, width, rows, column_of)


def receive_table(which, planes):
    rows = block(face_nodes(1, which)) + block(face_nodes(2, which), FACE)
    out = []
    for p in range(planes):
        place = {n: place_of(i, p) for i, n in enumerate(union_nodes(which))}
        out.append(table(2 * FACE, MAIN + tail_rows(planes), rows, lambda *n: place[n]))
    return np.stack(out)


def mm(a, b):
    return lax.dot_general(a, b, (((1,), (0,)), ((), ())), preferred_element_type=F32)


def mt(a, b):
    return lax.dot_general(a, b, (((1,), (1,)), ((), ())), preferred_element_type=F32)


def group(shape, width, at):
    lane = lax.broadcasted_iota(jnp.int32, shape, 1)
    return (lane >= at * width) & (lane < (at + 1) * width)


def split_lanes(value, width):
    lanes = value.shape[1]
    value = value.astype(F32)
    pad = jnp.zeros((SLOT - FACE, lanes), BF)
    parts = []
    for c in range(lanes // width):
        parts += [jnp.where(group(value.shape, width, c), value, 0.0).astype(BF), pad]
    return jnp.concatenate(parts, 0)


def own_lanes(values, width):
    out = values[0]
    for c in range(1, len(values)):
        out = jnp.where(group(out.shape, width, c), values[c], out)
    return out


def one_hot(source, start, height):
    row = lax.broadcasted_iota(jnp.int32, (height, source.shape[1]), 0) + start
    return jnp.where(row == source, 1.0, 0.0).astype(BF)


def chain_step(matrix, trace, rhs, rows=slice(None)):
    half = trace.shape[1] // 2
    return jnp.concatenate(
        [mm(matrix[h, rows], split_lanes(trace[:, h * half : (h + 1) * half], rhs)) for h in range(2)], 1
    )


def shared_target(row, which, plane, planes):
    rest = SHARED - MAIN
    i = jnp.where(row < MAIN, row, row - plane * rest)
    k = i % 15
    a = k // 5
    j = k % 5
    b = jnp.where(j < 3, which, j - 3 if which == 2 else j - 2)
    c = jnp.where(j < 3, j, which)
    inside = (row < MAIN) | ((i >= MAIN) & (i < SHARED))
    return jnp.where(inside, i // 15 * 27 + a * 9 + b * 3 + c, -1)


def picks(target, width):
    lane = lax.broadcasted_iota(jnp.int32, (target.shape[0], width), 1)
    return jnp.where(lane == target, 1.0, 0.0).astype(BF)


def rows_of(height):
    return lax.broadcasted_iota(jnp.int32, (height, 1), 0)


def first_target(row):
    return jnp.where(row < NT, row // 9 * 27 + row % 9, -1)


def c_target(row, which):
    return jnp.where(row < NT, row * 3 + which, -1)


def sources(neighbours, columns, rhs):
    place = lax.axis_index("cross")
    total = columns * lax.axis_size("cross")
    lane = lax.broadcasted_iota(jnp.int32, (1, columns * rhs), 1)
    out = []
    for face, first in ((2, place - 1), (3, place)):
        source = lane
        for c in range(columns):
            at = neighbours[face, c] - first * columns
            at = jnp.where(at < 0, at + total, at)
            at = jnp.where(at >= total, at - total, at)
            source = jnp.where(lane >= c * rhs, lane + (at - c) * rhs, source)
        out.append(source)
    return out


def even():
    return lax.rem(lax.axis_index("cross"), 2) == 0


def put_shared(out, near, far):
    height = out[0].shape[0] // 2
    messages = []
    for start in (0, height):
        tails = [x[start + MAIN : start + height] for x in out]
        parts = [x[start : start + MAIN] for x in out] + [sum(tails[1:], tails[0])]
        messages.append(jnp.concatenate(parts, 0))
    up, down = messages
    near[...] = jnp.where(even(), up, down).astype(BF)
    far[...] = jnp.where(even(), down, up).astype(BF)


def first_kernel(initial, near, far, above):
    planes, columns, rhs, width = initial.shape
    row = rows_of(MAIN + tail_rows(planes))
    out = []
    for p in range(planes):
        x = initial[p].reshape(columns * rhs, width)
        tables = [picks(shared_target(row, which, p, planes), width) for which in (2, 0)]
        out.append(mt(jnp.concatenate(tables, 0), x))
        if p == 0:
            above[...] = mt(picks(first_target(rows_of(FACE)), width), x).astype(BF)
    put_shared(out, near, far)


def turned(rows, raw, put):
    count, columns, width = rows.shape
    raw[0, : count * columns] = rows[:, :, :128].astype(F32).reshape(count * columns, 128)
    raw[1, : count * columns, : width - 128] = rows[:, :, 128:].astype(F32).reshape(count * columns, width - 128)
    for c in range(columns):
        put(c, jnp.concatenate([raw[i, pl.ds(c, FACE, stride=columns), :] for i in range(2)], 1))


def weight_kernel(
    inverse, couplings, right, initial_there, neighbours_there,
    known, lower, base, own, gathers,
    inverse_in, couplings_in, right_in, initial, neighbours, solves, faces, raw, done,
):
    planes, columns, rhs, width = initial.shape
    size = columns * rhs
    half = columns // 2
    early = [
        pltpu.make_async_copy(neighbours_there, neighbours, done.at[3, 0]),
        pltpu.make_async_copy(initial_there, initial, done.at[3, 1]),
    ]
    for copy in early:
        copy.start()
    copies = []
    for p in range(planes):
        pairs = ((inverse, inverse_in), (couplings, couplings_in), (right, right_in))
        copies.append([pltpu.make_async_copy(x.at[p], y.at[p], done.at[i, p]) for i, (x, y) in enumerate(pairs)])
        for copy in copies[p]:
            copy.start()
    faces[...] = jnp.zeros(faces.shape, BF)
    raw[...] = jnp.zeros(raw.shape, F32)
    for copy in early:
        copy.wait()
    source = sources(neighbours, columns, rhs)
    for i, start in enumerate((0, size)):
        for j in range(2):
            gathers[i, j] = one_hot(source[j], start, size)
    own_table = [picks(c_target(rows_of(FACE), which), width) for which in (2, 0)]
    first_table = picks(first_target(rows_of(FACE)), width)
    fields = [initial[p].reshape(size, width) for p in range(planes)]
    for j in range(2):
        mine = jnp.concatenate([mt(own_table[j], x).astype(BF) for x in fields], 0)
        mine = mm(mine, gathers[1 - j, j]).astype(BF)
        for p in range(planes):
            own[p, j * FACE : (j + 1) * FACE] = mine[p * FACE : (p + 1) * FACE]
    for p in range(planes):
        own[p, LAST] = mt(first_table, fields[min(p + 1, planes - 1)]).astype(BF)
    lane = lax.broadcasted_iota(jnp.int32, (ROWS, 2 * SLOT), 1)

    for p in range(planes):
        slot = p % 2
        for copy in copies[p]:
            copy.wait()
        faces[slot, :, 256 + SLOT : 256 + SLOT + rhs, :width] = right_in[p]
        for a in range(3):
            rows = [inverse_in[p, v * 27 + a * 9 : v * 27 + a * 9 + 9] for v in range(5)]

            def put(c, value):
                solves[slot, c, a * FACE : (a + 1) * FACE] = (-value).astype(BF)

            turned(jnp.concatenate(rows, 0), raw.at[slot, a], put)
        for f, place in enumerate((256, 4 * FACE, 0, FACE, 2 * FACE, 3 * FACE)):

            def put(c, value):
                faces[slot, c, place : place + FACE] = value.astype(BF)

            turned(couplings_in[p, f], raw.at[slot, 3 + f], put)
        bases, lowers = [], []
        before = None
        for c in range(columns):
            solve = solves[slot, c]
            known[p, c] = mt(solve, faces[slot, c, :256]).astype(BF)
            both = mt(solve, faces[slot, c, 256:])
            move = (c % half * rhs - SLOT) % 128
            bases.append(pltpu.roll(both, move, 1) if move else both)
            if c % 2 == 0:
                before = both
            else:
                lowers.append(jnp.where(lane < SLOT, before, pltpu.roll(both, SLOT, 1)).astype(BF))
        for h in range(2):
            lanes = slice(h * half * rhs, (h + 1) * half * rhs)
            lower[p, h, :ROWS] = jnp.concatenate(lowers[2 * h : 2 * h + 2], 1)
            base[p, :, lanes] = -own_lanes(bases[h * half : (h + 1) * half], rhs)
    chain_products(lower, LAST, range(planes))


def chain_products(matrix, rows, order):
    for h in range(2):
        total = None
        for q in order:
            step = matrix[q, h, rows]
            total = step.astype(F32) if total is None else mm(step, split_lanes(total, SLOT))
            matrix[q, h, PRODUCT] = total.astype(BF)


def gathered(near, far, own, up_sel, down_sel, gathers):
    planes = up_sel.shape[0]

    def faces(received, select):
        tail = received[planes * MAIN :]
        wholes = [jnp.concatenate([received[p * MAIN : (p + 1) * MAIN], tail], 0) for p in range(planes)]
        return [mm(select[p], wholes[p]).astype(BF) for p in range(planes)]

    low = faces(jnp.where(even(), far[...], near[...]), up_sel)
    high = faces(jnp.where(even(), near[...], far[...]), down_sel)
    sides = []
    for j, side in enumerate((low, high)):
        picked = mm(jnp.concatenate([x[FACE:] for x in side], 0), gathers[j, j]).astype(BF)
        sides.append([picked[p * FACE : (p + 1) * FACE] + own[p, j * FACE : (j + 1) * FACE] for p in range(planes)])
    return [jnp.concatenate([low[p][:FACE], high[p][:FACE], sides[0][p], sides[1][p]], 0) for p in range(planes)]


def known_part(known_c, operand, columns, rhs):
    half = columns // 2
    out = []
    for h in range(2):
        side = operand[:, h * half * rhs : (h + 1) * half * rhs]
        out.append(own_lanes([mm(known_c(h * half + c), side) for c in range(half)], rhs))
    return jnp.concatenate(out, 1)


def chain_kernel(known, base, matrix, wholes, outs, order, rows, rhs, last_face):
    part, traces, message = outs
    planes, columns = known.shape[:2]
    trace = None
    for p in order:
        whole = jnp.concatenate([wholes[p], last_face(p)], 0)
        value = base[p] + known_part(lambda c: known[p, c], whole, columns, rhs)
        part[p] = value
        value = value[rows]
        trace = value if trace is None else value + chain_step(matrix.at[p], trace, rhs, rows)
        traces[p] = trace
    message[FIRST] = trace.astype(BF)
    if message.shape[0] > FACE:
        for h in range(2):
            message[(1 + h) * FACE : (2 + h) * FACE] = matrix[order[-1], h, PRODUCT]


def forward_chain_kernel(near, far, above, own, gathers, up_sel, down_sel, known, lower, base, *outs, rhs):
    wholes = gathered(near, far, own, up_sel, down_sel, gathers)
    planes, size = len(wholes), above.shape[1]
    pad = jnp.zeros((256 - 5 * FACE, size), BF)
    last_face = lambda p: jnp.concatenate([own[p, LAST] if p + 1 < planes else above[...], pad], 0)
    chain_kernel(known, base, lower, wholes, outs, range(planes), LAST, rhs, last_face)


def backward_chain_kernel(near, far, own, gathers, up_sel, down_sel, known, upper, base, *outs, rhs):
    wholes = gathered(near, far, own, up_sel, down_sel, gathers)
    last_face = lambda p: jnp.zeros((256 - 4 * FACE, near.shape[1]), BF)
    chain_kernel(known, base, upper, wholes, outs, range(len(wholes) - 1, -1, -1), FIRST, rhs, last_face)


def incoming(messages, products, forward, rhs):
    here = lax.axis_index("sweep")
    n = messages.shape[0]
    trace = None
    for i in range(n - 1) if forward else range(n - 1, 0, -1):
        value = messages[i, FIRST].astype(F32)
        if trace is None:
            trace = jnp.zeros_like(value)
        else:
            half = value.shape[1] // 2
            halves = [trace[:, h * half : (h + 1) * half] for h in range(2)]
            value = value + jnp.concatenate([mm(m, split_lanes(t, rhs)) for m, t in zip(products(i), halves)], 1)
        trace = jnp.where(i < here if forward else i > here, value, trace)
    return trace


def forward_finish_kernel(
    messages, part, traces, lower, send, middle, change, near, far, *, rhs
):
    planes = part.shape[0]
    inside = lambda i: [messages[i, (1 + h) * FACE : (2 + h) * FACE] for h in range(2)]
    entry = incoming(messages, inside, True, rhs)
    out = []
    trace = entry
    for p in range(planes):
        delta = chain_step(lower.at[p], trace, rhs, FULL)
        change[p] = delta
        whole = (part[p] + delta).astype(BF)
        middle[p] = whole
        out.append(mm(send[p], whole))
        if p + 1 < planes:
            trace = traces[p] + chain_step(lower.at[p], entry, rhs, PRODUCT)
    put_shared(out, near, far)


def middle_kernel(middle, change, base, gathers, own_sel, known, own, out, upper):
    planes = middle.shape[0]
    mine = [mm(own_sel[...], middle[p]).astype(BF) for p in range(planes)]
    for j in range(2):
        side = jnp.concatenate([x[j * FACE : (j + 1) * FACE] for x in mine], 0)
        side = mm(side, gathers[1 - j, j]).astype(BF)
        for p in range(planes):
            own[p, j * FACE : (j + 1) * FACE] = side[p * FACE : (p + 1) * FACE]
    for p in range(planes):
        out[p] = base[p] + change[p]
    columns = known.shape[1]
    lane = lax.broadcasted_iota(jnp.int32, (ROWS, 2 * SLOT), 1)
    for p in range(planes):
        pairs = []
        for c in range(0, columns, 2):
            one, two = (known[p, c + i, :, 128:].astype(F32) for i in range(2))
            pairs.append(jnp.where(lane < SLOT, pltpu.roll(one, SLOT, 1), two).astype(BF))
        for h in range(2):
            upper[p, h, :ROWS] = jnp.concatenate(pairs[2 * h : 2 * h + 2], 1)
    chain_products(upper, FIRST, range(planes - 1, -1, -1))


def backward_finish_kernel(
    messages, near, next_near, part, traces, upper, back, result, results, sem, *, rhs
):
    planes = part.shape[0]
    here = lax.axis_index("sweep")
    beside = lambda i: [jnp.where(here + 1 == i, near[h], next_near[h]) for h in range(2)]
    entry = incoming(messages, beside, False, rhs)
    size = entry.shape[1]
    row = lax.broadcasted_iota(jnp.int32, (size, size), 0)
    column = lax.broadcasted_iota(jnp.int32, (size, size), 1)
    unit = jnp.where(row == column, 1.0, 0.0).astype(BF)
    columns, _, width = result.shape[1:]
    copies = []
    trace = entry
    for p in range(planes - 1, -1, -1):
        whole = part[p] + chain_step(upper.at[p], trace, rhs, FULL)
        flat = mm(back[...], whole.astype(BF)).astype(BF)
        results[p] = mt(unit, flat).astype(BF).reshape(columns, rhs, width)
        copies.append(pltpu.make_async_copy(results.at[p], result.at[p], sem.at[p]))
        copies[-1].start()
        if p:
            trace = traces[p] + chain_step(upper.at[p], entry, rhs, PRODUCT)
    for copy in copies:
        copy.wait()


def call(kernel, outs, operands, name, flops=2e8, far=(), scratch=(), out_space=pltpu.VMEM):
    shapes = [jax.ShapeDtypeStruct(s, d) for s, d in outs]
    nbytes = sum(x.size * x.dtype.itemsize for x in list(operands) + shapes)
    spaces = [pltpu.SMEM if x.dtype == jnp.int32 else pltpu.VMEM for x in operands]
    spaces = [pltpu.HBM if i in far else space for i, space in enumerate(spaces)]
    operands = [
        pltpu.with_memory_space_constraint(x, pltpu.HBM) if i in far else x for i, x in enumerate(operands)
    ]
    return pl.pallas_call(
        kernel,
        out_shape=shapes,
        in_specs=[pl.BlockSpec(memory_space=space) for space in spaces],
        out_specs=[pl.BlockSpec(memory_space=out_space)] * len(shapes),
        scratch_shapes=list(scratch),
        compiler_params=pltpu.CompilerParams(vmem_limit_bytes=24 * MIB),
        cost_estimate=pl.CostEstimate(flops=int(flops), bytes_accessed=int(nbytes), transcendentals=0),
        name=name,
    )(*operands)


def products(x, by):
    n = lax.axis_size("sweep")
    inner = range(1, n - 1)
    return [
        lax.ppermute(x, "sweep", [(i, i + step) for i in inner if 0 <= i + step < n]) for step in (by, 2 * by)
    ]


def weights(inverse, couplings, right, initial, neighbours):
    planes, columns, rhs, width = initial.shape
    size = columns * rhs
    pack = (planes, 2, ROWS + FACE, 256)
    field = (planes, ROWS, size)
    outs = [((planes, columns, ROWS, 256), BF), (pack, BF), (field, F32), (field, BF), ((2, 2, size, size), BF)]
    operands = (inverse, couplings, right, initial, neighbours)
    scratch = [pltpu.VMEM(x.shape, BF) for x in operands[:4]] + [
        pltpu.SMEM(neighbours.shape, jnp.int32),
        pltpu.VMEM((2, columns, ROWS, 256), BF),
        pltpu.VMEM((2, columns, 256 + 2 * SLOT, 256), BF),
        pltpu.VMEM((2, 9, 2, FACE * columns, 128), F32),
        pltpu.SemaphoreType.DMA((4, planes)),
    ]
    return call(weight_kernel, outs, operands, "weights", 1e10, (0, 1, 2, 3, 4), scratch)


def swapped(x, axis, first):
    n = lax.axis_size(axis)
    pairs = [(i, (i + 1) % n) for i in range(first, n, 2)]
    return lax.ppermute(x, axis, [pair for i, j in pairs for pair in ((i, j), (j, i))])


def shift(x, axis, by):
    n = lax.axis_size(axis)
    return lax.ppermute(x, axis, [(i, i + by) for i in range(n) if 0 <= i + by < n])


def local(right_sides, initial, inverse_blocks, couplings, neighbours):
    planes, columns, rhs, width = initial.shape
    size = columns * rhs
    const = lambda x: jnp.asarray(x, BF)
    send_in = const(send_table(ROWS, inner, planes))
    own_in = const(own_table(ROWS, inner))
    back = const(table(width, ROWS, [(natural(*n), n) for n in NODES], inner))
    up_sel = const(receive_table(2, planes))
    down_sel = const(receive_table(0, planes))
    beside = neighbours.T

    share = (planes * MAIN + tail_rows(planes), size)
    near, far, above = call(
        first_kernel,
        [(share, BF), (share, BF), ((FACE, size), BF)],
        (initial,),
        "initial_traces",
    )
    near, far, above, initial = lax.optimization_barrier((near, far, above, initial))
    near, far = swapped(near, "cross", 0), swapped(far, "cross", 1)
    from_above = shift(above, "sweep", -1)
    known, lower, base, own, gathers = weights(
        inverse_blocks.transpose(0, 2, 1, 3), couplings.transpose(0, 2, 3, 1, 4), right_sides, initial, beside
    )

    field = (planes, ROWS, size)
    trace = (planes, FACE, size)
    chain_outs = [(field, F32), (trace, F32)]
    part, traces, message = call(
        functools.partial(forward_chain_kernel, rhs=rhs),
        chain_outs + [((3 * FACE, size), BF)],
        (near, far, from_above, own, gathers, up_sel, down_sel, known, lower, base),
        "forward_chain",
    )
    messages = lax.all_gather(message, "sweep")
    middle, change, near, far = call(
        functools.partial(forward_finish_kernel, rhs=rhs),
        [(field, BF), (field, F32), (share, BF), (share, BF)],
        (messages, part, traces, lower, send_in),
        "forward_finish",
    )
    near, far = swapped(near, "cross", 0), swapped(far, "cross", 1)
    own, base, upper = call(
        middle_kernel,
        [((planes, 2 * FACE, size), BF), (field, F32), (lower.shape, BF)],
        (middle, change, base, gathers, own_in, known),
        "middle",
        2e9,
    )
    own, pass_b = lax.optimization_barrier((own, upper[0, :, PRODUCT]))
    passes = products(pass_b, -1)
    part, traces, message = call(
        functools.partial(backward_chain_kernel, rhs=rhs),
        chain_outs + [((FACE, size), BF)],
        (near, far, own, gathers, up_sel, down_sel, known, upper, base),
        "backward_chain",
    )
    messages = lax.all_gather(message, "sweep")
    (result,) = call(
        functools.partial(backward_finish_kernel, rhs=rhs),
        [(right_sides.shape, BF)],
        (messages, *passes, part, traces, upper, back),
        "backward_finish",
        scratch=[pltpu.VMEM(right_sides.shape, BF), pltpu.SemaphoreType.DMA((planes,))],
        out_space=pltpu.HBM,
    )
    return result


def solution(mesh):
    return jax.shard_map(
        local,
        mesh=mesh,
        in_specs=(
            P("sweep", "cross", None, None),
            P("sweep", "cross", None, None),
            P("sweep", "cross", None, None),
            P("sweep", "cross", None, None, None),
            P("cross", None),
        ),
        out_specs=P("sweep", "cross", None, None),
        check_vma=False,
    )
```

```python
import functools

import jax
import jax.numpy as jnp
import numpy as np
from jax import lax
from jax.experimental import pallas as pl
from jax.experimental.pallas import tpu as pltpu
from jax.sharding import PartitionSpec as P

BF = jnp.bfloat16
F32 = jnp.float32
NT = 45
FACE = 48
SLOT = 64
ROWS = 3 * FACE
SHARED = 75
MAIN = 64
MIB = 1 << 20
FIRST = slice(0, FACE)
LAST = slice(2 * FACE, ROWS)
FULL = slice(0, ROWS)
PRODUCT = slice(ROWS, ROWS + FACE)


def natural(v, a, b, c):
    return v * 27 + a * 9 + b * 3 + c


def inner(v, a, b, c):
    return a * FACE + v * 9 + b * 3 + c


NODES = [(v, a, b, c) for v in range(5) for a in range(3) for b in range(3) for c in range(3)]


def face_nodes(place, which):
    return [n for n in NODES if n[1 + place] == which]


def table(height, width, rows, column_of):
    out = np.zeros((height, width), np.float32)
    for row, node in rows:
        out[row, column_of(*node)] = 1
    return out


def block(nodes, start=0):
    return [(start + i, n) for i, n in enumerate(nodes)]


def tail_rows(planes):
    return -(-planes * (SHARED - MAIN) // 16) * 16


def union_nodes(which):
    others = [b for b in range(3) if b != which]
    spots = [(which, c) for c in range(3)] + [(b, which) for b in others]
    return [(v, a, b, c) for v in range(5) for a in range(3) for b, c in spots]


def place_of(i, plane):
    return i if i < MAIN else i + plane * (SHARED - MAIN)


def send_table(width, column_of, planes):
    height = MAIN + tail_rows(planes)
    out = []
    for p in range(planes):
        rows = [(place_of(i, p), n) for i, n in enumerate(union_nodes(2))]
        rows += [(height + place_of(i, p), n) for i, n in enumerate(union_nodes(0))]
        out.append(table(2 * height, width, rows, column_of))
    return np.stack(out)


def own_table(width, column_of):
    rows = block(face_nodes(2, 2)) + block(face_nodes(2, 0), FACE)
    return table(2 * FACE, width, rows, column_of)


def receive_table(which, planes):
    rows = block(face_nodes(1, which)) + block(face_nodes(2, which), FACE)
    out = []
    for p in range(planes):
        place = {n: place_of(i, p) for i, n in enumerate(union_nodes(which))}
        out.append(table(2 * FACE, MAIN + tail_rows(planes), rows, lambda *n: place[n]))
    return np.stack(out)


def mm(a, b):
    return lax.dot_general(a, b, (((1,), (0,)), ((), ())), preferred_element_type=F32)


def mt(a, b):
    return lax.dot_general(a, b, (((1,), (1,)), ((), ())), preferred_element_type=F32)


def group(shape, width, at):
    lane = lax.broadcasted_iota(jnp.int32, shape, 1)
    return (lane >= at * width) & (lane < (at + 1) * width)


def split_lanes(value, width):
    lanes = value.shape[1]
    value = value.astype(F32)
    pad = jnp.zeros((SLOT - FACE, lanes), BF)
    parts = []
    for c in range(lanes // width):
        parts += [jnp.where(group(value.shape, width, c), value, 0.0).astype(BF), pad]
    return jnp.concatenate(parts, 0)


def own_lanes(values, width):
    out = values[0]
    for c in range(1, len(values)):
        out = jnp.where(group(out.shape, width, c), values[c], out)
    return out


def one_hot(source, start, height):
    row = lax.broadcasted_iota(jnp.int32, (height, source.shape[1]), 0) + start
    return jnp.where(row == source, 1.0, 0.0).astype(BF)


def chain_step(matrix, trace, rhs, rows=slice(None)):
    half = trace.shape[1] // 2
    return jnp.concatenate(
        [mm(matrix[h, rows], split_lanes(trace[:, h * half : (h + 1) * half], rhs)) for h in range(2)], 1
    )


def shared_target(row, which, plane, planes):
    rest = SHARED - MAIN
    i = jnp.where(row < MAIN, row, row - plane * rest)
    k = i % 15
    a = k // 5
    j = k % 5
    b = jnp.where(j < 3, which, j - 3 if which == 2 else j - 2)
    c = jnp.where(j < 3, j, which)
    inside = (row < MAIN) | ((i >= MAIN) & (i < SHARED))
    return jnp.where(inside, i // 15 * 27 + a * 9 + b * 3 + c, -1)


def picks(target, width):
    lane = lax.broadcasted_iota(jnp.int32, (target.shape[0], width), 1)
    return jnp.where(lane == target, 1.0, 0.0).astype(BF)


def rows_of(height):
    return lax.broadcasted_iota(jnp.int32, (height, 1), 0)


def first_target(row):
    return jnp.where(row < NT, row // 9 * 27 + row % 9, -1)


def c_target(row, which):
    return jnp.where(row < NT, row * 3 + which, -1)


def sources(neighbours, columns, rhs):
    place = lax.axis_index("cross")
    total = columns * lax.axis_size("cross")
    lane = lax.broadcasted_iota(jnp.int32, (1, columns * rhs), 1)
    out = []
    for face, first in ((2, place - 1), (3, place)):
        source = lane
        for c in range(columns):
            at = neighbours[face, c] - first * columns
            at = jnp.where(at < 0, at + total, at)
            at = jnp.where(at >= total, at - total, at)
            source = jnp.where(lane >= c * rhs, lane + (at - c) * rhs, source)
        out.append(source)
    return out


def even():
    return lax.rem(lax.axis_index("cross"), 2) == 0


def put_shared(out, near, far):
    height = out[0].shape[0] // 2
    messages = []
    for start in (0, height):
        tails = [x[start + MAIN : start + height] for x in out]
        parts = [x[start : start + MAIN] for x in out] + [sum(tails[1:], tails[0])]
        messages.append(jnp.concatenate(parts, 0))
    up, down = messages
    near[...] = jnp.where(even(), up, down).astype(BF)
    far[...] = jnp.where(even(), down, up).astype(BF)


def first_kernel(initial, near, far, above):
    planes, columns, rhs, width = initial.shape
    row = rows_of(MAIN + tail_rows(planes))
    out = []
    for p in range(planes):
        x = initial[p].reshape(columns * rhs, width)
        tables = [picks(shared_target(row, which, p, planes), width) for which in (2, 0)]
        out.append(mt(jnp.concatenate(tables, 0), x))
        if p == 0:
            above[...] = mt(picks(first_target(rows_of(FACE)), width), x).astype(BF)
    put_shared(out, near, far)


def turned(rows, raw, put):
    count, columns, width = rows.shape
    raw[0, : count * columns] = rows[:, :, :128].astype(F32).reshape(count * columns, 128)
    rest = rows[:, :, 128:].astype(F32).reshape(count * columns, width - 128)
    raw[1, : count * columns] = jnp.concatenate([rest, jnp.zeros((count * columns, 256 - width), F32)], 1)
    for c in range(columns):
        put(c, jnp.concatenate([raw[i, pl.ds(c, FACE, stride=columns), :] for i in range(2)], 1))


def weight_kernel(
    inverse, couplings, right, initial_there, neighbours_there,
    known, lower, base, own, gathers,
    inverse_in, couplings_in, right_in, initial, neighbours, solves, faces, raw, done,
):
    planes, columns, rhs, width = initial.shape
    size = columns * rhs
    half = columns // 2
    early = [
        pltpu.make_async_copy(neighbours_there, neighbours, done.at[3, 0]),
        pltpu.make_async_copy(initial_there, initial, done.at[3, 1]),
    ]
    for copy in early:
        copy.start()
    copies = []
    for p in range(planes):
        pairs = ((inverse, inverse_in), (couplings, couplings_in), (right, right_in))
        copies.append([pltpu.make_async_copy(x.at[p], y.at[p], done.at[i, p]) for i, (x, y) in enumerate(pairs)])
        for copy in copies[p]:
            copy.start()
    for start, stop in ((5 * FACE, 256), (256 + FACE, 256 + 2 * SLOT)):
        faces[:, :, start:stop] = jnp.zeros((2, columns, stop - start, 256), BF)
    raw[:, :, :, NT * columns :] = jnp.zeros((2, 9, 2, (FACE - NT) * columns, 128), F32)
    for copy in early:
        copy.wait()
    source = sources(neighbours, columns, rhs)
    for i, start in enumerate((0, size)):
        for j in range(2):
            gathers[i, j] = one_hot(source[j], start, size)
    own_table = [picks(c_target(rows_of(FACE), which), width) for which in (2, 0)]
    first_table = picks(first_target(rows_of(FACE)), width)
    fields = [initial[p].reshape(size, width) for p in range(planes)]
    for j in range(2):
        mine = jnp.concatenate([mt(own_table[j], x).astype(BF) for x in fields], 0)
        mine = mm(mine, gathers[1 - j, j]).astype(BF)
        for p in range(planes):
            own[p, j * FACE : (j + 1) * FACE] = mine[p * FACE : (p + 1) * FACE]
    for p in range(planes):
        own[p, LAST] = mt(first_table, fields[min(p + 1, planes - 1)]).astype(BF)
    lane = lax.broadcasted_iota(jnp.int32, (ROWS, 2 * SLOT), 1)

    for p in range(planes):
        slot = p % 2
        for copy in copies[p]:
            copy.wait()
        faces[slot, :, 256 + SLOT : 256 + SLOT + rhs, :width] = right_in[p]
        for a in range(3):
            rows = [inverse_in[p, v * 27 + a * 9 : v * 27 + a * 9 + 9] for v in range(5)]

            def put(c, value):
                solves[slot, c, a * FACE : (a + 1) * FACE] = (-value).astype(BF)

            turned(jnp.concatenate(rows, 0), raw.at[slot, a], put)
        for f, place in enumerate((256, 4 * FACE, 0, FACE, 2 * FACE, 3 * FACE)):

            def put(c, value):
                faces[slot, c, place : place + FACE] = value.astype(BF)

            turned(couplings_in[p, f], raw.at[slot, 3 + f], put)
        bases, lowers = [], []
        before = None
        for c in range(columns):
            solve = solves[slot, c]
            known[p, c] = mt(solve, faces[slot, c, :256]).astype(BF)
            both = mt(solve, faces[slot, c, 256:])
            move = (c % half * rhs - SLOT) % 128
            bases.append(pltpu.roll(both, move, 1) if move else both)
            if c % 2 == 0:
                before = both
            else:
                lowers.append(jnp.where(lane < SLOT, before, pltpu.roll(both, SLOT, 1)).astype(BF))
        for h in range(2):
            lanes = slice(h * half * rhs, (h + 1) * half * rhs)
            lower[p, h, :ROWS] = jnp.concatenate(lowers[2 * h : 2 * h + 2], 1)
            base[p, :, lanes] = -own_lanes(bases[h * half : (h + 1) * half], rhs)
    chain_products(lower, LAST, range(planes))


def chain_products(matrix, rows, order):
    for h in range(2):
        total = None
        for q in order:
            step = matrix[q, h, rows]
            total = step.astype(F32) if total is None else mm(step, split_lanes(total, SLOT))
            matrix[q, h, PRODUCT] = total.astype(BF)


def gathered(near, far, own, up_sel, down_sel, gathers):
    planes = up_sel.shape[0]

    def faces(received, select):
        tail = received[planes * MAIN :]
        wholes = [jnp.concatenate([received[p * MAIN : (p + 1) * MAIN], tail], 0) for p in range(planes)]
        return [mm(select[p], wholes[p]).astype(BF) for p in range(planes)]

    low = faces(jnp.where(even(), far[...], near[...]), up_sel)
    high = faces(jnp.where(even(), near[...], far[...]), down_sel)
    sides = []
    for j, side in enumerate((low, high)):
        picked = mm(jnp.concatenate([x[FACE:] for x in side], 0), gathers[j, j]).astype(BF)
        sides.append([picked[p * FACE : (p + 1) * FACE] + own[p, j * FACE : (j + 1) * FACE] for p in range(planes)])
    return [jnp.concatenate([low[p][:FACE], high[p][:FACE], sides[0][p], sides[1][p]], 0) for p in range(planes)]


def known_part(known_c, operand, columns, rhs):
    half = columns // 2
    out = []
    for h in range(2):
        side = operand[:, h * half * rhs : (h + 1) * half * rhs]
        out.append(own_lanes([mm(known_c(h * half + c), side) for c in range(half)], rhs))
    return jnp.concatenate(out, 1)


def chain_kernel(known, base, matrix, wholes, outs, order, rows, rhs, last_face):
    part, traces, message = outs
    planes, columns = known.shape[:2]
    trace = None
    for p in order:
        whole = jnp.concatenate([wholes[p], last_face(p)], 0)
        value = base[p] + known_part(lambda c: known[p, c], whole, columns, rhs)
        part[p] = value
        value = value[rows]
        trace = value if trace is None else value + chain_step(matrix.at[p], trace, rhs, rows)
        traces[p] = trace
    message[FIRST] = trace.astype(BF)
    if message.shape[0] > FACE:
        for h in range(2):
            message[(1 + h) * FACE : (2 + h) * FACE] = matrix[order[-1], h, PRODUCT]


def forward_chain_kernel(near, far, above, own, gathers, up_sel, down_sel, known, lower, base, *outs, rhs):
    wholes = gathered(near, far, own, up_sel, down_sel, gathers)
    planes, size = len(wholes), above.shape[1]
    pad = jnp.zeros((256 - 5 * FACE, size), BF)
    last_face = lambda p: jnp.concatenate([own[p, LAST] if p + 1 < planes else above[...], pad], 0)
    chain_kernel(known, base, lower, wholes, outs, range(planes), LAST, rhs, last_face)


def backward_chain_kernel(near, far, own, gathers, up_sel, down_sel, known, upper, base, *outs, rhs):
    wholes = gathered(near, far, own, up_sel, down_sel, gathers)
    last_face = lambda p: jnp.zeros((256 - 4 * FACE, near.shape[1]), BF)
    chain_kernel(known, base, upper, wholes, outs, range(len(wholes) - 1, -1, -1), FIRST, rhs, last_face)


def incoming(messages, products, forward, rhs):
    here = lax.axis_index("sweep")
    n = messages.shape[0]
    trace = None
    for i in range(n - 1) if forward else range(n - 1, 0, -1):
        value = messages[i, FIRST].astype(F32)
        if trace is None:
            trace = jnp.zeros_like(value)
        else:
            half = value.shape[1] // 2
            halves = [trace[:, h * half : (h + 1) * half] for h in range(2)]
            value = value + jnp.concatenate([mm(m, split_lanes(t, rhs)) for m, t in zip(products(i), halves)], 1)
        trace = jnp.where(i < here if forward else i > here, value, trace)
    return trace


def forward_finish_kernel(
    messages, part, traces, lower, send, middle, change, near, far, *, rhs
):
    planes = part.shape[0]
    inside = lambda i: [messages[i, (1 + h) * FACE : (2 + h) * FACE] for h in range(2)]
    entry = incoming(messages, inside, True, rhs)
    out = []
    trace = entry
    for p in range(planes):
        delta = chain_step(lower.at[p], trace, rhs, FULL)
        change[p] = delta
        whole = (part[p] + delta).astype(BF)
        middle[p] = whole
        out.append(mm(send[p], whole))
        if p + 1 < planes:
            trace = traces[p] + chain_step(lower.at[p], entry, rhs, PRODUCT)
    put_shared(out, near, far)


def middle_kernel(middle, change, base, gathers, own_sel, known, own, out, upper):
    planes = middle.shape[0]
    mine = [mm(own_sel[...], middle[p]).astype(BF) for p in range(planes)]
    for j in range(2):
        side = jnp.concatenate([x[j * FACE : (j + 1) * FACE] for x in mine], 0)
        side = mm(side, gathers[1 - j, j]).astype(BF)
        for p in range(planes):
            own[p, j * FACE : (j + 1) * FACE] = side[p * FACE : (p + 1) * FACE]
    for p in range(planes):
        out[p] = base[p] + change[p]
    columns = known.shape[1]
    lane = lax.broadcasted_iota(jnp.int32, (ROWS, 2 * SLOT), 1)
    for p in range(planes):
        pairs = []
        for c in range(0, columns, 2):
            one, two = (known[p, c + i, :, 128:].astype(F32) for i in range(2))
            pairs.append(jnp.where(lane < SLOT, pltpu.roll(one, SLOT, 1), two).astype(BF))
        for h in range(2):
            upper[p, h, :ROWS] = jnp.concatenate(pairs[2 * h : 2 * h + 2], 1)
    chain_products(upper, FIRST, range(planes - 1, -1, -1))


def backward_finish_kernel(
    messages, near, next_near, part, traces, upper, back, result, results, sem, *, rhs
):
    planes = part.shape[0]
    here = lax.axis_index("sweep")
    beside = lambda i: [jnp.where(here + 1 == i, near[h], next_near[h]) for h in range(2)]
    entry = incoming(messages, beside, False, rhs)
    size = entry.shape[1]
    row = lax.broadcasted_iota(jnp.int32, (size, size), 0)
    column = lax.broadcasted_iota(jnp.int32, (size, size), 1)
    unit = jnp.where(row == column, 1.0, 0.0).astype(BF)
    columns, _, width = result.shape[1:]
    copies = []
    trace = entry
    for p in range(planes - 1, -1, -1):
        whole = part[p] + chain_step(upper.at[p], trace, rhs, FULL)
        flat = mm(back[...], whole.astype(BF)).astype(BF)
        results[p] = mt(unit, flat).astype(BF).reshape(columns, rhs, width)
        copies.append(pltpu.make_async_copy(results.at[p], result.at[p], sem.at[p]))
        copies[-1].start()
        if p:
            trace = traces[p] + chain_step(upper.at[p], entry, rhs, PRODUCT)
    for copy in copies:
        copy.wait()


def call(kernel, outs, operands, name, flops=2e8, far=(), scratch=(), out_space=pltpu.VMEM):
    shapes = [jax.ShapeDtypeStruct(s, d) for s, d in outs]
    nbytes = sum(x.size * x.dtype.itemsize for x in list(operands) + shapes)
    spaces = [pltpu.SMEM if x.dtype == jnp.int32 else pltpu.VMEM for x in operands]
    spaces = [pltpu.HBM if i in far else space for i, space in enumerate(spaces)]
    operands = [
        pltpu.with_memory_space_constraint(x, pltpu.HBM) if i in far else x for i, x in enumerate(operands)
    ]
    return pl.pallas_call(
        kernel,
        out_shape=shapes,
        in_specs=[pl.BlockSpec(memory_space=space) for space in spaces],
        out_specs=[pl.BlockSpec(memory_space=out_space)] * len(shapes),
        scratch_shapes=list(scratch),
        compiler_params=pltpu.CompilerParams(vmem_limit_bytes=24 * MIB),
        cost_estimate=pl.CostEstimate(flops=int(flops), bytes_accessed=int(nbytes), transcendentals=0),
        name=name,
    )(*operands)


def products(x, by):
    n = lax.axis_size("sweep")
    inner = range(1, n - 1)
    return [
        lax.ppermute(x, "sweep", [(i, i + step) for i in inner if 0 <= i + step < n]) for step in (by, 2 * by)
    ]


def weights(inverse, couplings, right, initial, neighbours):
    planes, columns, rhs, width = initial.shape
    size = columns * rhs
    pack = (planes, 2, ROWS + FACE, 256)
    field = (planes, ROWS, size)
    outs = [((planes, columns, ROWS, 256), BF), (pack, BF), (field, F32), (field, BF), ((2, 2, size, size), BF)]
    operands = (inverse, couplings, right, initial, neighbours)
    scratch = [pltpu.VMEM(x.shape, BF) for x in operands[:4]] + [
        pltpu.SMEM(neighbours.shape, jnp.int32),
        pltpu.VMEM((2, columns, ROWS, 256), BF),
        pltpu.VMEM((2, columns, 256 + 2 * SLOT, 256), BF),
        pltpu.VMEM((2, 9, 2, FACE * columns, 128), F32),
        pltpu.SemaphoreType.DMA((4, planes)),
    ]
    return call(weight_kernel, outs, operands, "weights", 1e10, (0, 1, 2, 3, 4), scratch)


def swapped(x, axis, first):
    n = lax.axis_size(axis)
    pairs = [(i, (i + 1) % n) for i in range(first, n, 2)]
    return lax.ppermute(x, axis, [pair for i, j in pairs for pair in ((i, j), (j, i))])


def shift(x, axis, by):
    n = lax.axis_size(axis)
    return lax.ppermute(x, axis, [(i, i + by) for i in range(n) if 0 <= i + by < n])


def local(right_sides, initial, inverse_blocks, couplings, neighbours):
    planes, columns, rhs, width = initial.shape
    size = columns * rhs
    const = lambda x: jnp.asarray(x, BF)
    send_in = const(send_table(ROWS, inner, planes))
    own_in = const(own_table(ROWS, inner))
    back = const(table(width, ROWS, [(natural(*n), n) for n in NODES], inner))
    up_sel = const(receive_table(2, planes))
    down_sel = const(receive_table(0, planes))
    beside = neighbours.T

    share = (planes * MAIN + tail_rows(planes), size)
    near, far, above = call(
        first_kernel,
        [(share, BF), (share, BF), ((FACE, size), BF)],
        (initial,),
        "initial_traces",
    )
    near, far, above, initial = lax.optimization_barrier((near, far, above, initial))
    near, far = swapped(near, "cross", 0), swapped(far, "cross", 1)
    from_above = shift(above, "sweep", -1)
    known, lower, base, own, gathers = weights(
        inverse_blocks.transpose(0, 2, 1, 3), couplings.transpose(0, 2, 3, 1, 4), right_sides, initial, beside
    )

    field = (planes, ROWS, size)
    trace = (planes, FACE, size)
    chain_outs = [(field, F32), (trace, F32)]
    part, traces, message = call(
        functools.partial(forward_chain_kernel, rhs=rhs),
        chain_outs + [((3 * FACE, size), BF)],
        (near, far, from_above, own, gathers, up_sel, down_sel, known, lower, base),
        "forward_chain",
    )
    messages = lax.all_gather(message, "sweep")
    middle, change, near, far = call(
        functools.partial(forward_finish_kernel, rhs=rhs),
        [(field, BF), (field, F32), (share, BF), (share, BF)],
        (messages, part, traces, lower, send_in),
        "forward_finish",
    )
    near, far = swapped(near, "cross", 0), swapped(far, "cross", 1)
    own, base, upper = call(
        middle_kernel,
        [((planes, 2 * FACE, size), BF), (field, F32), (lower.shape, BF)],
        (middle, change, base, gathers, own_in, known),
        "middle",
        2e9,
    )
    own, pass_b = lax.optimization_barrier((own, upper[0, :, PRODUCT]))
    passes = products(pass_b, -1)
    part, traces, message = call(
        functools.partial(backward_chain_kernel, rhs=rhs),
        chain_outs + [((FACE, size), BF)],
        (near, far, own, gathers, up_sel, down_sel, known, upper, base),
        "backward_chain",
    )
    messages = lax.all_gather(message, "sweep")
    (result,) = call(
        functools.partial(backward_finish_kernel, rhs=rhs),
        [(right_sides.shape, BF)],
        (messages, *passes, part, traces, upper, back),
        "backward_finish",
        scratch=[pltpu.VMEM(right_sides.shape, BF), pltpu.SemaphoreType.DMA((planes,))],
        out_space=pltpu.HBM,
    )
    return result


def solution(mesh):
    return jax.shard_map(
        local,
        mesh=mesh,
        in_specs=(
            P("sweep", "cross", None, None),
            P("sweep", "cross", None, None),
            P("sweep", "cross", None, None),
            P("sweep", "cross", None, None, None),
            P("cross", None),
        ),
        out_specs=P("sweep", "cross", None, None),
        check_vma=False,
    )
```

```python
import functools

import jax
import jax.numpy as jnp
import numpy as np
from jax import lax
from jax.experimental import pallas as pl
from jax.experimental.pallas import tpu as pltpu
from jax.sharding import PartitionSpec as P

BF = jnp.bfloat16
F32 = jnp.float32
NT = 45
FACE = 48
SLOT = 64
ROWS = 3 * FACE
SHARED = 75
MAIN = 64
MIB = 1 << 20
FIRST = slice(0, FACE)
LAST = slice(2 * FACE, ROWS)
FULL = slice(0, ROWS)
PRODUCT = slice(ROWS, ROWS + FACE)


def natural(v, a, b, c):
    return v * 27 + a * 9 + b * 3 + c


def inner(v, a, b, c):
    return a * FACE + v * 9 + b * 3 + c


NODES = [(v, a, b, c) for v in range(5) for a in range(3) for b in range(3) for c in range(3)]


def face_nodes(place, which):
    return [n for n in NODES if n[1 + place] == which]


def table(height, width, rows, column_of):
    out = np.zeros((height, width), np.float32)
    for row, node in rows:
        out[row, column_of(*node)] = 1
    return out


def block(nodes, start=0):
    return [(start + i, n) for i, n in enumerate(nodes)]


def tail_rows(planes):
    return -(-planes * (SHARED - MAIN) // 16) * 16


def union_nodes(which):
    others = [b for b in range(3) if b != which]
    spots = [(which, c) for c in range(3)] + [(b, which) for b in others]
    return [(v, a, b, c) for v in range(5) for a in range(3) for b, c in spots]


def place_of(i, plane):
    return i if i < MAIN else i + plane * (SHARED - MAIN)


def send_table(width, column_of, planes):
    height = MAIN + tail_rows(planes)
    out = []
    for p in range(planes):
        rows = [(place_of(i, p), n) for i, n in enumerate(union_nodes(2))]
        rows += [(height + place_of(i, p), n) for i, n in enumerate(union_nodes(0))]
        out.append(table(2 * height, width, rows, column_of))
    return np.stack(out)


def own_table(width, column_of):
    rows = block(face_nodes(2, 2)) + block(face_nodes(2, 0), FACE)
    return table(2 * FACE, width, rows, column_of)


def receive_table(which, planes):
    rows = block(face_nodes(1, which)) + block(face_nodes(2, which), FACE)
    out = []
    for p in range(planes):
        place = {n: place_of(i, p) for i, n in enumerate(union_nodes(which))}
        out.append(table(2 * FACE, MAIN + tail_rows(planes), rows, lambda *n: place[n]))
    return np.stack(out)


def mm(a, b):
    return lax.dot_general(a, b, (((1,), (0,)), ((), ())), preferred_element_type=F32)


def mt(a, b):
    return lax.dot_general(a, b, (((1,), (1,)), ((), ())), preferred_element_type=F32)


def group(shape, width, at):
    lane = lax.broadcasted_iota(jnp.int32, shape, 1)
    return (lane >= at * width) & (lane < (at + 1) * width)


def split_lanes(value, width):
    lanes = value.shape[1]
    value = value.astype(F32)
    pad = jnp.zeros((SLOT - FACE, lanes), BF)
    parts = []
    for c in range(lanes // width):
        parts += [jnp.where(group(value.shape, width, c), value, 0.0).astype(BF), pad]
    return jnp.concatenate(parts, 0)


def own_lanes(values, width):
    out = values[0]
    for c in range(1, len(values)):
        out = jnp.where(group(out.shape, width, c), values[c], out)
    return out


def one_hot(source, start, height):
    row = lax.broadcasted_iota(jnp.int32, (height, source.shape[1]), 0) + start
    return jnp.where(row == source, 1.0, 0.0).astype(BF)


def chain_step(matrix, trace, rhs, rows=slice(None)):
    half = trace.shape[1] // 2
    return jnp.concatenate(
        [mm(matrix[h, rows], split_lanes(trace[:, h * half : (h + 1) * half], rhs)) for h in range(2)], 1
    )


def shared_target(row, which, plane, planes):
    rest = SHARED - MAIN
    i = jnp.where(row < MAIN, row, row - plane * rest)
    k = i % 15
    a = k // 5
    j = k % 5
    b = jnp.where(j < 3, which, j - 3 if which == 2 else j - 2)
    c = jnp.where(j < 3, j, which)
    inside = (row < MAIN) | ((i >= MAIN) & (i < SHARED))
    return jnp.where(inside, i // 15 * 27 + a * 9 + b * 3 + c, -1)


def picks(target, width):
    lane = lax.broadcasted_iota(jnp.int32, (target.shape[0], width), 1)
    return jnp.where(lane == target, 1.0, 0.0).astype(BF)


def rows_of(height):
    return lax.broadcasted_iota(jnp.int32, (height, 1), 0)


def first_target(row):
    return jnp.where(row < NT, row // 9 * 27 + row % 9, -1)


def c_target(row, which):
    return jnp.where(row < NT, row * 3 + which, -1)


def sources(neighbours, columns, rhs):
    place = lax.axis_index("cross")
    total = columns * lax.axis_size("cross")
    lane = lax.broadcasted_iota(jnp.int32, (1, columns * rhs), 1)
    out = []
    for face, first in ((2, place - 1), (3, place)):
        source = lane
        for c in range(columns):
            at = neighbours[face, c] - first * columns
            at = jnp.where(at < 0, at + total, at)
            at = jnp.where(at >= total, at - total, at)
            source = jnp.where(lane >= c * rhs, lane + (at - c) * rhs, source)
        out.append(source)
    return out


def even():
    return lax.rem(lax.axis_index("cross"), 2) == 0


def put_shared(out, near, far):
    height = out[0].shape[0] // 2
    messages = []
    for start in (0, height):
        tails = [x[start + MAIN : start + height] for x in out]
        parts = [x[start : start + MAIN] for x in out] + [sum(tails[1:], tails[0])]
        messages.append(jnp.concatenate(parts, 0))
    up, down = messages
    near[...] = jnp.where(even(), up, down).astype(BF)
    far[...] = jnp.where(even(), down, up).astype(BF)


def first_kernel(initial, near, far, above):
    planes, columns, rhs, width = initial.shape
    row = rows_of(MAIN + tail_rows(planes))
    out = []
    for p in range(planes):
        x = initial[p].reshape(columns * rhs, width)
        tables = [picks(shared_target(row, which, p, planes), width) for which in (2, 0)]
        out.append(mt(jnp.concatenate(tables, 0), x))
        if p == 0:
            above[...] = mt(picks(first_target(rows_of(FACE)), width), x).astype(BF)
    put_shared(out, near, far)


def turned(rows, raw, put):
    count, columns, width = rows.shape
    raw[0, : count * columns] = rows[:, :, :128].astype(F32).reshape(count * columns, 128)
    rest = rows[:, :, 128:].astype(F32).reshape(count * columns, width - 128)
    raw[1, : count * columns] = jnp.concatenate([rest, jnp.zeros((count * columns, 256 - width), F32)], 1)
    for c in range(columns):
        put(c, jnp.concatenate([raw[i, pl.ds(c, FACE, stride=columns), :] for i in range(2)], 1))


def weight_kernel(
    inverse, couplings, right, initial_there, neighbours_there,
    known, lower, base, own, gathers,
    inverse_in, couplings_in, right_in, initial, neighbours, solves, faces, raw, done,
):
    planes, columns, rhs, width = initial.shape
    size = columns * rhs
    half = columns // 2
    early = [
        pltpu.make_async_copy(neighbours_there, neighbours, done.at[3, 0]),
        pltpu.make_async_copy(initial_there, initial, done.at[3, 1]),
    ]
    copies = []
    for p in range(planes):
        pairs = ((inverse, inverse_in), (couplings, couplings_in), (right, right_in))
        copies.append([pltpu.make_async_copy(x.at[p], y.at[p], done.at[i, p]) for i, (x, y) in enumerate(pairs)])
    for copy in copies[0] + early:
        copy.start()
    for start, stop in ((5 * FACE, 256), (256 + FACE, 256 + 2 * SLOT)):
        faces[:, :, start:stop] = jnp.zeros((2, columns, stop - start, 256), BF)
    raw[:, :, :, NT * columns :] = jnp.zeros((2, 9, 2, (FACE - NT) * columns, 128), F32)
    for copy in early:
        copy.wait()
    for copy in sum(copies[1:2], []):
        copy.start()
    source = sources(neighbours, columns, rhs)
    for i, start in enumerate((0, size)):
        for j in range(2):
            gathers[i, j] = one_hot(source[j], start, size)
    own_table = [picks(c_target(rows_of(FACE), which), width) for which in (2, 0)]
    first_table = picks(first_target(rows_of(FACE)), width)
    fields = [initial[p].reshape(size, width) for p in range(planes)]
    for j in range(2):
        mine = jnp.concatenate([mt(own_table[j], x).astype(BF) for x in fields], 0)
        mine = mm(mine, gathers[1 - j, j]).astype(BF)
        for p in range(planes):
            own[p, j * FACE : (j + 1) * FACE] = mine[p * FACE : (p + 1) * FACE]
    for p in range(planes):
        own[p, LAST] = mt(first_table, fields[min(p + 1, planes - 1)]).astype(BF)
    lane = lax.broadcasted_iota(jnp.int32, (ROWS, 2 * SLOT), 1)

    for p in range(planes):
        slot = p % 2
        for copy in copies[p]:
            copy.wait()
        for copy in sum(copies[p + 2 : p + 3], []):
            copy.start()
        faces[slot, :, 256 + SLOT : 256 + SLOT + rhs, :width] = right_in[p]
        for a in range(3):
            rows = [inverse_in[p, v * 27 + a * 9 : v * 27 + a * 9 + 9] for v in range(5)]

            def put(c, value):
                solves[slot, c, a * FACE : (a + 1) * FACE] = (-value).astype(BF)

            turned(jnp.concatenate(rows, 0), raw.at[slot, a], put)
        for f, place in enumerate((256, 4 * FACE, 0, FACE, 2 * FACE, 3 * FACE)):

            def put(c, value):
                faces[slot, c, place : place + FACE] = value.astype(BF)

            turned(couplings_in[p, f], raw.at[slot, 3 + f], put)
        bases, lowers = [], []
        before = None
        for c in range(columns):
            solve = solves[slot, c]
            known[p, c] = mt(solve, faces[slot, c, :256]).astype(BF)
            both = mt(solve, faces[slot, c, 256:])
            move = (c % half * rhs - SLOT) % 128
            bases.append(pltpu.roll(both, move, 1) if move else both)
            if c % 2 == 0:
                before = both
            else:
                lowers.append(jnp.where(lane < SLOT, before, pltpu.roll(both, SLOT, 1)).astype(BF))
        for h in range(2):
            lanes = slice(h * half * rhs, (h + 1) * half * rhs)
            lower[p, h, :ROWS] = jnp.concatenate(lowers[2 * h : 2 * h + 2], 1)
            base[p, :, lanes] = -own_lanes(bases[h * half : (h + 1) * half], rhs)
    chain_products(lower, LAST, range(planes))


def chain_products(matrix, rows, order):
    for h in range(2):
        total = None
        for q in order:
            step = matrix[q, h, rows]
            total = step.astype(F32) if total is None else mm(step, split_lanes(total, SLOT))
            matrix[q, h, PRODUCT] = total.astype(BF)


def gathered(near, far, own, up_sel, down_sel, gathers):
    planes = up_sel.shape[0]

    def faces(received, select):
        tail = received[planes * MAIN :]
        wholes = [jnp.concatenate([received[p * MAIN : (p + 1) * MAIN], tail], 0) for p in range(planes)]
        return [mm(select[p], wholes[p]).astype(BF) for p in range(planes)]

    low = faces(jnp.where(even(), far[...], near[...]), up_sel)
    high = faces(jnp.where(even(), near[...], far[...]), down_sel)
    sides = []
    for j, side in enumerate((low, high)):
        picked = mm(jnp.concatenate([x[FACE:] for x in side], 0), gathers[j, j]).astype(BF)
        sides.append([picked[p * FACE : (p + 1) * FACE] + own[p, j * FACE : (j + 1) * FACE] for p in range(planes)])
    return [jnp.concatenate([low[p][:FACE], high[p][:FACE], sides[0][p], sides[1][p]], 0) for p in range(planes)]


def known_part(known_c, operand, columns, rhs):
    half = columns // 2
    out = []
    for h in range(2):
        side = operand[:, h * half * rhs : (h + 1) * half * rhs]
        out.append(own_lanes([mm(known_c(h * half + c), side) for c in range(half)], rhs))
    return jnp.concatenate(out, 1)


def chain_kernel(known, base, matrix, wholes, outs, order, rows, rhs, last_face):
    part, traces, message = outs
    planes, columns = known.shape[:2]
    trace = None
    for p in order:
        whole = jnp.concatenate([wholes[p], last_face(p)], 0)
        value = base[p] + known_part(lambda c: known[p, c], whole, columns, rhs)
        part[p] = value
        value = value[rows]
        trace = value if trace is None else value + chain_step(matrix.at[p], trace, rhs, rows)
        traces[p] = trace
    message[FIRST] = trace.astype(BF)
    if message.shape[0] > FACE:
        for h in range(2):
            message[(1 + h) * FACE : (2 + h) * FACE] = matrix[order[-1], h, PRODUCT]


def forward_chain_kernel(near, far, above, own, gathers, up_sel, down_sel, known, lower, base, *outs, rhs):
    wholes = gathered(near, far, own, up_sel, down_sel, gathers)
    planes, size = len(wholes), above.shape[1]
    pad = jnp.zeros((256 - 5 * FACE, size), BF)
    last_face = lambda p: jnp.concatenate([own[p, LAST] if p + 1 < planes else above[...], pad], 0)
    chain_kernel(known, base, lower, wholes, outs, range(planes), LAST, rhs, last_face)


def backward_chain_kernel(near, far, own, gathers, up_sel, down_sel, known, upper, base, *outs, rhs):
    wholes = gathered(near, far, own, up_sel, down_sel, gathers)
    last_face = lambda p: jnp.zeros((256 - 4 * FACE, near.shape[1]), BF)
    chain_kernel(known, base, upper, wholes, outs, range(len(wholes) - 1, -1, -1), FIRST, rhs, last_face)


def incoming(messages, products, forward, rhs):
    here = lax.axis_index("sweep")
    n = messages.shape[0]
    trace = None
    for i in range(n - 1) if forward else range(n - 1, 0, -1):
        value = messages[i, FIRST].astype(F32)
        if trace is None:
            trace = jnp.zeros_like(value)
        else:
            half = value.shape[1] // 2
            halves = [trace[:, h * half : (h + 1) * half] for h in range(2)]
            value = value + jnp.concatenate([mm(m, split_lanes(t, rhs)) for m, t in zip(products(i), halves)], 1)
        trace = jnp.where(i < here if forward else i > here, value, trace)
    return trace


def forward_finish_kernel(
    messages, part, traces, lower, send, middle, change, near, far, *, rhs
):
    planes = part.shape[0]
    inside = lambda i: [messages[i, (1 + h) * FACE : (2 + h) * FACE] for h in range(2)]
    entry = incoming(messages, inside, True, rhs)
    out = []
    trace = entry
    for p in range(planes):
        delta = chain_step(lower.at[p], trace, rhs, FULL)
        change[p] = delta
        whole = (part[p] + delta).astype(BF)
        middle[p] = whole
        out.append(mm(send[p], whole))
        if p + 1 < planes:
            trace = traces[p] + chain_step(lower.at[p], entry, rhs, PRODUCT)
    put_shared(out, near, far)


def middle_kernel(middle, change, base, gathers, own_sel, known, own, out, upper):
    planes = middle.shape[0]
    mine = [mm(own_sel[...], middle[p]).astype(BF) for p in range(planes)]
    for j in range(2):
        side = jnp.concatenate([x[j * FACE : (j + 1) * FACE] for x in mine], 0)
        side = mm(side, gathers[1 - j, j]).astype(BF)
        for p in range(planes):
            own[p, j * FACE : (j + 1) * FACE] = side[p * FACE : (p + 1) * FACE]
    for p in range(planes):
        out[p] = base[p] + change[p]
    columns = known.shape[1]
    lane = lax.broadcasted_iota(jnp.int32, (ROWS, 2 * SLOT), 1)
    for p in range(planes):
        pairs = []
        for c in range(0, columns, 2):
            one, two = (known[p, c + i, :, 128:].astype(F32) for i in range(2))
            pairs.append(jnp.where(lane < SLOT, pltpu.roll(one, SLOT, 1), two).astype(BF))
        for h in range(2):
            upper[p, h, :ROWS] = jnp.concatenate(pairs[2 * h : 2 * h + 2], 1)
    chain_products(upper, FIRST, range(planes - 1, -1, -1))


def backward_finish_kernel(
    messages, near, next_near, part, traces, upper, back, result, results, sem, *, rhs
):
    planes = part.shape[0]
    here = lax.axis_index("sweep")
    beside = lambda i: [jnp.where(here + 1 == i, near[h], next_near[h]) for h in range(2)]
    entry = incoming(messages, beside, False, rhs)
    columns, _, width = result.shape[1:]
    copies = []
    trace = entry
    for p in range(planes - 1, -1, -1):
        whole = part[p] + chain_step(upper.at[p], trace, rhs, FULL)
        flat = lax.dot_general(whole.astype(BF), back[...], (((0,), (0,)), ((), ())), preferred_element_type=F32)
        results[p] = flat.astype(BF).reshape(columns, rhs, width)
        copies.append(pltpu.make_async_copy(results.at[p], result.at[p], sem.at[p]))
        copies[-1].start()
        if p:
            trace = traces[p] + chain_step(upper.at[p], entry, rhs, PRODUCT)
    for copy in copies:
        copy.wait()


def call(kernel, outs, operands, name, flops=2e8, far=(), scratch=(), out_space=pltpu.VMEM):
    shapes = [jax.ShapeDtypeStruct(s, d) for s, d in outs]
    nbytes = sum(x.size * x.dtype.itemsize for x in list(operands) + shapes)
    spaces = [pltpu.SMEM if x.dtype == jnp.int32 else pltpu.VMEM for x in operands]
    spaces = [pltpu.HBM if i in far else space for i, space in enumerate(spaces)]
    operands = [
        pltpu.with_memory_space_constraint(x, pltpu.HBM) if i in far else x for i, x in enumerate(operands)
    ]
    return pl.pallas_call(
        kernel,
        out_shape=shapes,
        in_specs=[pl.BlockSpec(memory_space=space) for space in spaces],
        out_specs=[pl.BlockSpec(memory_space=out_space)] * len(shapes),
        scratch_shapes=list(scratch),
        compiler_params=pltpu.CompilerParams(vmem_limit_bytes=24 * MIB),
        cost_estimate=pl.CostEstimate(flops=int(flops), bytes_accessed=int(nbytes), transcendentals=0),
        name=name,
    )(*operands)


def products(x, by):
    n = lax.axis_size("sweep")
    inner = range(1, n - 1)
    return [
        lax.ppermute(x, "sweep", [(i, i + step) for i in inner if 0 <= i + step < n]) for step in (by, 2 * by)
    ]


def weights(inverse, couplings, right, initial, neighbours):
    planes, columns, rhs, width = initial.shape
    size = columns * rhs
    pack = (planes, 2, ROWS + FACE, 256)
    field = (planes, ROWS, size)
    outs = [((planes, columns, ROWS, 256), BF), (pack, BF), (field, F32), (field, BF), ((2, 2, size, size), BF)]
    operands = (inverse, couplings, right, initial, neighbours)
    scratch = [pltpu.VMEM(x.shape, BF) for x in operands[:4]] + [
        pltpu.SMEM(neighbours.shape, jnp.int32),
        pltpu.VMEM((2, columns, ROWS, 256), BF),
        pltpu.VMEM((2, columns, 256 + 2 * SLOT, 256), BF),
        pltpu.VMEM((2, 9, 2, FACE * columns, 128), F32),
        pltpu.SemaphoreType.DMA((4, planes)),
    ]
    return call(weight_kernel, outs, operands, "weights", 1e10, (0, 1, 2, 3, 4), scratch)


def swapped(x, axis, first):
    n = lax.axis_size(axis)
    pairs = [(i, (i + 1) % n) for i in range(first, n, 2)]
    return lax.ppermute(x, axis, [pair for i, j in pairs for pair in ((i, j), (j, i))])


def shift(x, axis, by):
    n = lax.axis_size(axis)
    return lax.ppermute(x, axis, [(i, i + by) for i in range(n) if 0 <= i + by < n])


def local(right_sides, initial, inverse_blocks, couplings, neighbours):
    planes, columns, rhs, width = initial.shape
    size = columns * rhs
    const = lambda x: jnp.asarray(x, BF)
    send_in = const(send_table(ROWS, inner, planes))
    own_in = const(own_table(ROWS, inner))
    back = const(table(ROWS, width, [(inner(*n), n) for n in NODES], natural))
    up_sel = const(receive_table(2, planes))
    down_sel = const(receive_table(0, planes))
    beside = neighbours.T

    share = (planes * MAIN + tail_rows(planes), size)
    near, far, above = call(
        first_kernel,
        [(share, BF), (share, BF), ((FACE, size), BF)],
        (initial,),
        "initial_traces",
    )
    near, far, above, initial = lax.optimization_barrier((near, far, above, initial))
    near, far = swapped(near, "cross", 0), swapped(far, "cross", 1)
    from_above = shift(above, "sweep", -1)
    known, lower, base, own, gathers = weights(
        inverse_blocks.transpose(0, 2, 1, 3), couplings.transpose(0, 2, 3, 1, 4), right_sides, initial, beside
    )

    field = (planes, ROWS, size)
    trace = (planes, FACE, size)
    chain_outs = [(field, F32), (trace, F32)]
    part, traces, message = call(
        functools.partial(forward_chain_kernel, rhs=rhs),
        chain_outs + [((3 * FACE, size), BF)],
        (near, far, from_above, own, gathers, up_sel, down_sel, known, lower, base),
        "forward_chain",
    )
    messages = lax.all_gather(message, "sweep")
    middle, change, near, far = call(
        functools.partial(forward_finish_kernel, rhs=rhs),
        [(field, BF), (field, F32), (share, BF), (share, BF)],
        (messages, part, traces, lower, send_in),
        "forward_finish",
    )
    near, far = swapped(near, "cross", 0), swapped(far, "cross", 1)
    own, base, upper = call(
        middle_kernel,
        [((planes, 2 * FACE, size), BF), (field, F32), (lower.shape, BF)],
        (middle, change, base, gathers, own_in, known),
        "middle",
        2e9,
    )
    own, pass_b = lax.optimization_barrier((own, upper[0, :, PRODUCT]))
    passes = products(pass_b, -1)
    part, traces, message = call(
        functools.partial(backward_chain_kernel, rhs=rhs),
        chain_outs + [((FACE, size), BF)],
        (near, far, own, gathers, up_sel, down_sel, known, upper, base),
        "backward_chain",
    )
    messages = lax.all_gather(message, "sweep")
    (result,) = call(
        functools.partial(backward_finish_kernel, rhs=rhs),
        [(right_sides.shape, BF)],
        (messages, *passes, part, traces, upper, back),
        "backward_finish",
        scratch=[pltpu.VMEM(right_sides.shape, BF), pltpu.SemaphoreType.DMA((planes,))],
        out_space=pltpu.HBM,
    )
    return result


def solution(mesh):
    return jax.shard_map(
        local,
        mesh=mesh,
        in_specs=(
            P("sweep", "cross", None, None),
            P("sweep", "cross", None, None),
            P("sweep", "cross", None, None),
            P("sweep", "cross", None, None, None),
            P("cross", None),
        ),
        out_specs=P("sweep", "cross", None, None),
        check_vma=False,
    )
```

```python
import functools

import jax
import jax.numpy as jnp
import numpy as np
from jax import lax
from jax.experimental import pallas as pl
from jax.experimental.pallas import tpu as pltpu
from jax.sharding import PartitionSpec as P

BF = jnp.bfloat16
F32 = jnp.float32
NT = 45
FACE = 48
SLOT = 64
ROWS = 3 * FACE
SHARED = 75
MAIN = 64
MIB = 1 << 20
FIRST = slice(0, FACE)
LAST = slice(2 * FACE, ROWS)
FULL = slice(0, ROWS)
PRODUCT = slice(ROWS, ROWS + FACE)


def natural(v, a, b, c):
    return v * 27 + a * 9 + b * 3 + c


def inner(v, a, b, c):
    return a * FACE + v * 9 + b * 3 + c


NODES = [(v, a, b, c) for v in range(5) for a in range(3) for b in range(3) for c in range(3)]


def face_nodes(place, which):
    return [n for n in NODES if n[1 + place] == which]


def table(height, width, rows, column_of):
    out = np.zeros((height, width), np.float32)
    for row, node in rows:
        out[row, column_of(*node)] = 1
    return out


def block(nodes, start=0):
    return [(start + i, n) for i, n in enumerate(nodes)]


def tail_rows(planes):
    return -(-planes * (SHARED - MAIN) // 16) * 16


def union_nodes(which):
    others = [b for b in range(3) if b != which]
    spots = [(which, c) for c in range(3)] + [(b, which) for b in others]
    return [(v, a, b, c) for v in range(5) for a in range(3) for b, c in spots]


def place_of(i, plane):
    return i if i < MAIN else i + plane * (SHARED - MAIN)


def send_table(width, column_of, planes):
    height = MAIN + tail_rows(planes)
    out = []
    for p in range(planes):
        rows = [(place_of(i, p), n) for i, n in enumerate(union_nodes(2))]
        rows += [(height + place_of(i, p), n) for i, n in enumerate(union_nodes(0))]
        out.append(table(2 * height, width, rows, column_of))
    return np.stack(out)


def own_table(width, column_of):
    rows = block(face_nodes(2, 2)) + block(face_nodes(2, 0), FACE)
    return table(2 * FACE, width, rows, column_of)


def receive_table(which, planes):
    rows = block(face_nodes(1, which)) + block(face_nodes(2, which), FACE)
    out = []
    for p in range(planes):
        place = {n: place_of(i, p) for i, n in enumerate(union_nodes(which))}
        out.append(table(2 * FACE, MAIN + tail_rows(planes), rows, lambda *n: place[n]))
    return np.stack(out)


def mm(a, b):
    return lax.dot_general(a, b, (((1,), (0,)), ((), ())), preferred_element_type=F32)


def mt(a, b):
    return lax.dot_general(a, b, (((1,), (1,)), ((), ())), preferred_element_type=F32)


def group(shape, width, at):
    lane = lax.broadcasted_iota(jnp.int32, shape, 1)
    return (lane >= at * width) & (lane < (at + 1) * width)


def split_lanes(value, width):
    lanes = value.shape[1]
    value = value.astype(F32)
    pad = jnp.zeros((SLOT - FACE, lanes), BF)
    parts = []
    for c in range(lanes // width):
        parts += [jnp.where(group(value.shape, width, c), value, 0.0).astype(BF), pad]
    return jnp.concatenate(parts, 0)


def own_lanes(values, width):
    out = values[0]
    for c in range(1, len(values)):
        out = jnp.where(group(out.shape, width, c), values[c], out)
    return out


def one_hot(source, start, height):
    row = lax.broadcasted_iota(jnp.int32, (height, source.shape[1]), 0) + start
    return jnp.where(row == source, 1.0, 0.0).astype(BF)


def chain_step(matrix, trace, rhs, rows=slice(None)):
    half = trace.shape[1] // 2
    return jnp.concatenate(
        [mm(matrix[h, rows], split_lanes(trace[:, h * half : (h + 1) * half], rhs)) for h in range(2)], 1
    )


def shared_target(row, which, plane, planes):
    rest = SHARED - MAIN
    i = jnp.where(row < MAIN, row, row - plane * rest)
    k = i % 15
    a = k // 5
    j = k % 5
    b = jnp.where(j < 3, which, j - 3 if which == 2 else j - 2)
    c = jnp.where(j < 3, j, which)
    inside = (row < MAIN) | ((i >= MAIN) & (i < SHARED))
    return jnp.where(inside, i // 15 * 27 + a * 9 + b * 3 + c, -1)


def picks(target, width):
    lane = lax.broadcasted_iota(jnp.int32, (target.shape[0], width), 1)
    return jnp.where(lane == target, 1.0, 0.0).astype(BF)


def rows_of(height):
    return lax.broadcasted_iota(jnp.int32, (height, 1), 0)


def first_target(row):
    return jnp.where(row < NT, row // 9 * 27 + row % 9, -1)


def c_target(row, which):
    return jnp.where(row < NT, row * 3 + which, -1)


def sources(neighbours, columns, rhs):
    place = lax.axis_index("cross")
    total = columns * lax.axis_size("cross")
    lane = lax.broadcasted_iota(jnp.int32, (1, columns * rhs), 1)
    out = []
    for face, first in ((2, place - 1), (3, place)):
        source = lane
        for c in range(columns):
            at = neighbours[face, c] - first * columns
            at = jnp.where(at < 0, at + total, at)
            at = jnp.where(at >= total, at - total, at)
            source = jnp.where(lane >= c * rhs, lane + (at - c) * rhs, source)
        out.append(source)
    return out


def even():
    return lax.rem(lax.axis_index("cross"), 2) == 0


def put_shared(out, near, far):
    height = out[0].shape[0] // 2
    messages = []
    for start in (0, height):
        tails = [x[start + MAIN : start + height] for x in out]
        parts = [x[start : start + MAIN] for x in out] + [sum(tails[1:], tails[0])]
        messages.append(jnp.concatenate(parts, 0))
    up, down = messages
    near[...] = jnp.where(even(), up, down).astype(BF)
    far[...] = jnp.where(even(), down, up).astype(BF)


def first_kernel(initial, near, far, above):
    planes, columns, rhs, width = initial.shape
    row = rows_of(MAIN + tail_rows(planes))
    out = []
    for p in range(planes):
        x = initial[p].reshape(columns * rhs, width)
        tables = [picks(shared_target(row, which, p, planes), width) for which in (2, 0)]
        out.append(mt(jnp.concatenate(tables, 0), x))
        if p == 0:
            above[...] = mt(picks(first_target(rows_of(FACE)), width), x).astype(BF)
    put_shared(out, near, far)


def turned(rows, raw, put):
    count, columns, width = rows.shape
    raw[0, : count * columns] = rows[:, :, :128].astype(F32).reshape(count * columns, 128)
    rest = rows[:, :, 128:].astype(F32).reshape(count * columns, width - 128)
    raw[1, : count * columns] = jnp.concatenate([rest, jnp.zeros((count * columns, 256 - width), F32)], 1)
    for c in range(columns):
        put(c, jnp.concatenate([raw[i, pl.ds(c, FACE, stride=columns), :] for i in range(2)], 1))


def weight_kernel(
    inverse, couplings, right, initial_there, neighbours_there,
    known, lower, base, own, gathers,
    inverse_in, couplings_in, right_in, initial, neighbours, solves, faces, raw, done,
):
    planes, columns, rhs, width = initial.shape
    size = columns * rhs
    half = columns // 2
    early = [
        pltpu.make_async_copy(neighbours_there, neighbours, done.at[3, 0]),
        pltpu.make_async_copy(initial_there, initial, done.at[3, 1]),
    ]
    copies = []
    for p in range(planes):
        pairs = ((inverse, inverse_in), (couplings, couplings_in), (right, right_in))
        copies.append([pltpu.make_async_copy(x.at[p], y.at[p], done.at[i, p]) for i, (x, y) in enumerate(pairs)])
    for copy in early + sum(copies, []):
        copy.start()
    for start, stop in ((5 * FACE, 256), (256 + FACE, 256 + 2 * SLOT)):
        faces[:, :, start:stop] = jnp.zeros((2, columns, stop - start, 256), BF)
    raw[:, :, :, NT * columns :] = jnp.zeros((2, 9, 2, (FACE - NT) * columns, 128), F32)
    for copy in early:
        copy.wait()
    source = sources(neighbours, columns, rhs)
    for i, start in enumerate((0, size)):
        for j in range(2):
            gathers[i, j] = one_hot(source[j], start, size)
    own_table = [picks(c_target(rows_of(FACE), which), width) for which in (2, 0)]
    first_table = picks(first_target(rows_of(FACE)), width)
    fields = [initial[p].reshape(size, width) for p in range(planes)]
    for j in range(2):
        mine = jnp.concatenate([mt(own_table[j], x).astype(BF) for x in fields], 0)
        mine = mm(mine, gathers[1 - j, j]).astype(BF)
        for p in range(planes):
            own[p, j * FACE : (j + 1) * FACE] = mine[p * FACE : (p + 1) * FACE]
    for p in range(planes):
        own[p, LAST] = mt(first_table, fields[min(p + 1, planes - 1)]).astype(BF)
    lane = lax.broadcasted_iota(jnp.int32, (ROWS, 2 * SLOT), 1)

    def prepare(p):
        slot = p % 2
        for copy in copies[p]:
            copy.wait()
        faces[slot, :, 256 + SLOT : 256 + SLOT + rhs, :width] = right_in[p]
        for a in range(3):
            rows = [inverse_in[p, v * 27 + a * 9 : v * 27 + a * 9 + 9] for v in range(5)]

            def put(c, value):
                solves[slot, c, a * FACE : (a + 1) * FACE] = (-value).astype(BF)

            turned(jnp.concatenate(rows, 0), raw.at[slot, a], put)
        for f, place in enumerate((256, 4 * FACE, 0, FACE, 2 * FACE, 3 * FACE)):

            def put(c, value):
                faces[slot, c, place : place + FACE] = value.astype(BF)

            turned(couplings_in[p, f], raw.at[slot, 3 + f], put)

    prepare(0)
    for p in range(planes):
        slot = p % 2
        if p + 1 < planes:
            prepare(p + 1)
        bases, lowers = [], []
        before = None
        for c in range(columns):
            solve = solves[slot, c]
            known[p, c] = mt(solve, faces[slot, c, :256]).astype(BF)
            both = mt(solve, faces[slot, c, 256:])
            move = (c % half * rhs - SLOT) % 128
            bases.append(pltpu.roll(both, move, 1) if move else both)
            if c % 2 == 0:
                before = both
            else:
                lowers.append(jnp.where(lane < SLOT, before, pltpu.roll(both, SLOT, 1)).astype(BF))
        for h in range(2):
            lanes = slice(h * half * rhs, (h + 1) * half * rhs)
            lower[p, h, :ROWS] = jnp.concatenate(lowers[2 * h : 2 * h + 2], 1)
            base[p, :, lanes] = -own_lanes(bases[h * half : (h + 1) * half], rhs)
    chain_products(lower, LAST, range(planes))


def chain_products(matrix, rows, order):
    for h in range(2):
        total = None
        for q in order:
            step = matrix[q, h, rows]
            total = step.astype(F32) if total is None else mm(step, split_lanes(total, SLOT))
            matrix[q, h, PRODUCT] = total.astype(BF)


def gathered(near, far, own, up_sel, down_sel, gathers):
    planes = up_sel.shape[0]

    def faces(received, select):
        tail = received[planes * MAIN :]
        wholes = [jnp.concatenate([received[p * MAIN : (p + 1) * MAIN], tail], 0) for p in range(planes)]
        return [mm(select[p], wholes[p]).astype(BF) for p in range(planes)]

    low = faces(jnp.where(even(), far[...], near[...]), up_sel)
    high = faces(jnp.where(even(), near[...], far[...]), down_sel)
    sides = []
    for j, side in enumerate((low, high)):
        picked = mm(jnp.concatenate([x[FACE:] for x in side], 0), gathers[j, j]).astype(BF)
        sides.append([picked[p * FACE : (p + 1) * FACE] + own[p, j * FACE : (j + 1) * FACE] for p in range(planes)])
    return [jnp.concatenate([low[p][:FACE], high[p][:FACE], sides[0][p], sides[1][p]], 0) for p in range(planes)]


def known_part(known_c, operand, columns, rhs):
    half = columns // 2
    out = []
    for h in range(2):
        side = operand[:, h * half * rhs : (h + 1) * half * rhs]
        out.append(own_lanes([mm(known_c(h * half + c), side) for c in range(half)], rhs))
    return jnp.concatenate(out, 1)


def chain_kernel(known, base, matrix, wholes, outs, order, rows, rhs, last_face):
    part, traces, message = outs
    planes, columns = known.shape[:2]
    trace = None
    for p in order:
        whole = jnp.concatenate([wholes[p], last_face(p)], 0)
        value = base[p] + known_part(lambda c: known[p, c], whole, columns, rhs)
        part[p] = value
        value = value[rows]
        trace = value if trace is None else value + chain_step(matrix.at[p], trace, rhs, rows)
        traces[p] = trace
    message[FIRST] = trace.astype(BF)
    if message.shape[0] > FACE:
        for h in range(2):
            message[(1 + h) * FACE : (2 + h) * FACE] = matrix[order[-1], h, PRODUCT]


def forward_chain_kernel(near, far, above, own, gathers, up_sel, down_sel, known, lower, base, *outs, rhs):
    wholes = gathered(near, far, own, up_sel, down_sel, gathers)
    planes, size = len(wholes), above.shape[1]
    pad = jnp.zeros((256 - 5 * FACE, size), BF)
    last_face = lambda p: jnp.concatenate([own[p, LAST] if p + 1 < planes else above[...], pad], 0)
    chain_kernel(known, base, lower, wholes, outs, range(planes), LAST, rhs, last_face)


def backward_chain_kernel(near, far, own, gathers, up_sel, down_sel, known, upper, base, *outs, rhs):
    wholes = gathered(near, far, own, up_sel, down_sel, gathers)
    last_face = lambda p: jnp.zeros((256 - 4 * FACE, near.shape[1]), BF)
    chain_kernel(known, base, upper, wholes, outs, range(len(wholes) - 1, -1, -1), FIRST, rhs, last_face)


def incoming(messages, products, forward, rhs):
    here = lax.axis_index("sweep")
    n = messages.shape[0]
    trace = None
    for i in range(n - 1) if forward else range(n - 1, 0, -1):
        value = messages[i, FIRST].astype(F32)
        if trace is None:
            trace = jnp.zeros_like(value)
        else:
            half = value.shape[1] // 2
            halves = [trace[:, h * half : (h + 1) * half] for h in range(2)]
            value = value + jnp.concatenate([mm(m, split_lanes(t, rhs)) for m, t in zip(products(i), halves)], 1)
        trace = jnp.where(i < here if forward else i > here, value, trace)
    return trace


def forward_finish_kernel(
    messages, part, traces, lower, send, middle, change, near, far, *, rhs
):
    planes = part.shape[0]
    inside = lambda i: [messages[i, (1 + h) * FACE : (2 + h) * FACE] for h in range(2)]
    entry = incoming(messages, inside, True, rhs)
    out = []
    trace = entry
    for p in range(planes):
        delta = chain_step(lower.at[p], trace, rhs, FULL)
        change[p] = delta
        whole = (part[p] + delta).astype(BF)
        middle[p] = whole
        out.append(mm(send[p], whole))
        if p + 1 < planes:
            trace = traces[p] + chain_step(lower.at[p], entry, rhs, PRODUCT)
    put_shared(out, near, far)


def middle_kernel(middle, change, base, gathers, own_sel, known, own, out, upper):
    planes = middle.shape[0]
    mine = [mm(own_sel[...], middle[p]).astype(BF) for p in range(planes)]
    for j in range(2):
        side = jnp.concatenate([x[j * FACE : (j + 1) * FACE] for x in mine], 0)
        side = mm(side, gathers[1 - j, j]).astype(BF)
        for p in range(planes):
            own[p, j * FACE : (j + 1) * FACE] = side[p * FACE : (p + 1) * FACE]
    for p in range(planes):
        out[p] = base[p] + change[p]
    columns = known.shape[1]
    lane = lax.broadcasted_iota(jnp.int32, (ROWS, 2 * SLOT), 1)
    for p in range(planes):
        pairs = []
        for c in range(0, columns, 2):
            one, two = (known[p, c + i, :, 128:].astype(F32) for i in range(2))
            pairs.append(jnp.where(lane < SLOT, pltpu.roll(one, SLOT, 1), two).astype(BF))
        for h in range(2):
            upper[p, h, :ROWS] = jnp.concatenate(pairs[2 * h : 2 * h + 2], 1)
    chain_products(upper, FIRST, range(planes - 1, -1, -1))


def backward_finish_kernel(
    messages, near, next_near, part, traces, upper, back, result, results, sem, *, rhs
):
    planes = part.shape[0]
    here = lax.axis_index("sweep")
    beside = lambda i: [jnp.where(here + 1 == i, near[h], next_near[h]) for h in range(2)]
    entry = incoming(messages, beside, False, rhs)
    columns, _, width = result.shape[1:]
    copies = []
    trace = entry
    for p in range(planes - 1, -1, -1):
        whole = part[p] + chain_step(upper.at[p], trace, rhs, FULL)
        flat = lax.dot_general(whole.astype(BF), back[...], (((0,), (0,)), ((), ())), preferred_element_type=F32)
        results[p] = flat.astype(BF).reshape(columns, rhs, width)
        copies.append(pltpu.make_async_copy(results.at[p], result.at[p], sem.at[p]))
        copies[-1].start()
        if p:
            trace = traces[p] + chain_step(upper.at[p], entry, rhs, PRODUCT)
    for copy in copies:
        copy.wait()


def call(kernel, outs, operands, name, flops=2e8, far=(), scratch=(), out_space=pltpu.VMEM):
    shapes = [jax.ShapeDtypeStruct(s, d) for s, d in outs]
    nbytes = sum(x.size * x.dtype.itemsize for x in list(operands) + shapes)
    spaces = [pltpu.SMEM if x.dtype == jnp.int32 else pltpu.VMEM for x in operands]
    spaces = [pltpu.HBM if i in far else space for i, space in enumerate(spaces)]
    operands = [
        pltpu.with_memory_space_constraint(x, pltpu.HBM) if i in far else x for i, x in enumerate(operands)
    ]
    return pl.pallas_call(
        kernel,
        out_shape=shapes,
        in_specs=[pl.BlockSpec(memory_space=space) for space in spaces],
        out_specs=[pl.BlockSpec(memory_space=out_space)] * len(shapes),
        scratch_shapes=list(scratch),
        compiler_params=pltpu.CompilerParams(vmem_limit_bytes=24 * MIB),
        cost_estimate=pl.CostEstimate(flops=int(flops), bytes_accessed=int(nbytes), transcendentals=0),
        name=name,
    )(*operands)


def products(x, by):
    n = lax.axis_size("sweep")
    inner = range(1, n - 1)
    return [
        lax.ppermute(x, "sweep", [(i, i + step) for i in inner if 0 <= i + step < n]) for step in (by, 2 * by)
    ]


def weights(inverse, couplings, right, initial, neighbours):
    planes, columns, rhs, width = initial.shape
    size = columns * rhs
    pack = (planes, 2, ROWS + FACE, 256)
    field = (planes, ROWS, size)
    outs = [((planes, columns, ROWS, 256), BF), (pack, BF), (field, F32), (field, BF), ((2, 2, size, size), BF)]
    operands = (inverse, couplings, right, initial, neighbours)
    scratch = [pltpu.VMEM(x.shape, BF) for x in operands[:4]] + [
        pltpu.SMEM(neighbours.shape, jnp.int32),
        pltpu.VMEM((2, columns, ROWS, 256), BF),
        pltpu.VMEM((2, columns, 256 + 2 * SLOT, 256), BF),
        pltpu.VMEM((2, 9, 2, FACE * columns, 128), F32),
        pltpu.SemaphoreType.DMA((4, planes)),
    ]
    return call(weight_kernel, outs, operands, "weights", 1e10, (0, 1, 2, 3, 4), scratch)


def swapped(x, axis, first):
    n = lax.axis_size(axis)
    pairs = [(i, (i + 1) % n) for i in range(first, n, 2)]
    return lax.ppermute(x, axis, [pair for i, j in pairs for pair in ((i, j), (j, i))])


def shift(x, axis, by):
    n = lax.axis_size(axis)
    return lax.ppermute(x, axis, [(i, i + by) for i in range(n) if 0 <= i + by < n])


def local(right_sides, initial, inverse_blocks, couplings, neighbours):
    planes, columns, rhs, width = initial.shape
    size = columns * rhs
    const = lambda x: jnp.asarray(x, BF)
    send_in = const(send_table(ROWS, inner, planes))
    own_in = const(own_table(ROWS, inner))
    back = const(table(ROWS, width, [(inner(*n), n) for n in NODES], natural))
    up_sel = const(receive_table(2, planes))
    down_sel = const(receive_table(0, planes))
    beside = neighbours.T

    share = (planes * MAIN + tail_rows(planes), size)
    near, far, above = call(
        first_kernel,
        [(share, BF), (share, BF), ((FACE, size), BF)],
        (initial,),
        "initial_traces",
    )
    near, far, above, initial = lax.optimization_barrier((near, far, above, initial))
    near, far = swapped(near, "cross", 0), swapped(far, "cross", 1)
    from_above = shift(above, "sweep", -1)
    known, lower, base, own, gathers = weights(
        inverse_blocks.transpose(0, 2, 1, 3), couplings.transpose(0, 2, 3, 1, 4), right_sides, initial, beside
    )

    field = (planes, ROWS, size)
    trace = (planes, FACE, size)
    chain_outs = [(field, F32), (trace, F32)]
    part, traces, message = call(
        functools.partial(forward_chain_kernel, rhs=rhs),
        chain_outs + [((3 * FACE, size), BF)],
        (near, far, from_above, own, gathers, up_sel, down_sel, known, lower, base),
        "forward_chain",
    )
    messages = lax.all_gather(message, "sweep")
    middle, change, near, far = call(
        functools.partial(forward_finish_kernel, rhs=rhs),
        [(field, BF), (field, F32), (share, BF), (share, BF)],
        (messages, part, traces, lower, send_in),
        "forward_finish",
    )
    near, far = swapped(near, "cross", 0), swapped(far, "cross", 1)
    own, base, upper = call(
        middle_kernel,
        [((planes, 2 * FACE, size), BF), (field, F32), (lower.shape, BF)],
        (middle, change, base, gathers, own_in, known),
        "middle",
        2e9,
    )
    own, pass_b = lax.optimization_barrier((own, upper[0, :, PRODUCT]))
    passes = products(pass_b, -1)
    part, traces, message = call(
        functools.partial(backward_chain_kernel, rhs=rhs),
        chain_outs + [((FACE, size), BF)],
        (near, far, own, gathers, up_sel, down_sel, known, upper, base),
        "backward_chain",
    )
    messages = lax.all_gather(message, "sweep")
    (result,) = call(
        functools.partial(backward_finish_kernel, rhs=rhs),
        [(right_sides.shape, BF)],
        (messages, *passes, part, traces, upper, back),
        "backward_finish",
        scratch=[pltpu.VMEM(right_sides.shape, BF), pltpu.SemaphoreType.DMA((planes,))],
        out_space=pltpu.HBM,
    )
    return result


def solution(mesh):
    return jax.shard_map(
        local,
        mesh=mesh,
        in_specs=(
            P("sweep", "cross", None, None),
            P("sweep", "cross", None, None),
            P("sweep", "cross", None, None),
            P("sweep", "cross", None, None, None),
            P("cross", None),
        ),
        out_specs=P("sweep", "cross", None, None),
        check_vma=False,
    )
```

```python
import functools

import jax
import jax.numpy as jnp
import numpy as np
from jax import lax
from jax.experimental import pallas as pl
from jax.experimental.pallas import tpu as pltpu
from jax.sharding import PartitionSpec as P

BF = jnp.bfloat16
F32 = jnp.float32
NT = 45
FACE = 48
SLOT = 64
ROWS = 3 * FACE
SHARED = 75
MAIN = 64
MIB = 1 << 20
FIRST = slice(0, FACE)
LAST = slice(2 * FACE, ROWS)
FULL = slice(0, ROWS)
PRODUCT = slice(ROWS, ROWS + FACE)


def natural(v, a, b, c):
    return v * 27 + a * 9 + b * 3 + c


def inner(v, a, b, c):
    return a * FACE + v * 9 + b * 3 + c


NODES = [(v, a, b, c) for v in range(5) for a in range(3) for b in range(3) for c in range(3)]


def face_nodes(place, which):
    return [n for n in NODES if n[1 + place] == which]


def table(height, width, rows, column_of):
    out = np.zeros((height, width), np.float32)
    for row, node in rows:
        out[row, column_of(*node)] = 1
    return out


def block(nodes, start=0):
    return [(start + i, n) for i, n in enumerate(nodes)]


def tail_rows(planes):
    return -(-planes * (SHARED - MAIN) // 16) * 16


def union_nodes(which):
    others = [b for b in range(3) if b != which]
    spots = [(which, c) for c in range(3)] + [(b, which) for b in others]
    return [(v, a, b, c) for v in range(5) for a in range(3) for b, c in spots]


def place_of(i, plane):
    return i if i < MAIN else i + plane * (SHARED - MAIN)


def send_table(width, column_of, planes):
    height = MAIN + tail_rows(planes)
    out = []
    for p in range(planes):
        rows = [(place_of(i, p), n) for i, n in enumerate(union_nodes(2))]
        rows += [(height + place_of(i, p), n) for i, n in enumerate(union_nodes(0))]
        out.append(table(2 * height, width, rows, column_of))
    return np.stack(out)


def own_table(width, column_of):
    rows = block(face_nodes(2, 2)) + block(face_nodes(2, 0), FACE)
    return table(2 * FACE, width, rows, column_of)


def receive_table(which, planes):
    rows = block(face_nodes(1, which)) + block(face_nodes(2, which), FACE)
    out = []
    for p in range(planes):
        place = {n: place_of(i, p) for i, n in enumerate(union_nodes(which))}
        out.append(table(2 * FACE, MAIN + tail_rows(planes), rows, lambda *n: place[n]))
    return np.stack(out)


def mm(a, b):
    return lax.dot_general(a, b, (((1,), (0,)), ((), ())), preferred_element_type=F32)


def mt(a, b):
    return lax.dot_general(a, b, (((1,), (1,)), ((), ())), preferred_element_type=F32)


def group(shape, width, at):
    lane = lax.broadcasted_iota(jnp.int32, shape, 1)
    return (lane >= at * width) & (lane < (at + 1) * width)


def split_lanes(value, width):
    lanes = value.shape[1]
    value = value.astype(F32)
    pad = jnp.zeros((SLOT - FACE, lanes), BF)
    parts = []
    for c in range(lanes // width):
        parts += [jnp.where(group(value.shape, width, c), value, 0.0).astype(BF), pad]
    return jnp.concatenate(parts, 0)


def own_lanes(values, width):
    out = values[0]
    for c in range(1, len(values)):
        out = jnp.where(group(out.shape, width, c), values[c], out)
    return out


def one_hot(source, start, height):
    row = lax.broadcasted_iota(jnp.int32, (height, source.shape[1]), 0) + start
    return jnp.where(row == source, 1.0, 0.0).astype(BF)


def chain_step(matrix, trace, rhs, rows=slice(None)):
    half = trace.shape[1] // 2
    return jnp.concatenate(
        [mm(matrix[h, rows], split_lanes(trace[:, h * half : (h + 1) * half], rhs)) for h in range(2)], 1
    )


def shared_target(row, which, plane, planes):
    rest = SHARED - MAIN
    i = jnp.where(row < MAIN, row, row - plane * rest)
    k = i % 15
    a = k // 5
    j = k % 5
    b = jnp.where(j < 3, which, j - 3 if which == 2 else j - 2)
    c = jnp.where(j < 3, j, which)
    inside = (row < MAIN) | ((i >= MAIN) & (i < SHARED))
    return jnp.where(inside, i // 15 * 27 + a * 9 + b * 3 + c, -1)


def picks(target, width):
    lane = lax.broadcasted_iota(jnp.int32, (target.shape[0], width), 1)
    return jnp.where(lane == target, 1.0, 0.0).astype(BF)


def rows_of(height):
    return lax.broadcasted_iota(jnp.int32, (height, 1), 0)


def first_target(row):
    return jnp.where(row < NT, row // 9 * 27 + row % 9, -1)


def c_target(row, which):
    return jnp.where(row < NT, row * 3 + which, -1)


def sources(neighbours, columns, rhs):
    place = lax.axis_index("cross")
    total = columns * lax.axis_size("cross")
    lane = lax.broadcasted_iota(jnp.int32, (1, columns * rhs), 1)
    out = []
    for face, first in ((2, place - 1), (3, place)):
        source = lane
        for c in range(columns):
            at = neighbours[face, c] - first * columns
            at = jnp.where(at < 0, at + total, at)
            at = jnp.where(at >= total, at - total, at)
            source = jnp.where(lane >= c * rhs, lane + (at - c) * rhs, source)
        out.append(source)
    return out


def even():
    return lax.rem(lax.axis_index("cross"), 2) == 0


def put_shared(out, near, far):
    height = out[0].shape[0] // 2
    messages = []
    for start in (0, height):
        tails = [x[start + MAIN : start + height] for x in out]
        parts = [x[start : start + MAIN] for x in out] + [sum(tails[1:], tails[0])]
        messages.append(jnp.concatenate(parts, 0))
    up, down = messages
    near[...] = jnp.where(even(), up, down).astype(BF)
    far[...] = jnp.where(even(), down, up).astype(BF)


def first_kernel(initial, near, far, above):
    planes, columns, rhs, width = initial.shape
    row = rows_of(MAIN + tail_rows(planes))
    out = []
    for p in range(planes):
        x = initial[p].reshape(columns * rhs, width)
        tables = [picks(shared_target(row, which, p, planes), width) for which in (2, 0)]
        out.append(mt(jnp.concatenate(tables, 0), x))
        if p == 0:
            above[...] = mt(picks(first_target(rows_of(FACE)), width), x).astype(BF)
    put_shared(out, near, far)


def turned(rows, raw, put):
    count, columns, width = rows.shape
    raw[0, : count * columns] = rows[:, :, :128].astype(F32).reshape(count * columns, 128)
    rest = rows[:, :, 128:].astype(F32).reshape(count * columns, width - 128)
    raw[1, : count * columns] = jnp.concatenate([rest, jnp.zeros((count * columns, 256 - width), F32)], 1)
    for c in range(columns):
        put(c, jnp.concatenate([raw[i, pl.ds(c, FACE, stride=columns), :] for i in range(2)], 1))


def weight_kernel(
    inverse, couplings, right, initial_there, neighbours_there,
    known, lower, base, own, gathers,
    inverse_in, couplings_in, right_in, initial, neighbours, solves, faces, raw, done,
):
    planes, columns, rhs, width = initial.shape
    size = columns * rhs
    half = columns // 2
    early = [
        pltpu.make_async_copy(neighbours_there, neighbours, done.at[6, 0]),
        pltpu.make_async_copy(initial_there, initial, done.at[6, 1]),
    ]
    copies = []
    for p in range(planes):
        blocks = [(inverse, inverse_in, 0, 64), (inverse, inverse_in, 64, width - 64)]
        blocks += [(couplings, couplings_in, f, 2) for f in range(0, 6, 2)] + [(right, right_in, 0, columns)]
        copies.append(
            [
                pltpu.make_async_copy(x.at[p, pl.ds(start, count)], y.at[p, pl.ds(start, count)], done.at[i, p])
                for i, (x, y, start, count) in enumerate(blocks)
            ]
        )
    for copy in copies[0] + early + sum(copies[1:], []):
        copy.start()
    for start, stop in ((5 * FACE, 256), (256 + FACE, 256 + 2 * SLOT)):
        faces[:, :, start:stop] = jnp.zeros((2, columns, stop - start, 256), BF)
    raw[:, :, :, NT * columns :] = jnp.zeros((2, 9, 2, (FACE - NT) * columns, 128), F32)
    for copy in early:
        copy.wait()
    source = sources(neighbours, columns, rhs)
    for i, start in enumerate((0, size)):
        for j in range(2):
            gathers[i, j] = one_hot(source[j], start, size)
    own_table = [picks(c_target(rows_of(FACE), which), width) for which in (2, 0)]
    first_table = picks(first_target(rows_of(FACE)), width)
    fields = [initial[p].reshape(size, width) for p in range(planes)]
    for j in range(2):
        mine = jnp.concatenate([mt(own_table[j], x).astype(BF) for x in fields], 0)
        mine = mm(mine, gathers[1 - j, j]).astype(BF)
        for p in range(planes):
            own[p, j * FACE : (j + 1) * FACE] = mine[p * FACE : (p + 1) * FACE]
    for p in range(planes):
        own[p, LAST] = mt(first_table, fields[min(p + 1, planes - 1)]).astype(BF)
    lane = lax.broadcasted_iota(jnp.int32, (ROWS, 2 * SLOT), 1)

    def prepare(p):
        slot = p % 2
        for copy in copies[p]:
            copy.wait()
        faces[slot, :, 256 + SLOT : 256 + SLOT + rhs, :width] = right_in[p]
        for a in range(3):
            rows = [inverse_in[p, v * 27 + a * 9 : v * 27 + a * 9 + 9] for v in range(5)]

            def put(c, value):
                solves[slot, c, a * FACE : (a + 1) * FACE] = (-value).astype(BF)

            turned(jnp.concatenate(rows, 0), raw.at[slot, a], put)
        for f, place in enumerate((256, 4 * FACE, 0, FACE, 2 * FACE, 3 * FACE)):

            def put(c, value):
                faces[slot, c, place : place + FACE] = value.astype(BF)

            turned(couplings_in[p, f], raw.at[slot, 3 + f], put)

    for p in range(planes):
        slot = p % 2
        prepare(p)
        bases, lowers = [], []
        before = None
        for c in range(columns):
            solve = solves[slot, c]
            known[p, c] = mt(solve, faces[slot, c, :256]).astype(BF)
            both = mt(solve, faces[slot, c, 256:])
            move = (c % half * rhs - SLOT) % 128
            bases.append(pltpu.roll(both, move, 1) if move else both)
            if c % 2 == 0:
                before = both
            else:
                lowers.append(jnp.where(lane < SLOT, before, pltpu.roll(both, SLOT, 1)).astype(BF))
        for h in range(2):
            lanes = slice(h * half * rhs, (h + 1) * half * rhs)
            lower[p, h, :ROWS] = jnp.concatenate(lowers[2 * h : 2 * h + 2], 1)
            base[p, :, lanes] = -own_lanes(bases[h * half : (h + 1) * half], rhs)
    chain_products(lower, LAST, range(planes))


def chain_products(matrix, rows, order):
    for h in range(2):
        total = None
        for q in order:
            step = matrix[q, h, rows]
            total = step.astype(F32) if total is None else mm(step, split_lanes(total, SLOT))
            matrix[q, h, PRODUCT] = total.astype(BF)


def gathered(near, far, own, up_sel, down_sel, gathers):
    planes = up_sel.shape[0]

    def faces(received, select):
        tail = received[planes * MAIN :]
        wholes = [jnp.concatenate([received[p * MAIN : (p + 1) * MAIN], tail], 0) for p in range(planes)]
        return [mm(select[p], wholes[p]).astype(BF) for p in range(planes)]

    low = faces(jnp.where(even(), far[...], near[...]), up_sel)
    high = faces(jnp.where(even(), near[...], far[...]), down_sel)
    sides = []
    for j, side in enumerate((low, high)):
        picked = mm(jnp.concatenate([x[FACE:] for x in side], 0), gathers[j, j]).astype(BF)
        sides.append([picked[p * FACE : (p + 1) * FACE] + own[p, j * FACE : (j + 1) * FACE] for p in range(planes)])
    return [jnp.concatenate([low[p][:FACE], high[p][:FACE], sides[0][p], sides[1][p]], 0) for p in range(planes)]


def known_part(known_c, operand, columns, rhs):
    half = columns // 2
    out = []
    for h in range(2):
        side = operand[:, h * half * rhs : (h + 1) * half * rhs]
        out.append(own_lanes([mm(known_c(h * half + c), side) for c in range(half)], rhs))
    return jnp.concatenate(out, 1)


def chain_kernel(known, base, matrix, wholes, outs, order, rows, rhs, last_face):
    part, traces, message = outs
    planes, columns = known.shape[:2]
    trace = None
    for p in order:
        whole = jnp.concatenate([wholes[p], last_face(p)], 0)
        value = base[p] + known_part(lambda c: known[p, c], whole, columns, rhs)
        part[p] = value
        value = value[rows]
        trace = value if trace is None else value + chain_step(matrix.at[p], trace, rhs, rows)
        traces[p] = trace
    message[FIRST] = trace.astype(BF)
    if message.shape[0] > FACE:
        for h in range(2):
            message[(1 + h) * FACE : (2 + h) * FACE] = matrix[order[-1], h, PRODUCT]


def forward_chain_kernel(near, far, above, own, gathers, up_sel, down_sel, known, lower, base, *outs, rhs):
    wholes = gathered(near, far, own, up_sel, down_sel, gathers)
    planes, size = len(wholes), above.shape[1]
    pad = jnp.zeros((256 - 5 * FACE, size), BF)
    last_face = lambda p: jnp.concatenate([own[p, LAST] if p + 1 < planes else above[...], pad], 0)
    chain_kernel(known, base, lower, wholes, outs, range(planes), LAST, rhs, last_face)


def backward_chain_kernel(near, far, own, gathers, up_sel, down_sel, known, upper, base, *outs, rhs):
    wholes = gathered(near, far, own, up_sel, down_sel, gathers)
    last_face = lambda p: jnp.zeros((256 - 4 * FACE, near.shape[1]), BF)
    chain_kernel(known, base, upper, wholes, outs, range(len(wholes) - 1, -1, -1), FIRST, rhs, last_face)


def incoming(messages, products, forward, rhs):
    here = lax.axis_index("sweep")
    n = messages.shape[0]
    trace = None
    for i in range(n - 1) if forward else range(n - 1, 0, -1):
        value = messages[i, FIRST].astype(F32)
        if trace is None:
            trace = jnp.zeros_like(value)
        else:
            half = value.shape[1] // 2
            halves = [trace[:, h * half : (h + 1) * half] for h in range(2)]
            value = value + jnp.concatenate([mm(m, split_lanes(t, rhs)) for m, t in zip(products(i), halves)], 1)
        trace = jnp.where(i < here if forward else i > here, value, trace)
    return trace


def forward_finish_kernel(
    messages, part, traces, lower, send, middle, change, near, far, *, rhs
):
    planes = part.shape[0]
    inside = lambda i: [messages[i, (1 + h) * FACE : (2 + h) * FACE] for h in range(2)]
    entry = incoming(messages, inside, True, rhs)
    out = []
    trace = entry
    for p in range(planes):
        delta = chain_step(lower.at[p], trace, rhs, FULL)
        change[p] = delta
        whole = (part[p] + delta).astype(BF)
        middle[p] = whole
        out.append(mm(send[p], whole))
        if p + 1 < planes:
            trace = traces[p] + chain_step(lower.at[p], entry, rhs, PRODUCT)
    put_shared(out, near, far)


def middle_kernel(middle, change, base, gathers, own_sel, known, own, out, upper):
    planes = middle.shape[0]
    mine = [mm(own_sel[...], middle[p]).astype(BF) for p in range(planes)]
    for j in range(2):
        side = jnp.concatenate([x[j * FACE : (j + 1) * FACE] for x in mine], 0)
        side = mm(side, gathers[1 - j, j]).astype(BF)
        for p in range(planes):
            own[p, j * FACE : (j + 1) * FACE] = side[p * FACE : (p + 1) * FACE]
    for p in range(planes):
        out[p] = base[p] + change[p]
    columns = known.shape[1]
    lane = lax.broadcasted_iota(jnp.int32, (ROWS, 2 * SLOT), 1)
    for p in range(planes):
        pairs = []
        for c in range(0, columns, 2):
            one, two = (known[p, c + i, :, 128:].astype(F32) for i in range(2))
            pairs.append(jnp.where(lane < SLOT, pltpu.roll(one, SLOT, 1), two).astype(BF))
        for h in range(2):
            upper[p, h, :ROWS] = jnp.concatenate(pairs[2 * h : 2 * h + 2], 1)
    chain_products(upper, FIRST, range(planes - 1, -1, -1))


def backward_finish_kernel(
    messages, near, next_near, part, traces, upper, back, result, results, sem, *, rhs
):
    planes = part.shape[0]
    here = lax.axis_index("sweep")
    beside = lambda i: [jnp.where(here + 1 == i, near[h], next_near[h]) for h in range(2)]
    entry = incoming(messages, beside, False, rhs)
    columns, _, width = result.shape[1:]
    copies = []
    trace = entry
    for p in range(planes - 1, -1, -1):
        whole = part[p] + chain_step(upper.at[p], trace, rhs, FULL)
        flat = lax.dot_general(whole.astype(BF), back[...], (((0,), (0,)), ((), ())), preferred_element_type=F32)
        results[p] = flat.astype(BF).reshape(columns, rhs, width)
        copies.append(pltpu.make_async_copy(results.at[p], result.at[p], sem.at[p]))
        copies[-1].start()
        if p:
            trace = traces[p] + chain_step(upper.at[p], entry, rhs, PRODUCT)
    for copy in copies:
        copy.wait()


def call(kernel, outs, operands, name, flops=2e8, far=(), scratch=(), out_space=pltpu.VMEM):
    shapes = [jax.ShapeDtypeStruct(s, d) for s, d in outs]
    nbytes = sum(x.size * x.dtype.itemsize for x in list(operands) + shapes)
    spaces = [pltpu.SMEM if x.dtype == jnp.int32 else pltpu.VMEM for x in operands]
    spaces = [pltpu.HBM if i in far else space for i, space in enumerate(spaces)]
    operands = [
        pltpu.with_memory_space_constraint(x, pltpu.HBM) if i in far else x for i, x in enumerate(operands)
    ]
    return pl.pallas_call(
        kernel,
        out_shape=shapes,
        in_specs=[pl.BlockSpec(memory_space=space) for space in spaces],
        out_specs=[pl.BlockSpec(memory_space=out_space)] * len(shapes),
        scratch_shapes=list(scratch),
        compiler_params=pltpu.CompilerParams(vmem_limit_bytes=24 * MIB),
        cost_estimate=pl.CostEstimate(flops=int(flops), bytes_accessed=int(nbytes), transcendentals=0),
        name=name,
    )(*operands)


def products(x, by):
    n = lax.axis_size("sweep")
    inner = range(1, n - 1)
    return [
        lax.ppermute(x, "sweep", [(i, i + step) for i in inner if 0 <= i + step < n]) for step in (by, 2 * by)
    ]


def weights(inverse, couplings, right, initial, neighbours):
    planes, columns, rhs, width = initial.shape
    size = columns * rhs
    pack = (planes, 2, ROWS + FACE, 256)
    field = (planes, ROWS, size)
    outs = [((planes, columns, ROWS, 256), BF), (pack, BF), (field, F32), (field, BF), ((2, 2, size, size), BF)]
    operands = (inverse, couplings, right, initial, neighbours)
    scratch = [pltpu.VMEM(x.shape, BF) for x in operands[:4]] + [
        pltpu.SMEM(neighbours.shape, jnp.int32),
        pltpu.VMEM((2, columns, ROWS, 256), BF),
        pltpu.VMEM((2, columns, 256 + 2 * SLOT, 256), BF),
        pltpu.VMEM((2, 9, 2, FACE * columns, 128), F32),
        pltpu.SemaphoreType.DMA((7, planes)),
    ]
    return call(weight_kernel, outs, operands, "weights", 1e10, (0, 1, 2, 3, 4), scratch)


def swapped(x, axis, first):
    n = lax.axis_size(axis)
    pairs = [(i, (i + 1) % n) for i in range(first, n, 2)]
    return lax.ppermute(x, axis, [pair for i, j in pairs for pair in ((i, j), (j, i))])


def shift(x, axis, by):
    n = lax.axis_size(axis)
    return lax.ppermute(x, axis, [(i, i + by) for i in range(n) if 0 <= i + by < n])


def local(right_sides, initial, inverse_blocks, couplings, neighbours):
    planes, columns, rhs, width = initial.shape
    size = columns * rhs
    const = lambda x: jnp.asarray(x, BF)
    send_in = const(send_table(ROWS, inner, planes))
    own_in = const(own_table(ROWS, inner))
    back = const(table(ROWS, width, [(inner(*n), n) for n in NODES], natural))
    up_sel = const(receive_table(2, planes))
    down_sel = const(receive_table(0, planes))
    beside = neighbours.T

    share = (planes * MAIN + tail_rows(planes), size)
    near, far, above = call(
        first_kernel,
        [(share, BF), (share, BF), ((FACE, size), BF)],
        (initial,),
        "initial_traces",
    )
    near, far, above, initial = lax.optimization_barrier((near, far, above, initial))
    near, far = swapped(near, "cross", 0), swapped(far, "cross", 1)
    from_above = shift(above, "sweep", -1)
    known, lower, base, own, gathers = weights(
        inverse_blocks.transpose(0, 2, 1, 3), couplings.transpose(0, 2, 3, 1, 4), right_sides, initial, beside
    )

    field = (planes, ROWS, size)
    trace = (planes, FACE, size)
    chain_outs = [(field, F32), (trace, F32)]
    part, traces, message = call(
        functools.partial(forward_chain_kernel, rhs=rhs),
        chain_outs + [((3 * FACE, size), BF)],
        (near, far, from_above, own, gathers, up_sel, down_sel, known, lower, base),
        "forward_chain",
    )
    messages = lax.all_gather(message, "sweep")
    middle, change, near, far = call(
        functools.partial(forward_finish_kernel, rhs=rhs),
        [(field, BF), (field, F32), (share, BF), (share, BF)],
        (messages, part, traces, lower, send_in),
        "forward_finish",
    )
    near, far = swapped(near, "cross", 0), swapped(far, "cross", 1)
    own, base, upper = call(
        middle_kernel,
        [((planes, 2 * FACE, size), BF), (field, F32), (lower.shape, BF)],
        (middle, change, base, gathers, own_in, known),
        "middle",
        2e9,
    )
    own, pass_b = lax.optimization_barrier((own, upper[0, :, PRODUCT]))
    passes = products(pass_b, -1)
    part, traces, message = call(
        functools.partial(backward_chain_kernel, rhs=rhs),
        chain_outs + [((FACE, size), BF)],
        (near, far, own, gathers, up_sel, down_sel, known, upper, base),
        "backward_chain",
    )
    messages = lax.all_gather(message, "sweep")
    (result,) = call(
        functools.partial(backward_finish_kernel, rhs=rhs),
        [(right_sides.shape, BF)],
        (messages, *passes, part, traces, upper, back),
        "backward_finish",
        scratch=[pltpu.VMEM(right_sides.shape, BF), pltpu.SemaphoreType.DMA((planes,))],
        out_space=pltpu.HBM,
    )
    return result


def solution(mesh):
    return jax.shard_map(
        local,
        mesh=mesh,
        in_specs=(
            P("sweep", "cross", None, None),
            P("sweep", "cross", None, None),
            P("sweep", "cross", None, None),
            P("sweep", "cross", None, None, None),
            P("cross", None),
        ),
        out_specs=P("sweep", "cross", None, None),
        check_vma=False,
    )
```

```python
import functools

import jax
import jax.numpy as jnp
import numpy as np
from jax import lax
from jax.experimental import pallas as pl
from jax.experimental.pallas import tpu as pltpu
from jax.sharding import PartitionSpec as P

BF = jnp.bfloat16
F32 = jnp.float32
NT = 45
FACE = 48
SLOT = 64
ROWS = 3 * FACE
SHARED = 75
MAIN = 64
MIB = 1 << 20
FIRST = slice(0, FACE)
LAST = slice(2 * FACE, ROWS)
FULL = slice(0, ROWS)
PRODUCT = slice(ROWS, ROWS + FACE)


def natural(v, a, b, c):
    return v * 27 + a * 9 + b * 3 + c


def inner(v, a, b, c):
    return a * FACE + v * 9 + b * 3 + c


NODES = [(v, a, b, c) for v in range(5) for a in range(3) for b in range(3) for c in range(3)]


def face_nodes(place, which):
    return [n for n in NODES if n[1 + place] == which]


def table(height, width, rows, column_of):
    out = np.zeros((height, width), np.float32)
    for row, node in rows:
        out[row, column_of(*node)] = 1
    return out


def block(nodes, start=0):
    return [(start + i, n) for i, n in enumerate(nodes)]


def tail_rows(planes):
    return -(-planes * (SHARED - MAIN) // 16) * 16


def union_nodes(which):
    others = [b for b in range(3) if b != which]
    spots = [(which, c) for c in range(3)] + [(b, which) for b in others]
    return [(v, a, b, c) for v in range(5) for a in range(3) for b, c in spots]


def place_of(i, plane):
    return i if i < MAIN else i + plane * (SHARED - MAIN)


def send_table(width, column_of, planes):
    height = MAIN + tail_rows(planes)
    out = []
    for p in range(planes):
        rows = [(place_of(i, p), n) for i, n in enumerate(union_nodes(2))]
        rows += [(height + place_of(i, p), n) for i, n in enumerate(union_nodes(0))]
        out.append(table(2 * height, width, rows, column_of))
    return np.stack(out)


def own_table(width, column_of):
    rows = block(face_nodes(2, 2)) + block(face_nodes(2, 0), FACE)
    return table(2 * FACE, width, rows, column_of)


def receive_table(which, planes):
    rows = block(face_nodes(1, which)) + block(face_nodes(2, which), FACE)
    out = []
    for p in range(planes):
        place = {n: place_of(i, p) for i, n in enumerate(union_nodes(which))}
        out.append(table(2 * FACE, MAIN + tail_rows(planes), rows, lambda *n: place[n]))
    return np.stack(out)


def mm(a, b):
    return lax.dot_general(a, b, (((1,), (0,)), ((), ())), preferred_element_type=F32)


def mt(a, b):
    return lax.dot_general(a, b, (((1,), (1,)), ((), ())), preferred_element_type=F32)


def group(shape, width, at):
    lane = lax.broadcasted_iota(jnp.int32, shape, 1)
    return (lane >= at * width) & (lane < (at + 1) * width)


def split_lanes(value, width):
    lanes = value.shape[1]
    value = value.astype(F32)
    pad = jnp.zeros((SLOT - FACE, lanes), BF)
    parts = []
    for c in range(lanes // width):
        parts += [jnp.where(group(value.shape, width, c), value, 0.0).astype(BF), pad]
    return jnp.concatenate(parts, 0)


def own_lanes(values, width):
    out = values[0]
    for c in range(1, len(values)):
        out = jnp.where(group(out.shape, width, c), values[c], out)
    return out


def one_hot(source, start, height):
    row = lax.broadcasted_iota(jnp.int32, (height, source.shape[1]), 0) + start
    return jnp.where(row == source, 1.0, 0.0).astype(BF)


def chain_step(matrix, trace, rhs, rows=slice(None)):
    half = trace.shape[1] // 2
    return jnp.concatenate(
        [mm(matrix[h, rows], split_lanes(trace[:, h * half : (h + 1) * half], rhs)) for h in range(2)], 1
    )


def shared_target(row, which, plane, planes):
    rest = SHARED - MAIN
    i = jnp.where(row < MAIN, row, row - plane * rest)
    k = i % 15
    a = k // 5
    j = k % 5
    b = jnp.where(j < 3, which, j - 3 if which == 2 else j - 2)
    c = jnp.where(j < 3, j, which)
    inside = (row < MAIN) | ((i >= MAIN) & (i < SHARED))
    return jnp.where(inside, i // 15 * 27 + a * 9 + b * 3 + c, -1)


def picks(target, width):
    lane = lax.broadcasted_iota(jnp.int32, (target.shape[0], width), 1)
    return jnp.where(lane == target, 1.0, 0.0).astype(BF)


def rows_of(height):
    return lax.broadcasted_iota(jnp.int32, (height, 1), 0)


def first_target(row):
    return jnp.where(row < NT, row // 9 * 27 + row % 9, -1)


def c_target(row, which):
    return jnp.where(row < NT, row * 3 + which, -1)


def sources(neighbours, columns, rhs):
    place = lax.axis_index("cross")
    total = columns * lax.axis_size("cross")
    lane = lax.broadcasted_iota(jnp.int32, (1, columns * rhs), 1)
    out = []
    for face, first in ((2, place - 1), (3, place)):
        source = lane
        for c in range(columns):
            at = neighbours[face, c] - first * columns
            at = jnp.where(at < 0, at + total, at)
            at = jnp.where(at >= total, at - total, at)
            source = jnp.where(lane >= c * rhs, lane + (at - c) * rhs, source)
        out.append(source)
    return out


def even():
    return lax.rem(lax.axis_index("cross"), 2) == 0


def put_shared(out, near, far):
    height = out[0].shape[0] // 2
    messages = []
    for start in (0, height):
        tails = [x[start + MAIN : start + height] for x in out]
        parts = [x[start : start + MAIN] for x in out] + [sum(tails[1:], tails[0])]
        messages.append(jnp.concatenate(parts, 0))
    up, down = messages
    near[...] = jnp.where(even(), up, down).astype(BF)
    far[...] = jnp.where(even(), down, up).astype(BF)


def first_kernel(initial, near, far, above):
    planes, columns, rhs, width = initial.shape
    row = rows_of(MAIN + tail_rows(planes))
    out = []
    for p in range(planes):
        x = initial[p].reshape(columns * rhs, width)
        tables = [picks(shared_target(row, which, p, planes), width) for which in (2, 0)]
        out.append(mt(jnp.concatenate(tables, 0), x))
        if p == 0:
            above[...] = mt(picks(first_target(rows_of(FACE)), width), x).astype(BF)
    put_shared(out, near, far)


def turned(rows, raw, put):
    count, columns, width = rows.shape
    raw[0, : count * columns] = rows[:, :, :128].astype(F32).reshape(count * columns, 128)
    rest = rows[:, :, 128:].astype(F32).reshape(count * columns, width - 128)
    raw[1, : count * columns] = jnp.concatenate([rest, jnp.zeros((count * columns, 256 - width), F32)], 1)
    for c in range(columns):
        put(c, jnp.concatenate([raw[i, pl.ds(c, FACE, stride=columns), :] for i in range(2)], 1))


def weight_kernel(
    inverse, couplings, right, initial, neighbours_there,
    known, lower, base, own, gathers,
    inverse_in, couplings_in, right_in, neighbours, solves, faces, raw, done,
):
    planes, columns, rhs, width = initial.shape
    size = columns * rhs
    half = columns // 2
    early = pltpu.make_async_copy(neighbours_there, neighbours, done.at[3, 0])
    early.start()
    copies = []
    for p in range(planes):
        pairs = ((inverse, inverse_in), (couplings, couplings_in), (right, right_in))
        copies.append([pltpu.make_async_copy(x.at[p], y.at[p], done.at[i, p]) for i, (x, y) in enumerate(pairs)])
        for copy in copies[p]:
            copy.start()
    for start, stop in ((5 * FACE, 256), (256 + FACE, 256 + 2 * SLOT)):
        faces[:, :, start:stop] = jnp.zeros((2, columns, stop - start, 256), BF)
    raw[:, :, :, NT * columns :] = jnp.zeros((2, 9, 2, (FACE - NT) * columns, 128), F32)
    own_table = [picks(c_target(rows_of(FACE), which), width) for which in (2, 0)]
    first_table = picks(first_target(rows_of(FACE)), width)
    fields = [initial[p].reshape(size, width) for p in range(planes)]
    sides = [jnp.concatenate([mt(own_table[j], x).astype(BF) for x in fields], 0) for j in range(2)]
    for p in range(planes):
        own[p, LAST] = mt(first_table, fields[min(p + 1, planes - 1)]).astype(BF)
    early.wait()
    source = sources(neighbours, columns, rhs)
    for i, start in enumerate((0, size)):
        for j in range(2):
            gathers[i, j] = one_hot(source[j], start, size)
    for j in range(2):
        mine = mm(sides[j], gathers[1 - j, j]).astype(BF)
        for p in range(planes):
            own[p, j * FACE : (j + 1) * FACE] = mine[p * FACE : (p + 1) * FACE]
    lane = lax.broadcasted_iota(jnp.int32, (ROWS, 2 * SLOT), 1)

    def prepare(p):
        slot = p % 2
        for copy in copies[p]:
            copy.wait()
        faces[slot, :, 256 + SLOT : 256 + SLOT + rhs, :width] = right_in[p]
        for a in range(3):
            rows = [inverse_in[p, v * 27 + a * 9 : v * 27 + a * 9 + 9] for v in range(5)]

            def put(c, value):
                solves[slot, c, a * FACE : (a + 1) * FACE] = (-value).astype(BF)

            turned(jnp.concatenate(rows, 0), raw.at[slot, a], put)
        for f, place in enumerate((256, 4 * FACE, 0, FACE, 2 * FACE, 3 * FACE)):

            def put(c, value):
                faces[slot, c, place : place + FACE] = value.astype(BF)

            turned(couplings_in[p, f], raw.at[slot, 3 + f], put)

    for p in range(planes):
        slot = p % 2
        prepare(p)
        bases, lowers = [], []
        before = None
        for c in range(columns):
            solve = solves[slot, c]
            known[p, c] = mt(solve, faces[slot, c, :256]).astype(BF)
            both = mt(solve, faces[slot, c, 256:])
            move = (c % half * rhs - SLOT) % 128
            bases.append(pltpu.roll(both, move, 1) if move else both)
            if c % 2 == 0:
                before = both
            else:
                lowers.append(jnp.where(lane < SLOT, before, pltpu.roll(both, SLOT, 1)).astype(BF))
        for h in range(2):
            lanes = slice(h * half * rhs, (h + 1) * half * rhs)
            lower[p, h, :ROWS] = jnp.concatenate(lowers[2 * h : 2 * h + 2], 1)
            base[p, :, lanes] = -own_lanes(bases[h * half : (h + 1) * half], rhs)
    chain_products(lower, LAST, range(planes))


def chain_products(matrix, rows, order):
    for h in range(2):
        total = None
        for q in order:
            step = matrix[q, h, rows]
            total = step.astype(F32) if total is None else mm(step, split_lanes(total, SLOT))
            matrix[q, h, PRODUCT] = total.astype(BF)


def gathered(near, far, own, up_sel, down_sel, gathers):
    planes = up_sel.shape[0]

    def faces(received, select):
        tail = received[planes * MAIN :]
        wholes = [jnp.concatenate([received[p * MAIN : (p + 1) * MAIN], tail], 0) for p in range(planes)]
        return [mm(select[p], wholes[p]).astype(BF) for p in range(planes)]

    low = faces(jnp.where(even(), far[...], near[...]), up_sel)
    high = faces(jnp.where(even(), near[...], far[...]), down_sel)
    sides = []
    for j, side in enumerate((low, high)):
        picked = mm(jnp.concatenate([x[FACE:] for x in side], 0), gathers[j, j]).astype(BF)
        sides.append([picked[p * FACE : (p + 1) * FACE] + own[p, j * FACE : (j + 1) * FACE] for p in range(planes)])
    return [jnp.concatenate([low[p][:FACE], high[p][:FACE], sides[0][p], sides[1][p]], 0) for p in range(planes)]


def known_part(known_c, operand, columns, rhs):
    half = columns // 2
    out = []
    for h in range(2):
        side = operand[:, h * half * rhs : (h + 1) * half * rhs]
        out.append(own_lanes([mm(known_c(h * half + c), side) for c in range(half)], rhs))
    return jnp.concatenate(out, 1)


def chain_kernel(known, base, matrix, wholes, outs, order, rows, rhs, last_face):
    part, traces, message = outs
    planes, columns = known.shape[:2]
    trace = None
    for p in order:
        whole = jnp.concatenate([wholes[p], last_face(p)], 0)
        value = base[p] + known_part(lambda c: known[p, c], whole, columns, rhs)
        part[p] = value
        value = value[rows]
        trace = value if trace is None else value + chain_step(matrix.at[p], trace, rhs, rows)
        traces[p] = trace
    message[FIRST] = trace.astype(BF)
    if message.shape[0] > FACE:
        for h in range(2):
            message[(1 + h) * FACE : (2 + h) * FACE] = matrix[order[-1], h, PRODUCT]


def forward_chain_kernel(near, far, above, own, gathers, up_sel, down_sel, known, lower, base, *outs, rhs):
    wholes = gathered(near, far, own, up_sel, down_sel, gathers)
    planes, size = len(wholes), above.shape[1]
    pad = jnp.zeros((256 - 5 * FACE, size), BF)
    last_face = lambda p: jnp.concatenate([own[p, LAST] if p + 1 < planes else above[...], pad], 0)
    chain_kernel(known, base, lower, wholes, outs, range(planes), LAST, rhs, last_face)


def backward_chain_kernel(near, far, own, gathers, up_sel, down_sel, known, upper, base, *outs, rhs):
    wholes = gathered(near, far, own, up_sel, down_sel, gathers)
    last_face = lambda p: jnp.zeros((256 - 4 * FACE, near.shape[1]), BF)
    chain_kernel(known, base, upper, wholes, outs, range(len(wholes) - 1, -1, -1), FIRST, rhs, last_face)


def incoming(messages, products, forward, rhs):
    here = lax.axis_index("sweep")
    n = messages.shape[0]
    trace = None
    for i in range(n - 1) if forward else range(n - 1, 0, -1):
        value = messages[i, FIRST].astype(F32)
        if trace is None:
            trace = jnp.zeros_like(value)
        else:
            half = value.shape[1] // 2
            halves = [trace[:, h * half : (h + 1) * half] for h in range(2)]
            value = value + jnp.concatenate([mm(m, split_lanes(t, rhs)) for m, t in zip(products(i), halves)], 1)
        trace = jnp.where(i < here if forward else i > here, value, trace)
    return trace


def forward_finish_kernel(
    messages, part, traces, lower, send, middle, change, near, far, *, rhs
):
    planes = part.shape[0]
    inside = lambda i: [messages[i, (1 + h) * FACE : (2 + h) * FACE] for h in range(2)]
    entry = incoming(messages, inside, True, rhs)
    out = []
    trace = entry
    for p in range(planes):
        delta = chain_step(lower.at[p], trace, rhs, FULL)
        change[p] = delta
        whole = (part[p] + delta).astype(BF)
        middle[p] = whole
        out.append(mm(send[p], whole))
        if p + 1 < planes:
            trace = traces[p] + chain_step(lower.at[p], entry, rhs, PRODUCT)
    put_shared(out, near, far)


def middle_kernel(middle, change, base, gathers, own_sel, known, own, out, upper):
    planes = middle.shape[0]
    mine = [mm(own_sel[...], middle[p]).astype(BF) for p in range(planes)]
    for j in range(2):
        side = jnp.concatenate([x[j * FACE : (j + 1) * FACE] for x in mine], 0)
        side = mm(side, gathers[1 - j, j]).astype(BF)
        for p in range(planes):
            own[p, j * FACE : (j + 1) * FACE] = side[p * FACE : (p + 1) * FACE]
    for p in range(planes):
        out[p] = base[p] + change[p]
    columns = known.shape[1]
    lane = lax.broadcasted_iota(jnp.int32, (ROWS, 2 * SLOT), 1)
    for p in range(planes):
        pairs = []
        for c in range(0, columns, 2):
            one, two = (known[p, c + i, :, 128:].astype(F32) for i in range(2))
            pairs.append(jnp.where(lane < SLOT, pltpu.roll(one, SLOT, 1), two).astype(BF))
        for h in range(2):
            upper[p, h, :ROWS] = jnp.concatenate(pairs[2 * h : 2 * h + 2], 1)
    chain_products(upper, FIRST, range(planes - 1, -1, -1))


def backward_finish_kernel(
    messages, near, next_near, part, traces, upper, back, result, results, sem, *, rhs
):
    planes = part.shape[0]
    here = lax.axis_index("sweep")
    beside = lambda i: [jnp.where(here + 1 == i, near[h], next_near[h]) for h in range(2)]
    entry = incoming(messages, beside, False, rhs)
    columns, _, width = result.shape[1:]
    copies = []
    trace = entry
    for p in range(planes - 1, -1, -1):
        whole = part[p] + chain_step(upper.at[p], trace, rhs, FULL)
        flat = lax.dot_general(whole.astype(BF), back[...], (((0,), (0,)), ((), ())), preferred_element_type=F32)
        results[p] = flat.astype(BF).reshape(columns, rhs, width)
        copies.append(pltpu.make_async_copy(results.at[p], result.at[p], sem.at[p]))
        copies[-1].start()
        if p:
            trace = traces[p] + chain_step(upper.at[p], entry, rhs, PRODUCT)
    for copy in copies:
        copy.wait()


def call(kernel, outs, operands, name, flops=2e8, far=(), scratch=(), out_space=pltpu.VMEM):
    shapes = [jax.ShapeDtypeStruct(s, d) for s, d in outs]
    nbytes = sum(x.size * x.dtype.itemsize for x in list(operands) + shapes)
    spaces = [pltpu.SMEM if x.dtype == jnp.int32 else pltpu.VMEM for x in operands]
    spaces = [pltpu.HBM if i in far else space for i, space in enumerate(spaces)]
    operands = [
        pltpu.with_memory_space_constraint(x, pltpu.HBM) if i in far else x for i, x in enumerate(operands)
    ]
    return pl.pallas_call(
        kernel,
        out_shape=shapes,
        in_specs=[pl.BlockSpec(memory_space=space) for space in spaces],
        out_specs=[pl.BlockSpec(memory_space=out_space)] * len(shapes),
        scratch_shapes=list(scratch),
        compiler_params=pltpu.CompilerParams(vmem_limit_bytes=24 * MIB),
        cost_estimate=pl.CostEstimate(flops=int(flops), bytes_accessed=int(nbytes), transcendentals=0),
        name=name,
    )(*operands)


def products(x, by):
    n = lax.axis_size("sweep")
    inner = range(1, n - 1)
    return [
        lax.ppermute(x, "sweep", [(i, i + step) for i in inner if 0 <= i + step < n]) for step in (by, 2 * by)
    ]


def weights(inverse, couplings, right, initial, neighbours):
    planes, columns, rhs, width = initial.shape
    size = columns * rhs
    pack = (planes, 2, ROWS + FACE, 256)
    field = (planes, ROWS, size)
    outs = [((planes, columns, ROWS, 256), BF), (pack, BF), (field, F32), (field, BF), ((2, 2, size, size), BF)]
    operands = (inverse, couplings, right, initial, neighbours)
    scratch = [pltpu.VMEM(x.shape, BF) for x in operands[:3]] + [
        pltpu.SMEM(neighbours.shape, jnp.int32),
        pltpu.VMEM((2, columns, ROWS, 256), BF),
        pltpu.VMEM((2, columns, 256 + 2 * SLOT, 256), BF),
        pltpu.VMEM((2, 9, 2, FACE * columns, 128), F32),
        pltpu.SemaphoreType.DMA((4, planes)),
    ]
    return call(weight_kernel, outs, operands, "weights", 1e10, (0, 1, 2, 4), scratch)


def swapped(x, axis, first):
    n = lax.axis_size(axis)
    pairs = [(i, (i + 1) % n) for i in range(first, n, 2)]
    return lax.ppermute(x, axis, [pair for i, j in pairs for pair in ((i, j), (j, i))])


def shift(x, axis, by):
    n = lax.axis_size(axis)
    return lax.ppermute(x, axis, [(i, i + by) for i in range(n) if 0 <= i + by < n])


def local(right_sides, initial, inverse_blocks, couplings, neighbours):
    planes, columns, rhs, width = initial.shape
    size = columns * rhs
    const = lambda x: jnp.asarray(x, BF)
    send_in = const(send_table(ROWS, inner, planes))
    own_in = const(own_table(ROWS, inner))
    back = const(table(ROWS, width, [(inner(*n), n) for n in NODES], natural))
    up_sel = const(receive_table(2, planes))
    down_sel = const(receive_table(0, planes))
    beside = neighbours.T

    share = (planes * MAIN + tail_rows(planes), size)
    near, far, above = call(
        first_kernel,
        [(share, BF), (share, BF), ((FACE, size), BF)],
        (initial,),
        "initial_traces",
    )
    near, far, above, initial = lax.optimization_barrier((near, far, above, initial))
    near, far = swapped(near, "cross", 0), swapped(far, "cross", 1)
    from_above = shift(above, "sweep", -1)
    known, lower, base, own, gathers = weights(
        inverse_blocks.transpose(0, 2, 1, 3), couplings.transpose(0, 2, 3, 1, 4), right_sides, initial, beside
    )

    field = (planes, ROWS, size)
    trace = (planes, FACE, size)
    chain_outs = [(field, F32), (trace, F32)]
    part, traces, message = call(
        functools.partial(forward_chain_kernel, rhs=rhs),
        chain_outs + [((3 * FACE, size), BF)],
        (near, far, from_above, own, gathers, up_sel, down_sel, known, lower, base),
        "forward_chain",
    )
    messages = lax.all_gather(message, "sweep")
    middle, change, near, far = call(
        functools.partial(forward_finish_kernel, rhs=rhs),
        [(field, BF), (field, F32), (share, BF), (share, BF)],
        (messages, part, traces, lower, send_in),
        "forward_finish",
    )
    near, far = swapped(near, "cross", 0), swapped(far, "cross", 1)
    own, base, upper = call(
        middle_kernel,
        [((planes, 2 * FACE, size), BF), (field, F32), (lower.shape, BF)],
        (middle, change, base, gathers, own_in, known),
        "middle",
        2e9,
    )
    own, pass_b = lax.optimization_barrier((own, upper[0, :, PRODUCT]))
    passes = products(pass_b, -1)
    part, traces, message = call(
        functools.partial(backward_chain_kernel, rhs=rhs),
        chain_outs + [((FACE, size), BF)],
        (near, far, own, gathers, up_sel, down_sel, known, upper, base),
        "backward_chain",
    )
    messages = lax.all_gather(message, "sweep")
    (result,) = call(
        functools.partial(backward_finish_kernel, rhs=rhs),
        [(right_sides.shape, BF)],
        (messages, *passes, part, traces, upper, back),
        "backward_finish",
        scratch=[pltpu.VMEM(right_sides.shape, BF), pltpu.SemaphoreType.DMA((planes,))],
        out_space=pltpu.HBM,
    )
    return result


def solution(mesh):
    return jax.shard_map(
        local,
        mesh=mesh,
        in_specs=(
            P("sweep", "cross", None, None),
            P("sweep", "cross", None, None),
            P("sweep", "cross", None, None),
            P("sweep", "cross", None, None, None),
            P("cross", None),
        ),
        out_specs=P("sweep", "cross", None, None),
        check_vma=False,
    )
```

```python
import functools

import jax
import jax.numpy as jnp
import numpy as np
from jax import lax
from jax.experimental import pallas as pl
from jax.experimental.pallas import tpu as pltpu
from jax.sharding import PartitionSpec as P

BF = jnp.bfloat16
F32 = jnp.float32
NT = 45
FACE = 48
SLOT = 64
ROWS = 3 * FACE
SHARED = 75
MAIN = 64
MIB = 1 << 20
FIRST = slice(0, FACE)
LAST = slice(2 * FACE, ROWS)
FULL = slice(0, ROWS)
PRODUCT = slice(ROWS, ROWS + FACE)


def natural(v, a, b, c):
    return v * 27 + a * 9 + b * 3 + c


def inner(v, a, b, c):
    return a * FACE + v * 9 + b * 3 + c


NODES = [(v, a, b, c) for v in range(5) for a in range(3) for b in range(3) for c in range(3)]


def face_nodes(place, which):
    return [n for n in NODES if n[1 + place] == which]


def table(height, width, rows, column_of):
    out = np.zeros((height, width), np.float32)
    for row, node in rows:
        out[row, column_of(*node)] = 1
    return out


def block(nodes, start=0):
    return [(start + i, n) for i, n in enumerate(nodes)]


def tail_rows(planes):
    return -(-planes * (SHARED - MAIN) // 16) * 16


def union_nodes(which):
    others = [b for b in range(3) if b != which]
    spots = [(which, c) for c in range(3)] + [(b, which) for b in others]
    return [(v, a, b, c) for v in range(5) for a in range(3) for b, c in spots]


def place_of(i, plane):
    return i if i < MAIN else i + plane * (SHARED - MAIN)


def send_table(width, column_of, planes):
    height = MAIN + tail_rows(planes)
    out = []
    for p in range(planes):
        rows = [(place_of(i, p), n) for i, n in enumerate(union_nodes(2))]
        rows += [(height + place_of(i, p), n) for i, n in enumerate(union_nodes(0))]
        out.append(table(2 * height, width, rows, column_of))
    return np.stack(out)


def own_table(width, column_of):
    rows = block(face_nodes(2, 2)) + block(face_nodes(2, 0), FACE)
    return table(2 * FACE, width, rows, column_of)


def receive_table(which, planes):
    rows = block(face_nodes(1, which)) + block(face_nodes(2, which), FACE)
    out = []
    for p in range(planes):
        place = {n: place_of(i, p) for i, n in enumerate(union_nodes(which))}
        out.append(table(2 * FACE, MAIN + tail_rows(planes), rows, lambda *n: place[n]))
    return np.stack(out)


def mm(a, b):
    return lax.dot_general(a, b, (((1,), (0,)), ((), ())), preferred_element_type=F32)


def mt(a, b):
    return lax.dot_general(a, b, (((1,), (1,)), ((), ())), preferred_element_type=F32)


def group(shape, width, at):
    lane = lax.broadcasted_iota(jnp.int32, shape, 1)
    return (lane >= at * width) & (lane < (at + 1) * width)


def split_lanes(value, width):
    lanes = value.shape[1]
    value = value.astype(F32)
    pad = jnp.zeros((SLOT - FACE, lanes), BF)
    parts = []
    for c in range(lanes // width):
        parts += [jnp.where(group(value.shape, width, c), value, 0.0).astype(BF), pad]
    return jnp.concatenate(parts, 0)


def own_lanes(values, width):
    out = values[0]
    for c in range(1, len(values)):
        out = jnp.where(group(out.shape, width, c), values[c], out)
    return out


def one_hot(source, start, height):
    row = lax.broadcasted_iota(jnp.int32, (height, source.shape[1]), 0) + start
    return jnp.where(row == source, 1.0, 0.0).astype(BF)


def chain_step(matrix, trace, rhs, rows=slice(None)):
    half = trace.shape[1] // 2
    return jnp.concatenate(
        [mm(matrix[h, rows], split_lanes(trace[:, h * half : (h + 1) * half], rhs)) for h in range(2)], 1
    )


def shared_target(row, which, plane, planes):
    rest = SHARED - MAIN
    i = jnp.where(row < MAIN, row, row - plane * rest)
    k = i % 15
    a = k // 5
    j = k % 5
    b = jnp.where(j < 3, which, j - 3 if which == 2 else j - 2)
    c = jnp.where(j < 3, j, which)
    inside = (row < MAIN) | ((i >= MAIN) & (i < SHARED))
    return jnp.where(inside, i // 15 * 27 + a * 9 + b * 3 + c, -1)


def picks(target, width):
    lane = lax.broadcasted_iota(jnp.int32, (target.shape[0], width), 1)
    return jnp.where(lane == target, 1.0, 0.0).astype(BF)


def rows_of(height):
    return lax.broadcasted_iota(jnp.int32, (height, 1), 0)


def first_target(row):
    return jnp.where(row < NT, row // 9 * 27 + row % 9, -1)


def c_target(row, which):
    return jnp.where(row < NT, row * 3 + which, -1)


def sources(neighbours, columns, rhs):
    place = lax.axis_index("cross")
    total = columns * lax.axis_size("cross")
    lane = lax.broadcasted_iota(jnp.int32, (1, columns * rhs), 1)
    out = []
    for face, first in ((2, place - 1), (3, place)):
        source = lane
        for c in range(columns):
            at = neighbours[face, c] - first * columns
            at = jnp.where(at < 0, at + total, at)
            at = jnp.where(at >= total, at - total, at)
            source = jnp.where(lane >= c * rhs, lane + (at - c) * rhs, source)
        out.append(source)
    return out


def even():
    return lax.rem(lax.axis_index("cross"), 2) == 0


def put_shared(out, near, far):
    height = out[0].shape[0] // 2
    messages = []
    for start in (0, height):
        tails = [x[start + MAIN : start + height] for x in out]
        parts = [x[start : start + MAIN] for x in out] + [sum(tails[1:], tails[0])]
        messages.append(jnp.concatenate(parts, 0))
    up, down = messages
    near[...] = jnp.where(even(), up, down).astype(BF)
    far[...] = jnp.where(even(), down, up).astype(BF)


def first_kernel(initial, near, far, above):
    planes, columns, rhs, width = initial.shape
    row = rows_of(MAIN + tail_rows(planes))
    out = []
    for p in range(planes):
        x = initial[p].reshape(columns * rhs, width)
        tables = [picks(shared_target(row, which, p, planes), width) for which in (2, 0)]
        out.append(mt(jnp.concatenate(tables, 0), x))
        if p == 0:
            above[...] = mt(picks(first_target(rows_of(FACE)), width), x).astype(BF)
    put_shared(out, near, far)


def turned(rows, raw, put):
    count, columns, width = rows.shape
    raw[0, : count * columns] = rows[:, :, :128].astype(F32).reshape(count * columns, 128)
    rest = rows[:, :, 128:].astype(F32).reshape(count * columns, width - 128)
    raw[1, : count * columns] = jnp.concatenate([rest, jnp.zeros((count * columns, 256 - width), F32)], 1)
    for c in range(columns):
        put(c, jnp.concatenate([raw[i, pl.ds(c, FACE, stride=columns), :] for i in range(2)], 1))


def weight_kernel(
    inverse, couplings, right, initial, neighbours_there,
    known, lower, base, own, gathers,
    inverse_in, couplings_in, right_in, neighbours, solves, faces, raw, done,
):
    planes, columns, rhs, width = initial.shape
    size = columns * rhs
    half = columns // 2
    early = pltpu.make_async_copy(neighbours_there, neighbours, done.at[3, 0])
    early.start()
    copies = []
    for p in range(planes):
        pairs = ((inverse, inverse_in), (couplings, couplings_in), (right, right_in))
        copies.append([pltpu.make_async_copy(x.at[p], y.at[p], done.at[i, p]) for i, (x, y) in enumerate(pairs)])
        for copy in copies[p]:
            copy.start()
    for start, stop in ((5 * FACE, 256), (256 + FACE, 256 + 2 * SLOT)):
        faces[:, :, start:stop] = jnp.zeros((2, columns, stop - start, 256), BF)
    raw[:, :, :, NT * columns :] = jnp.zeros((2, 9, 2, (FACE - NT) * columns, 128), F32)
    own_table = [picks(c_target(rows_of(FACE), which), width) for which in (2, 0)]
    first_table = picks(first_target(rows_of(FACE)), width)
    fields = [initial[p].reshape(size, width) for p in range(planes)]
    sides = [jnp.concatenate([mt(own_table[j], x).astype(BF) for x in fields], 0) for j in range(2)]
    for p in range(planes):
        own[p, LAST] = mt(first_table, fields[min(p + 1, planes - 1)]).astype(BF)
    early.wait()
    source = sources(neighbours, columns, rhs)
    for i, start in enumerate((0, size)):
        for j in range(2):
            gathers[i, j] = one_hot(source[j], start, size)
    for j in range(2):
        mine = mm(sides[j], gathers[1 - j, j]).astype(BF)
        for p in range(planes):
            own[p, j * FACE : (j + 1) * FACE] = mine[p * FACE : (p + 1) * FACE]
    lane = lax.broadcasted_iota(jnp.int32, (ROWS, 2 * SLOT), 1)

    def prepare(p):
        slot = p % 2
        for copy in copies[p]:
            copy.wait()
        faces[slot, :, 256 + SLOT : 256 + SLOT + rhs, :width] = right_in[p]
        for a in range(3):
            rows = [inverse_in[p, v * 27 + a * 9 : v * 27 + a * 9 + 9] for v in range(5)]

            def put(c, value):
                solves[slot, c, a * FACE : (a + 1) * FACE] = (-value).astype(BF)

            turned(jnp.concatenate(rows, 0), raw.at[slot, a], put)
        for f, place in enumerate((256, 4 * FACE, 0, FACE, 2 * FACE, 3 * FACE)):

            def put(c, value):
                faces[slot, c, place : place + FACE] = value.astype(BF)

            turned(couplings_in[p, f], raw.at[slot, 3 + f], put)

    for p in range(planes):
        slot = p % 2
        prepare(p)
        bases, lowers = [], []
        before = None
        for c in range(columns):
            solve = solves[slot, c]
            known[p, c] = mt(solve, faces[slot, c, :256]).astype(BF)
            both = mt(solve, faces[slot, c, 256:])
            move = (c % half * rhs - SLOT) % 128
            bases.append(pltpu.roll(both, move, 1) if move else both)
            if c % 2 == 0:
                before = both
            else:
                lowers.append(jnp.where(lane < SLOT, before, pltpu.roll(both, SLOT, 1)).astype(BF))
        for h in range(2):
            lanes = slice(h * half * rhs, (h + 1) * half * rhs)
            lower[p, h, :ROWS] = jnp.concatenate(lowers[2 * h : 2 * h + 2], 1)
            base[p, :, lanes] = -own_lanes(bases[h * half : (h + 1) * half], rhs)
    chain_products(lower, LAST, range(planes))


def chain_products(matrix, rows, order):
    for h in range(2):
        total = None
        for q in order:
            step = matrix[q, h, rows]
            total = step.astype(F32) if total is None else mm(step, split_lanes(total, SLOT))
            matrix[q, h, PRODUCT] = total.astype(BF)


def gathered(near, far, own, up_sel, down_sel, gathers):
    planes = up_sel.shape[0]

    def faces(received, select):
        tail = received[planes * MAIN :]
        wholes = [jnp.concatenate([received[p * MAIN : (p + 1) * MAIN], tail], 0) for p in range(planes)]
        return [mm(select[p], wholes[p]).astype(BF) for p in range(planes)]

    low = faces(jnp.where(even(), far[...], near[...]), up_sel)
    high = faces(jnp.where(even(), near[...], far[...]), down_sel)
    sides = []
    for j, side in enumerate((low, high)):
        picked = mm(jnp.concatenate([x[FACE:] for x in side], 0), gathers[j, j]).astype(BF)
        sides.append([picked[p * FACE : (p + 1) * FACE] + own[p, j * FACE : (j + 1) * FACE] for p in range(planes)])
    return [jnp.concatenate([low[p][:FACE], high[p][:FACE], sides[0][p], sides[1][p]], 0) for p in range(planes)]


def known_part(known_c, operand, columns, rhs):
    half = columns // 2
    out = []
    for h in range(2):
        side = operand[:, h * half * rhs : (h + 1) * half * rhs]
        out.append(own_lanes([mm(known_c(h * half + c), side) for c in range(half)], rhs))
    return jnp.concatenate(out, 1)


def chain_kernel(known, base, matrix, wholes, outs, order, rows, rhs, last_face):
    part, traces, message = outs
    planes, columns = known.shape[:2]
    trace = None
    for p in order:
        whole = jnp.concatenate([wholes[p], last_face(p)], 0)
        value = base[p] + known_part(lambda c: known[p, c], whole, columns, rhs)
        part[p] = value
        value = value[rows]
        trace = value if trace is None else value + chain_step(matrix.at[p], trace, rhs, rows)
        traces[p] = trace
    message[FIRST] = trace.astype(BF)
    if message.shape[0] > FACE:
        for h in range(2):
            message[(1 + h) * FACE : (2 + h) * FACE] = matrix[order[-1], h, PRODUCT]


def forward_chain_kernel(near, far, above, own, gathers, up_sel, down_sel, known, lower, base, *outs, rhs):
    wholes = gathered(near, far, own, up_sel, down_sel, gathers)
    planes, size = len(wholes), above.shape[1]
    pad = jnp.zeros((256 - 5 * FACE, size), BF)
    last_face = lambda p: jnp.concatenate([own[p, LAST] if p + 1 < planes else above[...], pad], 0)
    chain_kernel(known, base, lower, wholes, outs, range(planes), LAST, rhs, last_face)


def backward_chain_kernel(near, far, own, gathers, up_sel, down_sel, known, upper, base, *outs, rhs):
    wholes = gathered(near, far, own, up_sel, down_sel, gathers)
    last_face = lambda p: jnp.zeros((256 - 4 * FACE, near.shape[1]), BF)
    chain_kernel(known, base, upper, wholes, outs, range(len(wholes) - 1, -1, -1), FIRST, rhs, last_face)


def incoming(messages, products, forward, rhs):
    here = lax.axis_index("sweep")
    n = messages.shape[0]
    trace = None
    for i in range(n - 1) if forward else range(n - 1, 0, -1):
        value = messages[i, FIRST].astype(F32)
        if trace is None:
            trace = jnp.zeros_like(value)
        else:
            half = value.shape[1] // 2
            halves = [trace[:, h * half : (h + 1) * half] for h in range(2)]
            value = value + jnp.concatenate([mm(m, split_lanes(t, rhs)) for m, t in zip(products(i), halves)], 1)
        trace = jnp.where(i < here if forward else i > here, value, trace)
    return trace


def forward_finish_kernel(
    messages, part, traces, lower, send, middle, change, near, far, *, rhs
):
    planes = part.shape[0]
    inside = lambda i: [messages[i, (1 + h) * FACE : (2 + h) * FACE] for h in range(2)]
    entry = incoming(messages, inside, True, rhs)
    out = []
    trace = entry
    for p in range(planes):
        delta = chain_step(lower.at[p], trace, rhs, FULL)
        change[p] = delta
        whole = (part[p] + delta).astype(BF)
        middle[p] = whole
        out.append(mm(send[p], whole))
        if p + 1 < planes:
            trace = traces[p] + chain_step(lower.at[p], entry, rhs, PRODUCT)
    put_shared(out, near, far)


def middle_kernel(middle, change, base, gathers, own_sel, known, own, out, upper):
    planes = middle.shape[0]
    mine = [mm(own_sel[...], middle[p]).astype(BF) for p in range(planes)]
    for j in range(2):
        side = jnp.concatenate([x[j * FACE : (j + 1) * FACE] for x in mine], 0)
        side = mm(side, gathers[1 - j, j]).astype(BF)
        for p in range(planes):
            own[p, j * FACE : (j + 1) * FACE] = side[p * FACE : (p + 1) * FACE]
    for p in range(planes):
        out[p] = base[p] + change[p]
    columns = known.shape[1]
    lane = lax.broadcasted_iota(jnp.int32, (ROWS, 2 * SLOT), 1)
    for p in range(planes):
        pairs = []
        for c in range(0, columns, 2):
            one, two = (known[p, c + i, :, 128:].astype(F32) for i in range(2))
            pairs.append(jnp.where(lane < SLOT, pltpu.roll(one, SLOT, 1), two).astype(BF))
        for h in range(2):
            upper[p, h, :ROWS] = jnp.concatenate(pairs[2 * h : 2 * h + 2], 1)
    chain_products(upper, FIRST, range(planes - 1, -1, -1))


def backward_finish_kernel(
    messages, near, next_near, part, traces, upper, back, result, results, sem, *, rhs
):
    planes = part.shape[0]
    here = lax.axis_index("sweep")
    beside = lambda i: [jnp.where(here + 1 == i, near[h], next_near[h]) for h in range(2)]
    entry = incoming(messages, beside, False, rhs)
    columns, _, width = result.shape[1:]
    copies = []
    trace = entry
    for p in range(planes - 1, -1, -1):
        whole = part[p] + chain_step(upper.at[p], trace, rhs, FULL)
        flat = lax.dot_general(whole.astype(BF), back[...], (((0,), (0,)), ((), ())), preferred_element_type=F32)
        results[p] = flat.astype(BF).reshape(columns, rhs, width)
        if p % 2 == 0:
            pair = pl.ds(p, min(2, planes - p))
            copies.append(pltpu.make_async_copy(results.at[pair], result.at[pair], sem.at[p]))
            copies[-1].start()
        if p:
            trace = traces[p] + chain_step(upper.at[p], entry, rhs, PRODUCT)
    for copy in copies:
        copy.wait()


def call(kernel, outs, operands, name, flops=2e8, far=(), scratch=(), out_space=pltpu.VMEM):
    shapes = [jax.ShapeDtypeStruct(s, d) for s, d in outs]
    nbytes = sum(x.size * x.dtype.itemsize for x in list(operands) + shapes)
    spaces = [pltpu.SMEM if x.dtype == jnp.int32 else pltpu.VMEM for x in operands]
    spaces = [pltpu.HBM if i in far else space for i, space in enumerate(spaces)]
    operands = [
        pltpu.with_memory_space_constraint(x, pltpu.HBM) if i in far else x for i, x in enumerate(operands)
    ]
    return pl.pallas_call(
        kernel,
        out_shape=shapes,
        in_specs=[pl.BlockSpec(memory_space=space) for space in spaces],
        out_specs=[pl.BlockSpec(memory_space=out_space)] * len(shapes),
        scratch_shapes=list(scratch),
        compiler_params=pltpu.CompilerParams(vmem_limit_bytes=24 * MIB),
        cost_estimate=pl.CostEstimate(flops=int(flops), bytes_accessed=int(nbytes), transcendentals=0),
        name=name,
    )(*operands)


def products(x, by):
    n = lax.axis_size("sweep")
    inner = range(1, n - 1)
    return [
        lax.ppermute(x, "sweep", [(i, i + step) for i in inner if 0 <= i + step < n]) for step in (by, 2 * by)
    ]


def weights(inverse, couplings, right, initial, neighbours):
    planes, columns, rhs, width = initial.shape
    size = columns * rhs
    pack = (planes, 2, ROWS + FACE, 256)
    field = (planes, ROWS, size)
    outs = [((planes, columns, ROWS, 256), BF), (pack, BF), (field, F32), (field, BF), ((2, 2, size, size), BF)]
    operands = (inverse, couplings, right, initial, neighbours)
    scratch = [pltpu.VMEM(x.shape, BF) for x in operands[:3]] + [
        pltpu.SMEM(neighbours.shape, jnp.int32),
        pltpu.VMEM((2, columns, ROWS, 256), BF),
        pltpu.VMEM((2, columns, 256 + 2 * SLOT, 256), BF),
        pltpu.VMEM((2, 9, 2, FACE * columns, 128), F32),
        pltpu.SemaphoreType.DMA((4, planes)),
    ]
    return call(weight_kernel, outs, operands, "weights", 1e10, (0, 1, 2, 4), scratch)


def swapped(x, axis, first):
    n = lax.axis_size(axis)
    pairs = [(i, (i + 1) % n) for i in range(first, n, 2)]
    return lax.ppermute(x, axis, [pair for i, j in pairs for pair in ((i, j), (j, i))])


def shift(x, axis, by):
    n = lax.axis_size(axis)
    return lax.ppermute(x, axis, [(i, i + by) for i in range(n) if 0 <= i + by < n])


def local(right_sides, initial, inverse_blocks, couplings, neighbours):
    planes, columns, rhs, width = initial.shape
    size = columns * rhs
    const = lambda x: jnp.asarray(x, BF)
    send_in = const(send_table(ROWS, inner, planes))
    own_in = const(own_table(ROWS, inner))
    back = const(table(ROWS, width, [(inner(*n), n) for n in NODES], natural))
    up_sel = const(receive_table(2, planes))
    down_sel = const(receive_table(0, planes))
    beside = neighbours.T

    share = (planes * MAIN + tail_rows(planes), size)
    near, far, above = call(
        first_kernel,
        [(share, BF), (share, BF), ((FACE, size), BF)],
        (initial,),
        "initial_traces",
    )
    near, far, above, initial = lax.optimization_barrier((near, far, above, initial))
    near, far = swapped(near, "cross", 0), swapped(far, "cross", 1)
    from_above = shift(above, "sweep", -1)
    known, lower, base, own, gathers = weights(
        inverse_blocks.transpose(0, 2, 1, 3), couplings.transpose(0, 2, 3, 1, 4), right_sides, initial, beside
    )

    field = (planes, ROWS, size)
    trace = (planes, FACE, size)
    chain_outs = [(field, F32), (trace, F32)]
    part, traces, message = call(
        functools.partial(forward_chain_kernel, rhs=rhs),
        chain_outs + [((3 * FACE, size), BF)],
        (near, far, from_above, own, gathers, up_sel, down_sel, known, lower, base),
        "forward_chain",
    )
    messages = lax.all_gather(message, "sweep")
    middle, change, near, far = call(
        functools.partial(forward_finish_kernel, rhs=rhs),
        [(field, BF), (field, F32), (share, BF), (share, BF)],
        (messages, part, traces, lower, send_in),
        "forward_finish",
    )
    near, far = swapped(near, "cross", 0), swapped(far, "cross", 1)
    own, base, upper = call(
        middle_kernel,
        [((planes, 2 * FACE, size), BF), (field, F32), (lower.shape, BF)],
        (middle, change, base, gathers, own_in, known),
        "middle",
        2e9,
    )
    own, pass_b = lax.optimization_barrier((own, upper[0, :, PRODUCT]))
    passes = products(pass_b, -1)
    part, traces, message = call(
        functools.partial(backward_chain_kernel, rhs=rhs),
        chain_outs + [((FACE, size), BF)],
        (near, far, own, gathers, up_sel, down_sel, known, upper, base),
        "backward_chain",
    )
    messages = lax.all_gather(message, "sweep")
    (result,) = call(
        functools.partial(backward_finish_kernel, rhs=rhs),
        [(right_sides.shape, BF)],
        (messages, *passes, part, traces, upper, back),
        "backward_finish",
        scratch=[pltpu.VMEM(right_sides.shape, BF), pltpu.SemaphoreType.DMA((planes,))],
        out_space=pltpu.HBM,
    )
    return result


def solution(mesh):
    return jax.shard_map(
        local,
        mesh=mesh,
        in_specs=(
            P("sweep", "cross", None, None),
            P("sweep", "cross", None, None),
            P("sweep", "cross", None, None),
            P("sweep", "cross", None, None, None),
            P("cross", None),
        ),
        out_specs=P("sweep", "cross", None, None),
        check_vma=False,
    )
```

```python
import functools

import jax
import jax.numpy as jnp
import numpy as np
from jax import lax
from jax.experimental import pallas as pl
from jax.experimental.pallas import tpu as pltpu
from jax.sharding import PartitionSpec as P

BF = jnp.bfloat16
F32 = jnp.float32
NT = 45
FACE = 48
SLOT = 64
ROWS = 3 * FACE
SHARED = 75
MAIN = 64
MIB = 1 << 20
FIRST = slice(0, FACE)
LAST = slice(2 * FACE, ROWS)
FULL = slice(0, ROWS)
PRODUCT = slice(ROWS, ROWS + FACE)


def natural(v, a, b, c):
    return v * 27 + a * 9 + b * 3 + c


def inner(v, a, b, c):
    return a * FACE + v * 9 + b * 3 + c


NODES = [(v, a, b, c) for v in range(5) for a in range(3) for b in range(3) for c in range(3)]


def face_nodes(place, which):
    return [n for n in NODES if n[1 + place] == which]


def table(height, width, rows, column_of):
    out = np.zeros((height, width), np.float32)
    for row, node in rows:
        out[row, column_of(*node)] = 1
    return out


def block(nodes, start=0):
    return [(start + i, n) for i, n in enumerate(nodes)]


def tail_rows(planes):
    return -(-planes * (SHARED - MAIN) // 16) * 16


def union_nodes(which):
    others = [b for b in range(3) if b != which]
    spots = [(which, c) for c in range(3)] + [(b, which) for b in others]
    return [(v, a, b, c) for v in range(5) for a in range(3) for b, c in spots]


def place_of(i, plane):
    return i if i < MAIN else i + plane * (SHARED - MAIN)


def send_table(width, column_of, planes):
    height = MAIN + tail_rows(planes)
    out = []
    for p in range(planes):
        rows = [(place_of(i, p), n) for i, n in enumerate(union_nodes(2))]
        rows += [(height + place_of(i, p), n) for i, n in enumerate(union_nodes(0))]
        out.append(table(2 * height, width, rows, column_of))
    return np.stack(out)


def own_table(width, column_of):
    rows = block(face_nodes(2, 2)) + block(face_nodes(2, 0), FACE)
    return table(2 * FACE, width, rows, column_of)


def receive_table(which, planes):
    rows = block(face_nodes(1, which)) + block(face_nodes(2, which), FACE)
    out = []
    for p in range(planes):
        place = {n: place_of(i, p) for i, n in enumerate(union_nodes(which))}
        out.append(table(2 * FACE, MAIN + tail_rows(planes), rows, lambda *n: place[n]))
    return np.stack(out)


def mm(a, b):
    return lax.dot_general(a, b, (((1,), (0,)), ((), ())), preferred_element_type=F32)


def mt(a, b):
    return lax.dot_general(a, b, (((1,), (1,)), ((), ())), preferred_element_type=F32)


def group(shape, width, at):
    lane = lax.broadcasted_iota(jnp.int32, shape, 1)
    return (lane >= at * width) & (lane < (at + 1) * width)


def split_lanes(value, width):
    lanes = value.shape[1]
    value = value.astype(F32)
    pad = jnp.zeros((SLOT - FACE, lanes), BF)
    parts = []
    for c in range(lanes // width):
        parts += [jnp.where(group(value.shape, width, c), value, 0.0).astype(BF), pad]
    return jnp.concatenate(parts, 0)


def own_lanes(values, width):
    out = values[0]
    for c in range(1, len(values)):
        out = jnp.where(group(out.shape, width, c), values[c], out)
    return out


def one_hot(source, start, height):
    row = lax.broadcasted_iota(jnp.int32, (height, source.shape[1]), 0) + start
    return jnp.where(row == source, 1.0, 0.0).astype(BF)


def chain_step(matrix, trace, rhs, rows=slice(None)):
    half = trace.shape[1] // 2
    return jnp.concatenate(
        [mm(matrix[h, rows], split_lanes(trace[:, h * half : (h + 1) * half], rhs)) for h in range(2)], 1
    )


def shared_target(row, which, plane, planes):
    rest = SHARED - MAIN
    i = jnp.where(row < MAIN, row, row - plane * rest)
    k = i % 15
    a = k // 5
    j = k % 5
    b = jnp.where(j < 3, which, j - 3 if which == 2 else j - 2)
    c = jnp.where(j < 3, j, which)
    inside = (row < MAIN) | ((i >= MAIN) & (i < SHARED))
    return jnp.where(inside, i // 15 * 27 + a * 9 + b * 3 + c, -1)


def picks(target, width):
    lane = lax.broadcasted_iota(jnp.int32, (target.shape[0], width), 1)
    return jnp.where(lane == target, 1.0, 0.0).astype(BF)


def rows_of(height):
    return lax.broadcasted_iota(jnp.int32, (height, 1), 0)


def first_target(row):
    return jnp.where(row < NT, row // 9 * 27 + row % 9, -1)


def c_target(row, which):
    return jnp.where(row < NT, row * 3 + which, -1)


def sources(neighbours, columns, rhs):
    place = lax.axis_index("cross")
    total = columns * lax.axis_size("cross")
    lane = lax.broadcasted_iota(jnp.int32, (1, columns * rhs), 1)
    out = []
    for face, first in ((2, place - 1), (3, place)):
        source = lane
        for c in range(columns):
            at = neighbours[face, c] - first * columns
            at = jnp.where(at < 0, at + total, at)
            at = jnp.where(at >= total, at - total, at)
            source = jnp.where(lane >= c * rhs, lane + (at - c) * rhs, source)
        out.append(source)
    return out


def even():
    return lax.rem(lax.axis_index("cross"), 2) == 0


def put_shared(out, near, far):
    height = out[0].shape[0] // 2
    messages = []
    for start in (0, height):
        tails = [x[start + MAIN : start + height] for x in out]
        parts = [x[start : start + MAIN] for x in out] + [sum(tails[1:], tails[0])]
        messages.append(jnp.concatenate(parts, 0))
    up, down = messages
    near[...] = jnp.where(even(), up, down).astype(BF)
    far[...] = jnp.where(even(), down, up).astype(BF)


def first_kernel(initial, near, far, above):
    planes, columns, rhs, width = initial.shape
    row = rows_of(MAIN + tail_rows(planes))
    out = []
    for p in range(planes):
        x = initial[p].reshape(columns * rhs, width)
        tables = [picks(shared_target(row, which, p, planes), width) for which in (2, 0)]
        out.append(mt(jnp.concatenate(tables, 0), x))
        if p == 0:
            above[...] = mt(picks(first_target(rows_of(FACE)), width), x).astype(BF)
    put_shared(out, near, far)


def turned(rows):
    pad = jnp.zeros((FACE - NT,) + rows.shape[1:], rows.dtype)
    return jnp.swapaxes(jnp.concatenate([rows, pad], 0), 0, 1)


def weight_kernel(
    inverse, couplings, right, initial, neighbours_there,
    known, lower, base, own, gathers,
    inverse_in, couplings_in, right_in, neighbours, solves, faces, done,
):
    planes, columns, rhs, width = initial.shape
    size = columns * rhs
    half = columns // 2
    early = pltpu.make_async_copy(neighbours_there, neighbours, done.at[3, 0])
    early.start()
    copies = []
    for p in range(planes):
        pairs = ((inverse, inverse_in), (couplings, couplings_in), (right, right_in))
        copies.append([pltpu.make_async_copy(x.at[p], y.at[p], done.at[i, p]) for i, (x, y) in enumerate(pairs)])
        for copy in copies[p]:
            copy.start()
    for start, stop in ((5 * FACE, 256), (256 + FACE, 256 + 2 * SLOT)):
        faces[:, :, start:stop] = jnp.zeros((2, columns, stop - start, 256), BF)
    faces[:, :, :, 128:] = jnp.zeros(faces.shape[:3] + (128,), BF)
    solves[:, :, :, 128:] = jnp.zeros(solves.shape[:3] + (128,), BF)
    own_table = [picks(c_target(rows_of(FACE), which), width) for which in (2, 0)]
    first_table = picks(first_target(rows_of(FACE)), width)
    fields = [initial[p].reshape(size, width) for p in range(planes)]
    sides = [jnp.concatenate([mt(own_table[j], x).astype(BF) for x in fields], 0) for j in range(2)]
    for p in range(planes):
        own[p, LAST] = mt(first_table, fields[min(p + 1, planes - 1)]).astype(BF)
    early.wait()
    source = sources(neighbours, columns, rhs)
    for i, start in enumerate((0, size)):
        for j in range(2):
            gathers[i, j] = one_hot(source[j], start, size)
    for j in range(2):
        mine = mm(sides[j], gathers[1 - j, j]).astype(BF)
        for p in range(planes):
            own[p, j * FACE : (j + 1) * FACE] = mine[p * FACE : (p + 1) * FACE]
    lane = lax.broadcasted_iota(jnp.int32, (ROWS, 2 * SLOT), 1)

    def prepare(p):
        slot = p % 2
        for copy in copies[p]:
            copy.wait()
        faces[slot, :, 256 + SLOT : 256 + SLOT + rhs, :width] = right_in[p]
        for a in range(3):
            rows = [inverse_in[p, v * 27 + a * 9 : v * 27 + a * 9 + 9] for v in range(5)]
            solves[slot, :, a * FACE : (a + 1) * FACE, :width] = -turned(jnp.concatenate(rows, 0))
        for f, place in enumerate((256, 4 * FACE, 0, FACE, 2 * FACE, 3 * FACE)):
            faces[slot, :, place : place + FACE, :width] = turned(couplings_in[p, f])

    for p in range(planes):
        slot = p % 2
        prepare(p)
        bases, lowers = [], []
        before = None
        for c in range(columns):
            solve = solves[slot, c]
            known[p, c] = mt(solve, faces[slot, c, :256]).astype(BF)
            both = mt(solve, faces[slot, c, 256:])
            move = (c % half * rhs - SLOT) % 128
            bases.append(pltpu.roll(both, move, 1) if move else both)
            if c % 2 == 0:
                before = both
            else:
                lowers.append(jnp.where(lane < SLOT, before, pltpu.roll(both, SLOT, 1)).astype(BF))
        for h in range(2):
            lanes = slice(h * half * rhs, (h + 1) * half * rhs)
            lower[p, h, :ROWS] = jnp.concatenate(lowers[2 * h : 2 * h + 2], 1)
            base[p, :, lanes] = -own_lanes(bases[h * half : (h + 1) * half], rhs)
    chain_products(lower, LAST, range(planes))


def chain_products(matrix, rows, order):
    for h in range(2):
        total = None
        for q in order:
            step = matrix[q, h, rows]
            total = step.astype(F32) if total is None else mm(step, split_lanes(total, SLOT))
            matrix[q, h, PRODUCT] = total.astype(BF)


def gathered(near, far, own, up_sel, down_sel, gathers):
    planes = up_sel.shape[0]

    def faces(received, select):
        tail = received[planes * MAIN :]
        wholes = [jnp.concatenate([received[p * MAIN : (p + 1) * MAIN], tail], 0) for p in range(planes)]
        return [mm(select[p], wholes[p]).astype(BF) for p in range(planes)]

    low = faces(jnp.where(even(), far[...], near[...]), up_sel)
    high = faces(jnp.where(even(), near[...], far[...]), down_sel)
    sides = []
    for j, side in enumerate((low, high)):
        picked = mm(jnp.concatenate([x[FACE:] for x in side], 0), gathers[j, j]).astype(BF)
        sides.append([picked[p * FACE : (p + 1) * FACE] + own[p, j * FACE : (j + 1) * FACE] for p in range(planes)])
    return [jnp.concatenate([low[p][:FACE], high[p][:FACE], sides[0][p], sides[1][p]], 0) for p in range(planes)]


def known_part(known_c, operand, columns, rhs):
    half = columns // 2
    out = []
    for h in range(2):
        side = operand[:, h * half * rhs : (h + 1) * half * rhs]
        out.append(own_lanes([mm(known_c(h * half + c), side) for c in range(half)], rhs))
    return jnp.concatenate(out, 1)


def chain_kernel(known, base, matrix, wholes, outs, order, rows, rhs, last_face):
    part, traces, message = outs
    planes, columns = known.shape[:2]
    trace = None
    for p in order:
        whole = jnp.concatenate([wholes[p], last_face(p)], 0)
        value = base[p] + known_part(lambda c: known[p, c], whole, columns, rhs)
        part[p] = value
        value = value[rows]
        trace = value if trace is None else value + chain_step(matrix.at[p], trace, rhs, rows)
        traces[p] = trace
    message[FIRST] = trace.astype(BF)
    if message.shape[0] > FACE:
        for h in range(2):
            message[(1 + h) * FACE : (2 + h) * FACE] = matrix[order[-1], h, PRODUCT]


def forward_chain_kernel(near, far, above, own, gathers, up_sel, down_sel, known, lower, base, *outs, rhs):
    wholes = gathered(near, far, own, up_sel, down_sel, gathers)
    planes, size = len(wholes), above.shape[1]
    pad = jnp.zeros((256 - 5 * FACE, size), BF)
    last_face = lambda p: jnp.concatenate([own[p, LAST] if p + 1 < planes else above[...], pad], 0)
    chain_kernel(known, base, lower, wholes, outs, range(planes), LAST, rhs, last_face)


def backward_chain_kernel(near, far, own, gathers, up_sel, down_sel, known, upper, base, *outs, rhs):
    wholes = gathered(near, far, own, up_sel, down_sel, gathers)
    last_face = lambda p: jnp.zeros((256 - 4 * FACE, near.shape[1]), BF)
    chain_kernel(known, base, upper, wholes, outs, range(len(wholes) - 1, -1, -1), FIRST, rhs, last_face)


def incoming(messages, products, forward, rhs):
    here = lax.axis_index("sweep")
    n = messages.shape[0]
    trace = None
    for i in range(n - 1) if forward else range(n - 1, 0, -1):
        value = messages[i, FIRST].astype(F32)
        if trace is None:
            trace = jnp.zeros_like(value)
        else:
            half = value.shape[1] // 2
            halves = [trace[:, h * half : (h + 1) * half] for h in range(2)]
            value = value + jnp.concatenate([mm(m, split_lanes(t, rhs)) for m, t in zip(products(i), halves)], 1)
        trace = jnp.where(i < here if forward else i > here, value, trace)
    return trace


def forward_finish_kernel(
    messages, part, traces, lower, send, middle, change, near, far, *, rhs
):
    planes = part.shape[0]
    inside = lambda i: [messages[i, (1 + h) * FACE : (2 + h) * FACE] for h in range(2)]
    entry = incoming(messages, inside, True, rhs)
    out = []
    trace = entry
    for p in range(planes):
        delta = chain_step(lower.at[p], trace, rhs, FULL)
        change[p] = delta
        whole = (part[p] + delta).astype(BF)
        middle[p] = whole
        out.append(mm(send[p], whole))
        if p + 1 < planes:
            trace = traces[p] + chain_step(lower.at[p], entry, rhs, PRODUCT)
    put_shared(out, near, far)


def middle_kernel(middle, change, base, gathers, own_sel, known, own, out, upper):
    planes = middle.shape[0]
    mine = [mm(own_sel[...], middle[p]).astype(BF) for p in range(planes)]
    for j in range(2):
        side = jnp.concatenate([x[j * FACE : (j + 1) * FACE] for x in mine], 0)
        side = mm(side, gathers[1 - j, j]).astype(BF)
        for p in range(planes):
            own[p, j * FACE : (j + 1) * FACE] = side[p * FACE : (p + 1) * FACE]
    for p in range(planes):
        out[p] = base[p] + change[p]
    columns = known.shape[1]
    lane = lax.broadcasted_iota(jnp.int32, (ROWS, 2 * SLOT), 1)
    for p in range(planes):
        pairs = []
        for c in range(0, columns, 2):
            one, two = (known[p, c + i, :, 128:].astype(F32) for i in range(2))
            pairs.append(jnp.where(lane < SLOT, pltpu.roll(one, SLOT, 1), two).astype(BF))
        for h in range(2):
            upper[p, h, :ROWS] = jnp.concatenate(pairs[2 * h : 2 * h + 2], 1)
    chain_products(upper, FIRST, range(planes - 1, -1, -1))


def backward_finish_kernel(
    messages, near, next_near, part, traces, upper, back, result, results, sem, *, rhs
):
    planes = part.shape[0]
    here = lax.axis_index("sweep")
    beside = lambda i: [jnp.where(here + 1 == i, near[h], next_near[h]) for h in range(2)]
    entry = incoming(messages, beside, False, rhs)
    columns, _, width = result.shape[1:]
    copies = []
    trace = entry
    for p in range(planes - 1, -1, -1):
        whole = part[p] + chain_step(upper.at[p], trace, rhs, FULL)
        flat = lax.dot_general(whole.astype(BF), back[...], (((0,), (0,)), ((), ())), preferred_element_type=F32)
        results[p] = flat.astype(BF).reshape(columns, rhs, width)
        copies.append(pltpu.make_async_copy(results.at[p], result.at[p], sem.at[p]))
        copies[-1].start()
        if p:
            trace = traces[p] + chain_step(upper.at[p], entry, rhs, PRODUCT)
    for copy in copies:
        copy.wait()


def call(kernel, outs, operands, name, flops=2e8, far=(), scratch=(), out_space=pltpu.VMEM):
    shapes = [jax.ShapeDtypeStruct(s, d) for s, d in outs]
    nbytes = sum(x.size * x.dtype.itemsize for x in list(operands) + shapes)
    spaces = [pltpu.SMEM if x.dtype == jnp.int32 else pltpu.VMEM for x in operands]
    spaces = [pltpu.HBM if i in far else space for i, space in enumerate(spaces)]
    operands = [
        pltpu.with_memory_space_constraint(x, pltpu.HBM) if i in far else x for i, x in enumerate(operands)
    ]
    return pl.pallas_call(
        kernel,
        out_shape=shapes,
        in_specs=[pl.BlockSpec(memory_space=space) for space in spaces],
        out_specs=[pl.BlockSpec(memory_space=out_space)] * len(shapes),
        scratch_shapes=list(scratch),
        compiler_params=pltpu.CompilerParams(vmem_limit_bytes=24 * MIB),
        cost_estimate=pl.CostEstimate(flops=int(flops), bytes_accessed=int(nbytes), transcendentals=0),
        name=name,
    )(*operands)


def products(x, by):
    n = lax.axis_size("sweep")
    inner = range(1, n - 1)
    return [
        lax.ppermute(x, "sweep", [(i, i + step) for i in inner if 0 <= i + step < n]) for step in (by, 2 * by)
    ]


def weights(inverse, couplings, right, initial, neighbours):
    planes, columns, rhs, width = initial.shape
    size = columns * rhs
    pack = (planes, 2, ROWS + FACE, 256)
    field = (planes, ROWS, size)
    outs = [((planes, columns, ROWS, 256), BF), (pack, BF), (field, F32), (field, BF), ((2, 2, size, size), BF)]
    operands = (inverse, couplings, right, initial, neighbours)
    scratch = [pltpu.VMEM(x.shape, BF) for x in operands[:3]] + [
        pltpu.SMEM(neighbours.shape, jnp.int32),
        pltpu.VMEM((2, columns, ROWS, 256), BF),
        pltpu.VMEM((2, columns, 256 + 2 * SLOT, 256), BF),
        pltpu.SemaphoreType.DMA((4, planes)),
    ]
    return call(weight_kernel, outs, operands, "weights", 1e10, (0, 1, 2, 4), scratch)


def swapped(x, axis, first):
    n = lax.axis_size(axis)
    pairs = [(i, (i + 1) % n) for i in range(first, n, 2)]
    return lax.ppermute(x, axis, [pair for i, j in pairs for pair in ((i, j), (j, i))])


def shift(x, axis, by):
    n = lax.axis_size(axis)
    return lax.ppermute(x, axis, [(i, i + by) for i in range(n) if 0 <= i + by < n])


def local(right_sides, initial, inverse_blocks, couplings, neighbours):
    planes, columns, rhs, width = initial.shape
    size = columns * rhs
    const = lambda x: jnp.asarray(x, BF)
    send_in = const(send_table(ROWS, inner, planes))
    own_in = const(own_table(ROWS, inner))
    back = const(table(ROWS, width, [(inner(*n), n) for n in NODES], natural))
    up_sel = const(receive_table(2, planes))
    down_sel = const(receive_table(0, planes))
    beside = neighbours.T

    share = (planes * MAIN + tail_rows(planes), size)
    near, far, above = call(
        first_kernel,
        [(share, BF), (share, BF), ((FACE, size), BF)],
        (initial,),
        "initial_traces",
    )
    near, far, above, initial = lax.optimization_barrier((near, far, above, initial))
    near, far = swapped(near, "cross", 0), swapped(far, "cross", 1)
    from_above = shift(above, "sweep", -1)
    known, lower, base, own, gathers = weights(
        inverse_blocks.transpose(0, 2, 1, 3), couplings.transpose(0, 2, 3, 1, 4), right_sides, initial, beside
    )

    field = (planes, ROWS, size)
    trace = (planes, FACE, size)
    chain_outs = [(field, F32), (trace, F32)]
    part, traces, message = call(
        functools.partial(forward_chain_kernel, rhs=rhs),
        chain_outs + [((3 * FACE, size), BF)],
        (near, far, from_above, own, gathers, up_sel, down_sel, known, lower, base),
        "forward_chain",
    )
    messages = lax.all_gather(message, "sweep")
    middle, change, near, far = call(
        functools.partial(forward_finish_kernel, rhs=rhs),
        [(field, BF), (field, F32), (share, BF), (share, BF)],
        (messages, part, traces, lower, send_in),
        "forward_finish",
    )
    near, far = swapped(near, "cross", 0), swapped(far, "cross", 1)
    own, base, upper = call(
        middle_kernel,
        [((planes, 2 * FACE, size), BF), (field, F32), (lower.shape, BF)],
        (middle, change, base, gathers, own_in, known),
        "middle",
        2e9,
    )
    own, pass_b = lax.optimization_barrier((own, upper[0, :, PRODUCT]))
    passes = products(pass_b, -1)
    part, traces, message = call(
        functools.partial(backward_chain_kernel, rhs=rhs),
        chain_outs + [((FACE, size), BF)],
        (near, far, own, gathers, up_sel, down_sel, known, upper, base),
        "backward_chain",
    )
    messages = lax.all_gather(message, "sweep")
    (result,) = call(
        functools.partial(backward_finish_kernel, rhs=rhs),
        [(right_sides.shape, BF)],
        (messages, *passes, part, traces, upper, back),
        "backward_finish",
        scratch=[pltpu.VMEM(right_sides.shape, BF), pltpu.SemaphoreType.DMA((planes,))],
        out_space=pltpu.HBM,
    )
    return result


def solution(mesh):
    return jax.shard_map(
        local,
        mesh=mesh,
        in_specs=(
            P("sweep", "cross", None, None),
            P("sweep", "cross", None, None),
            P("sweep", "cross", None, None),
            P("sweep", "cross", None, None, None),
            P("cross", None),
        ),
        out_specs=P("sweep", "cross", None, None),
        check_vma=False,
    )
```

```python
import functools

import jax
import jax.numpy as jnp
import numpy as np
from jax import lax
from jax.experimental import pallas as pl
from jax.experimental.pallas import tpu as pltpu
from jax.sharding import PartitionSpec as P

BF = jnp.bfloat16
F32 = jnp.float32
NT = 45
FACE = 48
SLOT = 64
ROWS = 3 * FACE
SHARED = 75
MAIN = 64
MIB = 1 << 20
FIRST = slice(0, FACE)
LAST = slice(2 * FACE, ROWS)
FULL = slice(0, ROWS)
PRODUCT = slice(ROWS, ROWS + FACE)


def natural(v, a, b, c):
    return v * 27 + a * 9 + b * 3 + c


def inner(v, a, b, c):
    return a * FACE + v * 9 + b * 3 + c


NODES = [(v, a, b, c) for v in range(5) for a in range(3) for b in range(3) for c in range(3)]


def face_nodes(place, which):
    return [n for n in NODES if n[1 + place] == which]


def table(height, width, rows, column_of):
    out = np.zeros((height, width), np.float32)
    for row, node in rows:
        out[row, column_of(*node)] = 1
    return out


def block(nodes, start=0):
    return [(start + i, n) for i, n in enumerate(nodes)]


def tail_rows(planes):
    return -(-planes * (SHARED - MAIN) // 16) * 16


def union_nodes(which):
    others = [b for b in range(3) if b != which]
    spots = [(which, c) for c in range(3)] + [(b, which) for b in others]
    return [(v, a, b, c) for v in range(5) for a in range(3) for b, c in spots]


def place_of(i, plane):
    return i if i < MAIN else i + plane * (SHARED - MAIN)


def send_table(width, column_of, planes):
    height = MAIN + tail_rows(planes)
    out = []
    for p in range(planes):
        rows = [(place_of(i, p), n) for i, n in enumerate(union_nodes(2))]
        rows += [(height + place_of(i, p), n) for i, n in enumerate(union_nodes(0))]
        out.append(table(2 * height, width, rows, column_of))
    return np.stack(out)


def own_table(width, column_of):
    rows = block(face_nodes(2, 2)) + block(face_nodes(2, 0), FACE)
    return table(2 * FACE, width, rows, column_of)


def receive_table(which, planes):
    rows = block(face_nodes(1, which)) + block(face_nodes(2, which), FACE)
    out = []
    for p in range(planes):
        place = {n: place_of(i, p) for i, n in enumerate(union_nodes(which))}
        out.append(table(2 * FACE, MAIN + tail_rows(planes), rows, lambda *n: place[n]))
    return np.stack(out)


def mm(a, b):
    return lax.dot_general(a, b, (((1,), (0,)), ((), ())), preferred_element_type=F32)


def mt(a, b):
    return lax.dot_general(a, b, (((1,), (1,)), ((), ())), preferred_element_type=F32)


def group(shape, width, at):
    lane = lax.broadcasted_iota(jnp.int32, shape, 1)
    return (lane >= at * width) & (lane < (at + 1) * width)


def split_lanes(value, width):
    lanes = value.shape[1]
    value = value.astype(F32)
    pad = jnp.zeros((SLOT - FACE, lanes), BF)
    parts = []
    for c in range(lanes // width):
        parts += [jnp.where(group(value.shape, width, c), value, 0.0).astype(BF), pad]
    return jnp.concatenate(parts, 0)


def own_lanes(values, width):
    out = values[0]
    for c in range(1, len(values)):
        out = jnp.where(group(out.shape, width, c), values[c], out)
    return out


def one_hot(source, start, height):
    row = lax.broadcasted_iota(jnp.int32, (height, source.shape[1]), 0) + start
    return jnp.where(row == source, 1.0, 0.0).astype(BF)


def chain_step(matrix, trace, rhs, rows=slice(None)):
    half = trace.shape[1] // 2
    return jnp.concatenate(
        [mm(matrix[h, rows], split_lanes(trace[:, h * half : (h + 1) * half], rhs)) for h in range(2)], 1
    )


def shared_target(row, which, plane, planes):
    rest = SHARED - MAIN
    i = jnp.where(row < MAIN, row, row - plane * rest)
    k = i % 15
    a = k // 5
    j = k % 5
    b = jnp.where(j < 3, which, j - 3 if which == 2 else j - 2)
    c = jnp.where(j < 3, j, which)
    inside = (row < MAIN) | ((i >= MAIN) & (i < SHARED))
    return jnp.where(inside, i // 15 * 27 + a * 9 + b * 3 + c, -1)


def picks(target, width):
    lane = lax.broadcasted_iota(jnp.int32, (target.shape[0], width), 1)
    return jnp.where(lane == target, 1.0, 0.0).astype(BF)


def rows_of(height):
    return lax.broadcasted_iota(jnp.int32, (height, 1), 0)


def first_target(row):
    return jnp.where(row < NT, row // 9 * 27 + row % 9, -1)


def c_target(row, which):
    return jnp.where(row < NT, row * 3 + which, -1)


def sources(neighbours, columns, rhs):
    place = lax.axis_index("cross")
    total = columns * lax.axis_size("cross")
    lane = lax.broadcasted_iota(jnp.int32, (1, columns * rhs), 1)
    out = []
    for face, first in ((2, place - 1), (3, place)):
        source = lane
        for c in range(columns):
            at = neighbours[face, c] - first * columns
            at = jnp.where(at < 0, at + total, at)
            at = jnp.where(at >= total, at - total, at)
            source = jnp.where(lane >= c * rhs, lane + (at - c) * rhs, source)
        out.append(source)
    return out


def even():
    return lax.rem(lax.axis_index("cross"), 2) == 0


def put_shared(out, near, far):
    height = out[0].shape[0] // 2
    messages = []
    for start in (0, height):
        tails = [x[start + MAIN : start + height] for x in out]
        parts = [x[start : start + MAIN] for x in out] + [sum(tails[1:], tails[0])]
        messages.append(jnp.concatenate(parts, 0))
    up, down = messages
    near[...] = jnp.where(even(), up, down).astype(BF)
    far[...] = jnp.where(even(), down, up).astype(BF)


def first_kernel(initial, near, far, above):
    planes, columns, rhs, width = initial.shape
    row = rows_of(MAIN + tail_rows(planes))
    out = []
    for p in range(planes):
        x = initial[p].reshape(columns * rhs, width)
        tables = [picks(shared_target(row, which, p, planes), width) for which in (2, 0)]
        out.append(mt(jnp.concatenate(tables, 0), x))
        if p == 0:
            above[...] = mt(picks(first_target(rows_of(FACE)), width), x).astype(BF)
    put_shared(out, near, far)


def turned(rows):
    pad = jnp.zeros((FACE - NT,) + rows.shape[1:], rows.dtype)
    return jnp.swapaxes(jnp.concatenate([rows, pad], 0), 0, 1)


def weight_kernel(
    inverse, couplings, right, initial, neighbours_there,
    known, lower, base, own, gathers,
    inverse_in, couplings_in, right_in, neighbours, solves, faces, done,
):
    planes, columns, rhs, width = initial.shape
    size = columns * rhs
    half = columns // 2
    early = pltpu.make_async_copy(neighbours_there, neighbours, done.at[3, 0])
    early.start()
    copies = []
    for p in range(planes):
        pairs = ((inverse, inverse_in), (couplings, couplings_in), (right, right_in))
        copies.append([pltpu.make_async_copy(x.at[p], y.at[p], done.at[i, p]) for i, (x, y) in enumerate(pairs)])
        for copy in copies[p]:
            copy.start()
    for start, stop in ((5 * FACE, 256), (256 + FACE, 256 + 2 * SLOT)):
        faces[:, :, start:stop] = jnp.zeros((2, columns, stop - start, 256), BF)
    faces[:, :, :, 128:] = jnp.zeros(faces.shape[:3] + (128,), BF)
    solves[:, :, :, 128:] = jnp.zeros(solves.shape[:3] + (128,), BF)
    own_table = [picks(c_target(rows_of(FACE), which), width) for which in (2, 0)]
    first_table = picks(first_target(rows_of(FACE)), width)
    fields = [initial[p].reshape(size, width) for p in range(planes)]
    sides = [jnp.concatenate([mt(own_table[j], x).astype(BF) for x in fields], 0) for j in range(2)]
    for p in range(planes):
        own[p, LAST] = mt(first_table, fields[min(p + 1, planes - 1)]).astype(BF)
    early.wait()
    source = sources(neighbours, columns, rhs)
    for i, start in enumerate((0, size)):
        for j in range(2):
            gathers[i, j] = one_hot(source[j], start, size)
    for j in range(2):
        mine = mm(sides[j], gathers[1 - j, j]).astype(BF)
        for p in range(planes):
            own[p, j * FACE : (j + 1) * FACE] = mine[p * FACE : (p + 1) * FACE]
    lane = lax.broadcasted_iota(jnp.int32, (ROWS, 2 * SLOT), 1)

    def prepare(p):
        slot = p % 2
        for copy in copies[p]:
            copy.wait()
        faces[slot, :, 256 + SLOT : 256 + SLOT + rhs, :width] = right_in[p]
        for a in range(3):
            rows = [inverse_in[p, v * 27 + a * 9 : v * 27 + a * 9 + 9] for v in range(5)]
            solves[slot, :, a * FACE : (a + 1) * FACE, :width] = -turned(jnp.concatenate(rows, 0))
        for f, place in enumerate((256, 4 * FACE, 0, FACE, 2 * FACE, 3 * FACE)):
            faces[slot, :, place : place + FACE, :width] = turned(couplings_in[p, f])

    totals = [None, None]

    def carry(q):
        for h in range(2):
            step = lower[q, h, LAST]
            totals[h] = mm(step, split_lanes(totals[h], SLOT)) if q else step.astype(F32)
            lower[q, h, PRODUCT] = totals[h].astype(BF)

    for p in range(planes):
        slot = p % 2
        prepare(p)
        if p:
            carry(p - 1)
        bases, lowers = [], []
        before = None
        for c in range(columns):
            solve = solves[slot, c]
            known[p, c] = mt(solve, faces[slot, c, :256]).astype(BF)
            both = mt(solve, faces[slot, c, 256:])
            move = (c % half * rhs - SLOT) % 128
            bases.append(pltpu.roll(both, move, 1) if move else both)
            if c % 2 == 0:
                before = both
            else:
                lowers.append(jnp.where(lane < SLOT, before, pltpu.roll(both, SLOT, 1)).astype(BF))
        for h in range(2):
            lanes = slice(h * half * rhs, (h + 1) * half * rhs)
            lower[p, h, :ROWS] = jnp.concatenate(lowers[2 * h : 2 * h + 2], 1)
            base[p, :, lanes] = -own_lanes(bases[h * half : (h + 1) * half], rhs)
    carry(planes - 1)


def chain_products(matrix, rows, order):
    for h in range(2):
        total = None
        for q in order:
            step = matrix[q, h, rows]
            total = step.astype(F32) if total is None else mm(step, split_lanes(total, SLOT))
            matrix[q, h, PRODUCT] = total.astype(BF)


def gathered(near, far, own, up_sel, down_sel, gathers):
    planes = up_sel.shape[0]

    def faces(received, select):
        tail = received[planes * MAIN :]
        wholes = [jnp.concatenate([received[p * MAIN : (p + 1) * MAIN], tail], 0) for p in range(planes)]
        return [mm(select[p], wholes[p]).astype(BF) for p in range(planes)]

    low = faces(jnp.where(even(), far[...], near[...]), up_sel)
    high = faces(jnp.where(even(), near[...], far[...]), down_sel)
    sides = []
    for j, side in enumerate((low, high)):
        picked = mm(jnp.concatenate([x[FACE:] for x in side], 0), gathers[j, j]).astype(BF)
        sides.append([picked[p * FACE : (p + 1) * FACE] + own[p, j * FACE : (j + 1) * FACE] for p in range(planes)])
    return [jnp.concatenate([low[p][:FACE], high[p][:FACE], sides[0][p], sides[1][p]], 0) for p in range(planes)]


def known_part(known_c, operand, columns, rhs):
    half = columns // 2
    out = []
    for h in range(2):
        side = operand[:, h * half * rhs : (h + 1) * half * rhs]
        out.append(own_lanes([mm(known_c(h * half + c), side) for c in range(half)], rhs))
    return jnp.concatenate(out, 1)


def chain_kernel(known, base, matrix, wholes, outs, order, rows, rhs, last_face):
    part, traces, message = outs
    planes, columns = known.shape[:2]
    trace = None
    for p in order:
        whole = jnp.concatenate([wholes[p], last_face(p)], 0)
        value = base[p] + known_part(lambda c: known[p, c], whole, columns, rhs)
        part[p] = value
        value = value[rows]
        trace = value if trace is None else value + chain_step(matrix.at[p], trace, rhs, rows)
        traces[p] = trace
    message[FIRST] = trace.astype(BF)
    if message.shape[0] > FACE:
        for h in range(2):
            message[(1 + h) * FACE : (2 + h) * FACE] = matrix[order[-1], h, PRODUCT]


def forward_chain_kernel(near, far, above, own, gathers, up_sel, down_sel, known, lower, base, *outs, rhs):
    wholes = gathered(near, far, own, up_sel, down_sel, gathers)
    planes, size = len(wholes), above.shape[1]
    pad = jnp.zeros((256 - 5 * FACE, size), BF)
    last_face = lambda p: jnp.concatenate([own[p, LAST] if p + 1 < planes else above[...], pad], 0)
    chain_kernel(known, base, lower, wholes, outs, range(planes), LAST, rhs, last_face)


def backward_chain_kernel(near, far, own, gathers, up_sel, down_sel, known, upper, base, *outs, rhs):
    wholes = gathered(near, far, own, up_sel, down_sel, gathers)
    last_face = lambda p: jnp.zeros((256 - 4 * FACE, near.shape[1]), BF)
    chain_kernel(known, base, upper, wholes, outs, range(len(wholes) - 1, -1, -1), FIRST, rhs, last_face)


def incoming(messages, products, forward, rhs):
    here = lax.axis_index("sweep")
    n = messages.shape[0]
    trace = None
    for i in range(n - 1) if forward else range(n - 1, 0, -1):
        value = messages[i, FIRST].astype(F32)
        if trace is None:
            trace = jnp.zeros_like(value)
        else:
            half = value.shape[1] // 2
            halves = [trace[:, h * half : (h + 1) * half] for h in range(2)]
            value = value + jnp.concatenate([mm(m, split_lanes(t, rhs)) for m, t in zip(products(i), halves)], 1)
        trace = jnp.where(i < here if forward else i > here, value, trace)
    return trace


def forward_finish_kernel(
    messages, part, traces, lower, send, middle, change, near, far, *, rhs
):
    planes = part.shape[0]
    inside = lambda i: [messages[i, (1 + h) * FACE : (2 + h) * FACE] for h in range(2)]
    entry = incoming(messages, inside, True, rhs)
    out = []
    trace = entry
    for p in range(planes):
        delta = chain_step(lower.at[p], trace, rhs, FULL)
        change[p] = delta
        whole = (part[p] + delta).astype(BF)
        middle[p] = whole
        out.append(mm(send[p], whole))
        if p + 1 < planes:
            trace = traces[p] + chain_step(lower.at[p], entry, rhs, PRODUCT)
    put_shared(out, near, far)


def middle_kernel(middle, change, base, gathers, own_sel, known, own, out, upper):
    planes = middle.shape[0]
    mine = [mm(own_sel[...], middle[p]).astype(BF) for p in range(planes)]
    for j in range(2):
        side = jnp.concatenate([x[j * FACE : (j + 1) * FACE] for x in mine], 0)
        side = mm(side, gathers[1 - j, j]).astype(BF)
        for p in range(planes):
            own[p, j * FACE : (j + 1) * FACE] = side[p * FACE : (p + 1) * FACE]
    for p in range(planes):
        out[p] = base[p] + change[p]
    columns = known.shape[1]
    lane = lax.broadcasted_iota(jnp.int32, (ROWS, 2 * SLOT), 1)
    for p in range(planes):
        pairs = []
        for c in range(0, columns, 2):
            one, two = (known[p, c + i, :, 128:].astype(F32) for i in range(2))
            pairs.append(jnp.where(lane < SLOT, pltpu.roll(one, SLOT, 1), two).astype(BF))
        for h in range(2):
            upper[p, h, :ROWS] = jnp.concatenate(pairs[2 * h : 2 * h + 2], 1)
    chain_products(upper, FIRST, range(planes - 1, -1, -1))


def backward_finish_kernel(
    messages, near, next_near, part, traces, upper, back, result, results, sem, *, rhs
):
    planes = part.shape[0]
    here = lax.axis_index("sweep")
    beside = lambda i: [jnp.where(here + 1 == i, near[h], next_near[h]) for h in range(2)]
    entry = incoming(messages, beside, False, rhs)
    columns, _, width = result.shape[1:]
    copies = []
    trace = entry
    for p in range(planes - 1, -1, -1):
        whole = part[p] + chain_step(upper.at[p], trace, rhs, FULL)
        flat = lax.dot_general(whole.astype(BF), back[...], (((0,), (0,)), ((), ())), preferred_element_type=F32)
        results[p] = flat.astype(BF).reshape(columns, rhs, width)
        copies.append(pltpu.make_async_copy(results.at[p], result.at[p], sem.at[p]))
        copies[-1].start()
        if p:
            trace = traces[p] + chain_step(upper.at[p], entry, rhs, PRODUCT)
    for copy in copies:
        copy.wait()


def call(kernel, outs, operands, name, flops=2e8, far=(), scratch=(), out_space=pltpu.VMEM):
    shapes = [jax.ShapeDtypeStruct(s, d) for s, d in outs]
    nbytes = sum(x.size * x.dtype.itemsize for x in list(operands) + shapes)
    spaces = [pltpu.SMEM if x.dtype == jnp.int32 else pltpu.VMEM for x in operands]
    spaces = [pltpu.HBM if i in far else space for i, space in enumerate(spaces)]
    operands = [
        pltpu.with_memory_space_constraint(x, pltpu.HBM) if i in far else x for i, x in enumerate(operands)
    ]
    return pl.pallas_call(
        kernel,
        out_shape=shapes,
        in_specs=[pl.BlockSpec(memory_space=space) for space in spaces],
        out_specs=[pl.BlockSpec(memory_space=out_space)] * len(shapes),
        scratch_shapes=list(scratch),
        compiler_params=pltpu.CompilerParams(vmem_limit_bytes=24 * MIB),
        cost_estimate=pl.CostEstimate(flops=int(flops), bytes_accessed=int(nbytes), transcendentals=0),
        name=name,
    )(*operands)


def products(x, by):
    n = lax.axis_size("sweep")
    inner = range(1, n - 1)
    return [
        lax.ppermute(x, "sweep", [(i, i + step) for i in inner if 0 <= i + step < n]) for step in (by, 2 * by)
    ]


def weights(inverse, couplings, right, initial, neighbours):
    planes, columns, rhs, width = initial.shape
    size = columns * rhs
    pack = (planes, 2, ROWS + FACE, 256)
    field = (planes, ROWS, size)
    outs = [((planes, columns, ROWS, 256), BF), (pack, BF), (field, F32), (field, BF), ((2, 2, size, size), BF)]
    operands = (inverse, couplings, right, initial, neighbours)
    scratch = [pltpu.VMEM(x.shape, BF) for x in operands[:3]] + [
        pltpu.SMEM(neighbours.shape, jnp.int32),
        pltpu.VMEM((2, columns, ROWS, 256), BF),
        pltpu.VMEM((2, columns, 256 + 2 * SLOT, 256), BF),
        pltpu.SemaphoreType.DMA((4, planes)),
    ]
    return call(weight_kernel, outs, operands, "weights", 1e10, (0, 1, 2, 4), scratch)


def swapped(x, axis, first):
    n = lax.axis_size(axis)
    pairs = [(i, (i + 1) % n) for i in range(first, n, 2)]
    return lax.ppermute(x, axis, [pair for i, j in pairs for pair in ((i, j), (j, i))])


def shift(x, axis, by):
    n = lax.axis_size(axis)
    return lax.ppermute(x, axis, [(i, i + by) for i in range(n) if 0 <= i + by < n])


def local(right_sides, initial, inverse_blocks, couplings, neighbours):
    planes, columns, rhs, width = initial.shape
    size = columns * rhs
    const = lambda x: jnp.asarray(x, BF)
    send_in = const(send_table(ROWS, inner, planes))
    own_in = const(own_table(ROWS, inner))
    back = const(table(ROWS, width, [(inner(*n), n) for n in NODES], natural))
    up_sel = const(receive_table(2, planes))
    down_sel = const(receive_table(0, planes))
    beside = neighbours.T

    share = (planes * MAIN + tail_rows(planes), size)
    near, far, above = call(
        first_kernel,
        [(share, BF), (share, BF), ((FACE, size), BF)],
        (initial,),
        "initial_traces",
    )
    near, far, above, initial = lax.optimization_barrier((near, far, above, initial))
    near, far = swapped(near, "cross", 0), swapped(far, "cross", 1)
    from_above = shift(above, "sweep", -1)
    known, lower, base, own, gathers = weights(
        inverse_blocks.transpose(0, 2, 1, 3), couplings.transpose(0, 2, 3, 1, 4), right_sides, initial, beside
    )

    field = (planes, ROWS, size)
    trace = (planes, FACE, size)
    chain_outs = [(field, F32), (trace, F32)]
    part, traces, message = call(
        functools.partial(forward_chain_kernel, rhs=rhs),
        chain_outs + [((3 * FACE, size), BF)],
        (near, far, from_above, own, gathers, up_sel, down_sel, known, lower, base),
        "forward_chain",
    )
    messages = lax.all_gather(message, "sweep")
    middle, change, near, far = call(
        functools.partial(forward_finish_kernel, rhs=rhs),
        [(field, BF), (field, F32), (share, BF), (share, BF)],
        (messages, part, traces, lower, send_in),
        "forward_finish",
    )
    near, far = swapped(near, "cross", 0), swapped(far, "cross", 1)
    own, base, upper = call(
        middle_kernel,
        [((planes, 2 * FACE, size), BF), (field, F32), (lower.shape, BF)],
        (middle, change, base, gathers, own_in, known),
        "middle",
        2e9,
    )
    own, pass_b = lax.optimization_barrier((own, upper[0, :, PRODUCT]))
    passes = products(pass_b, -1)
    part, traces, message = call(
        functools.partial(backward_chain_kernel, rhs=rhs),
        chain_outs + [((FACE, size), BF)],
        (near, far, own, gathers, up_sel, down_sel, known, upper, base),
        "backward_chain",
    )
    messages = lax.all_gather(message, "sweep")
    (result,) = call(
        functools.partial(backward_finish_kernel, rhs=rhs),
        [(right_sides.shape, BF)],
        (messages, *passes, part, traces, upper, back),
        "backward_finish",
        scratch=[pltpu.VMEM(right_sides.shape, BF), pltpu.SemaphoreType.DMA((planes,))],
        out_space=pltpu.HBM,
    )
    return result


def solution(mesh):
    return jax.shard_map(
        local,
        mesh=mesh,
        in_specs=(
            P("sweep", "cross", None, None),
            P("sweep", "cross", None, None),
            P("sweep", "cross", None, None),
            P("sweep", "cross", None, None, None),
            P("cross", None),
        ),
        out_specs=P("sweep", "cross", None, None),
        check_vma=False,
    )
```
